256 devices in a mesh: tgt: 8 (over y, core), src: 32 (over x, z).
Axes of the slice: x: 4, y: 4, z: 8, core: 2. Of those that a mesh axis runs over, the one named last changes fastest.
Arguments:
- queries: bfloat16 [4096, 1024], P(('tgt', 'src')), may hold values from -6 to 6
- keys: bfloat16 [8192, 1024], P('src'), may hold values from -6 to 6
- values: bfloat16 [8192, 1024], P('src'), may hold values from -6 to 6
- grad_out: bfloat16 [4096, 1024], P(('tgt', 'src')), may hold values from -6 to 6
- read_len: int32 [4096], P('tgt'), may hold values from 128 to 8192, as said below
Outputs:
- grad_queries: float32 [4096, 1024], P(('tgt', 'src'))
- grad_keys: float32 [8192, 1024], P('src', 'tgt')
- grad_values: float32 [8192, 1024], P('src', 'tgt')
The draws below stay inside these ranges and needn't reach their ends.
Inputs may be any that keep to these rules, and one draw needn't show every extreme that they name: `read_len`: multiples of 128, never falling along the target tokens; the first token reads 128 frames and the last reads all 8192.
All inputs are finite; a program needn't handle non-finite values.
Results may differ from the reference program's by a relative error of at most 0.008.
Values may be sent and summed in bfloat16 or wider, within the bound.
A program may use at most 64 MiB of HBM per device.

```python
import math
import jax
import jax.numpy as jnp
from jax import lax

H = 16
DH = 64
D = 1024
TGT_DEV = 512
TGT = 4096
SRC = 8192


def draw_queries(key, part):
    key = jax.random.fold_in(key, 1)
    base = jnp.clip(jax.random.normal(key, (TGT, D), jnp.float32), -4.0, 4.0)
    return base.astype(jnp.bfloat16)


def draw_keys(key, part):
    key = jax.random.fold_in(key, 2)
    base = jnp.clip(jax.random.normal(key, (SRC, D), jnp.float32), -4.0, 4.0)
    return base.astype(jnp.bfloat16)


def draw_read_len(key, part):
    key = jax.random.fold_in(key, 3)
    blocks = SRC // 128
    picks = jnp.sort(jax.random.randint(key, (TGT,), 1, blocks + 1))
    picks = picks.at[0].set(1).at[TGT - 1].set(blocks)
    return (picks * 128).astype(jnp.int32)


def shard_levels(own_key, extent, pieces, least, largest):
    factor_of = 1.0
    for axis_at, parts in pieces:
        draws = jax.random.uniform(jax.random.fold_in(jax.random.fold_in(own_key, 6), axis_at), (parts,), jnp.float32, least / len(pieces), largest / len(pieces))
        factor_of = factor_of * jnp.repeat(jnp.exp(draws), extent[axis_at] // parts).reshape((-1,) + (1,) * (len(extent) - 1 - axis_at))
    return factor_of


def scatter_about(stream_key, shape, scale, bound, pieces=(), kind=jnp.bfloat16):
    result = jax.random.normal(stream_key, shape, jnp.float32) * scale
    if len(pieces) > 0:
        result = shard_levels(stream_key, shape, pieces, -0.22, 0.18) * result
    return jnp.clip(result, min=-bound, max=bound).astype(kind)


def setup_inputs(seed: int = 0) -> dict:
    splits = jax.random.split(jax.random.key(seed), 6)
    queries = draw_queries(jax.random.fold_in(splits[5], 71), 0)
    keys = draw_keys(jax.random.fold_in(splits[5], 71), 0)
    values = scatter_about(splits[2], (SRC, D), 1.0, 6.0, ((0, 32),))
    grad_out = scatter_about(splits[3], (TGT, D), 1.0, 6.0, ((0, 256),))
    read_len = draw_read_len(jax.random.fold_in(splits[5], 71), 0)
    return {"queries": queries, "keys": keys, "values": values, "grad_out": grad_out, "read_len": read_len}


masked_score = -1e+30

def head_grads(query_head, key_head, value_head, grad_head, read_len):
    frames_all = key_head.shape[0]
    count = query_head.shape[0] // TGT_DEV
    positions = jnp.arange(frames_all, dtype=jnp.int32)
    scale = 1.0 / math.sqrt(DH)

    def step(carry, item):
        query_blk, grad_blk, length_blk = item
        raw = jnp.dot(query_blk, key_head.T, preferred_element_type=jnp.float32) * scale
        visible = positions[None, :] < length_blk[:, None]
        scored = jnp.where(visible, raw, masked_score)
        top = lax.optimization_barrier(jnp.max(scored, axis=1, keepdims=True))
        weights = jnp.where(visible, jnp.exp(scored - top), 0.0)
        total = lax.optimization_barrier(jnp.sum(weights, axis=1, keepdims=True))
        grad_prob = jnp.dot(grad_blk, value_head.T, preferred_element_type=jnp.float32)
        row_term = lax.optimization_barrier(jnp.sum(weights * grad_prob, axis=1, keepdims=True)) / total
        prob = weights / total
        grad_score = (prob * (grad_prob - row_term)).astype(jnp.bfloat16)
        prob_b = prob.astype(jnp.bfloat16)
        grad_v = carry[1] + jnp.dot(prob_b.T, grad_blk, preferred_element_type=jnp.float32)
        grad_k = carry[0] + jnp.dot(grad_score.T, query_blk, preferred_element_type=jnp.float32) * scale
        grad_q = jnp.dot(grad_score, key_head, preferred_element_type=jnp.float32) * scale
        return ((grad_k, grad_v), grad_q)
    start = (jnp.zeros((frames_all, DH), jnp.float32), jnp.zeros((frames_all, DH), jnp.float32))
    items = (query_head.reshape(count, TGT_DEV, DH), grad_head.reshape(count, TGT_DEV, DH), read_len.astype(jnp.int32).reshape(count, TGT_DEV))
    (grad_k, grad_v), grad_q = lax.scan(step, start, items)
    return (grad_q.reshape(count * TGT_DEV, DH), grad_k, grad_v)

def reference(queries, keys, values, grad_out, read_len):
    tokens = queries.shape[0]
    frames_all = keys.shape[0]
    query_heads = queries.reshape(tokens, H, DH).transpose(1, 0, 2)
    grad_heads = grad_out.reshape(tokens, H, DH).transpose(1, 0, 2)
    key_heads = keys.reshape(frames_all, H, DH).transpose(1, 0, 2)
    value_heads = values.reshape(frames_all, H, DH).transpose(1, 0, 2)
    grad_q, grad_k, grad_v = lax.map(lambda items: head_grads(items[0], items[1], items[2], items[3], read_len), (query_heads, key_heads, value_heads, grad_heads))
    grad_queries = grad_q.transpose(1, 0, 2).reshape(tokens, H * DH)
    grad_keys = grad_k.transpose(1, 0, 2).reshape(frames_all, H * DH)
    grad_values = grad_v.transpose(1, 0, 2).reshape(frames_all, H * DH)
    return (grad_queries, grad_keys, grad_values)
```

```python
import jax
import jax.numpy as jnp
from jax import lax
from jax.experimental import pallas as pl
from jax.experimental.pallas import tpu as pltpu
from jax.sharding import PartitionSpec as P

MESH = pl.DeviceIdType.MESH
NX, NZ = 4, 8
COLS = 128
MASK_BLOCK = 128
F32, BF16 = jnp.float32, jnp.bfloat16
HIDDEN = -1e30
SCALE = 0.125

REL = [0]
for _d in range(1, NZ // 2 + 1):
    REL += [_d] if 2 * _d == NZ else [_d, NZ - _d]
POS = {d: p for p, d in enumerate(REL)}


def kernel(
    NT, q_hbm, k_hbm, v_hbm, g_hbm, len_ref, dq_out, dk_out, dv_out,
    QG, KV, L, lrow, M, K2, V2, KT, W, G, MR, ST, CF, RT, DQS, DQR, DQO, DQF, DQI, DK, DV, DKVS, DKVR,
    lsem, as_, ar, bs, br, cs, cr, ds_, dr, es, er, fs, fr, gs, gr,
):
    t = lax.axis_index("tgt")
    s = lax.axis_index("src")
    x = s // NZ
    z = s % NZ
    R, F = q_hbm.shape[0], k_hbm.shape[0]
    TOK = NT * R
    CH = 2 * TOK
    NC = NZ // 2

    def tpeer(d):
        return (lax.rem(t + d, NT), s)

    def zpeer(d):
        return (t, x * NZ + lax.rem(z + d, NZ))

    def xpeer(d):
        return (t, lax.rem(x + d, NX) * NZ + z)

    def cols(i):
        return pl.ds(pl.multiple_of(i * COLS, COLS), COLS)

    def remote(src, dst, ssem, rsem, dev):
        return pltpu.make_async_remote_copy(
            src_ref=src, dst_ref=dst, send_sem=ssem, recv_sem=rsem, device_id=dev, device_id_type=MESH
        )

    local = [
        pltpu.make_async_copy(q_hbm.at[:, cols(t)], QG.at[0, 0, t], lsem.at[0]),
        pltpu.make_async_copy(g_hbm.at[:, cols(t)], QG.at[0, 1, t], lsem.at[1]),
        pltpu.make_async_copy(k_hbm.at[:, cols(t)], KV.at[0, 0], lsem.at[2]),
        pltpu.make_async_copy(v_hbm.at[:, cols(t)], KV.at[0, 1], lsem.at[3]),
    ]
    for copy in local:
        copy.start()
    row = len_ref[pl.ds(x, 1), :].astype(F32)
    lrow[...] = jnp.broadcast_to(row, lrow.shape)
    L[pl.ds(t, 1)] = jnp.broadcast_to(row[None], (1,) + lrow.shape)

    barrier = pltpu.get_barrier_semaphore()
    peers = [tpeer(d) for d in range(1, NT)] + [zpeer(d) for d in range(1, NZ)] + [xpeer(d) for d in range(1, NX)]
    for dev in peers:
        pl.semaphore_signal(barrier, inc=1, device_id=dev, device_id_type=MESH)
    pl.semaphore_wait(barrier, len(peers))

    sent = []
    for d in range(1, NT):
        there = lax.rem(t + d, NT)
        sent += [
            remote(q_hbm.at[:, cols(there)], QG.at[0, 0, t], as_.at[0, d], ar.at[0, d], tpeer(d)),
            remote(g_hbm.at[:, cols(there)], QG.at[0, 1, t], as_.at[1, d], ar.at[1, d], tpeer(d)),
            remote(lrow, L.at[t], as_.at[2, d], ar.at[2, d], tpeer(d)),
        ]
    for d in range(1, NX):
        sent += [
            remote(k_hbm.at[:, cols(t)], KV.at[NX - d, 0], cs.at[0, d], cr.at[0, NX - d], xpeer(d)),
            remote(v_hbm.at[:, cols(t)], KV.at[NX - d, 1], cs.at[1, d], cr.at[1, NX - d], xpeer(d)),
        ]
    for copy in sent:
        copy.start()
    local[0].wait()
    local[1].wait()
    for d in range(1, NT):
        source = lax.rem(t + NT - d, NT)
        remote(q_hbm.at[:, cols(t)], QG.at[0, 0, source], as_.at[0, d], ar.at[0, d], tpeer(d)).wait_recv()
        remote(q_hbm.at[:, cols(t)], QG.at[0, 1, source], as_.at[1, d], ar.at[1, d], tpeer(d)).wait_recv()

    gather = []
    for d in REL[1:]:
        slot = POS[(NZ - d) % NZ]
        gather.append(remote(QG.at[0], QG.at[slot], bs.at[d], br.at[slot], zpeer(d)))
    for copy in gather:
        copy.start()
    sent += gather

    for d in range(1, NT):
        source = lax.rem(t + NT - d, NT)
        remote(lrow, L.at[source], as_.at[2, d], ar.at[2, d], tpeer(d)).wait_recv()
    lane3 = lax.broadcasted_iota(jnp.int32, (NT, R, COLS), 2)
    row3 = lax.broadcasted_iota(jnp.int32, (NT, R, COLS), 1)
    lens = jnp.broadcast_to(L[:, 0:1, :], (NT, R, COLS))
    per = F // MASK_BLOCK
    lanes = lax.broadcasted_iota(jnp.int32, (1, 1, COLS), 2)
    first = ((lax.rem(x + lanes // per, NX) * NZ + z) * per + lax.rem(lanes, per)) * MASK_BLOCK
    first = jnp.where(lanes < per * NX, first, -1).astype(F32)

    def mask_slot(p, rel):
        pick = lax.rem(z + rel, NZ) * R + row3
        column = jnp.sum(jnp.where(lane3 == pick, lens, 0.0), axis=2, keepdims=True)
        M[p] = jnp.where(first >= column, HIDDEN, 0.0).astype(BF16).reshape(TOK, COLS)

    for p in range(NZ):
        mask_slot(p, REL[p])

    lane2 = lax.broadcasted_iota(jnp.int32, (1, COLS), 1)
    head = [(lane2 < COLS // 2).astype(F32), (lane2 >= COLS // 2).astype(F32)]
    rows2 = lax.broadcasted_iota(jnp.int32, (F, COLS), 0)
    lanes2 = lax.broadcasted_iota(jnp.int32, (F, COLS), 1)
    for r in range(NX):
        if r == 0:
            local[2].wait()
            local[3].wait()
        else:
            remote(k_hbm.at[:, cols(t)], KV.at[r, 0], cs.at[0, r], cr.at[0, r], xpeer(r)).wait_recv()
            remote(k_hbm.at[:, cols(t)], KV.at[r, 1], cs.at[1, r], cr.at[1, r], xpeer(r)).wait_recv()
        kb = KV[r, 0].astype(F32)
        vb = KV[r, 1].astype(F32)
        hot = (lanes2 == rows2 // MASK_BLOCK + per * r).astype(F32).astype(BF16)
        for h in range(2):
            kh = (kb * (head[h] * SCALE)).astype(F32)
            K2[r, h * F : (h + 1) * F, 0:COLS] = kh.astype(BF16)
            K2[r, h * F : (h + 1) * F, COLS : 2 * COLS] = hot
            V2[r, h * F : (h + 1) * F, :] = (vb * head[h]).astype(BF16)
            KT[r, :, h * F : (h + 1) * F] = kh.T.astype(BF16)

    def block(ref, c, which):
        return ref[pl.ds(2 * c, 2), which].reshape(CH, COLS)

    nt = (((1,), (1,)), ((), ()))

    def arrived(p):
        remote(QG.at[0], QG.at[p], bs.at[REL[1]], br.at[p], zpeer(1)).wait_recv()

    arrived(1)

    def pass1(c, _):
        qe = jnp.concatenate([block(QG, c, 0), M[pl.ds(2 * c, 2)].reshape(CH, COLS)], axis=1)
        ge = block(QG, c, 1)
        ms, ls, ts = [], [], []
        for r in range(NX):
            sc = lax.dot_general(K2[r], qe, nt, preferred_element_type=F32).reshape(2, F, CH)
            m = jnp.max(sc, axis=1, keepdims=True)
            w = jnp.exp(sc - m)
            gp = lax.dot_general(V2[r], ge, nt, preferred_element_type=F32).reshape(2, F, CH)
            W[c, r] = w
            G[c, r] = gp
            ms.append(m)
            ls.append(jnp.sum(w, axis=1, keepdims=True))
            ts.append(jnp.sum(w * gp, axis=1, keepdims=True))
            for h in range(2):
                MR[c, 2 * r + h : 2 * r + h + 1, :] = m[h]
        top = ms[0]
        for m in ms[1:]:
            top = jnp.maximum(top, m)
        total = jnp.zeros_like(top)
        term = jnp.zeros_like(top)
        for m, l, tt in zip(ms, ls, ts):
            a = jnp.exp(m - top)
            total += a * l
            term += a * tt
        lse = top + jnp.log(total)
        term = term / total
        for half in range(2):
            dist = jnp.int32(REL[half])
            for i in range(1, NC):
                dist = jnp.where(c == i, REL[2 * i + half], dist)
            where = lax.rem(z + dist, NZ)
            for h in range(2):
                ST[0, h, pl.ds(where, 1), :] = lse[h, :, half * TOK : (half + 1) * TOK]
                ST[0, 2 + h, pl.ds(where, 1), :] = term[h, :, half * TOK : (half + 1) * TOK]

        @pl.when(c < NC - 1)
        def _():
            for p in range(2):
                slot = 2 * c + 2 + p
                remote(QG.at[0], QG.at[slot], bs.at[REL[1]], br.at[slot], zpeer(1)).wait_recv()

        return 0

    lax.fori_loop(0, NC, pass1, 0)

    stats = []
    for d in REL[1:]:
        stats.append(remote(ST.at[0], ST.at[NZ - d], ds_.at[d], dr.at[NZ - d], zpeer(d)))
    for copy in stats:
        copy.start()
    sent += stats
    DK[...] = jnp.zeros_like(DK)
    DV[...] = jnp.zeros_like(DV)
    for d in range(1, NZ):
        remote(ST.at[0], ST.at[d], ds_.at[d], dr.at[d], zpeer(d)).wait_recv()
    for h in range(2):
        parts = [ST[d, h] for d in range(NZ)]
        top = parts[0]
        for part in parts[1:]:
            top = jnp.maximum(top, part)
        weights = [jnp.exp(part - top) for part in parts]
        total = weights[0]
        term = weights[0] * ST[0, 2 + h]
        for d in range(1, NZ):
            total += weights[d]
            term += weights[d] * ST[d, 2 + h]
        CF[h] = top + jnp.log(total)
        RT[h] = term / total

    masks = [m.astype(BF16) for m in head]

    def pass2(i, _):
        c = NC - 1 - i
        qb, gb = block(QG, c, 0), block(QG, c, 1)
        q2 = jnp.concatenate([qb * masks[0], qb * masks[1]], axis=0)
        g2 = jnp.concatenate([gb * masks[0], gb * masks[1]], axis=0)
        lse, term = [], []
        for half in range(2):
            dist = jnp.int32(REL[half])
            for k in range(1, NC):
                dist = jnp.where(c == k, REL[2 * k + half], dist)
            where = lax.rem(z + dist, NZ)
            lse.append([CF[h, pl.ds(where, 1), :] for h in range(2)])
            term.append([RT[h, pl.ds(where, 1), :] for h in range(2)])
        lse = [jnp.concatenate([lse[0][h], lse[1][h]], axis=1) for h in range(2)]
        term = [jnp.concatenate([term[0][h], term[1][h]], axis=1) for h in range(2)]
        dqt = jnp.zeros((COLS, CH), F32)
        for r in range(NX):
            ps, gs_ = [], []
            for h in range(2):
                cf = jnp.exp(MR[c, 2 * r + h : 2 * r + h + 1, :] - lse[h])
                p = W[c, r, h] * cf
                ps.append(p.astype(BF16))
                gs_.append((p * (G[c, r, h] - term[h])).astype(BF16))
            DV[r] += jnp.dot(jnp.concatenate(ps, axis=1), g2, preferred_element_type=F32)
            DK[r] += jnp.dot(jnp.concatenate(gs_, axis=1), q2, preferred_element_type=F32)
            dqt += jnp.dot(KT[r], jnp.concatenate(gs_, axis=0), preferred_element_type=F32)
        dq = dqt.T

        DQS[pl.ds(2 * c, 2)] = dq.astype(BF16).reshape(2, TOK, COLS)

        @pl.when(c == 0)
        def _():
            DQO[...] = dq[0:TOK]

        return 0

    lax.fori_loop(0, NC, pass2, 0)

    back = []
    for d in REL[1:]:
        back.append(remote(DQS.at[POS[d]], DQR.at[NZ - d], es.at[d], er.at[NZ - d], zpeer(d)))
    for copy in back:
        copy.start()
    sent += back
    back = []
    for d in range(1, NX):
        DKVS[d, 0] = DK[d].astype(BF16)
        DKVS[d, 1] = DV[d].astype(BF16)
        back.append(remote(DKVS.at[d], DKVR.at[NX - d], fs.at[d], fr.at[NX - d], xpeer(d)))
        back[-1].start()
    sent += back

    for d in range(1, NZ):
        remote(DQS.at[0], DQR.at[d], es.at[d], er.at[d], zpeer(d)).wait_recv()
    dq = DQO[...]
    for d in range(1, NZ):
        dq += DQR[d].astype(F32)
    DQF[...] = dq.reshape(NT, R, COLS)
    back = []
    for d in range(1, NT):
        back.append(remote(DQF.at[lax.rem(t + d, NT)], DQI.at[t], gs.at[d], gr.at[d], tpeer(d)))
        back[-1].start()
    sent += back
    DQI[pl.ds(t, 1)] = DQF[pl.ds(t, 1)]

    for d in range(1, NX):
        remote(DKVS.at[d], DKVR.at[d], fs.at[d], fr.at[d], xpeer(d)).wait_recv()
    dk, dv = DK[0], DV[0]
    for d in range(1, NX):
        dk += DKVR[d, 0].astype(F32)
        dv += DKVR[d, 1].astype(F32)
    dk_out[...] = dk * SCALE
    dv_out[...] = dv

    for d in range(1, NT):
        source = lax.rem(t + NT - d, NT)
        remote(DQF.at[0], DQI.at[source], gs.at[d], gr.at[d], tpeer(d)).wait_recv()
    for i in range(NT):
        dq_out[:, i * COLS : (i + 1) * COLS] = DQI[i]
    for copy in sent:
        copy.wait_send()


def body(queries, keys, values, grad_out, read_len, *, NT):
    R, D = queries.shape
    F = keys.shape[0]
    TOK, CH, NC = NT * R, 2 * NT * R, NZ // 2
    lens = read_len.reshape(NX, NZ * R)
    any_ = pl.BlockSpec(memory_space=pl.ANY)
    vmem = pl.BlockSpec(memory_space=pltpu.VMEM)
    dma = pltpu.SemaphoreType.DMA
    V = pltpu.VMEM
    return pl.pallas_call(
        lambda *refs: kernel(NT, *refs),
        out_shape=(
            jax.ShapeDtypeStruct((R, D), F32),
            jax.ShapeDtypeStruct((F, COLS), F32),
            jax.ShapeDtypeStruct((F, COLS), F32),
        ),
        in_specs=[any_, any_, any_, any_, vmem],
        out_specs=(vmem, vmem, vmem),
        scratch_shapes=[
            V((NZ, 2, NT, R, COLS), BF16),
            V((NX, 2, F, COLS), BF16),
            V((NT, 8, COLS), F32),
            V((8, COLS), F32),
            V((NZ, TOK, COLS), BF16),
            V((NX, 2 * F, 2 * COLS), BF16),
            V((NX, 2 * F, COLS), BF16),
            V((NX, COLS, 2 * F), BF16),
            V((NC, NX, 2, F, CH), F32),
            V((NC, NX, 2, F, CH), F32),
            V((NC, 2 * NX, CH), F32),
            V((NZ, 4, NZ, TOK), F32),
            V((2, NZ, TOK), F32),
            V((2, NZ, TOK), F32),
            V((NZ, TOK, COLS), BF16),
            V((NZ, TOK, COLS), BF16),
            V((TOK, COLS), F32),
            V((NT, R, COLS), F32),
            V((NT, R, COLS), F32),
            V((NX, F, COLS), F32),
            V((NX, F, COLS), F32),
            V((NX, 2, F, COLS), BF16),
            V((NX, 2, F, COLS), BF16),
            dma((4,)),
            dma((3, NT)), dma((3, NT)),
            dma((NZ,)), dma((NZ,)),
            dma((2, NX)), dma((2, NX)),
            dma((NZ,)), dma((NZ,)),
            dma((NZ,)), dma((NZ,)),
            dma((NX,)), dma((NX,)),
            dma((NT,)), dma((NT,)),
        ],
        compiler_params=pltpu.CompilerParams(
            collective_id=0, has_side_effects=True, vmem_limit_bytes=48 * 1024 * 1024
        ),
    )(queries, keys, values, grad_out, lens)


def solution(mesh):
    NT = mesh.shape["tgt"]
    return jax.shard_map(
        lambda *args: body(*args, NT=NT),
        mesh=mesh,
        in_specs=(
            P(("tgt", "src"), None),
            P("src", None),
            P("src", None),
            P(("tgt", "src"), None),
            P("tgt"),
        ),
        out_specs=(P(("tgt", "src"), None), P("src", "tgt"), P("src", "tgt")),
        check_vma=False,
    )
```

```python
import jax
import jax.numpy as jnp
from jax import lax
from jax.experimental import pallas as pl
from jax.experimental.pallas import tpu as pltpu
from jax.sharding import PartitionSpec as P

MESH = pl.DeviceIdType.MESH
NX, NZ = 4, 8
COLS = 128
MASK_BLOCK = 128
F32, BF16 = jnp.float32, jnp.bfloat16
HIDDEN = -1e30
SCALE = 0.125

REL = [0]
for _d in range(1, NZ // 2 + 1):
    REL += [_d] if 2 * _d == NZ else [_d, NZ - _d]
POS = {d: p for p, d in enumerate(REL)}


def kernel(
    NT, q_hbm, k_hbm, v_hbm, g_hbm, len_ref, dq_out, dk_out, dv_out,
    QI, GI, QG, KV, L, lrow, M, K2, V2, KT, W, G, MR, ST, CF, RT, DQS, DQR, DQO, DQF, DQI, DK, DV, DKVS, DKVR,
    lsem, as_, ar, bs, br, cs, cr, ds_, dr, es, er, fs, fr, gs, gr,
):
    t = lax.axis_index("tgt")
    s = lax.axis_index("src")
    x = s // NZ
    z = s % NZ
    R, F = q_hbm.shape[0], k_hbm.shape[0]
    TOK = NT * R
    CH = 2 * TOK
    NC = NZ // 2

    def tpeer(d):
        return (lax.rem(t + d, NT), s)

    def zpeer(d):
        return (t, x * NZ + lax.rem(z + d, NZ))

    def xpeer(d):
        return (t, lax.rem(x + d, NX) * NZ + z)

    def cols(i):
        return pl.ds(pl.multiple_of(i * COLS, COLS), COLS)

    def remote(src, dst, ssem, rsem, dev):
        return pltpu.make_async_remote_copy(
            src_ref=src, dst_ref=dst, send_sem=ssem, recv_sem=rsem, device_id=dev, device_id_type=MESH
        )

    local = [
        pltpu.make_async_copy(q_hbm, QI, lsem.at[0]),
        pltpu.make_async_copy(g_hbm, GI, lsem.at[1]),
        pltpu.make_async_copy(k_hbm.at[:, cols(t)], KV.at[0, 0], lsem.at[2]),
        pltpu.make_async_copy(v_hbm.at[:, cols(t)], KV.at[0, 1], lsem.at[3]),
    ]
    for copy in local:
        copy.start()
    row = len_ref[pl.ds(x, 1), :].astype(F32)
    lrow[...] = jnp.broadcast_to(row, lrow.shape)
    L[pl.ds(t, 1)] = jnp.broadcast_to(row[None], (1,) + lrow.shape)

    barrier = pltpu.get_barrier_semaphore()
    peers = [tpeer(d) for d in range(1, NT)] + [zpeer(d) for d in range(1, NZ)] + [xpeer(d) for d in range(1, NX)]
    for dev in peers:
        pl.semaphore_signal(barrier, inc=1, device_id=dev, device_id_type=MESH)
    pl.semaphore_wait(barrier, len(peers))

    for copy in local:
        copy.wait()
    sent = []
    for d in range(1, NT):
        there = lax.rem(t + d, NT)
        sent += [
            remote(QI.at[:, cols(there)], QG.at[0, 0, t], as_.at[0, d], ar.at[0, d], tpeer(d)),
            remote(GI.at[:, cols(there)], QG.at[0, 1, t], as_.at[1, d], ar.at[1, d], tpeer(d)),
            remote(lrow, L.at[t], as_.at[2, d], ar.at[2, d], tpeer(d)),
        ]
    for d in range(1, NX):
        sent += [
            remote(KV.at[0, 0], KV.at[NX - d, 0], cs.at[0, d], cr.at[0, NX - d], xpeer(d)),
            remote(KV.at[0, 1], KV.at[NX - d, 1], cs.at[1, d], cr.at[1, NX - d], xpeer(d)),
        ]
    for copy in sent:
        copy.start()
    QG[0, 0, pl.ds(t, 1)] = QI[:, cols(t)][None]
    QG[0, 1, pl.ds(t, 1)] = GI[:, cols(t)][None]
    for d in range(1, NT):
        source = lax.rem(t + NT - d, NT)
        remote(QI.at[:, cols(t)], QG.at[0, 0, source], as_.at[0, d], ar.at[0, d], tpeer(d)).wait_recv()
        remote(QI.at[:, cols(t)], QG.at[0, 1, source], as_.at[1, d], ar.at[1, d], tpeer(d)).wait_recv()

    gather = []
    for d in REL[1:]:
        slot = POS[(NZ - d) % NZ]
        gather.append(remote(QG.at[0], QG.at[slot], bs.at[d], br.at[slot], zpeer(d)))
    for copy in gather:
        copy.start()
    sent += gather

    for d in range(1, NT):
        source = lax.rem(t + NT - d, NT)
        remote(lrow, L.at[source], as_.at[2, d], ar.at[2, d], tpeer(d)).wait_recv()
    lane3 = lax.broadcasted_iota(jnp.int32, (NT, R, COLS), 2)
    row3 = lax.broadcasted_iota(jnp.int32, (NT, R, COLS), 1)
    lens = jnp.broadcast_to(L[:, 0:1, :], (NT, R, COLS))
    per = F // MASK_BLOCK
    lanes = lax.broadcasted_iota(jnp.int32, (1, 1, COLS), 2)
    first = ((lax.rem(x + lanes // per, NX) * NZ + z) * per + lax.rem(lanes, per)) * MASK_BLOCK
    first = jnp.where(lanes < per * NX, first, -1).astype(F32)

    def mask_slot(p, rel):
        pick = lax.rem(z + rel, NZ) * R + row3
        column = jnp.sum(jnp.where(lane3 == pick, lens, 0.0), axis=2, keepdims=True)
        M[p] = jnp.where(first >= column, HIDDEN, 0.0).astype(BF16).reshape(TOK, COLS)

    for p in range(NZ):
        mask_slot(p, REL[p])

    lane2 = lax.broadcasted_iota(jnp.int32, (1, COLS), 1)
    head = [(lane2 < COLS // 2).astype(F32), (lane2 >= COLS // 2).astype(F32)]
    rows2 = lax.broadcasted_iota(jnp.int32, (F, COLS), 0)
    lanes2 = lax.broadcasted_iota(jnp.int32, (F, COLS), 1)
    for r in range(NX):
        if r > 0:
            remote(KV.at[0, 0], KV.at[r, 0], cs.at[0, r], cr.at[0, r], xpeer(r)).wait_recv()
            remote(KV.at[0, 0], KV.at[r, 1], cs.at[1, r], cr.at[1, r], xpeer(r)).wait_recv()
        kb = KV[r, 0].astype(F32)
        vb = KV[r, 1].astype(F32)
        hot = (lanes2 == rows2 // MASK_BLOCK + per * r).astype(F32).astype(BF16)
        for h in range(2):
            kh = (kb * (head[h] * SCALE)).astype(F32)
            K2[r, h * F : (h + 1) * F, 0:COLS] = kh.astype(BF16)
            K2[r, h * F : (h + 1) * F, COLS : 2 * COLS] = hot
            V2[r, h * F : (h + 1) * F, :] = (vb * head[h]).astype(BF16)
            KT[r, :, h * F : (h + 1) * F] = kh.T.astype(BF16)

    def block(ref, c, which):
        return ref[pl.ds(2 * c, 2), which].reshape(CH, COLS)

    nt = (((1,), (1,)), ((), ()))

    def arrived(p):
        remote(QG.at[0], QG.at[p], bs.at[REL[1]], br.at[p], zpeer(1)).wait_recv()

    arrived(1)

    def pass1(c, _):
        qe = jnp.concatenate([block(QG, c, 0), M[pl.ds(2 * c, 2)].reshape(CH, COLS)], axis=1)
        ge = block(QG, c, 1)
        ms, ls, ts = [], [], []
        for r in range(NX):
            sc = lax.dot_general(K2[r], qe, nt, preferred_element_type=F32).reshape(2, F, CH)
            m = jnp.max(sc, axis=1, keepdims=True)
            w = jnp.exp(sc - m)
            gp = lax.dot_general(V2[r], ge, nt, preferred_element_type=F32).reshape(2, F, CH)
            W[c, r] = w
            G[c, r] = gp
            ms.append(m)
            ls.append(jnp.sum(w, axis=1, keepdims=True))
            ts.append(jnp.sum(w * gp, axis=1, keepdims=True))
            for h in range(2):
                MR[c, 2 * r + h : 2 * r + h + 1, :] = m[h]
        top = ms[0]
        for m in ms[1:]:
            top = jnp.maximum(top, m)
        total = jnp.zeros_like(top)
        term = jnp.zeros_like(top)
        for m, l, tt in zip(ms, ls, ts):
            a = jnp.exp(m - top)
            total += a * l
            term += a * tt
        lse = top + jnp.log(total)
        term = term / total
        for half in range(2):
            dist = jnp.int32(REL[half])
            for i in range(1, NC):
                dist = jnp.where(c == i, REL[2 * i + half], dist)
            where = lax.rem(z + dist, NZ)
            for h in range(2):
                ST[0, h, pl.ds(where, 1), :] = lse[h, :, half * TOK : (half + 1) * TOK]
                ST[0, 2 + h, pl.ds(where, 1), :] = term[h, :, half * TOK : (half + 1) * TOK]

        @pl.when(c < NC - 1)
        def _():
            for p in range(2):
                slot = 2 * c + 2 + p
                remote(QG.at[0], QG.at[slot], bs.at[REL[1]], br.at[slot], zpeer(1)).wait_recv()

        return 0

    lax.fori_loop(0, NC, pass1, 0)

    stats = []
    for d in REL[1:]:
        stats.append(remote(ST.at[0], ST.at[NZ - d], ds_.at[d], dr.at[NZ - d], zpeer(d)))
    for copy in stats:
        copy.start()
    sent += stats
    DK[...] = jnp.zeros_like(DK)
    DV[...] = jnp.zeros_like(DV)
    for d in range(1, NZ):
        remote(ST.at[0], ST.at[d], ds_.at[d], dr.at[d], zpeer(d)).wait_recv()
    for h in range(2):
        parts = [ST[d, h] for d in range(NZ)]
        top = parts[0]
        for part in parts[1:]:
            top = jnp.maximum(top, part)
        weights = [jnp.exp(part - top) for part in parts]
        total = weights[0]
        term = weights[0] * ST[0, 2 + h]
        for d in range(1, NZ):
            total += weights[d]
            term += weights[d] * ST[d, 2 + h]
        CF[h] = top + jnp.log(total)
        RT[h] = term / total

    masks = [m.astype(BF16) for m in head]

    def pass2(i, _):
        c = NC - 1 - i
        qb, gb = block(QG, c, 0), block(QG, c, 1)
        q2 = jnp.concatenate([qb * masks[0], qb * masks[1]], axis=0)
        g2 = jnp.concatenate([gb * masks[0], gb * masks[1]], axis=0)
        lse, term = [], []
        for half in range(2):
            dist = jnp.int32(REL[half])
            for k in range(1, NC):
                dist = jnp.where(c == k, REL[2 * k + half], dist)
            where = lax.rem(z + dist, NZ)
            lse.append([CF[h, pl.ds(where, 1), :] for h in range(2)])
            term.append([RT[h, pl.ds(where, 1), :] for h in range(2)])
        lse = [jnp.concatenate([lse[0][h], lse[1][h]], axis=1) for h in range(2)]
        term = [jnp.concatenate([term[0][h], term[1][h]], axis=1) for h in range(2)]
        dqt = jnp.zeros((COLS, CH), F32)
        for r in range(NX):
            ps, gs_ = [], []
            for h in range(2):
                cf = jnp.exp(MR[c, 2 * r + h : 2 * r + h + 1, :] - lse[h])
                p = W[c, r, h] * cf
                ps.append(p.astype(BF16))
                gs_.append((p * (G[c, r, h] - term[h])).astype(BF16))
            DV[r] += jnp.dot(jnp.concatenate(ps, axis=1), g2, preferred_element_type=F32)
            DK[r] += jnp.dot(jnp.concatenate(gs_, axis=1), q2, preferred_element_type=F32)
            dqt += jnp.dot(KT[r], jnp.concatenate(gs_, axis=0), preferred_element_type=F32)
        dq = dqt.T

        DQS[pl.ds(2 * c, 2)] = dq.astype(BF16).reshape(2, TOK, COLS)

        @pl.when(c == 0)
        def _():
            DQO[...] = dq[0:TOK]

        return 0

    lax.fori_loop(0, NC, pass2, 0)

    back = []
    for d in REL[1:]:
        back.append(remote(DQS.at[POS[d]], DQR.at[NZ - d], es.at[d], er.at[NZ - d], zpeer(d)))
    for copy in back:
        copy.start()
    sent += back
    back = []
    for d in range(1, NX):
        DKVS[d, 0] = DK[d].astype(BF16)
        DKVS[d, 1] = DV[d].astype(BF16)
        back.append(remote(DKVS.at[d], DKVR.at[NX - d], fs.at[d], fr.at[NX - d], xpeer(d)))
        back[-1].start()
    sent += back

    for d in range(1, NZ):
        remote(DQS.at[0], DQR.at[d], es.at[d], er.at[d], zpeer(d)).wait_recv()
    dq = DQO[...]
    for d in range(1, NZ):
        dq += DQR[d].astype(F32)
    DQF[...] = dq.reshape(NT, R, COLS)
    back = []
    for d in range(1, NT):
        back.append(remote(DQF.at[lax.rem(t + d, NT)], DQI.at[t], gs.at[d], gr.at[d], tpeer(d)))
        back[-1].start()
    sent += back
    DQI[pl.ds(t, 1)] = DQF[pl.ds(t, 1)]

    for d in range(1, NX):
        remote(DKVS.at[d], DKVR.at[d], fs.at[d], fr.at[d], xpeer(d)).wait_recv()
    dk, dv = DK[0], DV[0]
    for d in range(1, NX):
        dk += DKVR[d, 0].astype(F32)
        dv += DKVR[d, 1].astype(F32)
    dk_out[...] = dk * SCALE
    dv_out[...] = dv

    for d in range(1, NT):
        source = lax.rem(t + NT - d, NT)
        remote(DQF.at[0], DQI.at[source], gs.at[d], gr.at[d], tpeer(d)).wait_recv()
    for i in range(NT):
        dq_out[:, i * COLS : (i + 1) * COLS] = DQI[i]
    for copy in sent:
        copy.wait_send()


def body(queries, keys, values, grad_out, read_len, *, NT):
    R, D = queries.shape
    F = keys.shape[0]
    TOK, CH, NC = NT * R, 2 * NT * R, NZ // 2
    lens = read_len.reshape(NX, NZ * R)
    any_ = pl.BlockSpec(memory_space=pl.ANY)
    vmem = pl.BlockSpec(memory_space=pltpu.VMEM)
    dma = pltpu.SemaphoreType.DMA
    V = pltpu.VMEM
    return pl.pallas_call(
        lambda *refs: kernel(NT, *refs),
        out_shape=(
            jax.ShapeDtypeStruct((R, D), F32),
            jax.ShapeDtypeStruct((F, COLS), F32),
            jax.ShapeDtypeStruct((F, COLS), F32),
        ),
        in_specs=[any_, any_, any_, any_, vmem],
        out_specs=(vmem, vmem, vmem),
        scratch_shapes=[
            V((R, D), BF16),
            V((R, D), BF16),
            V((NZ, 2, NT, R, COLS), BF16),
            V((NX, 2, F, COLS), BF16),
            V((NT, 8, COLS), F32),
            V((8, COLS), F32),
            V((NZ, TOK, COLS), BF16),
            V((NX, 2 * F, 2 * COLS), BF16),
            V((NX, 2 * F, COLS), BF16),
            V((NX, COLS, 2 * F), BF16),
            V((NC, NX, 2, F, CH), F32),
            V((NC, NX, 2, F, CH), F32),
            V((NC, 2 * NX, CH), F32),
            V((NZ, 4, NZ, TOK), F32),
            V((2, NZ, TOK), F32),
            V((2, NZ, TOK), F32),
            V((NZ, TOK, COLS), BF16),
            V((NZ, TOK, COLS), BF16),
            V((TOK, COLS), F32),
            V((NT, R, COLS), F32),
            V((NT, R, COLS), F32),
            V((NX, F, COLS), F32),
            V((NX, F, COLS), F32),
            V((NX, 2, F, COLS), BF16),
            V((NX, 2, F, COLS), BF16),
            dma((4,)),
            dma((3, NT)), dma((3, NT)),
            dma((NZ,)), dma((NZ,)),
            dma((2, NX)), dma((2, NX)),
            dma((NZ,)), dma((NZ,)),
            dma((NZ,)), dma((NZ,)),
            dma((NX,)), dma((NX,)),
            dma((NT,)), dma((NT,)),
        ],
        compiler_params=pltpu.CompilerParams(
            collective_id=0, has_side_effects=True, vmem_limit_bytes=62 * 1024 * 1024
        ),
    )(queries, keys, values, grad_out, lens)


def solution(mesh):
    NT = mesh.shape["tgt"]
    return jax.shard_map(
        lambda *args: body(*args, NT=NT),
        mesh=mesh,
        in_specs=(
            P(("tgt", "src"), None),
            P("src", None),
            P("src", None),
            P(("tgt", "src"), None),
            P("tgt"),
        ),
        out_specs=(P(("tgt", "src"), None), P("src", "tgt"), P("src", "tgt")),
        check_vma=False,
    )
```

```python
import jax
import jax.numpy as jnp
from jax import lax
from jax.experimental import pallas as pl
from jax.experimental.pallas import tpu as pltpu
from jax.sharding import PartitionSpec as P

MESH = pl.DeviceIdType.MESH
NX, NZ = 4, 8
COLS = 128
MASK_BLOCK = 128
F32, BF16 = jnp.float32, jnp.bfloat16
HIDDEN = -1e30
SCALE = 0.125

REL = [0]
for _d in range(1, NZ // 2 + 1):
    REL += [_d] if 2 * _d == NZ else [_d, NZ - _d]
POS = {d: p for p, d in enumerate(REL)}


def kernel(
    NT, q_hbm, k_hbm, v_hbm, g_hbm, len_ref, dq_out, dk_out, dv_out,
    QI, GI, QG, KV, L, lrow, M, K2, V2, KT, W, G, MR, SM, SR, CF, RT, DQS, DQR, DQO, DQF, DQI, DK, DV, DKVS, DKVR,
    lsem, as_, ar, bs, br, cs, cr, ds_, dr, es, er, fs, fr, gs, gr,
):
    t = lax.axis_index("tgt")
    s = lax.axis_index("src")
    x = s // NZ
    z = s % NZ
    R, F = q_hbm.shape[0], k_hbm.shape[0]
    TOK = NT * R
    CH = 2 * TOK
    NC = NZ // 2

    def tpeer(d):
        return (lax.rem(t + d, NT), s)

    def zpeer(d):
        return (t, x * NZ + lax.rem(z + d, NZ))

    def xpeer(d):
        return (t, lax.rem(x + d, NX) * NZ + z)

    def cols(i):
        return pl.ds(pl.multiple_of(i * COLS, COLS), COLS)

    def remote(src, dst, ssem, rsem, dev):
        return pltpu.make_async_remote_copy(
            src_ref=src, dst_ref=dst, send_sem=ssem, recv_sem=rsem, device_id=dev, device_id_type=MESH
        )

    local = [
        pltpu.make_async_copy(q_hbm, QI, lsem.at[0]),
        pltpu.make_async_copy(g_hbm, GI, lsem.at[1]),
        pltpu.make_async_copy(k_hbm.at[:, cols(t)], KV.at[0, 0], lsem.at[2]),
        pltpu.make_async_copy(v_hbm.at[:, cols(t)], KV.at[0, 1], lsem.at[3]),
    ]
    for copy in local:
        copy.start()
    row = len_ref[pl.ds(x, 1), :].astype(F32)
    lrow[...] = jnp.broadcast_to(row, lrow.shape)
    L[pl.ds(t, 1)] = jnp.broadcast_to(row[None], (1,) + lrow.shape)

    barrier = pltpu.get_barrier_semaphore()
    peers = [tpeer(d) for d in range(1, NT)] + [zpeer(d) for d in range(1, NZ)] + [xpeer(d) for d in range(1, NX)]
    for dev in peers:
        pl.semaphore_signal(barrier, inc=1, device_id=dev, device_id_type=MESH)
    pl.semaphore_wait(barrier, len(peers))

    for copy in local:
        copy.wait()
    sent = []
    for d in range(1, NT):
        there = lax.rem(t + d, NT)
        sent += [
            remote(QI.at[:, cols(there)], QG.at[0, 0, t], as_.at[0, d], ar.at[0, d], tpeer(d)),
            remote(GI.at[:, cols(there)], QG.at[0, 1, t], as_.at[1, d], ar.at[1, d], tpeer(d)),
            remote(lrow, L.at[t], as_.at[2, d], ar.at[2, d], tpeer(d)),
        ]
    for d in range(1, NX):
        sent += [
            remote(KV.at[0, 0], KV.at[NX - d, 0], cs.at[0, d], cr.at[0, NX - d], xpeer(d)),
            remote(KV.at[0, 1], KV.at[NX - d, 1], cs.at[1, d], cr.at[1, NX - d], xpeer(d)),
        ]
    for copy in sent:
        copy.start()
    QG[0, 0, pl.ds(t, 1)] = QI[:, cols(t)][None]
    QG[0, 1, pl.ds(t, 1)] = GI[:, cols(t)][None]
    for d in range(1, NT):
        source = lax.rem(t + NT - d, NT)
        remote(QI.at[:, cols(t)], QG.at[0, 0, source], as_.at[0, d], ar.at[0, d], tpeer(d)).wait_recv()
        remote(QI.at[:, cols(t)], QG.at[0, 1, source], as_.at[1, d], ar.at[1, d], tpeer(d)).wait_recv()

    gather = []
    for d in REL[1:]:
        slot = POS[(NZ - d) % NZ]
        gather.append(remote(QG.at[0], QG.at[slot], bs.at[d], br.at[slot], zpeer(d)))
    for copy in gather:
        copy.start()
    sent += gather

    for d in range(1, NT):
        source = lax.rem(t + NT - d, NT)
        remote(lrow, L.at[source], as_.at[2, d], ar.at[2, d], tpeer(d)).wait_recv()
    lane3 = lax.broadcasted_iota(jnp.int32, (NT, R, COLS), 2)
    row3 = lax.broadcasted_iota(jnp.int32, (NT, R, COLS), 1)
    lens = jnp.broadcast_to(L[:, 0:1, :], (NT, R, COLS))
    per = F // MASK_BLOCK
    lanes = lax.broadcasted_iota(jnp.int32, (1, 1, COLS), 2)
    first = ((lax.rem(x + lanes // per, NX) * NZ + z) * per + lax.rem(lanes, per)) * MASK_BLOCK
    first = jnp.where(lanes < per * NX, first, -1).astype(F32)

    def mask_slot(p, rel):
        pick = lax.rem(z + rel, NZ) * R + row3
        column = jnp.sum(jnp.where(lane3 == pick, lens, 0.0), axis=2, keepdims=True)
        M[p] = jnp.where(first >= column, HIDDEN, 0.0).astype(BF16).reshape(TOK, COLS)

    for p in range(NZ):
        mask_slot(p, REL[p])

    lane2 = lax.broadcasted_iota(jnp.int32, (1, COLS), 1)
    head = [(lane2 < COLS // 2).astype(F32), (lane2 >= COLS // 2).astype(F32)]
    rows2 = lax.broadcasted_iota(jnp.int32, (F, COLS), 0)
    lanes2 = lax.broadcasted_iota(jnp.int32, (F, COLS), 1)
    for r in range(NX):
        if r > 0:
            remote(KV.at[0, 0], KV.at[r, 0], cs.at[0, r], cr.at[0, r], xpeer(r)).wait_recv()
            remote(KV.at[0, 0], KV.at[r, 1], cs.at[1, r], cr.at[1, r], xpeer(r)).wait_recv()
        kb = KV[r, 0].astype(F32)
        vb = KV[r, 1].astype(F32)
        hot = (lanes2 == rows2 // MASK_BLOCK + per * r).astype(F32).astype(BF16)
        for h in range(2):
            kh = (kb * (head[h] * SCALE)).astype(F32)
            K2[r, h * F : (h + 1) * F, 0:COLS] = kh.astype(BF16)
            K2[r, h * F : (h + 1) * F, COLS : 2 * COLS] = hot
            V2[r, h * F : (h + 1) * F, :] = (vb * head[h]).astype(BF16)
            KT[r, :, h * F : (h + 1) * F] = kh.T.astype(BF16)

    def block(ref, c, which):
        return ref[pl.ds(2 * c, 2), which].reshape(CH, COLS)

    nt = (((1,), (1,)), ((), ()))

    def arrived(p):
        remote(QG.at[0], QG.at[p], bs.at[REL[1]], br.at[p], zpeer(1)).wait_recv()

    arrived(1)

    def pass1(c, _):
        qe = jnp.concatenate([block(QG, c, 0), M[pl.ds(2 * c, 2)].reshape(CH, COLS)], axis=1)
        ge = block(QG, c, 1)
        ms, ls, ts = [], [], []
        for r in range(NX):
            sc = lax.dot_general(K2[r], qe, nt, preferred_element_type=F32).reshape(2, F, CH)
            m = jnp.max(sc, axis=1, keepdims=True)
            w = jnp.exp(sc - m)
            gp = lax.dot_general(V2[r], ge, nt, preferred_element_type=F32).reshape(2, F, CH)
            W[c, r] = w
            G[c, r] = gp
            ms.append(m)
            ls.append(jnp.sum(w, axis=1, keepdims=True))
            ts.append(jnp.sum(w * gp, axis=1, keepdims=True))
            for h in range(2):
                MR[c, 2 * r + h : 2 * r + h + 1, :] = m[h]
        top = ms[0]
        for m in ms[1:]:
            top = jnp.maximum(top, m)
        total = jnp.zeros_like(top)
        term = jnp.zeros_like(top)
        for m, l, tt in zip(ms, ls, ts):
            a = jnp.exp(m - top)
            total += a * l
            term += a * tt
        lse = top + jnp.log(total)
        term = term / total
        for half in range(2):
            for h in range(2):
                row = 2 * half + h
                piece = slice(half * TOK, (half + 1) * TOK)
                SM[c, row : row + 1, :] = lse[h][:, piece]
                SM[c, 4 + row : 5 + row, :] = term[h][:, piece]
        for d in REL[1:]:
            remote(SM.at[c], SR.at[NZ - d, c], ds_.at[d], dr.at[NZ - d], zpeer(d)).start()

        @pl.when(c < NC - 1)
        def _():
            for p in range(2):
                slot = 2 * c + 2 + p
                remote(QG.at[0], QG.at[slot], bs.at[REL[1]], br.at[slot], zpeer(1)).wait_recv()

        return 0

    lax.fori_loop(0, NC, pass1, 0)

    DK[...] = jnp.zeros_like(DK)
    DV[...] = jnp.zeros_like(DV)
    masks = [m.astype(BF16) for m in head]

    for d in range(1, NZ):
        remote(SM, SR.at[d], ds_.at[d], dr.at[d], zpeer(d)).wait_recv()

    def combine(p):
        parts, terms = [], []
        for d in range(NZ):
            theirs = POS[(REL[p] - d) % NZ]
            ref = SM if d == 0 else SR.at[d]
            row = 2 * (theirs % 2)
            parts.append(ref[theirs // 2, row : row + 2, :])
            terms.append(ref[theirs // 2, 4 + row : 6 + row, :])
        top = parts[0]
        for part in parts[1:]:
            top = jnp.maximum(top, part)
        total = jnp.zeros_like(top)
        term = jnp.zeros_like(top)
        for part, other in zip(parts, terms):
            weight = jnp.exp(part - top)
            total += weight
            term += weight * other
        CF[:, p * TOK : (p + 1) * TOK] = top + jnp.log(total)
        RT[:, p * TOK : (p + 1) * TOK] = term / total

    for p in range(NZ):
        combine(p)

    def two_heads(v):
        return jnp.concatenate([v * masks[0], v * masks[1]], axis=0)

    def tile(c, r):
        ps, gs_ = [], []
        for h in range(2):
            cf = jnp.exp(MR[c, 2 * r + h : 2 * r + h + 1, :] - CF[h : h + 1, c * CH : (c + 1) * CH])
            p = W[c, r, h] * cf
            ps.append(p.astype(BF16))
            gs_.append((p * (G[c, r, h] - RT[h : h + 1, c * CH : (c + 1) * CH])).astype(BF16))
        q2, g2 = two_heads(block(QG, c, 0)), two_heads(block(QG, c, 1))
        dv = jnp.dot(jnp.concatenate(ps, axis=1), g2, preferred_element_type=F32)
        dk = jnp.dot(jnp.concatenate(gs_, axis=1), q2, preferred_element_type=F32)
        dqt = jnp.dot(KT[r], jnp.concatenate(gs_, axis=0), preferred_element_type=F32)
        return dk, dv, dqt

    def send_dq(p):
        d = REL[p]
        sent.append(remote(DQS.at[p], DQR.at[NZ - d], es.at[d], er.at[NZ - d], zpeer(d)))
        sent[-1].start()

    for c in range(NC - 1, 1, -1):
        dq = jnp.zeros((COLS, CH), F32)
        for r in range(NX):
            dk, dv, dqt = tile(c, r)
            DK[r] += dk
            DV[r] += dv
            dq += dqt
        DQS[2 * c : 2 * c + 2] = dq.T.astype(BF16).reshape(2, TOK, COLS)
        send_dq(2 * c)
        send_dq(2 * c + 1)

    near = [jnp.zeros((COLS, CH), F32)] * 2
    for r in [NX // 2] + [i for i in range(1, NX) if i != NX // 2] + [0]:
        dk, dv = DK[r], DV[r]
        for c in range(2):
            dk1, dv1, dqt = tile(c, r)
            dk += dk1
            dv += dv1
            near[c] += dqt
        if r == 0:
            DK[0] = dk
            DV[0] = dv
        else:
            DKVS[r, 0] = dk.astype(BF16)
            DKVS[r, 1] = dv.astype(BF16)
            sent.append(remote(DKVS.at[r], DKVR.at[NX - r], fs.at[r], fr.at[NX - r], xpeer(r)))
            sent[-1].start()
    for c in [1, 0]:
        dq = near[c].T
        DQS[2 * c : 2 * c + 2] = dq.astype(BF16).reshape(2, TOK, COLS)
        for p in [2 * c, 2 * c + 1]:
            if p > 0:
                send_dq(p)
            else:
                DQO[...] = dq[0:TOK]

    for d in range(1, NZ):
        remote(DQS.at[0], DQR.at[d], es.at[d], er.at[d], zpeer(d)).wait_recv()
    dq = DQO[...]
    for d in range(1, NZ):
        dq += DQR[d].astype(F32)
    DQF[...] = dq.reshape(NT, R, COLS)
    back = []
    for d in range(1, NT):
        back.append(remote(DQF.at[lax.rem(t + d, NT)], DQI.at[t], gs.at[d], gr.at[d], tpeer(d)))
        back[-1].start()
    sent += back
    DQI[pl.ds(t, 1)] = DQF[pl.ds(t, 1)]

    for d in range(1, NX):
        remote(DKVS.at[d], DKVR.at[d], fs.at[d], fr.at[d], xpeer(d)).wait_recv()
    dk, dv = DK[0], DV[0]
    for d in range(1, NX):
        dk += DKVR[d, 0].astype(F32)
        dv += DKVR[d, 1].astype(F32)
    dk_out[...] = dk * SCALE
    dv_out[...] = dv

    for d in range(1, NT):
        source = lax.rem(t + NT - d, NT)
        remote(DQF.at[0], DQI.at[source], gs.at[d], gr.at[d], tpeer(d)).wait_recv()
    for i in range(NT):
        dq_out[:, i * COLS : (i + 1) * COLS] = DQI[i]
    for copy in sent:
        copy.wait_send()
    for d in range(1, NZ):
        remote(SM, SR.at[NZ - d], ds_.at[d], dr.at[NZ - d], zpeer(d)).wait_send()


def body(queries, keys, values, grad_out, read_len, *, NT):
    R, D = queries.shape
    F = keys.shape[0]
    TOK, CH, NC = NT * R, 2 * NT * R, NZ // 2
    lens = read_len.reshape(NX, NZ * R)
    any_ = pl.BlockSpec(memory_space=pl.ANY)
    vmem = pl.BlockSpec(memory_space=pltpu.VMEM)
    dma = pltpu.SemaphoreType.DMA
    V = pltpu.VMEM
    return pl.pallas_call(
        lambda *refs: kernel(NT, *refs),
        out_shape=(
            jax.ShapeDtypeStruct((R, D), F32),
            jax.ShapeDtypeStruct((F, COLS), F32),
            jax.ShapeDtypeStruct((F, COLS), F32),
        ),
        in_specs=[any_, any_, any_, any_, vmem],
        out_specs=(vmem, vmem, vmem),
        scratch_shapes=[
            V((R, D), BF16),
            V((R, D), BF16),
            V((NZ, 2, NT, R, COLS), BF16),
            V((NX, 2, F, COLS), BF16),
            V((NT, 8, COLS), F32),
            V((8, COLS), F32),
            V((NZ, TOK, COLS), BF16),
            V((NX, 2 * F, 2 * COLS), BF16),
            V((NX, 2 * F, COLS), BF16),
            V((NX, COLS, 2 * F), BF16),
            V((NC, NX, 2, F, CH), F32),
            V((NC, NX, 2, F, CH), F32),
            V((NC, 2 * NX, CH), F32),
            V((NC, 8, TOK), F32),
            V((NZ, NC, 8, TOK), F32),
            V((2, NZ * TOK), F32),
            V((2, NZ * TOK), F32),
            V((NZ, TOK, COLS), BF16),
            V((NZ, TOK, COLS), BF16),
            V((TOK, COLS), F32),
            V((NT, R, COLS), F32),
            V((NT, R, COLS), F32),
            V((NX, F, COLS), F32),
            V((NX, F, COLS), F32),
            V((NX, 2, F, COLS), BF16),
            V((NX, 2, F, COLS), BF16),
            dma((4,)),
            dma((3, NT)), dma((3, NT)),
            dma((NZ,)), dma((NZ,)),
            dma((2, NX)), dma((2, NX)),
            dma((NZ,)), dma((NZ,)),
            dma((NZ,)), dma((NZ,)),
            dma((NX,)), dma((NX,)),
            dma((NT,)), dma((NT,)),
        ],
        compiler_params=pltpu.CompilerParams(
            collective_id=0, has_side_effects=True, vmem_limit_bytes=62 * 1024 * 1024
        ),
    )(queries, keys, values, grad_out, lens)


def solution(mesh):
    NT = mesh.shape["tgt"]
    return jax.shard_map(
        lambda *args: body(*args, NT=NT),
        mesh=mesh,
        in_specs=(
            P(("tgt", "src"), None),
            P("src", None),
            P("src", None),
            P(("tgt", "src"), None),
            P("tgt"),
        ),
        out_specs=(P(("tgt", "src"), None), P("src", "tgt"), P("src", "tgt")),
        check_vma=False,
    )
```

```python
import jax
import jax.numpy as jnp
from jax import lax
from jax.experimental import pallas as pl
from jax.experimental.pallas import tpu as pltpu
from jax.sharding import PartitionSpec as P

MESH = pl.DeviceIdType.MESH
NX, NZ = 4, 8
COLS = 128
MASK_BLOCK = 128
F32, BF16 = jnp.float32, jnp.bfloat16
HIDDEN = -1e30
SCALE = 0.125

REL = [0]
for _d in range(1, NZ // 2 + 1):
    REL += [_d] if 2 * _d == NZ else [_d, NZ - _d]
POS = {d: p for p, d in enumerate(REL)}


def kernel(
    NT, q_hbm, k_hbm, v_hbm, g_hbm, len_ref, dq_out, dk_out, dv_out,
    QI, GI, QG, KV, L, lrow, M, K2, V2, KT, W, G, MR, SM, SR, CF, RT, DQS, DQR, DQO, DQF, DQI, DK, DV, DKVS, DKVR,
    lsem, as_, ar, bs, br, cs, cr, ds_, dr, es, er, fs, fr, gs, gr,
):
    t = lax.axis_index("tgt")
    s = lax.axis_index("src")
    x = s // NZ
    z = s % NZ
    R, F = q_hbm.shape[0], k_hbm.shape[0]
    TOK = NT * R
    CH = 2 * TOK
    NC = NZ // 2

    def tpeer(d):
        return (lax.rem(t + d, NT), s)

    def zpeer(d):
        return (t, x * NZ + lax.rem(z + d, NZ))

    def xpeer(d):
        return (t, lax.rem(x + d, NX) * NZ + z)

    def cols(i):
        return pl.ds(pl.multiple_of(i * COLS, COLS), COLS)

    def remote(src, dst, ssem, rsem, dev):
        return pltpu.make_async_remote_copy(
            src_ref=src, dst_ref=dst, send_sem=ssem, recv_sem=rsem, device_id=dev, device_id_type=MESH
        )

    local = [
        pltpu.make_async_copy(q_hbm, QI, lsem.at[0]),
        pltpu.make_async_copy(g_hbm, GI, lsem.at[1]),
        pltpu.make_async_copy(k_hbm.at[:, cols(t)], KV.at[0, 0], lsem.at[2]),
        pltpu.make_async_copy(v_hbm.at[:, cols(t)], KV.at[0, 1], lsem.at[3]),
    ]
    for copy in local:
        copy.start()
    row = len_ref[pl.ds(x, 1), :].astype(F32)
    lrow[...] = jnp.broadcast_to(row, lrow.shape)
    L[pl.ds(t, 1)] = jnp.broadcast_to(row[None], (1,) + lrow.shape)

    barrier = pltpu.get_barrier_semaphore()
    peers = [tpeer(d) for d in range(1, NT)] + [zpeer(d) for d in range(1, NZ)] + [xpeer(d) for d in range(1, NX)]
    for dev in peers:
        pl.semaphore_signal(barrier, inc=1, device_id=dev, device_id_type=MESH)
    pl.semaphore_wait(barrier, len(peers))

    for copy in local:
        copy.wait()
    sent = []
    for d in range(1, NT):
        there = lax.rem(t + d, NT)
        sent += [
            remote(QI.at[:, cols(there)], QG.at[0, 0, t], as_.at[0, d], ar.at[0, d], tpeer(d)),
            remote(GI.at[:, cols(there)], QG.at[0, 1, t], as_.at[1, d], ar.at[1, d], tpeer(d)),
            remote(lrow, L.at[t], as_.at[2, d], ar.at[2, d], tpeer(d)),
        ]
    for d in range(1, NX):
        sent += [
            remote(KV.at[0, 0], KV.at[NX - d, 0], cs.at[0, d], cr.at[0, NX - d], xpeer(d)),
            remote(KV.at[0, 1], KV.at[NX - d, 1], cs.at[1, d], cr.at[1, NX - d], xpeer(d)),
        ]
    for copy in sent:
        copy.start()
    QG[0, 0, pl.ds(t, 1)] = QI[:, cols(t)][None]
    QG[0, 1, pl.ds(t, 1)] = GI[:, cols(t)][None]
    for d in range(1, NT):
        source = lax.rem(t + NT - d, NT)
        remote(QI.at[:, cols(t)], QG.at[0, 0, source], as_.at[0, d], ar.at[0, d], tpeer(d)).wait_recv()
        remote(QI.at[:, cols(t)], QG.at[0, 1, source], as_.at[1, d], ar.at[1, d], tpeer(d)).wait_recv()

    gather = []
    for d in REL[1:]:
        slot = POS[(NZ - d) % NZ]
        gather.append(remote(QG.at[0], QG.at[slot], bs.at[d], br.at[slot], zpeer(d)))
    for copy in gather:
        copy.start()
    sent += gather

    for d in range(1, NT):
        source = lax.rem(t + NT - d, NT)
        remote(lrow, L.at[source], as_.at[2, d], ar.at[2, d], tpeer(d)).wait_recv()
    lane3 = lax.broadcasted_iota(jnp.int32, (NT, R, COLS), 2)
    row3 = lax.broadcasted_iota(jnp.int32, (NT, R, COLS), 1)
    lens = jnp.broadcast_to(L[:, 0:1, :], (NT, R, COLS))
    per = F // MASK_BLOCK
    lanes = lax.broadcasted_iota(jnp.int32, (1, 1, COLS), 2)
    first = ((lax.rem(x + lanes // per, NX) * NZ + z) * per + lax.rem(lanes, per)) * MASK_BLOCK
    first = jnp.where(lanes < per * NX, first, -1).astype(F32)

    def mask_slot(p, rel):
        pick = lax.rem(z + rel, NZ) * R + row3
        column = jnp.sum(jnp.where(lane3 == pick, lens, 0.0), axis=2, keepdims=True)
        M[p] = jnp.where(first >= column, HIDDEN, 0.0).reshape(TOK, COLS).T.astype(BF16)

    for p in range(NZ):
        mask_slot(p, REL[p])

    lane2 = lax.broadcasted_iota(jnp.int32, (1, COLS), 1)
    head = [(lane2 < COLS // 2).astype(F32), (lane2 >= COLS // 2).astype(F32)]
    rows2 = lax.broadcasted_iota(jnp.int32, (F, COLS), 0)
    lanes2 = lax.broadcasted_iota(jnp.int32, (F, COLS), 1)
    for r in range(NX):
        if r > 0:
            remote(KV.at[0, 0], KV.at[r, 0], cs.at[0, r], cr.at[0, r], xpeer(r)).wait_recv()
            remote(KV.at[0, 0], KV.at[r, 1], cs.at[1, r], cr.at[1, r], xpeer(r)).wait_recv()
        kb = KV[r, 0].astype(F32)
        vb = KV[r, 1].astype(F32)
        hot = (lanes2 == rows2 // MASK_BLOCK + per * r).astype(F32).astype(BF16)
        for h in range(2):
            kh = (kb * (head[h] * SCALE)).astype(F32)
            K2[r, h * F : (h + 1) * F, 0:COLS] = kh.astype(BF16)
            K2[r, h * F : (h + 1) * F, COLS : 2 * COLS] = hot
            V2[r, h * F : (h + 1) * F, :] = (vb * head[h]).astype(BF16)
            KT[r, :, h * F : (h + 1) * F] = kh.T.astype(BF16)

    def block(ref, c, which):
        return ref[pl.ds(2 * c, 2), which].reshape(CH, COLS)

    def arrived(p):
        remote(QG.at[0], QG.at[p], bs.at[REL[1]], br.at[p], zpeer(1)).wait_recv()

    arrived(1)

    def pass1(c, _):
        qt = jnp.concatenate([block(QG, c, 0).T, jnp.concatenate([M[2 * c], M[2 * c + 1]], axis=1)], axis=0)
        gt = block(QG, c, 1).T
        found = [[] for _ in range(4)]

        def products(r, h):
            rows = slice(h * F, (h + 1) * F)
            W[c, r, h] = jnp.dot(K2[r, rows], qt, preferred_element_type=F32)
            G[c, r, h] = jnp.dot(V2[r, rows], gt, preferred_element_type=F32)

        def reduce(r, h):
            for half in range(2):
                piece = slice(half * TOK, (half + 1) * TOK)
                sc = W[c, r, h, :, piece]
                m = jnp.max(sc, axis=0, keepdims=True)
                w = jnp.exp(sc - m)
                W[c, r, h, :, piece] = w
                MR[c, 2 * r + h : 2 * r + h + 1, piece] = m
                l = jnp.sum(w, axis=0, keepdims=True)
                found[2 * h + half].append((m, l, jnp.sum(w * G[c, r, h, :, piece], axis=0, keepdims=True)))

        order = [(r, h) for r in range(NX) for h in range(2)]
        products(*order[0])
        for now, later in zip(order, order[1:] + [None]):
            if later is not None:
                products(*later)
            reduce(*now)
        for h in range(2):
            for half in range(2):
                top = found[2 * h + half][0][0]
                for m, _, _ in found[2 * h + half][1:]:
                    top = jnp.maximum(top, m)
                total = jnp.zeros_like(top)
                term = jnp.zeros_like(top)
                for m, l, tt in found[2 * h + half]:
                    a = jnp.exp(m - top)
                    total += a * l
                    term += a * tt
                row = 2 * half + h
                SM[c, row : row + 1, :] = top + jnp.log(total)
                SM[c, 4 + row : 5 + row, :] = term / total
        for d in REL[1:]:
            remote(SM.at[c], SR.at[NZ - d, c], ds_.at[d], dr.at[NZ - d], zpeer(d)).start()

        @pl.when(c < NC - 1)
        def _():
            for p in range(2):
                slot = 2 * c + 2 + p
                remote(QG.at[0], QG.at[slot], bs.at[REL[1]], br.at[slot], zpeer(1)).wait_recv()

        return 0

    lax.fori_loop(0, NC, pass1, 0)

    DK[...] = jnp.zeros_like(DK)
    DV[...] = jnp.zeros_like(DV)
    masks = [m.astype(BF16) for m in head]

    for d in range(1, NZ):
        remote(SM, SR.at[d], ds_.at[d], dr.at[d], zpeer(d)).wait_recv()

    def combine(p):
        parts, terms = [], []
        for d in range(NZ):
            theirs = POS[(REL[p] - d) % NZ]
            ref = SM if d == 0 else SR.at[d]
            row = 2 * (theirs % 2)
            parts.append(ref[theirs // 2, row : row + 2, :])
            terms.append(ref[theirs // 2, 4 + row : 6 + row, :])
        top = parts[0]
        for part in parts[1:]:
            top = jnp.maximum(top, part)
        total = jnp.zeros_like(top)
        term = jnp.zeros_like(top)
        for part, other in zip(parts, terms):
            weight = jnp.exp(part - top)
            total += weight
            term += weight * other
        CF[:, p * TOK : (p + 1) * TOK] = top + jnp.log(total)
        RT[:, p * TOK : (p + 1) * TOK] = term / total

    for p in range(NZ):
        combine(p)

    def two_heads(v):
        return jnp.concatenate([v * masks[0], v * masks[1]], axis=0)

    def tile(c, r):
        ps, gs_ = [], []
        for h in range(2):
            cf = jnp.exp(MR[c, 2 * r + h : 2 * r + h + 1, :] - CF[h : h + 1, c * CH : (c + 1) * CH])
            p = W[c, r, h] * cf
            ps.append(p.astype(BF16))
            gs_.append((p * (G[c, r, h] - RT[h : h + 1, c * CH : (c + 1) * CH])).astype(BF16))
        q2, g2 = two_heads(block(QG, c, 0)), two_heads(block(QG, c, 1))
        dv = jnp.dot(jnp.concatenate(ps, axis=1), g2, preferred_element_type=F32)
        dk = jnp.dot(jnp.concatenate(gs_, axis=1), q2, preferred_element_type=F32)
        dqt = jnp.dot(KT[r], jnp.concatenate(gs_, axis=0), preferred_element_type=F32)
        return dk, dv, dqt

    def send_dq(p):
        d = REL[p]
        sent.append(remote(DQS.at[p], DQR.at[NZ - d], es.at[d], er.at[NZ - d], zpeer(d)))
        sent[-1].start()

    for c in range(NC - 1, 1, -1):
        dq = jnp.zeros((COLS, CH), F32)
        for r in range(NX):
            dk, dv, dqt = tile(c, r)
            DK[r] += dk
            DV[r] += dv
            dq += dqt
        DQS[2 * c : 2 * c + 2] = dq.T.astype(BF16).reshape(2, TOK, COLS)
        send_dq(2 * c)
        send_dq(2 * c + 1)

    near = [jnp.zeros((COLS, CH), F32)] * 2
    for r in [NX // 2] + [i for i in range(1, NX) if i != NX // 2] + [0]:
        dk, dv = DK[r], DV[r]
        for c in range(2):
            dk1, dv1, dqt = tile(c, r)
            dk += dk1
            dv += dv1
            near[c] += dqt
        if r == 0:
            DK[0] = dk
            DV[0] = dv
        else:
            DKVS[r, 0] = dk.astype(BF16)
            DKVS[r, 1] = dv.astype(BF16)
            sent.append(remote(DKVS.at[r], DKVR.at[NX - r], fs.at[r], fr.at[NX - r], xpeer(r)))
            sent[-1].start()
    for c in [1, 0]:
        dq = near[c].T
        DQS[2 * c : 2 * c + 2] = dq.astype(BF16).reshape(2, TOK, COLS)
        for p in [2 * c, 2 * c + 1]:
            if p > 0:
                send_dq(p)
            else:
                DQO[...] = dq[0:TOK]

    for d in range(1, NZ):
        remote(DQS.at[0], DQR.at[d], es.at[d], er.at[d], zpeer(d)).wait_recv()
    dq = DQO[...]
    for d in range(1, NZ):
        dq += DQR[d].astype(F32)
    DQF[...] = dq.reshape(NT, R, COLS)
    back = []
    for d in range(1, NT):
        back.append(remote(DQF.at[lax.rem(t + d, NT)], DQI.at[t], gs.at[d], gr.at[d], tpeer(d)))
        back[-1].start()
    sent += back
    DQI[pl.ds(t, 1)] = DQF[pl.ds(t, 1)]

    for d in range(1, NX):
        remote(DKVS.at[d], DKVR.at[d], fs.at[d], fr.at[d], xpeer(d)).wait_recv()
    dk, dv = DK[0], DV[0]
    for d in range(1, NX):
        dk += DKVR[d, 0].astype(F32)
        dv += DKVR[d, 1].astype(F32)
    dk_out[...] = dk * SCALE
    dv_out[...] = dv

    for d in range(1, NT):
        source = lax.rem(t + NT - d, NT)
        remote(DQF.at[0], DQI.at[source], gs.at[d], gr.at[d], tpeer(d)).wait_recv()
    for i in range(NT):
        dq_out[:, i * COLS : (i + 1) * COLS] = DQI[i]
    for copy in sent:
        copy.wait_send()
    for d in range(1, NZ):
        remote(SM, SR.at[NZ - d], ds_.at[d], dr.at[NZ - d], zpeer(d)).wait_send()


def body(queries, keys, values, grad_out, read_len, *, NT):
    R, D = queries.shape
    F = keys.shape[0]
    TOK, CH, NC = NT * R, 2 * NT * R, NZ // 2
    lens = read_len.reshape(NX, NZ * R)
    any_ = pl.BlockSpec(memory_space=pl.ANY)
    vmem = pl.BlockSpec(memory_space=pltpu.VMEM)
    dma = pltpu.SemaphoreType.DMA
    V = pltpu.VMEM
    return pl.pallas_call(
        lambda *refs: kernel(NT, *refs),
        out_shape=(
            jax.ShapeDtypeStruct((R, D), F32),
            jax.ShapeDtypeStruct((F, COLS), F32),
            jax.ShapeDtypeStruct((F, COLS), F32),
        ),
        in_specs=[any_, any_, any_, any_, vmem],
        out_specs=(vmem, vmem, vmem),
        scratch_shapes=[
            V((R, D), BF16),
            V((R, D), BF16),
            V((NZ, 2, NT, R, COLS), BF16),
            V((NX, 2, F, COLS), BF16),
            V((NT, 8, COLS), F32),
            V((8, COLS), F32),
            V((NZ, COLS, TOK), BF16),
            V((NX, 2 * F, 2 * COLS), BF16),
            V((NX, 2 * F, COLS), BF16),
            V((NX, COLS, 2 * F), BF16),
            V((NC, NX, 2, F, CH), F32),
            V((NC, NX, 2, F, CH), F32),
            V((NC, 2 * NX, CH), F32),
            V((NC, 8, TOK), F32),
            V((NZ, NC, 8, TOK), F32),
            V((2, NZ * TOK), F32),
            V((2, NZ * TOK), F32),
            V((NZ, TOK, COLS), BF16),
            V((NZ, TOK, COLS), BF16),
            V((TOK, COLS), F32),
            V((NT, R, COLS), F32),
            V((NT, R, COLS), F32),
            V((NX, F, COLS), F32),
            V((NX, F, COLS), F32),
            V((NX, 2, F, COLS), BF16),
            V((NX, 2, F, COLS), BF16),
            dma((4,)),
            dma((3, NT)), dma((3, NT)),
            dma((NZ,)), dma((NZ,)),
            dma((2, NX)), dma((2, NX)),
            dma((NZ,)), dma((NZ,)),
            dma((NZ,)), dma((NZ,)),
            dma((NX,)), dma((NX,)),
            dma((NT,)), dma((NT,)),
        ],
        compiler_params=pltpu.CompilerParams(
            collective_id=0, has_side_effects=True, vmem_limit_bytes=62 * 1024 * 1024
        ),
    )(queries, keys, values, grad_out, lens)


def solution(mesh):
    NT = mesh.shape["tgt"]
    return jax.shard_map(
        lambda *args: body(*args, NT=NT),
        mesh=mesh,
        in_specs=(
            P(("tgt", "src"), None),
            P("src", None),
            P("src", None),
            P(("tgt", "src"), None),
            P("tgt"),
        ),
        out_specs=(P(("tgt", "src"), None), P("src", "tgt"), P("src", "tgt")),
        check_vma=False,
    )
```

```python
import jax
import jax.numpy as jnp
from jax import lax
from jax.experimental import pallas as pl
from jax.experimental.pallas import tpu as pltpu
from jax.sharding import PartitionSpec as P

MESH = pl.DeviceIdType.MESH
NX, NZ = 4, 8
COLS = 128
MASK_BLOCK = 128
F32, BF16 = jnp.float32, jnp.bfloat16
HIDDEN = -1e30
SCALE = 0.125

REL = [0]
for _d in range(1, NZ // 2 + 1):
    REL += [_d] if 2 * _d == NZ else [_d, NZ - _d]
POS = {d: p for p, d in enumerate(REL)}


def kernel(
    NT, q_hbm, k_hbm, v_hbm, g_hbm, len_ref, dq_out, dk_out, dv_out,
    QI, GI, QG, KV, L, lrow, M, K2, V2, KT, W, G, MR, SM, SR, CF, RT, DQS, DQR, DQO, DQF, DQI, DK, DV, DKVS, DKVR,
    lsem, as_, ar, bs, br, cs, cr, ds_, dr, es, er, fs, fr, gs, gr,
):
    t = lax.axis_index("tgt")
    s = lax.axis_index("src")
    x = s // NZ
    z = s % NZ
    R, F = q_hbm.shape[0], k_hbm.shape[0]
    TOK = NT * R
    CH = 2 * TOK
    NC = NZ // 2

    def tpeer(d):
        return (lax.rem(t + d, NT), s)

    def zpeer(d):
        return (t, x * NZ + lax.rem(z + NZ + d, NZ))

    def xpeer(d):
        return (t, lax.rem(x + d, NX) * NZ + z)

    def cols(i):
        return pl.ds(pl.multiple_of(i * COLS, COLS), COLS)

    def remote(src, dst, ssem, rsem, dev):
        return pltpu.make_async_remote_copy(
            src_ref=src, dst_ref=dst, send_sem=ssem, recv_sem=rsem, device_id=dev, device_id_type=MESH
        )

    local = [
        pltpu.make_async_copy(q_hbm, QI, lsem.at[0]),
        pltpu.make_async_copy(g_hbm, GI, lsem.at[1]),
        pltpu.make_async_copy(k_hbm.at[:, cols(t)], KV.at[0, 0], lsem.at[2]),
        pltpu.make_async_copy(v_hbm.at[:, cols(t)], KV.at[0, 1], lsem.at[3]),
    ]
    for copy in local:
        copy.start()
    row = len_ref[pl.ds(x, 1), :].astype(F32)
    lrow[...] = jnp.broadcast_to(row, lrow.shape)
    L[pl.ds(t, 1)] = jnp.broadcast_to(row[None], (1,) + lrow.shape)

    barrier = pltpu.get_barrier_semaphore()
    peers = [tpeer(d) for d in range(1, NT)] + [zpeer(d) for d in range(1, NZ)] + [xpeer(d) for d in range(1, NX)]
    for dev in peers:
        pl.semaphore_signal(barrier, inc=1, device_id=dev, device_id_type=MESH)
    pl.semaphore_wait(barrier, len(peers))

    for copy in local:
        copy.wait()
    sent = []
    for d in range(1, NT):
        there = lax.rem(t + d, NT)
        sent += [
            remote(QI.at[:, cols(there)], QG.at[0, 0, t], as_.at[0, d], ar.at[0, d], tpeer(d)),
            remote(GI.at[:, cols(there)], QG.at[0, 1, t], as_.at[1, d], ar.at[1, d], tpeer(d)),
            remote(lrow, L.at[t], as_.at[2, d], ar.at[2, d], tpeer(d)),
        ]
    for d in range(1, NX):
        sent += [
            remote(KV.at[0, 0], KV.at[NX - d, 0], cs.at[0, d], cr.at[0, NX - d], xpeer(d)),
            remote(KV.at[0, 1], KV.at[NX - d, 1], cs.at[1, d], cr.at[1, NX - d], xpeer(d)),
        ]
    for copy in sent:
        copy.start()
    QG[0, 0, pl.ds(t, 1)] = QI[:, cols(t)][None]
    QG[0, 1, pl.ds(t, 1)] = GI[:, cols(t)][None]
    for d in range(1, NT):
        source = lax.rem(t + NT - d, NT)
        remote(QI.at[:, cols(t)], QG.at[0, 0, source], as_.at[0, d], ar.at[0, d], tpeer(d)).wait_recv()
        remote(QI.at[:, cols(t)], QG.at[0, 1, source], as_.at[1, d], ar.at[1, d], tpeer(d)).wait_recv()

    def hop(part, slot, dest):
        dev = zpeer(1 - 2 * (dest % 2)) if isinstance(dest, int) else zpeer(1 - 2 * lax.rem(dest, 2))
        return remote(QG.at[slot, part], QG.at[dest, part], bs.at[part, dest], br.at[part, dest], dev)

    for part in range(2):
        for dest in (1, 2):
            sent.append(hop(part, 0, dest))
            sent[-1].start()

    for d in range(1, NT):
        source = lax.rem(t + NT - d, NT)
        remote(lrow, L.at[source], as_.at[2, d], ar.at[2, d], tpeer(d)).wait_recv()
    lane3 = lax.broadcasted_iota(jnp.int32, (NT, R, COLS), 2)
    row3 = lax.broadcasted_iota(jnp.int32, (NT, R, COLS), 1)
    lens = jnp.broadcast_to(L[:, 0:1, :], (NT, R, COLS))
    per = F // MASK_BLOCK
    lanes = lax.broadcasted_iota(jnp.int32, (1, 1, COLS), 2)
    first = ((lax.rem(x + lanes // per, NX) * NZ + z) * per + lax.rem(lanes, per)) * MASK_BLOCK
    first = jnp.where(lanes < per * NX, first, -1).astype(F32)

    def mask_slot(p, rel):
        pick = lax.rem(z + rel, NZ) * R + row3
        column = jnp.sum(jnp.where(lane3 == pick, lens, 0.0), axis=2, keepdims=True)
        M[p] = jnp.where(first >= column, HIDDEN, 0.0).reshape(TOK, COLS).T.astype(BF16)

    for p in range(NZ):
        mask_slot(p, REL[p])

    lane2 = lax.broadcasted_iota(jnp.int32, (1, COLS), 1)
    head = [(lane2 < COLS // 2).astype(F32), (lane2 >= COLS // 2).astype(F32)]
    rows2 = lax.broadcasted_iota(jnp.int32, (F, COLS), 0)
    lanes2 = lax.broadcasted_iota(jnp.int32, (F, COLS), 1)
    for r in range(NX):
        if r > 0:
            remote(KV.at[0, 0], KV.at[r, 0], cs.at[0, r], cr.at[0, r], xpeer(r)).wait_recv()
            remote(KV.at[0, 0], KV.at[r, 1], cs.at[1, r], cr.at[1, r], xpeer(r)).wait_recv()
        kb = KV[r, 0].astype(F32)
        vb = KV[r, 1].astype(F32)
        hot = (lanes2 == rows2 // MASK_BLOCK + per * r).astype(F32).astype(BF16)
        for h in range(2):
            kh = (kb * (head[h] * SCALE)).astype(F32)
            K2[r, h * F : (h + 1) * F, 0:COLS] = kh.astype(BF16)
            K2[r, h * F : (h + 1) * F, COLS : 2 * COLS] = hot
            V2[r, h * F : (h + 1) * F, :] = (vb * head[h]).astype(BF16)
            KT[r, :, h * F : (h + 1) * F] = kh.T.astype(BF16)

    def block(ref, c, which):
        return ref[pl.ds(2 * c, 2), which].reshape(CH, COLS)

    def arrived(part, slot):
        remote(QG.at[0, part], QG.at[slot, part], bs.at[part, 1], br.at[part, slot], zpeer(1)).wait_recv()

    def last_hop(part):
        dev = zpeer(1) if part == 0 else zpeer(-1)
        slot = NZ - 2 - part
        return remote(QG.at[slot, part], QG.at[NZ - 1, part], bs.at[part, NZ - 1], br.at[part, NZ - 1], dev)

    def pass1(c, _):
        @pl.when(c < NC - 1)
        def _():
            for part in range(2):
                for one in (1, 2):
                    slot = 2 * c + one
                    arrived(part, slot)

                    @pl.when(c < NC - 2)
                    def _():
                        hop(part, slot, slot + 2).start()

                @pl.when(c == NC - 2)
                def _():
                    last_hop(part).start()

        @pl.when(c == NC - 1)
        def _():
            for part in range(2):
                arrived(part, NZ - 1)

        qt = jnp.concatenate([block(QG, c, 0).T, jnp.concatenate([M[2 * c], M[2 * c + 1]], axis=1)], axis=0)
        gt = block(QG, c, 1).T
        found = [[] for _ in range(4)]

        def products(r, h):
            rows = slice(h * F, (h + 1) * F)
            W[c, r, h] = jnp.dot(K2[r, rows], qt, preferred_element_type=F32)
            G[c, r, h] = jnp.dot(V2[r, rows], gt, preferred_element_type=F32)

        def reduce(r, h):
            for half in range(2):
                piece = slice(half * TOK, (half + 1) * TOK)
                sc = W[c, r, h, :, piece]
                m = jnp.max(sc, axis=0, keepdims=True)
                w = jnp.exp(sc - m)
                W[c, r, h, :, piece] = w
                MR[c, 2 * r + h : 2 * r + h + 1, piece] = m
                l = jnp.sum(w, axis=0, keepdims=True)
                found[2 * h + half].append((m, l, jnp.sum(w * G[c, r, h, :, piece], axis=0, keepdims=True)))

        order = [(r, h) for r in range(NX) for h in range(2)]
        products(*order[0])
        for now, later in zip(order, order[1:] + [None]):
            if later is not None:
                products(*later)
            reduce(*now)
        for h in range(2):
            for half in range(2):
                top = found[2 * h + half][0][0]
                for m, _, _ in found[2 * h + half][1:]:
                    top = jnp.maximum(top, m)
                total = jnp.zeros_like(top)
                term = jnp.zeros_like(top)
                for m, l, tt in found[2 * h + half]:
                    a = jnp.exp(m - top)
                    total += a * l
                    term += a * tt
                row = 2 * half + h
                SM[c, row : row + 1, :] = top + jnp.log(total)
                SM[c, 4 + row : 5 + row, :] = term / total
        for d in REL[1:]:
            remote(SM.at[c], SR.at[NZ - d, c], ds_.at[d], dr.at[NZ - d], zpeer(d)).start()

        return 0

    lax.fori_loop(0, NC, pass1, 0)

    DK[...] = jnp.zeros_like(DK)
    DV[...] = jnp.zeros_like(DV)
    masks = [m.astype(BF16) for m in head]

    for d in range(1, NZ):
        remote(SM, SR.at[d], ds_.at[d], dr.at[d], zpeer(d)).wait_recv()

    def combine(p):
        parts, terms = [], []
        for d in range(NZ):
            theirs = POS[(REL[p] - d) % NZ]
            ref = SM if d == 0 else SR.at[d]
            row = 2 * (theirs % 2)
            parts.append(ref[theirs // 2, row : row + 2, :])
            terms.append(ref[theirs // 2, 4 + row : 6 + row, :])
        top = parts[0]
        for part in parts[1:]:
            top = jnp.maximum(top, part)
        total = jnp.zeros_like(top)
        term = jnp.zeros_like(top)
        for part, other in zip(parts, terms):
            weight = jnp.exp(part - top)
            total += weight
            term += weight * other
        CF[:, p * TOK : (p + 1) * TOK] = top + jnp.log(total)
        RT[:, p * TOK : (p + 1) * TOK] = term / total

    for p in range(NZ):
        combine(p)

    def two_heads(v):
        return jnp.concatenate([v * masks[0], v * masks[1]], axis=0)

    def tile(c, r):
        ps, gs_ = [], []
        for h in range(2):
            cf = jnp.exp(MR[c, 2 * r + h : 2 * r + h + 1, :] - CF[h : h + 1, c * CH : (c + 1) * CH])
            p = W[c, r, h] * cf
            ps.append(p.astype(BF16))
            gs_.append((p * (G[c, r, h] - RT[h : h + 1, c * CH : (c + 1) * CH])).astype(BF16))
        q2, g2 = two_heads(block(QG, c, 0)), two_heads(block(QG, c, 1))
        dv = jnp.dot(jnp.concatenate(ps, axis=1), g2, preferred_element_type=F32)
        dk = jnp.dot(jnp.concatenate(gs_, axis=1), q2, preferred_element_type=F32)
        dqt = jnp.dot(KT[r], jnp.concatenate(gs_, axis=0), preferred_element_type=F32)
        return dk, dv, dqt

    def send_dq(p):
        d = REL[p]
        sent.append(remote(DQS.at[p], DQR.at[NZ - d], es.at[d], er.at[NZ - d], zpeer(d)))
        sent[-1].start()

    for c in range(NC - 1, 1, -1):
        dq = jnp.zeros((COLS, CH), F32)
        for r in range(NX):
            dk, dv, dqt = tile(c, r)
            DK[r] += dk
            DV[r] += dv
            dq += dqt
        DQS[2 * c : 2 * c + 2] = dq.T.astype(BF16).reshape(2, TOK, COLS)
        send_dq(2 * c)
        send_dq(2 * c + 1)

    near = [jnp.zeros((COLS, CH), F32)] * 2
    for r in [NX // 2] + [i for i in range(1, NX) if i != NX // 2] + [0]:
        dk, dv = DK[r], DV[r]
        for c in range(2):
            dk1, dv1, dqt = tile(c, r)
            dk += dk1
            dv += dv1
            near[c] += dqt
        if r == 0:
            DK[0] = dk
            DV[0] = dv
        else:
            DKVS[r, 0] = dk.astype(BF16)
            DKVS[r, 1] = dv.astype(BF16)
            sent.append(remote(DKVS.at[r], DKVR.at[NX - r], fs.at[r], fr.at[NX - r], xpeer(r)))
            sent[-1].start()
    for c in [1, 0]:
        dq = near[c].T
        DQS[2 * c : 2 * c + 2] = dq.astype(BF16).reshape(2, TOK, COLS)
        for p in [2 * c, 2 * c + 1]:
            if p > 0:
                send_dq(p)
            else:
                DQO[...] = dq[0:TOK]

    for d in range(1, NZ):
        remote(DQS.at[0], DQR.at[d], es.at[d], er.at[d], zpeer(d)).wait_recv()
    dq = DQO[...]
    for d in range(1, NZ):
        dq += DQR[d].astype(F32)
    DQF[...] = dq.reshape(NT, R, COLS)
    back = []
    for d in range(1, NT):
        back.append(remote(DQF.at[lax.rem(t + d, NT)], DQI.at[t], gs.at[d], gr.at[d], tpeer(d)))
        back[-1].start()
    sent += back
    DQI[pl.ds(t, 1)] = DQF[pl.ds(t, 1)]

    for d in range(1, NX):
        remote(DKVS.at[d], DKVR.at[d], fs.at[d], fr.at[d], xpeer(d)).wait_recv()
    dk, dv = DK[0], DV[0]
    for d in range(1, NX):
        dk += DKVR[d, 0].astype(F32)
        dv += DKVR[d, 1].astype(F32)
    dk_out[...] = dk * SCALE
    dv_out[...] = dv

    for d in range(1, NT):
        source = lax.rem(t + NT - d, NT)
        remote(DQF.at[0], DQI.at[source], gs.at[d], gr.at[d], tpeer(d)).wait_recv()
    for i in range(NT):
        dq_out[:, i * COLS : (i + 1) * COLS] = DQI[i]
    for copy in sent:
        copy.wait_send()
    for part in range(2):
        for dest in range(3, NZ - 1):
            hop(part, dest - 2, dest).wait_send()
        last_hop(part).wait_send()
    for d in range(1, NZ):
        remote(SM, SR.at[NZ - d], ds_.at[d], dr.at[NZ - d], zpeer(d)).wait_send()


def body(queries, keys, values, grad_out, read_len, *, NT):
    R, D = queries.shape
    F = keys.shape[0]
    TOK, CH, NC = NT * R, 2 * NT * R, NZ // 2
    lens = read_len.reshape(NX, NZ * R)
    any_ = pl.BlockSpec(memory_space=pl.ANY)
    vmem = pl.BlockSpec(memory_space=pltpu.VMEM)
    dma = pltpu.SemaphoreType.DMA
    V = pltpu.VMEM
    return pl.pallas_call(
        lambda *refs: kernel(NT, *refs),
        out_shape=(
            jax.ShapeDtypeStruct((R, D), F32),
            jax.ShapeDtypeStruct((F, COLS), F32),
            jax.ShapeDtypeStruct((F, COLS), F32),
        ),
        in_specs=[any_, any_, any_, any_, vmem],
        out_specs=(vmem, vmem, vmem),
        scratch_shapes=[
            V((R, D), BF16),
            V((R, D), BF16),
            V((NZ, 2, NT, R, COLS), BF16),
            V((NX, 2, F, COLS), BF16),
            V((NT, 8, COLS), F32),
            V((8, COLS), F32),
            V((NZ, COLS, TOK), BF16),
            V((NX, 2 * F, 2 * COLS), BF16),
            V((NX, 2 * F, COLS), BF16),
            V((NX, COLS, 2 * F), BF16),
            V((NC, NX, 2, F, CH), F32),
            V((NC, NX, 2, F, CH), F32),
            V((NC, 2 * NX, CH), F32),
            V((NC, 8, TOK), F32),
            V((NZ, NC, 8, TOK), F32),
            V((2, NZ * TOK), F32),
            V((2, NZ * TOK), F32),
            V((NZ, TOK, COLS), BF16),
            V((NZ, TOK, COLS), BF16),
            V((TOK, COLS), F32),
            V((NT, R, COLS), F32),
            V((NT, R, COLS), F32),
            V((NX, F, COLS), F32),
            V((NX, F, COLS), F32),
            V((NX, 2, F, COLS), BF16),
            V((NX, 2, F, COLS), BF16),
            dma((4,)),
            dma((3, NT)), dma((3, NT)),
            dma((2, NZ)), dma((2, NZ)),
            dma((2, NX)), dma((2, NX)),
            dma((NZ,)), dma((NZ,)),
            dma((NZ,)), dma((NZ,)),
            dma((NX,)), dma((NX,)),
            dma((NT,)), dma((NT,)),
        ],
        compiler_params=pltpu.CompilerParams(
            collective_id=0, has_side_effects=True, vmem_limit_bytes=62 * 1024 * 1024
        ),
    )(queries, keys, values, grad_out, lens)


def solution(mesh):
    NT = mesh.shape["tgt"]
    return jax.shard_map(
        lambda *args: body(*args, NT=NT),
        mesh=mesh,
        in_specs=(
            P(("tgt", "src"), None),
            P("src", None),
            P("src", None),
            P(("tgt", "src"), None),
            P("tgt"),
        ),
        out_specs=(P(("tgt", "src"), None), P("src", "tgt"), P("src", "tgt")),
        check_vma=False,
    )
```

```python
import jax
import jax.numpy as jnp
from jax import lax
from jax.experimental import pallas as pl
from jax.experimental.pallas import tpu as pltpu
from jax.sharding import PartitionSpec as P

MESH = pl.DeviceIdType.MESH
NX, NZ = 4, 8
COLS = 128
MASK_BLOCK = 128
F32, BF16 = jnp.float32, jnp.bfloat16
HIDDEN = -1e30
SCALE = 0.125

REL = [0]
for _d in range(1, NZ // 2 + 1):
    REL += [_d] if 2 * _d == NZ else [_d, NZ - _d]
POS = {d: p for p, d in enumerate(REL)}


def kernel(
    NT, q_hbm, k_hbm, v_hbm, g_hbm, len_ref, dq_out, dk_out, dv_out,
    QI, GI, QG, KV, L, lrow, M, K2, V2, KT, W, G, MR, SM, SR, CF, RT, DQS, DQR, DK, DV, DKVS, DKVR,
    lsem, as_, ar, bs, br, cs, cr, ds_, dr, es, er, fs, fr, gs, gr,
):
    t = lax.axis_index("tgt")
    s = lax.axis_index("src")
    x = s // NZ
    z = s % NZ
    R, F = q_hbm.shape[0], k_hbm.shape[0]
    TOK = NT * R
    CH = 2 * TOK
    NC = NZ // 2

    def tpeer(d):
        return (lax.rem(t + d, NT), s)

    def zpeer(d):
        return (t, x * NZ + lax.rem(z + NZ + d, NZ))

    def xpeer(d):
        return (t, lax.rem(x + d, NX) * NZ + z)

    def cols(i):
        return pl.ds(pl.multiple_of(i * COLS, COLS), COLS)

    def remote(src, dst, ssem, rsem, dev):
        return pltpu.make_async_remote_copy(
            src_ref=src, dst_ref=dst, send_sem=ssem, recv_sem=rsem, device_id=dev, device_id_type=MESH
        )

    local = [
        pltpu.make_async_copy(q_hbm, QI, lsem.at[0]),
        pltpu.make_async_copy(g_hbm, GI, lsem.at[1]),
        pltpu.make_async_copy(k_hbm.at[:, cols(t)], KV.at[0, 0], lsem.at[2]),
        pltpu.make_async_copy(v_hbm.at[:, cols(t)], KV.at[0, 1], lsem.at[3]),
    ]
    for copy in local:
        copy.start()
    row = len_ref[pl.ds(x, 1), :].astype(F32)
    lrow[...] = jnp.broadcast_to(row, lrow.shape)
    L[pl.ds(t, 1)] = jnp.broadcast_to(row[None], (1,) + lrow.shape)

    barrier = pltpu.get_barrier_semaphore()
    peers = [tpeer(d) for d in range(1, NT)] + [zpeer(d) for d in range(1, NZ)] + [xpeer(d) for d in range(1, NX)]
    for dev in peers:
        pl.semaphore_signal(barrier, inc=1, device_id=dev, device_id_type=MESH)
    pl.semaphore_wait(barrier, len(peers))

    for copy in local:
        copy.wait()
    sent = []
    for d in range(1, NT):
        there = lax.rem(t + d, NT)
        sent += [
            remote(QI.at[:, cols(there)], QG.at[0, 0, t], as_.at[0, d], ar.at[0, d], tpeer(d)),
            remote(GI.at[:, cols(there)], QG.at[0, 1, t], as_.at[1, d], ar.at[1, d], tpeer(d)),
            remote(lrow, L.at[t], as_.at[2, d], ar.at[2, d], tpeer(d)),
        ]
    for d in range(1, NX):
        sent += [
            remote(KV.at[0, 0], KV.at[NX - d, 0], cs.at[0, d], cr.at[0, NX - d], xpeer(d)),
            remote(KV.at[0, 1], KV.at[NX - d, 1], cs.at[1, d], cr.at[1, NX - d], xpeer(d)),
        ]
    for copy in sent:
        copy.start()
    QG[0, 0, pl.ds(t, 1)] = QI[:, cols(t)][None]
    QG[0, 1, pl.ds(t, 1)] = GI[:, cols(t)][None]
    for d in range(1, NT):
        source = lax.rem(t + NT - d, NT)
        remote(QI.at[:, cols(t)], QG.at[0, 0, source], as_.at[0, d], ar.at[0, d], tpeer(d)).wait_recv()
        remote(QI.at[:, cols(t)], QG.at[0, 1, source], as_.at[1, d], ar.at[1, d], tpeer(d)).wait_recv()

    def hop(part, slot, dest):
        dev = zpeer(1 - 2 * (dest % 2)) if isinstance(dest, int) else zpeer(1 - 2 * lax.rem(dest, 2))
        return remote(QG.at[slot, part], QG.at[dest, part], bs.at[part, dest], br.at[part, dest], dev)

    for part in range(2):
        for dest in (1, 2):
            sent.append(hop(part, 0, dest))
            sent[-1].start()

    for d in range(1, NT):
        source = lax.rem(t + NT - d, NT)
        remote(lrow, L.at[source], as_.at[2, d], ar.at[2, d], tpeer(d)).wait_recv()
    lane3 = lax.broadcasted_iota(jnp.int32, (NT, R, COLS), 2)
    row3 = lax.broadcasted_iota(jnp.int32, (NT, R, COLS), 1)
    lens = jnp.broadcast_to(L[:, 0:1, :], (NT, R, COLS))
    per = F // MASK_BLOCK
    lanes = lax.broadcasted_iota(jnp.int32, (1, 1, COLS), 2)
    first = ((lax.rem(x + lanes // per, NX) * NZ + z) * per + lax.rem(lanes, per)) * MASK_BLOCK
    first = jnp.where(lanes < per * NX, first, -1).astype(F32)

    def mask_slot(p, rel):
        pick = lax.rem(z + rel, NZ) * R + row3
        column = jnp.sum(jnp.where(lane3 == pick, lens, 0.0), axis=2, keepdims=True)
        M[p] = jnp.where(first >= column, HIDDEN, 0.0).reshape(TOK, COLS).T.astype(BF16)

    for p in range(NZ):
        mask_slot(p, REL[p])

    def arrived(part, slot):
        remote(QG.at[0, part], QG.at[slot, part], bs.at[part, 1], br.at[part, slot], zpeer(1)).wait_recv()

    def last_hop(part):
        dev = zpeer(1) if part == 0 else zpeer(-1)
        slot = NZ - 2 - part
        return remote(QG.at[slot, part], QG.at[NZ - 1, part], bs.at[part, NZ - 1], br.at[part, NZ - 1], dev)

    for part in range(2):
        for slot in (1, 2):
            arrived(part, slot)
            hop(part, slot, slot + 2).start()

    lane2 = lax.broadcasted_iota(jnp.int32, (1, COLS), 1)
    head = [(lane2 < COLS // 2).astype(F32), (lane2 >= COLS // 2).astype(F32)]
    rows2 = lax.broadcasted_iota(jnp.int32, (F, COLS), 0)
    lanes2 = lax.broadcasted_iota(jnp.int32, (F, COLS), 1)
    for r in range(NX):
        if r > 0:
            remote(KV.at[0, 0], KV.at[r, 0], cs.at[0, r], cr.at[0, r], xpeer(r)).wait_recv()
            remote(KV.at[0, 0], KV.at[r, 1], cs.at[1, r], cr.at[1, r], xpeer(r)).wait_recv()
        kb = KV[r, 0].astype(F32)
        vb = KV[r, 1].astype(F32)
        hot = (lanes2 == rows2 // MASK_BLOCK + per * r).astype(F32).astype(BF16)
        for h in range(2):
            kh = (kb * (head[h] * SCALE)).astype(F32)
            K2[r, h * F : (h + 1) * F, 0:COLS] = kh.astype(BF16)
            K2[r, h * F : (h + 1) * F, COLS : 2 * COLS] = hot
            V2[r, h * F : (h + 1) * F, :] = (vb * head[h]).astype(BF16)
            KT[r, :, h * F : (h + 1) * F] = kh.T.astype(BF16)

    def block(ref, c, which):
        return ref[pl.ds(2 * c, 2), which].reshape(CH, COLS)

    def pass1(c, _):
        qt = jnp.concatenate([block(QG, c, 0).T, jnp.concatenate([M[2 * c], M[2 * c + 1]], axis=1)], axis=0)
        gt = block(QG, c, 1).T
        found = [[] for _ in range(4)]

        def products(r, h):
            rows = slice(h * F, (h + 1) * F)
            W[c, r, h] = jnp.dot(K2[r, rows], qt, preferred_element_type=F32)
            G[c, r, h] = jnp.dot(V2[r, rows], gt, preferred_element_type=F32)

        def reduce(r, h):
            for half in range(2):
                piece = slice(half * TOK, (half + 1) * TOK)
                sc = W[c, r, h, :, piece]
                m = jnp.max(sc, axis=0, keepdims=True)
                w = jnp.exp(sc - m)
                W[c, r, h, :, piece] = w
                MR[c, 2 * r + h : 2 * r + h + 1, piece] = m
                l = jnp.sum(w, axis=0, keepdims=True)
                found[2 * h + half].append((m, l, jnp.sum(w * G[c, r, h, :, piece], axis=0, keepdims=True)))

        order = [(r, h) for r in range(NX) for h in range(2)]
        products(*order[0])
        for now, later in zip(order, order[1:] + [None]):
            if later is not None:
                products(*later)
            reduce(*now)
        for h in range(2):
            for half in range(2):
                top = found[2 * h + half][0][0]
                for m, _, _ in found[2 * h + half][1:]:
                    top = jnp.maximum(top, m)
                total = jnp.zeros_like(top)
                term = jnp.zeros_like(top)
                for m, l, tt in found[2 * h + half]:
                    a = jnp.exp(m - top)
                    total += a * l
                    term += a * tt
                row = 2 * half + h
                SM[c, row : row + 1, :] = top + jnp.log(total)
                SM[c, 4 + row : 5 + row, :] = term / total
        for d in REL[1:]:
            remote(SM.at[c], SR.at[NZ - d, c], ds_.at[d], dr.at[NZ - d], zpeer(d)).start()

        @pl.when(c < NC - 2)
        def _():
            for part in range(2):
                for one in (3, 4):
                    arrived(part, 2 * c + one)

                    @pl.when(c < NC - 3)
                    def _():
                        hop(part, 2 * c + one, 2 * c + one + 2).start()

                @pl.when(c == NC - 3)
                def _():
                    last_hop(part).start()

        @pl.when(c == NC - 2)
        def _():
            for part in range(2):
                arrived(part, NZ - 1)

        return 0

    lax.fori_loop(0, NC, pass1, 0)

    DK[...] = jnp.zeros_like(DK)
    DV[...] = jnp.zeros_like(DV)
    masks = [m.astype(BF16) for m in head]

    for d in range(1, NZ):
        remote(SM, SR.at[d], ds_.at[d], dr.at[d], zpeer(d)).wait_recv()

    def combine(p):
        parts, terms = [], []
        for d in range(NZ):
            theirs = POS[(REL[p] - d) % NZ]
            ref = SM if d == 0 else SR.at[d]
            row = 2 * (theirs % 2)
            parts.append(ref[theirs // 2, row : row + 2, :])
            terms.append(ref[theirs // 2, 4 + row : 6 + row, :])
        top = parts[0]
        for part in parts[1:]:
            top = jnp.maximum(top, part)
        total = jnp.zeros_like(top)
        term = jnp.zeros_like(top)
        for part, other in zip(parts, terms):
            weight = jnp.exp(part - top)
            total += weight
            term += weight * other
        CF[:, p * TOK : (p + 1) * TOK] = top + jnp.log(total)
        RT[:, p * TOK : (p + 1) * TOK] = term / total

    for p in range(NZ):
        combine(p)

    def two_heads(v):
        return jnp.concatenate([v * masks[0], v * masks[1]], axis=0)

    def tile(c, r):
        ps, gs_ = [], []
        for h in range(2):
            cf = jnp.exp(MR[c, 2 * r + h : 2 * r + h + 1, :] - CF[h : h + 1, c * CH : (c + 1) * CH])
            p = W[c, r, h] * cf
            ps.append(p.astype(BF16))
            gs_.append((p * (G[c, r, h] - RT[h : h + 1, c * CH : (c + 1) * CH])).astype(BF16))
        q2, g2 = two_heads(block(QG, c, 0)), two_heads(block(QG, c, 1))
        dv = jnp.dot(jnp.concatenate(ps, axis=1), g2, preferred_element_type=F32)
        dk = jnp.dot(jnp.concatenate(gs_, axis=1), q2, preferred_element_type=F32)
        dqt = jnp.dot(KT[r], jnp.concatenate(gs_, axis=0), preferred_element_type=F32)
        return dk, dv, dqt

    def send_dq(p):
        d = REL[p]
        for i in range(NT):
            if p > 0 or i > 0:
                there = lax.rem(t + i, NT)
                remote(
                    DQS.at[p, there], DQR.at[(NZ - d) % NZ, t],
                    es.at[d] if d else gs.at[i], er.at[(NZ - d) % NZ] if d else gr.at[i],
                    (there, x * NZ + lax.rem(z + d, NZ)),
                ).start()

    for c in range(NC - 1, 1, -1):
        dq = jnp.zeros((COLS, CH), F32)
        for r in range(NX):
            dk, dv, dqt = tile(c, r)
            DK[r] += dk
            DV[r] += dv
            dq += dqt
        DQS[2 * c : 2 * c + 2] = dq.T.astype(BF16).reshape(2, NT, R, COLS)
        send_dq(2 * c)
        send_dq(2 * c + 1)

    near = [jnp.zeros((COLS, CH), F32)] * 2
    for r in [NX // 2] + [i for i in range(1, NX) if i != NX // 2] + [0]:
        dk, dv = DK[r], DV[r]
        for c in range(2):
            dk1, dv1, dqt = tile(c, r)
            dk += dk1
            dv += dv1
            near[c] += dqt
        if r == 0:
            DK[0] = dk
            DV[0] = dv
        else:
            DKVS[r, 0] = dk.astype(BF16)
            DKVS[r, 1] = dv.astype(BF16)
            sent.append(remote(DKVS.at[r], DKVR.at[NX - r], fs.at[r], fr.at[NX - r], xpeer(r)))
            sent[-1].start()
    for c in [1, 0]:
        DQS[2 * c : 2 * c + 2] = near[c].T.astype(BF16).reshape(2, NT, R, COLS)
        send_dq(2 * c + 1)
        send_dq(2 * c)
    DQR[0, pl.ds(t, 1)] = DQS[0, pl.ds(t, 1)]

    for d in range(1, NX):
        remote(DKVS.at[d], DKVR.at[d], fs.at[d], fr.at[d], xpeer(d)).wait_recv()
    dk, dv = DK[0], DV[0]
    for d in range(1, NX):
        dk += DKVR[d, 0].astype(F32)
        dv += DKVR[d, 1].astype(F32)
    dk_out[...] = dk * SCALE
    dv_out[...] = dv

    for d in range(1, NT):
        source = lax.rem(t + NT - d, NT)
        remote(DQS.at[0, 0], DQR.at[0, source], gs.at[d], gr.at[d], tpeer(d)).wait_recv()
    for d in range(1, NZ):
        remote(DQS.at[POS[d]], DQR.at[d], es.at[d], er.at[d], zpeer(d)).wait_recv()
    for i in range(NT):
        dq = DQR[0, i].astype(F32)
        for d in range(1, NZ):
            dq += DQR[d, i].astype(F32)
        dq_out[:, i * COLS : (i + 1) * COLS] = dq
    for copy in sent:
        copy.wait_send()
    for part in range(2):
        for dest in range(3, NZ - 1):
            hop(part, dest - 2, dest).wait_send()
        last_hop(part).wait_send()
    for d in range(1, NT):
        remote(DQS.at[0, 0], DQR.at[0, 0], gs.at[d], gr.at[d], tpeer(d)).wait_send()
    for d in range(1, NZ):
        remote(DQS.at[POS[d]], DQR.at[d], es.at[d], er.at[d], zpeer(d)).wait_send()
    for d in range(1, NZ):
        remote(SM, SR.at[NZ - d], ds_.at[d], dr.at[NZ - d], zpeer(d)).wait_send()


def body(queries, keys, values, grad_out, read_len, *, NT):
    R, D = queries.shape
    F = keys.shape[0]
    TOK, CH, NC = NT * R, 2 * NT * R, NZ // 2
    lens = read_len.reshape(NX, NZ * R)
    any_ = pl.BlockSpec(memory_space=pl.ANY)
    vmem = pl.BlockSpec(memory_space=pltpu.VMEM)
    dma = pltpu.SemaphoreType.DMA
    V = pltpu.VMEM
    return pl.pallas_call(
        lambda *refs: kernel(NT, *refs),
        out_shape=(
            jax.ShapeDtypeStruct((R, D), F32),
            jax.ShapeDtypeStruct((F, COLS), F32),
            jax.ShapeDtypeStruct((F, COLS), F32),
        ),
        in_specs=[any_, any_, any_, any_, vmem],
        out_specs=(vmem, vmem, vmem),
        scratch_shapes=[
            V((R, D), BF16),
            V((R, D), BF16),
            V((NZ, 2, NT, R, COLS), BF16),
            V((NX, 2, F, COLS), BF16),
            V((NT, 8, COLS), F32),
            V((8, COLS), F32),
            V((NZ, COLS, TOK), BF16),
            V((NX, 2 * F, 2 * COLS), BF16),
            V((NX, 2 * F, COLS), BF16),
            V((NX, COLS, 2 * F), BF16),
            V((NC, NX, 2, F, CH), F32),
            V((NC, NX, 2, F, CH), F32),
            V((NC, 2 * NX, CH), F32),
            V((NC, 8, TOK), F32),
            V((NZ, NC, 8, TOK), F32),
            V((2, NZ * TOK), F32),
            V((2, NZ * TOK), F32),
            V((NZ, NT, R, COLS), BF16),
            V((NZ, NT, R, COLS), BF16),
            V((NX, F, COLS), F32),
            V((NX, F, COLS), F32),
            V((NX, 2, F, COLS), BF16),
            V((NX, 2, F, COLS), BF16),
            dma((4,)),
            dma((3, NT)), dma((3, NT)),
            dma((2, NZ)), dma((2, NZ)),
            dma((2, NX)), dma((2, NX)),
            dma((NZ,)), dma((NZ,)),
            dma((NZ,)), dma((NZ,)),
            dma((NX,)), dma((NX,)),
            dma((NT,)), dma((NT,)),
        ],
        compiler_params=pltpu.CompilerParams(
            collective_id=0, has_side_effects=True, vmem_limit_bytes=62 * 1024 * 1024
        ),
    )(queries, keys, values, grad_out, lens)


def solution(mesh):
    NT = mesh.shape["tgt"]
    return jax.shard_map(
        lambda *args: body(*args, NT=NT),
        mesh=mesh,
        in_specs=(
            P(("tgt", "src"), None),
            P("src", None),
            P("src", None),
            P(("tgt", "src"), None),
            P("tgt"),
        ),
        out_specs=(P(("tgt", "src"), None), P("src", "tgt"), P("src", "tgt")),
        check_vma=False,
    )
```

```python
import jax
import jax.numpy as jnp
from jax import lax
from jax.experimental import pallas as pl
from jax.experimental.pallas import tpu as pltpu
from jax.sharding import PartitionSpec as P

MESH = pl.DeviceIdType.MESH
NX, NZ = 4, 8
COLS = 128
MASK_BLOCK = 128
F32, BF16 = jnp.float32, jnp.bfloat16
HIDDEN = -1e30
SCALE = 0.125

REL = [0]
for _d in range(1, NZ // 2 + 1):
    REL += [_d] if 2 * _d == NZ else [_d, NZ - _d]
POS = {d: p for p, d in enumerate(REL)}


def kernel(
    NT, q_hbm, k_hbm, v_hbm, g_hbm, len_ref, dq_out, dk_out, dv_out,
    QI, GI, QG, KV, L, lrow, M, K2, V2, KT, W, G, MR, SM, SR, CF, RT, DQS, DQR, DK, DV, DKVS, DKVR,
    lsem, as_, ar, bs, br, cs, cr, ds_, dr, es, er, fs, fr, gs, gr,
):
    t = lax.axis_index("tgt")
    s = lax.axis_index("src")
    x = s // NZ
    z = s % NZ
    R, F = q_hbm.shape[0], k_hbm.shape[0]
    TOK = NT * R
    CH = 2 * TOK
    NC = NZ // 2

    def tpeer(d):
        return (lax.rem(t + d, NT), s)

    def zpeer(d):
        return (t, x * NZ + lax.rem(z + NZ + d, NZ))

    def xpeer(d):
        return (t, lax.rem(x + d, NX) * NZ + z)

    def cols(i):
        return pl.ds(pl.multiple_of(i * COLS, COLS), COLS)

    def remote(src, dst, ssem, rsem, dev):
        return pltpu.make_async_remote_copy(
            src_ref=src, dst_ref=dst, send_sem=ssem, recv_sem=rsem, device_id=dev, device_id_type=MESH
        )

    local = [
        pltpu.make_async_copy(q_hbm, QI, lsem.at[0]),
        pltpu.make_async_copy(g_hbm, GI, lsem.at[1]),
        pltpu.make_async_copy(k_hbm.at[:, cols(t)], KV.at[0, 0], lsem.at[2]),
        pltpu.make_async_copy(v_hbm.at[:, cols(t)], KV.at[0, 1], lsem.at[3]),
    ]
    for copy in local:
        copy.start()
    row = len_ref[pl.ds(x, 1), :].astype(F32)
    lrow[...] = jnp.broadcast_to(row, lrow.shape)
    L[pl.ds(t, 1)] = jnp.broadcast_to(row[None], (1,) + lrow.shape)

    barrier = pltpu.get_barrier_semaphore()
    peers = [tpeer(d) for d in range(1, NT)] + [zpeer(d) for d in range(1, NZ)] + [xpeer(d) for d in range(1, NX)]
    for dev in peers:
        pl.semaphore_signal(barrier, inc=1, device_id=dev, device_id_type=MESH)
    pl.semaphore_wait(barrier, len(peers))

    for copy in local:
        copy.wait()
    sent = []
    for d in range(1, NT):
        there = lax.rem(t + d, NT)
        sent += [
            remote(QI.at[:, cols(there)], QG.at[0, 0, t], as_.at[0, d], ar.at[0, d], tpeer(d)),
            remote(GI.at[:, cols(there)], QG.at[0, 1, t], as_.at[1, d], ar.at[1, d], tpeer(d)),
            remote(lrow, L.at[t], as_.at[2, d], ar.at[2, d], tpeer(d)),
        ]
    for d in range(1, NX):
        sent += [
            remote(KV.at[0, 0], KV.at[NX - d, 0], cs.at[0, d], cr.at[0, NX - d], xpeer(d)),
            remote(KV.at[0, 1], KV.at[NX - d, 1], cs.at[1, d], cr.at[1, NX - d], xpeer(d)),
        ]
    for copy in sent:
        copy.start()
    QG[0, 0, pl.ds(t, 1)] = QI[:, cols(t)][None]
    QG[0, 1, pl.ds(t, 1)] = GI[:, cols(t)][None]
    for d in range(1, NT):
        source = lax.rem(t + NT - d, NT)
        remote(QI.at[:, cols(t)], QG.at[0, 0, source], as_.at[0, d], ar.at[0, d], tpeer(d)).wait_recv()
        remote(QI.at[:, cols(t)], QG.at[0, 1, source], as_.at[1, d], ar.at[1, d], tpeer(d)).wait_recv()

    def hop(part, slot, dest):
        dev = zpeer(1 - 2 * (dest % 2)) if isinstance(dest, int) else zpeer(1 - 2 * lax.rem(dest, 2))
        return remote(QG.at[slot, part], QG.at[dest, part], bs.at[part, dest], br.at[part, dest], dev)

    for part in range(2):
        for dest in (1, 2):
            sent.append(hop(part, 0, dest))
            sent[-1].start()

    for d in range(1, NT):
        source = lax.rem(t + NT - d, NT)
        remote(lrow, L.at[source], as_.at[2, d], ar.at[2, d], tpeer(d)).wait_recv()
    lane3 = lax.broadcasted_iota(jnp.int32, (NT, R, COLS), 2)
    row3 = lax.broadcasted_iota(jnp.int32, (NT, R, COLS), 1)
    lens = jnp.broadcast_to(L[:, 0:1, :], (NT, R, COLS))
    per = F // MASK_BLOCK
    lanes = lax.broadcasted_iota(jnp.int32, (1, 1, COLS), 2)
    first = ((lax.rem(x + lanes // per, NX) * NZ + z) * per + lax.rem(lanes, per)) * MASK_BLOCK
    first = jnp.where(lanes < per * NX, first, -1).astype(F32)

    def mask_slot(p, rel):
        pick = lax.rem(z + rel, NZ) * R + row3
        column = jnp.sum(jnp.where(lane3 == pick, lens, 0.0), axis=2, keepdims=True)
        M[p] = jnp.where(first >= column, HIDDEN, 0.0).reshape(TOK, COLS).T.astype(BF16)

    for p in range(NZ):
        mask_slot(p, REL[p])

    def arrived(part, slot):
        remote(QG.at[0, part], QG.at[slot, part], bs.at[part, 1], br.at[part, slot], zpeer(1)).wait_recv()

    def last_hop(part):
        dev = zpeer(1) if part == 0 else zpeer(-1)
        slot = NZ - 2 - part
        return remote(QG.at[slot, part], QG.at[NZ - 1, part], bs.at[part, NZ - 1], br.at[part, NZ - 1], dev)

    for part in range(2):
        for slot in (1, 2):
            arrived(part, slot)
            hop(part, slot, slot + 2).start()

    lane2 = lax.broadcasted_iota(jnp.int32, (1, COLS), 1)
    head = [(lane2 < COLS // 2).astype(F32), (lane2 >= COLS // 2).astype(F32)]
    rows2 = lax.broadcasted_iota(jnp.int32, (F, COLS), 0)
    lanes2 = lax.broadcasted_iota(jnp.int32, (F, COLS), 1)
    for r in range(NX):
        if r > 0:
            remote(KV.at[0, 0], KV.at[r, 0], cs.at[0, r], cr.at[0, r], xpeer(r)).wait_recv()
            remote(KV.at[0, 0], KV.at[r, 1], cs.at[1, r], cr.at[1, r], xpeer(r)).wait_recv()
        kb = KV[r, 0].astype(F32)
        vb = KV[r, 1].astype(F32)
        hot = (lanes2 == rows2 // MASK_BLOCK + per * r).astype(F32).astype(BF16)
        for h in range(2):
            kh = (kb * (head[h] * SCALE)).astype(F32)
            K2[r, h * F : (h + 1) * F, 0:COLS] = kh.astype(BF16)
            K2[r, h * F : (h + 1) * F, COLS : 2 * COLS] = hot
            V2[r, h * F : (h + 1) * F, :] = (vb * head[h]).astype(BF16)
            KT[r, :, h * F : (h + 1) * F] = kh.T.astype(BF16)

    def block(ref, c, which):
        return ref[pl.ds(2 * c, 2), which].reshape(CH, COLS)

    def pass1(c, _):
        qt = jnp.concatenate([block(QG, c, 0).T, jnp.concatenate([M[2 * c], M[2 * c + 1]], axis=1)], axis=0)
        gt = block(QG, c, 1).T
        found = [[] for _ in range(4)]

        def products(r, h):
            rows = slice(h * F, (h + 1) * F)
            W[c, r, h] = jnp.dot(K2[r, rows], qt, preferred_element_type=F32)
            G[c, r, h] = jnp.dot(V2[r, rows], gt, preferred_element_type=F32)

        def reduce(r, h):
            for half in range(2):
                piece = slice(half * TOK, (half + 1) * TOK)
                sc = W[c, r, h, :, piece]
                m = jnp.max(sc, axis=0, keepdims=True)
                w = jnp.exp(sc - m)
                W[c, r, h, :, piece] = w
                MR[c, 2 * r + h : 2 * r + h + 1, piece] = m
                l = jnp.sum(w, axis=0, keepdims=True)
                found[2 * h + half].append((m, l, jnp.sum(w * G[c, r, h, :, piece], axis=0, keepdims=True)))

        order = [(r, h) for r in range(NX) for h in range(2)]
        products(*order[0])
        for now, later in zip(order, order[1:] + [None]):
            if later is not None:
                products(*later)
            reduce(*now)
        for h in range(2):
            for half in range(2):
                top = found[2 * h + half][0][0]
                for m, _, _ in found[2 * h + half][1:]:
                    top = jnp.maximum(top, m)
                total = jnp.zeros_like(top)
                term = jnp.zeros_like(top)
                for m, l, tt in found[2 * h + half]:
                    a = jnp.exp(m - top)
                    total += a * l
                    term += a * tt
                row = 2 * half + h
                SM[c, row : row + 1, :] = top + jnp.log(total)
                SM[c, 4 + row : 5 + row, :] = term / total
        for d in REL[1:]:
            remote(SM.at[c], SR.at[NZ - d, c], ds_.at[d], dr.at[NZ - d], zpeer(d)).start()

        @pl.when(c < NC - 2)
        def _():
            for part in range(2):
                for one in (3, 4):
                    arrived(part, 2 * c + one)

                    @pl.when(c < NC - 3)
                    def _():
                        hop(part, 2 * c + one, 2 * c + one + 2).start()

                @pl.when(c == NC - 3)
                def _():
                    last_hop(part).start()

        @pl.when(c == NC - 2)
        def _():
            for part in range(2):
                arrived(part, NZ - 1)

        return 0

    lax.fori_loop(0, NC, pass1, 0)

    DK[...] = jnp.zeros_like(DK)
    DV[...] = jnp.zeros_like(DV)
    masks = [m.astype(BF16) for m in head]

    for d in range(1, NZ):
        remote(SM, SR.at[d], ds_.at[d], dr.at[d], zpeer(d)).wait_recv()

    def combine(p):
        parts, terms = [], []
        for d in range(NZ):
            theirs = POS[(REL[p] - d) % NZ]
            ref = SM if d == 0 else SR.at[d]
            row = 2 * (theirs % 2)
            parts.append(ref[theirs // 2, row : row + 2, :])
            terms.append(ref[theirs // 2, 4 + row : 6 + row, :])
        top = parts[0]
        for part in parts[1:]:
            top = jnp.maximum(top, part)
        total = jnp.zeros_like(top)
        term = jnp.zeros_like(top)
        for part, other in zip(parts, terms):
            weight = jnp.exp(part - top)
            total += weight
            term += weight * other
        CF[:, p * TOK : (p + 1) * TOK] = top + jnp.log(total)
        RT[:, p * TOK : (p + 1) * TOK] = term / total

    for p in range(NZ):
        combine(p)

    def two_heads(v):
        return jnp.concatenate([v * masks[0], v * masks[1]], axis=0)

    def tile(c, r):
        ps, gs_ = [], []
        for h in range(2):
            cf = jnp.exp(MR[c, 2 * r + h : 2 * r + h + 1, :] - CF[h : h + 1, c * CH : (c + 1) * CH])
            p = W[c, r, h] * cf
            ps.append(p.astype(BF16))
            gs_.append((p * (G[c, r, h] - RT[h : h + 1, c * CH : (c + 1) * CH])).astype(BF16))
        q2, g2 = two_heads(block(QG, c, 0)), two_heads(block(QG, c, 1))
        dv = jnp.dot(jnp.concatenate(ps, axis=1), g2, preferred_element_type=F32)
        dk = jnp.dot(jnp.concatenate(gs_, axis=1), q2, preferred_element_type=F32)
        dqt = jnp.dot(KT[r], jnp.concatenate(gs_, axis=0), preferred_element_type=F32)
        return dk, dv, dqt

    def send_dq(p):
        d = REL[p]
        for i in range(NT):
            if p > 0 or i > 0:
                there = lax.rem(t + i, NT)
                remote(
                    DQS.at[p, there], DQR.at[(NZ - d) % NZ, t],
                    es.at[d] if d else gs.at[i], er.at[(NZ - d) % NZ] if d else gr.at[i],
                    (there, x * NZ + lax.rem(z + d, NZ)),
                ).start()

    for c in range(NC - 1, 1, -1):
        dq = jnp.zeros((COLS, CH), F32)
        for r in range(NX):
            dk, dv, dqt = tile(c, r)
            DK[r] += dk
            DV[r] += dv
            dq += dqt
        DQS[2 * c : 2 * c + 2] = dq.T.astype(BF16).reshape(2, NT, R, COLS)
        send_dq(2 * c)
        send_dq(2 * c + 1)

    near = [jnp.zeros((COLS, CH), F32)] * 2
    for r in [NX // 2] + [i for i in range(1, NX) if i != NX // 2] + [0]:
        dk, dv = DK[r], DV[r]
        for c in range(2):
            dk1, dv1, dqt = tile(c, r)
            dk += dk1
            dv += dv1
            near[c] += dqt
        if r == 0:
            DK[0] = dk
            DV[0] = dv
        else:
            DKVS[r, 0] = dk.astype(BF16)
            DKVS[r, 1] = dv.astype(BF16)
            sent.append(remote(DKVS.at[r], DKVR.at[NX - r], fs.at[r], fr.at[NX - r], xpeer(r)))
            sent[-1].start()
    for c in [1, 0]:
        DQS[2 * c : 2 * c + 2] = near[c].T.astype(BF16).reshape(2, NT, R, COLS)
        send_dq(2 * c + 1)
        send_dq(2 * c)
    DQR[0, pl.ds(t, 1)] = DQS[0, pl.ds(t, 1)]

    for d in range(1, NX):
        remote(DKVS.at[d], DKVR.at[d], fs.at[d], fr.at[d], xpeer(d)).wait_recv()
    dk, dv = DK[0], DV[0]
    for d in range(1, NX):
        dk += DKVR[d, 0].astype(F32)
        dv += DKVR[d, 1].astype(F32)
    dk_out[...] = dk * SCALE
    dv_out[...] = dv

    for d in range(1, NT):
        source = lax.rem(t + NT - d, NT)
        remote(DQS.at[0, 0], DQR.at[0, source], gs.at[d], gr.at[d], tpeer(d)).wait_recv()
    for d in range(1, NZ):
        remote(DQS.at[POS[d]], DQR.at[d], es.at[d], er.at[d], zpeer(d)).wait_recv()
    for i in range(NT):
        dq = DQR[0, i].astype(F32)
        for d in range(1, NZ):
            dq += DQR[d, i].astype(F32)
        dq_out[:, i * COLS : (i + 1) * COLS] = dq
    for copy in sent:
        copy.wait_send()
    for part in range(2):
        for dest in range(3, NZ - 1):
            hop(part, dest - 2, dest).wait_send()
        last_hop(part).wait_send()
    for d in range(1, NT):
        remote(DQS.at[0, 0], DQR.at[0, 0], gs.at[d], gr.at[d], tpeer(d)).wait_send()
    for d in range(1, NZ):
        remote(DQS.at[POS[d]], DQR.at[d], es.at[d], er.at[d], zpeer(d)).wait_send()
    for d in range(1, NZ):
        remote(SM, SR.at[NZ - d], ds_.at[d], dr.at[NZ - d], zpeer(d)).wait_send()


def write_out(dq, dk, dv, dq_out, dk_out, dv_out, sem):
    copies = [
        pltpu.make_async_copy(src, dst, sem.at[i])
        for i, (src, dst) in enumerate([(dk, dk_out), (dv, dv_out), (dq, dq_out)])
    ]
    for copy in copies:
        copy.start()
    for copy in copies:
        copy.wait()


def body(queries, keys, values, grad_out, read_len, *, NT):
    R, D = queries.shape
    F = keys.shape[0]
    TOK, CH, NC = NT * R, 2 * NT * R, NZ // 2
    lens = read_len.reshape(NX, NZ * R)
    any_ = pl.BlockSpec(memory_space=pltpu.HBM)
    vmem = pl.BlockSpec(memory_space=pltpu.VMEM)
    dma = pltpu.SemaphoreType.DMA
    V = pltpu.VMEM
    outs = pl.pallas_call(
        lambda *refs: kernel(NT, *refs),
        out_shape=(V((R, D), F32), V((F, COLS), F32), V((F, COLS), F32)),
        in_specs=[any_, any_, any_, any_, vmem],
        out_specs=(vmem, vmem, vmem),
        scratch_shapes=[
            V((R, D), BF16),
            V((R, D), BF16),
            V((NZ, 2, NT, R, COLS), BF16),
            V((NX, 2, F, COLS), BF16),
            V((NT, 8, COLS), F32),
            V((8, COLS), F32),
            V((NZ, COLS, TOK), BF16),
            V((NX, 2 * F, 2 * COLS), BF16),
            V((NX, 2 * F, COLS), BF16),
            V((NX, COLS, 2 * F), BF16),
            V((NC, NX, 2, F, CH), F32),
            V((NC, NX, 2, F, CH), F32),
            V((NC, 2 * NX, CH), F32),
            V((NC, 8, TOK), F32),
            V((NZ, NC, 8, TOK), F32),
            V((2, NZ * TOK), F32),
            V((2, NZ * TOK), F32),
            V((NZ, NT, R, COLS), BF16),
            V((NZ, NT, R, COLS), BF16),
            V((NX, F, COLS), F32),
            V((NX, F, COLS), F32),
            V((NX, 2, F, COLS), BF16),
            V((NX, 2, F, COLS), BF16),
            dma((4,)),
            dma((3, NT)), dma((3, NT)),
            dma((2, NZ)), dma((2, NZ)),
            dma((2, NX)), dma((2, NX)),
            dma((NZ,)), dma((NZ,)),
            dma((NZ,)), dma((NZ,)),
            dma((NX,)), dma((NX,)),
            dma((NT,)), dma((NT,)),
        ],
        compiler_params=pltpu.CompilerParams(
            collective_id=0, has_side_effects=True, vmem_limit_bytes=62 * 1024 * 1024
        ),
    )(queries, keys, values, grad_out, lens)
    return pl.pallas_call(
        write_out,
        out_shape=tuple(jax.ShapeDtypeStruct(o.shape, F32) for o in outs),
        in_specs=[vmem] * 3,
        out_specs=[pl.BlockSpec(memory_space=pltpu.HBM)] * 3,
        scratch_shapes=[dma((3,))],
    )(*outs)


def solution(mesh):
    NT = mesh.shape["tgt"]
    return jax.shard_map(
        lambda *args: body(*args, NT=NT),
        mesh=mesh,
        in_specs=(
            P(("tgt", "src"), None),
            P("src", None),
            P("src", None),
            P(("tgt", "src"), None),
            P("tgt"),
        ),
        out_specs=(P(("tgt", "src"), None), P("src", "tgt"), P("src", "tgt")),
        check_vma=False,
    )
```

```python
import jax
import jax.numpy as jnp
from jax import lax
from jax.experimental import pallas as pl
from jax.experimental.pallas import tpu as pltpu
from jax.sharding import PartitionSpec as P

MESH = pl.DeviceIdType.MESH
NX, NZ = 4, 8
COLS = 128
MASK_BLOCK = 128
F32, BF16 = jnp.float32, jnp.bfloat16
HIDDEN = -1e30
SCALE = 0.125

REL = [0]
for _d in range(1, NZ // 2 + 1):
    REL += [_d] if 2 * _d == NZ else [_d, NZ - _d]
POS = {d: p for p, d in enumerate(REL)}


def kernel(
    NT, q_hbm, k_hbm, v_hbm, g_hbm, len_hbm, dq_out, dk_out, dv_out,
    len_ref, QI, GI, QG, KV, L, lrow, M, K2, V2, KT, W, G, MR, SM, SR, CF, RT, DQS, DQR, DK, DV, DKVS, DKVR,
    lsem, as_, ar, bs, br, cs, cr, ds_, dr, es, er, fs, fr, gs, gr,
):
    t = lax.axis_index("tgt")
    s = lax.axis_index("src")
    x = s // NZ
    z = s % NZ
    R, F = q_hbm.shape[0], k_hbm.shape[0]
    TOK = NT * R
    CH = 2 * TOK
    NC = NZ // 2

    def tpeer(d):
        return (lax.rem(t + d, NT), s)

    def zpeer(d):
        return (t, x * NZ + lax.rem(z + NZ + d, NZ))

    def xpeer(d):
        return (t, lax.rem(x + d, NX) * NZ + z)

    def cols(i):
        return pl.ds(pl.multiple_of(i * COLS, COLS), COLS)

    def remote(src, dst, ssem, rsem, dev):
        return pltpu.make_async_remote_copy(
            src_ref=src, dst_ref=dst, send_sem=ssem, recv_sem=rsem, device_id=dev, device_id_type=MESH
        )

    local = [
        pltpu.make_async_copy(q_hbm, QI, lsem.at[0]),
        pltpu.make_async_copy(g_hbm, GI, lsem.at[1]),
        pltpu.make_async_copy(k_hbm.at[:, cols(t)], KV.at[0, 0], lsem.at[2]),
        pltpu.make_async_copy(v_hbm.at[:, cols(t)], KV.at[0, 1], lsem.at[3]),
        pltpu.make_async_copy(len_hbm, len_ref, lsem.at[4]),
    ]
    for copy in local:
        copy.start()
    barrier = pltpu.get_barrier_semaphore()
    peers = [tpeer(d) for d in range(1, NT)] + [zpeer(d) for d in range(1, NZ)] + [xpeer(d) for d in range(1, NX)]
    for dev in peers:
        pl.semaphore_signal(barrier, inc=1, device_id=dev, device_id_type=MESH)
    pl.semaphore_wait(barrier, len(peers))

    for copy in local:
        copy.wait()
    row = len_ref[pl.ds(x, 1), :].astype(F32)
    lrow[...] = jnp.broadcast_to(row, lrow.shape)
    L[pl.ds(t, 1)] = jnp.broadcast_to(row[None], (1,) + lrow.shape)
    sent = []
    for d in range(1, NT):
        there = lax.rem(t + d, NT)
        sent += [
            remote(QI.at[:, cols(there)], QG.at[0, 0, t], as_.at[0, d], ar.at[0, d], tpeer(d)),
            remote(GI.at[:, cols(there)], QG.at[0, 1, t], as_.at[1, d], ar.at[1, d], tpeer(d)),
            remote(lrow, L.at[t], as_.at[2, d], ar.at[2, d], tpeer(d)),
        ]
    for d in range(1, NX):
        sent += [
            remote(KV.at[0, 0], KV.at[NX - d, 0], cs.at[0, d], cr.at[0, NX - d], xpeer(d)),
            remote(KV.at[0, 1], KV.at[NX - d, 1], cs.at[1, d], cr.at[1, NX - d], xpeer(d)),
        ]
    for copy in sent:
        copy.start()
    QG[0, 0, pl.ds(t, 1)] = QI[:, cols(t)][None]
    QG[0, 1, pl.ds(t, 1)] = GI[:, cols(t)][None]
    for d in range(1, NT):
        source = lax.rem(t + NT - d, NT)
        remote(QI.at[:, cols(t)], QG.at[0, 0, source], as_.at[0, d], ar.at[0, d], tpeer(d)).wait_recv()
        remote(QI.at[:, cols(t)], QG.at[0, 1, source], as_.at[1, d], ar.at[1, d], tpeer(d)).wait_recv()

    def hop(part, slot, dest):
        dev = zpeer(1 - 2 * (dest % 2)) if isinstance(dest, int) else zpeer(1 - 2 * lax.rem(dest, 2))
        return remote(QG.at[slot, part], QG.at[dest, part], bs.at[part, dest], br.at[part, dest], dev)

    for part in range(2):
        for dest in (1, 2):
            sent.append(hop(part, 0, dest))
            sent[-1].start()

    for d in range(1, NT):
        source = lax.rem(t + NT - d, NT)
        remote(lrow, L.at[source], as_.at[2, d], ar.at[2, d], tpeer(d)).wait_recv()
    lane3 = lax.broadcasted_iota(jnp.int32, (NT, R, COLS), 2)
    row3 = lax.broadcasted_iota(jnp.int32, (NT, R, COLS), 1)
    lens = jnp.broadcast_to(L[:, 0:1, :], (NT, R, COLS))
    per = F // MASK_BLOCK
    lanes = lax.broadcasted_iota(jnp.int32, (1, 1, COLS), 2)
    first = ((lax.rem(x + lanes // per, NX) * NZ + z) * per + lax.rem(lanes, per)) * MASK_BLOCK
    first = jnp.where(lanes < per * NX, first, -1).astype(F32)

    def mask_slot(p, rel):
        pick = lax.rem(z + rel, NZ) * R + row3
        column = jnp.sum(jnp.where(lane3 == pick, lens, 0.0), axis=2, keepdims=True)
        M[p] = jnp.where(first >= column, HIDDEN, 0.0).reshape(TOK, COLS).T.astype(BF16)

    for p in range(NZ):
        mask_slot(p, REL[p])

    def arrived(part, slot):
        remote(QG.at[0, part], QG.at[slot, part], bs.at[part, 1], br.at[part, slot], zpeer(1)).wait_recv()

    def last_hop(part):
        dev = zpeer(1) if part == 0 else zpeer(-1)
        slot = NZ - 2 - part
        return remote(QG.at[slot, part], QG.at[NZ - 1, part], bs.at[part, NZ - 1], br.at[part, NZ - 1], dev)

    for part in range(2):
        for slot in (1, 2):
            arrived(part, slot)
            hop(part, slot, slot + 2).start()

    lane2 = lax.broadcasted_iota(jnp.int32, (1, COLS), 1)
    head = [(lane2 < COLS // 2).astype(F32), (lane2 >= COLS // 2).astype(F32)]
    rows2 = lax.broadcasted_iota(jnp.int32, (F, COLS), 0)
    lanes2 = lax.broadcasted_iota(jnp.int32, (F, COLS), 1)
    for r in range(NX):
        if r > 0:
            remote(KV.at[0, 0], KV.at[r, 0], cs.at[0, r], cr.at[0, r], xpeer(r)).wait_recv()
            remote(KV.at[0, 0], KV.at[r, 1], cs.at[1, r], cr.at[1, r], xpeer(r)).wait_recv()
        kb = KV[r, 0].astype(F32)
        vb = KV[r, 1].astype(F32)
        hot = (lanes2 == rows2 // MASK_BLOCK + per * r).astype(F32).astype(BF16)
        for h in range(2):
            kh = (kb * (head[h] * SCALE)).astype(F32)
            K2[r, h * F : (h + 1) * F, 0:COLS] = kh.astype(BF16)
            K2[r, h * F : (h + 1) * F, COLS : 2 * COLS] = hot
            V2[r, h * F : (h + 1) * F, :] = (vb * head[h]).astype(BF16)
            KT[r, :, h * F : (h + 1) * F] = kh.T.astype(BF16)

    def block(ref, c, which):
        return ref[pl.ds(2 * c, 2), which].reshape(CH, COLS)

    def pass1(c, _):
        qt = jnp.concatenate([block(QG, c, 0).T, jnp.concatenate([M[2 * c], M[2 * c + 1]], axis=1)], axis=0)
        gt = block(QG, c, 1).T
        found = [[] for _ in range(4)]

        def products(r, h):
            rows = slice(h * F, (h + 1) * F)
            W[c, r, h] = jnp.dot(K2[r, rows], qt, preferred_element_type=F32)
            G[c, r, h] = jnp.dot(V2[r, rows], gt, preferred_element_type=F32)

        def reduce(r, h):
            for half in range(2):
                piece = slice(half * TOK, (half + 1) * TOK)
                sc = W[c, r, h, :, piece]
                m = jnp.max(sc, axis=0, keepdims=True)
                w = jnp.exp(sc - m)
                W[c, r, h, :, piece] = w
                MR[c, 2 * r + h : 2 * r + h + 1, piece] = m
                l = jnp.sum(w, axis=0, keepdims=True)
                found[2 * h + half].append((m, l, jnp.sum(w * G[c, r, h, :, piece], axis=0, keepdims=True)))

        order = [(r, h) for r in range(NX) for h in range(2)]
        products(*order[0])
        for now, later in zip(order, order[1:] + [None]):
            if later is not None:
                products(*later)
            reduce(*now)
        for h in range(2):
            for half in range(2):
                top = found[2 * h + half][0][0]
                for m, _, _ in found[2 * h + half][1:]:
                    top = jnp.maximum(top, m)
                total = jnp.zeros_like(top)
                term = jnp.zeros_like(top)
                for m, l, tt in found[2 * h + half]:
                    a = jnp.exp(m - top)
                    total += a * l
                    term += a * tt
                row = 2 * half + h
                SM[c, row : row + 1, :] = top + jnp.log(total)
                SM[c, 4 + row : 5 + row, :] = term / total
        for d in REL[1:]:
            remote(SM.at[c], SR.at[NZ - d, c], ds_.at[d], dr.at[NZ - d], zpeer(d)).start()

        @pl.when(c < NC - 2)
        def _():
            for part in range(2):
                for one in (3, 4):
                    arrived(part, 2 * c + one)

                    @pl.when(c < NC - 3)
                    def _():
                        hop(part, 2 * c + one, 2 * c + one + 2).start()

                @pl.when(c == NC - 3)
                def _():
                    last_hop(part).start()

        @pl.when(c == NC - 2)
        def _():
            for part in range(2):
                arrived(part, NZ - 1)

        return 0

    lax.fori_loop(0, NC, pass1, 0)

    DK[...] = jnp.zeros_like(DK)
    DV[...] = jnp.zeros_like(DV)
    masks = [m.astype(BF16) for m in head]

    for d in range(1, NZ):
        remote(SM, SR.at[d], ds_.at[d], dr.at[d], zpeer(d)).wait_recv()

    def combine(p):
        parts, terms = [], []
        for d in range(NZ):
            theirs = POS[(REL[p] - d) % NZ]
            ref = SM if d == 0 else SR.at[d]
            row = 2 * (theirs % 2)
            parts.append(ref[theirs // 2, row : row + 2, :])
            terms.append(ref[theirs // 2, 4 + row : 6 + row, :])
        top = parts[0]
        for part in parts[1:]:
            top = jnp.maximum(top, part)
        total = jnp.zeros_like(top)
        term = jnp.zeros_like(top)
        for part, other in zip(parts, terms):
            weight = jnp.exp(part - top)
            total += weight
            term += weight * other
        CF[:, p * TOK : (p + 1) * TOK] = top + jnp.log(total)
        RT[:, p * TOK : (p + 1) * TOK] = term / total

    for p in range(NZ):
        combine(p)

    def two_heads(v):
        return jnp.concatenate([v * masks[0], v * masks[1]], axis=0)

    def tile(c, r):
        ps, gs_ = [], []
        for h in range(2):
            cf = jnp.exp(MR[c, 2 * r + h : 2 * r + h + 1, :] - CF[h : h + 1, c * CH : (c + 1) * CH])
            p = W[c, r, h] * cf
            ps.append(p.astype(BF16))
            gs_.append((p * (G[c, r, h] - RT[h : h + 1, c * CH : (c + 1) * CH])).astype(BF16))
        q2, g2 = two_heads(block(QG, c, 0)), two_heads(block(QG, c, 1))
        dv = jnp.dot(jnp.concatenate(ps, axis=1), g2, preferred_element_type=F32)
        dk = jnp.dot(jnp.concatenate(gs_, axis=1), q2, preferred_element_type=F32)
        dqt = jnp.dot(KT[r], jnp.concatenate(gs_, axis=0), preferred_element_type=F32)
        return dk, dv, dqt

    def send_dq(p):
        d = REL[p]
        for i in range(NT):
            if p > 0 or i > 0:
                there = lax.rem(t + i, NT)
                remote(
                    DQS.at[p, there], DQR.at[(NZ - d) % NZ, t],
                    es.at[d] if d else gs.at[i], er.at[(NZ - d) % NZ] if d else gr.at[i],
                    (there, x * NZ + lax.rem(z + d, NZ)),
                ).start()

    for c in range(NC - 1, 1, -1):
        dq = jnp.zeros((COLS, CH), F32)
        for r in range(NX):
            dk, dv, dqt = tile(c, r)
            DK[r] += dk
            DV[r] += dv
            dq += dqt
        DQS[2 * c : 2 * c + 2] = dq.T.astype(BF16).reshape(2, NT, R, COLS)
        send_dq(2 * c)
        send_dq(2 * c + 1)

    near = [jnp.zeros((COLS, CH), F32)] * 2
    for r in [NX // 2] + [i for i in range(1, NX) if i != NX // 2] + [0]:
        dk, dv = DK[r], DV[r]
        for c in range(2):
            dk1, dv1, dqt = tile(c, r)
            dk += dk1
            dv += dv1
            near[c] += dqt
        if r == 0:
            DK[0] = dk
            DV[0] = dv
        else:
            DKVS[r, 0] = dk.astype(BF16)
            DKVS[r, 1] = dv.astype(BF16)
            sent.append(remote(DKVS.at[r], DKVR.at[NX - r], fs.at[r], fr.at[NX - r], xpeer(r)))
            sent[-1].start()
    for c in [1, 0]:
        DQS[2 * c : 2 * c + 2] = near[c].T.astype(BF16).reshape(2, NT, R, COLS)
        send_dq(2 * c + 1)
        send_dq(2 * c)
    DQR[0, pl.ds(t, 1)] = DQS[0, pl.ds(t, 1)]

    for d in range(1, NX):
        remote(DKVS.at[d], DKVR.at[d], fs.at[d], fr.at[d], xpeer(d)).wait_recv()
    dk, dv = DK[0], DV[0]
    for d in range(1, NX):
        dk += DKVR[d, 0].astype(F32)
        dv += DKVR[d, 1].astype(F32)
    dk_out[...] = dk * SCALE
    dv_out[...] = dv

    for d in range(1, NT):
        source = lax.rem(t + NT - d, NT)
        remote(DQS.at[0, 0], DQR.at[0, source], gs.at[d], gr.at[d], tpeer(d)).wait_recv()
    for d in range(1, NZ):
        remote(DQS.at[POS[d]], DQR.at[d], es.at[d], er.at[d], zpeer(d)).wait_recv()
    for i in range(NT):
        dq = DQR[0, i].astype(F32)
        for d in range(1, NZ):
            dq += DQR[d, i].astype(F32)
        dq_out[:, i * COLS : (i + 1) * COLS] = dq
    for copy in sent:
        copy.wait_send()
    for part in range(2):
        for dest in range(3, NZ - 1):
            hop(part, dest - 2, dest).wait_send()
        last_hop(part).wait_send()
    for d in range(1, NT):
        remote(DQS.at[0, 0], DQR.at[0, 0], gs.at[d], gr.at[d], tpeer(d)).wait_send()
    for d in range(1, NZ):
        remote(DQS.at[POS[d]], DQR.at[d], es.at[d], er.at[d], zpeer(d)).wait_send()
    for d in range(1, NZ):
        remote(SM, SR.at[NZ - d], ds_.at[d], dr.at[NZ - d], zpeer(d)).wait_send()


def body(queries, keys, values, grad_out, read_len, *, NT):
    R, D = queries.shape
    F = keys.shape[0]
    TOK, CH, NC = NT * R, 2 * NT * R, NZ // 2
    lens = read_len.reshape(NX, NZ * R)
    hbm = pl.BlockSpec(memory_space=pltpu.HBM)
    vmem = pl.BlockSpec(memory_space=pltpu.VMEM)
    dma = pltpu.SemaphoreType.DMA
    V = pltpu.VMEM
    return pl.pallas_call(
        lambda *refs: kernel(NT, *refs),
        out_shape=(
            jax.ShapeDtypeStruct((R, D), F32),
            jax.ShapeDtypeStruct((F, COLS), F32),
            jax.ShapeDtypeStruct((F, COLS), F32),
        ),
        in_specs=[hbm] * 5,
        out_specs=(vmem, vmem, vmem),
        scratch_shapes=[
            V((NX, NZ * R), jnp.int32),
            V((R, D), BF16),
            V((R, D), BF16),
            V((NZ, 2, NT, R, COLS), BF16),
            V((NX, 2, F, COLS), BF16),
            V((NT, 8, COLS), F32),
            V((8, COLS), F32),
            V((NZ, COLS, TOK), BF16),
            V((NX, 2 * F, 2 * COLS), BF16),
            V((NX, 2 * F, COLS), BF16),
            V((NX, COLS, 2 * F), BF16),
            V((NC, NX, 2, F, CH), F32),
            V((NC, NX, 2, F, CH), F32),
            V((NC, 2 * NX, CH), F32),
            V((NC, 8, TOK), F32),
            V((NZ, NC, 8, TOK), F32),
            V((2, NZ * TOK), F32),
            V((2, NZ * TOK), F32),
            V((NZ, NT, R, COLS), BF16),
            V((NZ, NT, R, COLS), BF16),
            V((NX, F, COLS), F32),
            V((NX, F, COLS), F32),
            V((NX, 2, F, COLS), BF16),
            V((NX, 2, F, COLS), BF16),
            dma((5,)),
            dma((3, NT)), dma((3, NT)),
            dma((2, NZ)), dma((2, NZ)),
            dma((2, NX)), dma((2, NX)),
            dma((NZ,)), dma((NZ,)),
            dma((NZ,)), dma((NZ,)),
            dma((NX,)), dma((NX,)),
            dma((NT,)), dma((NT,)),
        ],
        compiler_params=pltpu.CompilerParams(
            collective_id=0, has_side_effects=True, vmem_limit_bytes=48 * 1024 * 1024
        ),
    )(queries, keys, values, grad_out, lens)


def solution(mesh):
    NT = mesh.shape["tgt"]
    return jax.shard_map(
        lambda *args: body(*args, NT=NT),
        mesh=mesh,
        in_specs=(
            P(("tgt", "src"), None),
            P("src", None),
            P("src", None),
            P(("tgt", "src"), None),
            P("tgt"),
        ),
        out_specs=(P(("tgt", "src"), None), P("src", "tgt"), P("src", "tgt")),
        check_vma=False,
    )
```

```python
import jax
import jax.numpy as jnp
from jax import lax
from jax.experimental import pallas as pl
from jax.experimental.pallas import tpu as pltpu
from jax.sharding import PartitionSpec as P

MESH = pl.DeviceIdType.MESH
NX, NZ = 4, 8
COLS = 128
MASK_BLOCK = 128
F32, BF16 = jnp.float32, jnp.bfloat16
HIDDEN = -1e30
SCALE = 0.125

REL = [0]
for _d in range(1, NZ // 2 + 1):
    REL += [_d] if 2 * _d == NZ else [_d, NZ - _d]
POS = {d: p for p, d in enumerate(REL)}


def kernel(
    NT, q_hbm, k_hbm, v_hbm, g_hbm, len_hbm, dq_out, dk_out, dv_out,
    len_ref, QI, GI, QGI, QG, KV, L, lrow, M, K2, V2, KT, W, G, MR, SM, SR, CF, RT, PS, GS, Q2, G2, DQT, DQS, DQR, DK, DV, DKVS, DKVR,
    lsem, as_, ar, bs, br, cs, cr, ds_, dr, es, er, fs, fr, gs, gr,
):
    t = lax.axis_index("tgt")
    s = lax.axis_index("src")
    x = s // NZ
    z = s % NZ
    R, F = q_hbm.shape[0], k_hbm.shape[0]
    TOK = NT * R
    CH = 2 * TOK
    NC = NZ // 2

    def tpeer(d):
        return (lax.rem(t + d, NT), s)

    def zpeer(d):
        return (t, x * NZ + lax.rem(z + NZ + d, NZ))

    def xpeer(d):
        return (t, lax.rem(x + d, NX) * NZ + z)

    def cols(i):
        return pl.ds(pl.multiple_of(i * COLS, COLS), COLS)

    def remote(src, dst, ssem, rsem, dev):
        return pltpu.make_async_remote_copy(
            src_ref=src, dst_ref=dst, send_sem=ssem, recv_sem=rsem, device_id=dev, device_id_type=MESH
        )

    local = [
        pltpu.make_async_copy(q_hbm, QI, lsem.at[0]),
        pltpu.make_async_copy(g_hbm, GI, lsem.at[1]),
        pltpu.make_async_copy(k_hbm.at[:, cols(t)], KV.at[0, 0], lsem.at[2]),
        pltpu.make_async_copy(v_hbm.at[:, cols(t)], KV.at[0, 1], lsem.at[3]),
        pltpu.make_async_copy(len_hbm, len_ref, lsem.at[4]),
    ]
    for copy in local:
        copy.start()
    barrier = pltpu.get_barrier_semaphore()
    peers = [tpeer(d) for d in range(1, NT)] + [zpeer(d) for d in range(1, NZ)] + [xpeer(d) for d in range(1, NX)]
    for dev in peers:
        pl.semaphore_signal(barrier, inc=1, device_id=dev, device_id_type=MESH)
    pl.semaphore_wait(barrier, len(peers))

    for copy in local:
        copy.wait()
    row = len_ref[pl.ds(x, 1), :].astype(F32)
    lrow[...] = jnp.broadcast_to(row, lrow.shape)
    L[pl.ds(t, 1)] = jnp.broadcast_to(row[None], (1,) + lrow.shape)
    sent = []
    for i in range(NT):
        QGI[i, 0] = QI[:, i * COLS : (i + 1) * COLS]
        QGI[i, 1] = GI[:, i * COLS : (i + 1) * COLS]
    for d in range(1, NT):
        sent.append(remote(QGI.at[lax.rem(t + d, NT)], QG.at[0, :, t], as_.at[0, d], ar.at[0, d], tpeer(d)))
    for d in range(1, NT):
        sent.append(remote(lrow, L.at[t], as_.at[1, d], ar.at[1, d], tpeer(d)))
    for d in range(1, NX):
        sent += [
            remote(KV.at[0, 0], KV.at[NX - d, 0], cs.at[0, d], cr.at[0, NX - d], xpeer(d)),
            remote(KV.at[0, 1], KV.at[NX - d, 1], cs.at[1, d], cr.at[1, NX - d], xpeer(d)),
        ]
    for copy in sent:
        copy.start()
    for part in range(2):
        QG[0, part, pl.ds(t, 1)] = QGI[pl.ds(t, 1), part]
    for d in range(1, NT):
        source = lax.rem(t + NT - d, NT)
        remote(QGI.at[0], QG.at[0, :, source], as_.at[0, d], ar.at[0, d], tpeer(d)).wait_recv()

    def hop(part, slot, dest):
        dev = zpeer(1 - 2 * (dest % 2)) if isinstance(dest, int) else zpeer(1 - 2 * lax.rem(dest, 2))
        return remote(QG.at[slot, part], QG.at[dest, part], bs.at[part, dest], br.at[part, dest], dev)

    for part in range(2):
        for dest in (1, 2):
            sent.append(hop(part, 0, dest))
            sent[-1].start()

    for d in range(1, NT):
        source = lax.rem(t + NT - d, NT)
        remote(lrow, L.at[source], as_.at[1, d], ar.at[1, d], tpeer(d)).wait_recv()
    lane3 = lax.broadcasted_iota(jnp.int32, (NT, R, COLS), 2)
    row3 = lax.broadcasted_iota(jnp.int32, (NT, R, COLS), 1)
    lens = jnp.broadcast_to(L[:, 0:1, :], (NT, R, COLS))
    per = F // MASK_BLOCK
    lanes = lax.broadcasted_iota(jnp.int32, (1, 1, COLS), 2)
    first = ((lax.rem(x + lanes // per, NX) * NZ + z) * per + lax.rem(lanes, per)) * MASK_BLOCK
    first = jnp.where(lanes < per * NX, first, -1).astype(F32)

    def mask_slot(p, rel):
        pick = lax.rem(z + rel, NZ) * R + row3
        column = jnp.sum(jnp.where(lane3 == pick, lens, 0.0), axis=2, keepdims=True)
        M[p] = jnp.where(first >= column, HIDDEN, 0.0).reshape(TOK, COLS).T.astype(BF16)

    for p in range(NZ):
        mask_slot(p, REL[p])

    def arrived(part, slot):
        remote(QG.at[0, part], QG.at[slot, part], bs.at[part, 1], br.at[part, slot], zpeer(1)).wait_recv()

    def last_hop(part):
        dev = zpeer(1) if part == 0 else zpeer(-1)
        slot = NZ - 2 - part
        return remote(QG.at[slot, part], QG.at[NZ - 1, part], bs.at[part, NZ - 1], br.at[part, NZ - 1], dev)

    for part in range(2):
        for slot in (1, 2):
            arrived(part, slot)
            hop(part, slot, slot + 2).start()

    lane2 = lax.broadcasted_iota(jnp.int32, (1, COLS), 1)
    head = [(lane2 < COLS // 2).astype(F32), (lane2 >= COLS // 2).astype(F32)]
    rows2 = lax.broadcasted_iota(jnp.int32, (F, COLS), 0)
    lanes2 = lax.broadcasted_iota(jnp.int32, (F, COLS), 1)
    for r in range(NX):
        if r > 0:
            remote(KV.at[0, 0], KV.at[r, 0], cs.at[0, r], cr.at[0, r], xpeer(r)).wait_recv()
            remote(KV.at[0, 0], KV.at[r, 1], cs.at[1, r], cr.at[1, r], xpeer(r)).wait_recv()
        kb = KV[r, 0].astype(F32)
        vb = KV[r, 1].astype(F32)
        hot = (lanes2 == rows2 // MASK_BLOCK + per * r).astype(F32).astype(BF16)
        for h in range(2):
            kh = (kb * (head[h] * SCALE)).astype(F32)
            K2[r, h * F : (h + 1) * F, 0:COLS] = kh.astype(BF16)
            K2[r, h * F : (h + 1) * F, COLS : 2 * COLS] = hot
            V2[r, h * F : (h + 1) * F, :] = (vb * head[h]).astype(BF16)
            KT[r, :, h * F : (h + 1) * F] = kh.T.astype(BF16)

    masks = [m.astype(BF16) for m in head]

    def block(ref, c, which):
        return ref[pl.ds(2 * c, 2), which].reshape(CH, COLS)

    def pass1(c, _):
        qt = jnp.concatenate([block(QG, c, 0).T, jnp.concatenate([M[2 * c], M[2 * c + 1]], axis=1)], axis=0)
        gt = block(QG, c, 1).T
        for h in range(2):
            rows = slice(h * CH, (h + 1) * CH)
            Q2[c, rows] = block(QG, c, 0) * masks[h]
            G2[c, rows] = block(QG, c, 1) * masks[h]
        found = [[] for _ in range(4)]

        def products(r, h):
            rows = slice(h * F, (h + 1) * F)
            W[c, r, h] = jnp.dot(K2[r, rows], qt, preferred_element_type=F32)
            G[c, r, h] = jnp.dot(V2[r, rows], gt, preferred_element_type=F32)

        def reduce(r, h):
            for half in range(2):
                piece = slice(half * TOK, (half + 1) * TOK)
                sc = W[c, r, h, :, piece]
                m = jnp.max(sc, axis=0, keepdims=True)
                w = jnp.exp(sc - m)
                W[c, r, h, :, piece] = w
                MR[c, 2 * r + h : 2 * r + h + 1, piece] = m
                l = jnp.sum(w, axis=0, keepdims=True)
                found[2 * h + half].append((m, l, jnp.sum(w * G[c, r, h, :, piece], axis=0, keepdims=True)))

        order = [(r, h) for r in range(NX) for h in range(2)]
        products(*order[0])
        for now, later in zip(order, order[1:] + [None]):
            if later is not None:
                products(*later)
            reduce(*now)
        for h in range(2):
            for half in range(2):
                top = found[2 * h + half][0][0]
                for m, _, _ in found[2 * h + half][1:]:
                    top = jnp.maximum(top, m)
                total = jnp.zeros_like(top)
                term = jnp.zeros_like(top)
                for m, l, tt in found[2 * h + half]:
                    a = jnp.exp(m - top)
                    total += a * l
                    term += a * tt
                row = 2 * half + h
                SM[c, row : row + 1, :] = top + jnp.log(total)
                SM[c, 4 + row : 5 + row, :] = term / total
        for d in REL[1:]:
            remote(SM.at[c], SR.at[NZ - d, c], ds_.at[d], dr.at[NZ - d], zpeer(d)).start()

        @pl.when(c < NC - 2)
        def _():
            for part in range(2):
                for one in (3, 4):
                    arrived(part, 2 * c + one)

                    @pl.when(c < NC - 3)
                    def _():
                        hop(part, 2 * c + one, 2 * c + one + 2).start()

                @pl.when(c == NC - 3)
                def _():
                    last_hop(part).start()

        @pl.when(c == NC - 2)
        def _():
            for part in range(2):
                arrived(part, NZ - 1)

        return 0

    lax.fori_loop(0, NC, pass1, 0)

    for d in range(1, NZ):
        remote(SM, SR.at[d], ds_.at[d], dr.at[d], zpeer(d)).wait_recv()

    def combine(p):
        parts, terms = [], []
        for d in range(NZ):
            theirs = POS[(REL[p] - d) % NZ]
            ref = SM if d == 0 else SR.at[d]
            row = 2 * (theirs % 2)
            parts.append(ref[theirs // 2, row : row + 2, :])
            terms.append(ref[theirs // 2, 4 + row : 6 + row, :])
        top = parts[0]
        for part in parts[1:]:
            top = jnp.maximum(top, part)
        total = jnp.zeros_like(top)
        term = jnp.zeros_like(top)
        for part, other in zip(parts, terms):
            weight = jnp.exp(part - top)
            total += weight
            term += weight * other
        CF[:, p * TOK : (p + 1) * TOK] = top + jnp.log(total)
        RT[:, p * TOK : (p + 1) * TOK] = term / total

    for p in range(NZ):
        combine(p)

    def make(c, r):
        piece = slice(c * CH, (c + 1) * CH)
        for h in range(2):
            cf = jnp.exp(MR[c, 2 * r + h : 2 * r + h + 1, :] - CF[h : h + 1, piece])
            term = RT[h : h + 1, piece]
            for lo in range(0, F, 64):
                rows = slice(lo, lo + 64)
                p = W[c, r, h, rows, :] * cf
                PS[c, r, rows, h * CH : (h + 1) * CH] = p.astype(BF16)
                GS[c, r, rows, h * CH : (h + 1) * CH] = (p * (G[c, r, h, rows, :] - term)).astype(BF16)

    def use(c, r):
        first = c == NC - 1
        dv = jnp.dot(PS[c, r], G2[c], preferred_element_type=F32)
        dk = jnp.dot(GS[c, r], Q2[c], preferred_element_type=F32)
        DV[r] = dv if first else DV[r] + dv
        DK[r] = dk if first else DK[r] + dk
        dq = jnp.dot(KT[r, :, 0:F], GS[c, r, :, 0:CH], preferred_element_type=F32)
        dq += jnp.dot(KT[r, :, F : 2 * F], GS[c, r, :, CH : 2 * CH], preferred_element_type=F32)
        DQT[c] = dq if r == ORDER[0] else DQT[c] + dq

    def send_dq(p):
        d = REL[p]
        for i in range(NT):
            if p > 0 or i > 0:
                there = lax.rem(t + i, NT)
                remote(
                    DQS.at[p, there], DQR.at[(NZ - d) % NZ, t],
                    es.at[d] if d else gs.at[i], er.at[(NZ - d) % NZ] if d else gr.at[i],
                    (there, x * NZ + lax.rem(z + d, NZ)),
                ).start()

    def done_dq(c):
        DQS[2 * c : 2 * c + 2] = DQT[c].T.astype(BF16).reshape(2, NT, R, COLS)
        send_dq(2 * c + 1)
        send_dq(2 * c)

    def done_kv(r):
        DKVS[r, 0] = DK[r].astype(BF16)
        DKVS[r, 1] = DV[r].astype(BF16)
        sent.append(remote(DKVS.at[r], DKVR.at[NX - r], fs.at[r], fr.at[NX - r], xpeer(r)))
        sent[-1].start()

    ORDER = [NX // 2] + [i for i in range(1, NX) if i != NX // 2] + [0]
    steps = [(c, r) for c in range(NC - 1, 1, -1) for r in ORDER] + [(c, r) for r in ORDER for c in (1, 0)]
    make(*steps[0])
    for (c, r), later in zip(steps, steps[1:] + [None]):
        if later is not None:
            make(*later)
        use(c, r)
        if r == ORDER[-1]:
            done_dq(c)
        if c == 0 and r > 0:
            done_kv(r)
    DQR[0, pl.ds(t, 1)] = DQS[0, pl.ds(t, 1)]

    for d in range(1, NX):
        remote(DKVS.at[d], DKVR.at[d], fs.at[d], fr.at[d], xpeer(d)).wait_recv()
    dk, dv = DK[0], DV[0]
    for d in range(1, NX):
        dk += DKVR[d, 0].astype(F32)
        dv += DKVR[d, 1].astype(F32)
    dk_out[...] = dk * SCALE
    dv_out[...] = dv

    for d in range(1, NT):
        source = lax.rem(t + NT - d, NT)
        remote(DQS.at[0, 0], DQR.at[0, source], gs.at[d], gr.at[d], tpeer(d)).wait_recv()
    for d in range(1, NZ):
        remote(DQS.at[POS[d]], DQR.at[d], es.at[d], er.at[d], zpeer(d)).wait_recv()
    for i in range(NT):
        dq = DQR[0, i].astype(F32)
        for d in range(1, NZ):
            dq += DQR[d, i].astype(F32)
        dq_out[:, i * COLS : (i + 1) * COLS] = dq
    for copy in sent:
        copy.wait_send()
    for part in range(2):
        for dest in range(3, NZ - 1):
            hop(part, dest - 2, dest).wait_send()
        last_hop(part).wait_send()
    for d in range(1, NT):
        remote(DQS.at[0, 0], DQR.at[0, 0], gs.at[d], gr.at[d], tpeer(d)).wait_send()
    for d in range(1, NZ):
        remote(DQS.at[POS[d]], DQR.at[d], es.at[d], er.at[d], zpeer(d)).wait_send()
    for d in range(1, NZ):
        remote(SM, SR.at[NZ - d], ds_.at[d], dr.at[NZ - d], zpeer(d)).wait_send()


def body(queries, keys, values, grad_out, read_len, *, NT):
    R, D = queries.shape
    F = keys.shape[0]
    TOK, CH, NC = NT * R, 2 * NT * R, NZ // 2
    lens = read_len.reshape(NX, NZ * R)
    hbm = pl.BlockSpec(memory_space=pltpu.HBM)
    vmem = pl.BlockSpec(memory_space=pltpu.VMEM)
    dma = pltpu.SemaphoreType.DMA
    V = pltpu.VMEM
    return pl.pallas_call(
        lambda *refs: kernel(NT, *refs),
        out_shape=(V((R, D), F32), V((F, COLS), F32), V((F, COLS), F32)),
        in_specs=[hbm] * 5,
        out_specs=(vmem, vmem, vmem),
        scratch_shapes=[
            V((NX, NZ * R), jnp.int32),
            V((R, D), BF16),
            V((R, D), BF16),
            V((NT, 2, R, COLS), BF16),
            V((NZ, 2, NT, R, COLS), BF16),
            V((NX, 2, F, COLS), BF16),
            V((NT, 8, COLS), F32),
            V((8, COLS), F32),
            V((NZ, COLS, TOK), BF16),
            V((NX, 2 * F, 2 * COLS), BF16),
            V((NX, 2 * F, COLS), BF16),
            V((NX, COLS, 2 * F), BF16),
            V((NC, NX, 2, F, CH), F32),
            V((NC, NX, 2, F, CH), F32),
            V((NC, 2 * NX, CH), F32),
            V((NC, 8, TOK), F32),
            V((NZ, NC, 8, TOK), F32),
            V((2, NZ * TOK), F32),
            V((2, NZ * TOK), F32),
            V((NC, NX, F, 2 * CH), BF16),
            V((NC, NX, F, 2 * CH), BF16),
            V((NC, 2 * CH, COLS), BF16),
            V((NC, 2 * CH, COLS), BF16),
            V((NC, COLS, CH), F32),
            V((NZ, NT, R, COLS), BF16),
            V((NZ, NT, R, COLS), BF16),
            V((NX, F, COLS), F32),
            V((NX, F, COLS), F32),
            V((NX, 2, F, COLS), BF16),
            V((NX, 2, F, COLS), BF16),
            dma((5,)),
            dma((2, NT)), dma((2, NT)),
            dma((2, NZ)), dma((2, NZ)),
            dma((2, NX)), dma((2, NX)),
            dma((NZ,)), dma((NZ,)),
            dma((NZ,)), dma((NZ,)),
            dma((NX,)), dma((NX,)),
            dma((NT,)), dma((NT,)),
        ],
        compiler_params=pltpu.CompilerParams(
            collective_id=0, has_side_effects=True, vmem_limit_bytes=62 * 1024 * 1024
        ),
    )(queries, keys, values, grad_out, lens)


def solution(mesh):
    NT = mesh.shape["tgt"]
    return jax.shard_map(
        lambda *args: body(*args, NT=NT),
        mesh=mesh,
        in_specs=(
            P(("tgt", "src"), None),
            P("src", None),
            P("src", None),
            P(("tgt", "src"), None),
            P("tgt"),
        ),
        out_specs=(P(("tgt", "src"), None), P("src", "tgt"), P("src", "tgt")),
        check_vma=False,
    )
```

```python
import jax
import jax.numpy as jnp
from jax import lax
from jax.experimental import pallas as pl
from jax.experimental.pallas import tpu as pltpu
from jax.sharding import PartitionSpec as P

MESH = pl.DeviceIdType.MESH
NX, NZ = 4, 8
COLS = 128
MASK_BLOCK = 128
F32, BF16 = jnp.float32, jnp.bfloat16
HIDDEN = -1e30
SCALE = 0.125

REL = [0]
for _d in range(1, NZ // 2 + 1):
    REL += [_d] if 2 * _d == NZ else [_d, NZ - _d]
POS = {d: p for p, d in enumerate(REL)}


def kernel(
    NT, q_hbm, k_hbm, v_hbm, g_hbm, len_hbm, dq_out, dk_out, dv_out,
    len_ref, QI, GI, QGI, QG, KV, L, lrow, M, K2, V2, KT, W, G, MR, SM, SR, CF, RT, PS, GS, Q2, G2, DQT, DQS, DQR, DK, DV, DKVS, DKVR,
    lsem, as_, ar, bs, br, cs, cr, ds_, dr, es, er, fs, fr, gs, gr,
):
    t = lax.axis_index("tgt")
    s = lax.axis_index("src")
    x = s // NZ
    z = s % NZ
    R, F = q_hbm.shape[0], k_hbm.shape[0]
    TOK = NT * R
    CH = 2 * TOK
    NC = NZ // 2

    def tpeer(d):
        return (lax.rem(t + d, NT), s)

    def zpeer(d):
        return (t, x * NZ + lax.rem(z + NZ + d, NZ))

    def xpeer(d):
        return (t, lax.rem(x + d, NX) * NZ + z)

    def cols(i):
        return pl.ds(pl.multiple_of(i * COLS, COLS), COLS)

    def remote(src, dst, ssem, rsem, dev):
        return pltpu.make_async_remote_copy(
            src_ref=src, dst_ref=dst, send_sem=ssem, recv_sem=rsem, device_id=dev, device_id_type=MESH
        )

    local = [
        pltpu.make_async_copy(q_hbm, QI, lsem.at[0]),
        pltpu.make_async_copy(g_hbm, GI, lsem.at[1]),
        pltpu.make_async_copy(k_hbm.at[:, cols(t)], KV.at[0, 0], lsem.at[2]),
        pltpu.make_async_copy(v_hbm.at[:, cols(t)], KV.at[0, 1], lsem.at[3]),
        pltpu.make_async_copy(len_hbm, len_ref, lsem.at[4]),
    ]
    for copy in local:
        copy.start()
    barrier = pltpu.get_barrier_semaphore()
    peers = [tpeer(d) for d in range(1, NT)] + [zpeer(d) for d in range(1, NZ)] + [xpeer(d) for d in range(1, NX)]
    for dev in peers:
        pl.semaphore_signal(barrier, inc=1, device_id=dev, device_id_type=MESH)
    pl.semaphore_wait(barrier, len(peers))

    for copy in local:
        copy.wait()
    row = len_ref[pl.ds(x, 1), :].astype(F32)
    lrow[...] = jnp.broadcast_to(row, lrow.shape)
    L[pl.ds(t, 1)] = jnp.broadcast_to(row[None], (1,) + lrow.shape)
    sent = []
    for i in range(NT):
        QGI[i, 0] = QI[:, i * COLS : (i + 1) * COLS]
        QGI[i, 1] = GI[:, i * COLS : (i + 1) * COLS]
    for d in range(1, NT):
        sent.append(remote(QGI.at[lax.rem(t + d, NT)], QG.at[0, :, t], as_.at[0, d], ar.at[0, d], tpeer(d)))
    for d in range(1, NT):
        sent.append(remote(lrow, L.at[t], as_.at[1, d], ar.at[1, d], tpeer(d)))
    def xhop(part, slot, dest, step):
        return remote(KV.at[slot, part], KV.at[dest, part], cs.at[part, dest], cr.at[part, dest], xpeer(step))

    sent += [xhop(0, 0, NX - 1, 1), xhop(1, 0, 1, NX - 1), xhop(0, 0, 1, NX - 1), xhop(1, 0, NX - 1, 1)]
    for copy in sent:
        copy.start()
    for part in range(2):
        QG[0, part, pl.ds(t, 1)] = QGI[pl.ds(t, 1), part]
    for d in range(1, NT):
        source = lax.rem(t + NT - d, NT)
        remote(QGI.at[0], QG.at[0, :, source], as_.at[0, d], ar.at[0, d], tpeer(d)).wait_recv()

    def hop(part, slot, dest):
        dev = zpeer(1 - 2 * (dest % 2)) if isinstance(dest, int) else zpeer(1 - 2 * lax.rem(dest, 2))
        return remote(QG.at[slot, part], QG.at[dest, part], bs.at[part, dest], br.at[part, dest], dev)

    for part in range(2):
        for dest in (1, 2):
            sent.append(hop(part, 0, dest))
            sent[-1].start()

    for d in range(1, NT):
        source = lax.rem(t + NT - d, NT)
        remote(lrow, L.at[source], as_.at[1, d], ar.at[1, d], tpeer(d)).wait_recv()
    lane3 = lax.broadcasted_iota(jnp.int32, (NT, R, COLS), 2)
    row3 = lax.broadcasted_iota(jnp.int32, (NT, R, COLS), 1)
    lens = jnp.broadcast_to(L[:, 0:1, :], (NT, R, COLS))
    per = F // MASK_BLOCK
    lanes = lax.broadcasted_iota(jnp.int32, (1, 1, COLS), 2)
    first = ((lax.rem(x + lanes // per, NX) * NZ + z) * per + lax.rem(lanes, per)) * MASK_BLOCK
    first = jnp.where(lanes < per * NX, first, -1).astype(F32)

    def mask_slot(p, rel):
        pick = lax.rem(z + rel, NZ) * R + row3
        column = jnp.sum(jnp.where(lane3 == pick, lens, 0.0), axis=2, keepdims=True)
        M[p] = jnp.where(first >= column, HIDDEN, 0.0).reshape(TOK, COLS).T.astype(BF16)

    for p in range(NZ):
        mask_slot(p, REL[p])

    def arrived(part, slot):
        remote(QG.at[0, part], QG.at[slot, part], bs.at[part, 1], br.at[part, slot], zpeer(1)).wait_recv()

    def last_hop(part):
        dev = zpeer(1) if part == 0 else zpeer(-1)
        slot = NZ - 2 - part
        return remote(QG.at[slot, part], QG.at[NZ - 1, part], bs.at[part, NZ - 1], br.at[part, NZ - 1], dev)

    lane2 = lax.broadcasted_iota(jnp.int32, (1, COLS), 1)
    head = [(lane2 < COLS // 2).astype(F32), (lane2 >= COLS // 2).astype(F32)]
    rows2 = lax.broadcasted_iota(jnp.int32, (F, COLS), 0)
    lanes2 = lax.broadcasted_iota(jnp.int32, (F, COLS), 1)

    def kv_arrived(part, r):
        xhop(part, 0, r, 1).wait_recv()

    def build(r):
        kb = KV[r, 0].astype(F32)
        vb = KV[r, 1].astype(F32)
        hot = (lanes2 == rows2 // MASK_BLOCK + per * r).astype(F32).astype(BF16)
        for h in range(2):
            kh = kb * (head[h] * SCALE)
            K2[r, h * F : (h + 1) * F, 0:COLS] = kh.astype(BF16)
            K2[r, h * F : (h + 1) * F, COLS : 2 * COLS] = hot
            V2[r, h * F : (h + 1) * F, :] = (vb * head[h]).astype(BF16)
            KT[r, :, h * F : (h + 1) * F] = kh.T.astype(BF16)

    build(0)
    for part in range(2):
        for slot in (1, 2):
            arrived(part, slot)
            hop(part, slot, slot + 2).start()

    kv_arrived(0, NX - 1)
    sent.append(xhop(0, NX - 1, NX // 2, 1))
    sent[-1].start()
    kv_arrived(1, 1)
    sent.append(xhop(1, 1, NX // 2, NX - 1))
    sent[-1].start()

    masks = [m.astype(BF16) for m in head]

    def block(ref, c, which):
        return ref[pl.ds(2 * c, 2), which].reshape(CH, COLS)

    def pass1(c, fresh):
        qt = jnp.concatenate([block(QG, c, 0).T, jnp.concatenate([M[2 * c], M[2 * c + 1]], axis=1)], axis=0)
        gt = block(QG, c, 1).T
        for h in range(2):
            rows = slice(h * CH, (h + 1) * CH)
            Q2[c, rows] = block(QG, c, 0) * masks[h]
            G2[c, rows] = block(QG, c, 1) * masks[h]
        found = [[] for _ in range(4)]

        def products(r, h):
            rows = slice(h * F, (h + 1) * F)
            W[c, r, h] = jnp.dot(K2[r, rows], qt, preferred_element_type=F32)
            G[c, r, h] = jnp.dot(V2[r, rows], gt, preferred_element_type=F32)

        def reduce(r, h):
            for half in range(2):
                piece = slice(half * TOK, (half + 1) * TOK)
                sc = W[c, r, h, :, piece]
                m = jnp.max(sc, axis=0, keepdims=True)
                w = jnp.exp(sc - m)
                W[c, r, h, :, piece] = w
                MR[c, 2 * r + h : 2 * r + h + 1, piece] = m
                l = jnp.sum(w, axis=0, keepdims=True)
                found[2 * h + half].append((m, l, jnp.sum(w * G[c, r, h, :, piece], axis=0, keepdims=True)))

        order = [(r, h) for r in (0, 1, 3, 2) for h in range(2)]
        products(*order[0])
        for now, later in zip(order, order[1:] + [None]):
            if later is not None:
                if fresh and later[1] == 0:
                    for part in range(2):
                        if (part, later[0]) not in ((0, NX - 1), (1, 1)):
                            kv_arrived(part, later[0])
                    build(later[0])
                products(*later)
            reduce(*now)
        for h in range(2):
            for half in range(2):
                top = found[2 * h + half][0][0]
                for m, _, _ in found[2 * h + half][1:]:
                    top = jnp.maximum(top, m)
                total = jnp.zeros_like(top)
                term = jnp.zeros_like(top)
                for m, l, tt in found[2 * h + half]:
                    a = jnp.exp(m - top)
                    total += a * l
                    term += a * tt
                row = 2 * half + h
                SM[c, row : row + 1, :] = top + jnp.log(total)
                SM[c, 4 + row : 5 + row, :] = term / total
        for d in REL[1:]:
            remote(SM.at[c], SR.at[NZ - d, c], ds_.at[d], dr.at[NZ - d], zpeer(d)).start()

        @pl.when(c < NC - 2)
        def _():
            for part in range(2):
                for one in (3, 4):
                    arrived(part, 2 * c + one)

                    @pl.when(c < NC - 3)
                    def _():
                        hop(part, 2 * c + one, 2 * c + one + 2).start()

                @pl.when(c == NC - 3)
                def _():
                    last_hop(part).start()

        @pl.when(c == NC - 2)
        def _():
            for part in range(2):
                arrived(part, NZ - 1)

        return 0

    pass1(0, True)
    lax.fori_loop(1, NC, lambda c, _: pass1(c, False), 0)

    for d in range(1, NZ):
        remote(SM, SR.at[d], ds_.at[d], dr.at[d], zpeer(d)).wait_recv()

    def combine(p):
        parts, terms = [], []
        for d in range(NZ):
            theirs = POS[(REL[p] - d) % NZ]
            ref = SM if d == 0 else SR.at[d]
            row = 2 * (theirs % 2)
            parts.append(ref[theirs // 2, row : row + 2, :])
            terms.append(ref[theirs // 2, 4 + row : 6 + row, :])
        top = parts[0]
        for part in parts[1:]:
            top = jnp.maximum(top, part)
        total = jnp.zeros_like(top)
        term = jnp.zeros_like(top)
        for part, other in zip(parts, terms):
            weight = jnp.exp(part - top)
            total += weight
            term += weight * other
        CF[:, p * TOK : (p + 1) * TOK] = top + jnp.log(total)
        RT[:, p * TOK : (p + 1) * TOK] = term / total

    for p in range(NZ):
        combine(p)

    def make(c, r):
        piece = slice(c * CH, (c + 1) * CH)
        for h in range(2):
            cf = jnp.exp(MR[c, 2 * r + h : 2 * r + h + 1, :] - CF[h : h + 1, piece])
            term = RT[h : h + 1, piece]
            for lo in range(0, F, 64):
                rows = slice(lo, lo + 64)
                p = W[c, r, h, rows, :] * cf
                PS[c, r, rows, h * CH : (h + 1) * CH] = p.astype(BF16)
                GS[c, r, rows, h * CH : (h + 1) * CH] = (p * (G[c, r, h, rows, :] - term)).astype(BF16)

    def use(c, r):
        first = c == NC - 1
        dv = jnp.dot(PS[c, r], G2[c], preferred_element_type=F32)
        dk = jnp.dot(GS[c, r], Q2[c], preferred_element_type=F32)
        DV[r] = dv if first else DV[r] + dv
        DK[r] = dk if first else DK[r] + dk
        dq = jnp.dot(KT[r, :, 0:F], GS[c, r, :, 0:CH], preferred_element_type=F32)
        dq += jnp.dot(KT[r, :, F : 2 * F], GS[c, r, :, CH : 2 * CH], preferred_element_type=F32)
        DQT[c] = dq if r == ORDER[0] else DQT[c] + dq

    def send_dq(p):
        d = REL[p]
        for i in range(NT):
            if p > 0 or i > 0:
                there = lax.rem(t + i, NT)
                remote(
                    DQS.at[p, there], DQR.at[(NZ - d) % NZ, t],
                    es.at[d] if d else gs.at[i], er.at[(NZ - d) % NZ] if d else gr.at[i],
                    (there, x * NZ + lax.rem(z + d, NZ)),
                ).start()

    def done_dq(c):
        DQS[2 * c : 2 * c + 2] = DQT[c].T.astype(BF16).reshape(2, NT, R, COLS)
        send_dq(2 * c + 1)
        send_dq(2 * c)

    def done_kv(r):
        DKVS[r, 0] = DK[r].astype(BF16)
        DKVS[r, 1] = DV[r].astype(BF16)
        sent.append(remote(DKVS.at[r], DKVR.at[NX - r], fs.at[r], fr.at[NX - r], xpeer(r)))
        sent[-1].start()

    ORDER = [NX // 2] + [i for i in range(1, NX) if i != NX // 2] + [0]
    steps = [(c, r) for c in range(NC - 1, 1, -1) for r in ORDER] + [(c, r) for r in ORDER for c in (1, 0)]
    make(*steps[0])
    for (c, r), later in zip(steps, steps[1:] + [None]):
        if later is not None:
            make(*later)
        use(c, r)
        if r == ORDER[-1]:
            done_dq(c)
        if c == 0 and r > 0:
            done_kv(r)
    DQR[0, pl.ds(t, 1)] = DQS[0, pl.ds(t, 1)]

    for d in range(1, NX):
        remote(DKVS.at[d], DKVR.at[d], fs.at[d], fr.at[d], xpeer(d)).wait_recv()
    dk, dv = DK[0], DV[0]
    for d in range(1, NX):
        dk += DKVR[d, 0].astype(F32)
        dv += DKVR[d, 1].astype(F32)
    dk_out[...] = dk * SCALE
    dv_out[...] = dv

    for d in range(1, NT):
        source = lax.rem(t + NT - d, NT)
        remote(DQS.at[0, 0], DQR.at[0, source], gs.at[d], gr.at[d], tpeer(d)).wait_recv()
    for d in range(1, NZ):
        remote(DQS.at[POS[d]], DQR.at[d], es.at[d], er.at[d], zpeer(d)).wait_recv()
    for i in range(NT):
        dq = DQR[0, i].astype(F32)
        for d in range(1, NZ):
            dq += DQR[d, i].astype(F32)
        dq_out[:, i * COLS : (i + 1) * COLS] = dq
    for copy in sent:
        copy.wait_send()
    for part in range(2):
        for dest in range(3, NZ - 1):
            hop(part, dest - 2, dest).wait_send()
        last_hop(part).wait_send()
    for d in range(1, NT):
        remote(DQS.at[0, 0], DQR.at[0, 0], gs.at[d], gr.at[d], tpeer(d)).wait_send()
    for d in range(1, NZ):
        remote(DQS.at[POS[d]], DQR.at[d], es.at[d], er.at[d], zpeer(d)).wait_send()
    for d in range(1, NZ):
        remote(SM, SR.at[NZ - d], ds_.at[d], dr.at[NZ - d], zpeer(d)).wait_send()


def body(queries, keys, values, grad_out, read_len, *, NT):
    R, D = queries.shape
    F = keys.shape[0]
    TOK, CH, NC = NT * R, 2 * NT * R, NZ // 2
    lens = read_len.reshape(NX, NZ * R)
    hbm = pl.BlockSpec(memory_space=pltpu.HBM)
    vmem = pl.BlockSpec(memory_space=pltpu.VMEM)
    dma = pltpu.SemaphoreType.DMA
    V = pltpu.VMEM
    return pl.pallas_call(
        lambda *refs: kernel(NT, *refs),
        out_shape=(V((R, D), F32), V((F, COLS), F32), V((F, COLS), F32)),
        in_specs=[hbm] * 5,
        out_specs=(vmem, vmem, vmem),
        scratch_shapes=[
            V((NX, NZ * R), jnp.int32),
            V((R, D), BF16),
            V((R, D), BF16),
            V((NT, 2, R, COLS), BF16),
            V((NZ, 2, NT, R, COLS), BF16),
            V((NX, 2, F, COLS), BF16),
            V((NT, 8, COLS), F32),
            V((8, COLS), F32),
            V((NZ, COLS, TOK), BF16),
            V((NX, 2 * F, 2 * COLS), BF16),
            V((NX, 2 * F, COLS), BF16),
            V((NX, COLS, 2 * F), BF16),
            V((NC, NX, 2, F, CH), F32),
            V((NC, NX, 2, F, CH), F32),
            V((NC, 2 * NX, CH), F32),
            V((NC, 8, TOK), F32),
            V((NZ, NC, 8, TOK), F32),
            V((2, NZ * TOK), F32),
            V((2, NZ * TOK), F32),
            V((NC, NX, F, 2 * CH), BF16),
            V((NC, NX, F, 2 * CH), BF16),
            V((NC, 2 * CH, COLS), BF16),
            V((NC, 2 * CH, COLS), BF16),
            V((NC, COLS, CH), F32),
            V((NZ, NT, R, COLS), BF16),
            V((NZ, NT, R, COLS), BF16),
            V((NX, F, COLS), F32),
            V((NX, F, COLS), F32),
            V((NX, 2, F, COLS), BF16),
            V((NX, 2, F, COLS), BF16),
            dma((5,)),
            dma((2, NT)), dma((2, NT)),
            dma((2, NZ)), dma((2, NZ)),
            dma((2, NX)), dma((2, NX)),
            dma((NZ,)), dma((NZ,)),
            dma((NZ,)), dma((NZ,)),
            dma((NX,)), dma((NX,)),
            dma((NT,)), dma((NT,)),
        ],
        compiler_params=pltpu.CompilerParams(
            collective_id=0, has_side_effects=True, vmem_limit_bytes=62 * 1024 * 1024
        ),
    )(queries, keys, values, grad_out, lens)


def solution(mesh):
    NT = mesh.shape["tgt"]
    return jax.shard_map(
        lambda *args: body(*args, NT=NT),
        mesh=mesh,
        in_specs=(
            P(("tgt", "src"), None),
            P("src", None),
            P("src", None),
            P(("tgt", "src"), None),
            P("tgt"),
        ),
        out_specs=(P(("tgt", "src"), None), P("src", "tgt"), P("src", "tgt")),
        check_vma=False,
    )
```

```python
import jax
import jax.numpy as jnp
from jax import lax
from jax.experimental import pallas as pl
from jax.experimental.pallas import tpu as pltpu
from jax.sharding import PartitionSpec as P

MESH = pl.DeviceIdType.MESH
NX, NZ = 4, 8
COLS = 128
MASK_BLOCK = 128
F32, BF16 = jnp.float32, jnp.bfloat16
HIDDEN = -1e30
SCALE = 0.125

REL = [0]
for _d in range(1, NZ // 2 + 1):
    REL += [_d] if 2 * _d == NZ else [_d, NZ - _d]
POS = {d: p for p, d in enumerate(REL)}


def kernel(
    NT, q_hbm, k_hbm, v_hbm, g_hbm, len_hbm, dq_out, dk_out, dv_out,
    len_ref, QI, GI, QGI, QG, KV, L, lrow, M, K2, V2, KT, W, G, MR, SM, SR, CF, RT, PA, GA, PB, GB, Q2, G2, DQT, DQS, DQR, DK, DV, DKVS, DKVR,
    lsem, as_, ar, bs, br, cs, cr, ds_, dr, es, er, fs, fr, gs, gr,
):
    t = lax.axis_index("tgt")
    s = lax.axis_index("src")
    x = s // NZ
    z = s % NZ
    R, F = q_hbm.shape[0], k_hbm.shape[0]
    TOK = NT * R
    CH = 2 * TOK
    NC = NZ // 2

    def tpeer(d):
        return (lax.rem(t + d, NT), s)

    def zpeer(d):
        return (t, x * NZ + lax.rem(z + NZ + d, NZ))

    def xpeer(d):
        return (t, lax.rem(x + d, NX) * NZ + z)

    def cols(i):
        return pl.ds(pl.multiple_of(i * COLS, COLS), COLS)

    def remote(src, dst, ssem, rsem, dev):
        return pltpu.make_async_remote_copy(
            src_ref=src, dst_ref=dst, send_sem=ssem, recv_sem=rsem, device_id=dev, device_id_type=MESH
        )

    local = [
        pltpu.make_async_copy(q_hbm, QI, lsem.at[0]),
        pltpu.make_async_copy(g_hbm, GI, lsem.at[1]),
        pltpu.make_async_copy(k_hbm.at[:, cols(t)], KV.at[0, 0], lsem.at[2]),
        pltpu.make_async_copy(v_hbm.at[:, cols(t)], KV.at[0, 1], lsem.at[3]),
        pltpu.make_async_copy(len_hbm, len_ref, lsem.at[4]),
    ]
    for copy in local:
        copy.start()
    barrier = pltpu.get_barrier_semaphore()
    peers = [tpeer(d) for d in range(1, NT)] + [zpeer(d) for d in range(1, NZ)] + [xpeer(d) for d in range(1, NX)]
    for dev in peers:
        pl.semaphore_signal(barrier, inc=1, device_id=dev, device_id_type=MESH)
    pl.semaphore_wait(barrier, len(peers))

    for copy in local:
        copy.wait()
    row = len_ref[pl.ds(x, 1), :].astype(F32)
    lrow[...] = jnp.broadcast_to(row, lrow.shape)
    L[pl.ds(t, 1)] = jnp.broadcast_to(row[None], (1,) + lrow.shape)
    sent = []
    for i in range(NT):
        QGI[i, 0] = QI[:, i * COLS : (i + 1) * COLS]
        QGI[i, 1] = GI[:, i * COLS : (i + 1) * COLS]
    for d in range(1, NT):
        sent.append(remote(QGI.at[lax.rem(t + d, NT)], QG.at[0, :, t], as_.at[0, d], ar.at[0, d], tpeer(d)))
    for d in range(1, NT):
        sent.append(remote(lrow, L.at[t], as_.at[1, d], ar.at[1, d], tpeer(d)))
    for d in range(1, NX):
        sent += [
            remote(KV.at[0, 0], KV.at[NX - d, 0], cs.at[0, d], cr.at[0, NX - d], xpeer(d)),
            remote(KV.at[0, 1], KV.at[NX - d, 1], cs.at[1, d], cr.at[1, NX - d], xpeer(d)),
        ]
    for copy in sent:
        copy.start()
    for part in range(2):
        QG[0, part, pl.ds(t, 1)] = QGI[pl.ds(t, 1), part]
    for d in range(1, NT):
        source = lax.rem(t + NT - d, NT)
        remote(QGI.at[0], QG.at[0, :, source], as_.at[0, d], ar.at[0, d], tpeer(d)).wait_recv()

    def hop(part, slot, dest):
        dev = zpeer(1 - 2 * (dest % 2)) if isinstance(dest, int) else zpeer(1 - 2 * lax.rem(dest, 2))
        return remote(QG.at[slot, part], QG.at[dest, part], bs.at[part, dest], br.at[part, dest], dev)

    for part in range(2):
        for dest in (1, 2):
            sent.append(hop(part, 0, dest))
            sent[-1].start()

    for d in range(1, NT):
        source = lax.rem(t + NT - d, NT)
        remote(lrow, L.at[source], as_.at[1, d], ar.at[1, d], tpeer(d)).wait_recv()
    lane3 = lax.broadcasted_iota(jnp.int32, (NT, R, COLS), 2)
    row3 = lax.broadcasted_iota(jnp.int32, (NT, R, COLS), 1)
    lens = jnp.broadcast_to(L[:, 0:1, :], (NT, R, COLS))
    per = F // MASK_BLOCK
    lanes = lax.broadcasted_iota(jnp.int32, (1, 1, COLS), 2)
    first = ((lax.rem(x + lanes // per, NX) * NZ + z) * per + lax.rem(lanes, per)) * MASK_BLOCK
    first = jnp.where(lanes < per * NX, first, -1).astype(F32)

    def mask_slot(p, rel):
        pick = lax.rem(z + rel, NZ) * R + row3
        column = jnp.sum(jnp.where(lane3 == pick, lens, 0.0), axis=2, keepdims=True)
        M[p] = jnp.where(first >= column, HIDDEN, 0.0).reshape(TOK, COLS).T.astype(BF16)

    for p in range(NZ):
        mask_slot(p, REL[p])

    def arrived(part, slot):
        remote(QG.at[0, part], QG.at[slot, part], bs.at[part, 1], br.at[part, slot], zpeer(1)).wait_recv()

    def last_hop(part):
        dev = zpeer(1) if part == 0 else zpeer(-1)
        slot = NZ - 2 - part
        return remote(QG.at[slot, part], QG.at[NZ - 1, part], bs.at[part, NZ - 1], br.at[part, NZ - 1], dev)

    for part in range(2):
        for slot in (1, 2):
            arrived(part, slot)
            hop(part, slot, slot + 2).start()

    lane2 = lax.broadcasted_iota(jnp.int32, (1, COLS), 1)
    head = [(lane2 < COLS // 2).astype(F32), (lane2 >= COLS // 2).astype(F32)]
    rows2 = lax.broadcasted_iota(jnp.int32, (F, COLS), 0)
    lanes2 = lax.broadcasted_iota(jnp.int32, (F, COLS), 1)
    for r in range(NX):
        if r > 0:
            remote(KV.at[0, 0], KV.at[r, 0], cs.at[0, r], cr.at[0, r], xpeer(r)).wait_recv()
            remote(KV.at[0, 0], KV.at[r, 1], cs.at[1, r], cr.at[1, r], xpeer(r)).wait_recv()
        kb = KV[r, 0].astype(F32)
        vb = KV[r, 1].astype(F32)
        hot = (lanes2 == rows2 // MASK_BLOCK + per * r).astype(F32).astype(BF16)
        for h in range(2):
            kh = (kb * (head[h] * SCALE)).astype(F32)
            K2[r, h * F : (h + 1) * F, 0:COLS] = kh.astype(BF16)
            K2[r, h * F : (h + 1) * F, COLS : 2 * COLS] = hot
            V2[r, h * F : (h + 1) * F, :] = (vb * head[h]).astype(BF16)
            KT[r, :, h * F : (h + 1) * F] = kh.T.astype(BF16)

    masks = [m.astype(BF16) for m in head]

    def block(ref, c, which):
        return ref[pl.ds(2 * c, 2), which].reshape(CH, COLS)

    def pass1(c, _):
        qt = jnp.concatenate([block(QG, c, 0).T, jnp.concatenate([M[2 * c], M[2 * c + 1]], axis=1)], axis=0)
        gt = block(QG, c, 1).T
        for h in range(2):
            rows = slice(h * CH, (h + 1) * CH)
            Q2[c, rows] = block(QG, c, 0) * masks[h]
            G2[c, rows] = block(QG, c, 1) * masks[h]
        found = [[] for _ in range(4)]

        def products(r, h):
            rows = slice(h * F, (h + 1) * F)
            W[c, r, h] = jnp.dot(K2[r, rows], qt, preferred_element_type=F32)
            G[c, r, h] = jnp.dot(V2[r, rows], gt, preferred_element_type=F32)

        def reduce(r, h):
            for half in range(2):
                piece = slice(half * TOK, (half + 1) * TOK)
                sc = W[c, r, h, :, piece]
                m = jnp.max(sc, axis=0, keepdims=True)
                w = jnp.exp(sc - m)
                W[c, r, h, :, piece] = w
                MR[c, r, h : h + 1, piece] = m
                l = jnp.sum(w, axis=0, keepdims=True)
                found[2 * h + half].append((m, l, jnp.sum(w * G[c, r, h, :, piece], axis=0, keepdims=True)))

        order = [(r, h) for r in range(NX) for h in range(2)]
        products(*order[0])
        for now, later in zip(order, order[1:] + [None]):
            if later is not None:
                products(*later)
            reduce(*now)
        for h in range(2):
            for half in range(2):
                top = found[2 * h + half][0][0]
                for m, _, _ in found[2 * h + half][1:]:
                    top = jnp.maximum(top, m)
                total = jnp.zeros_like(top)
                term = jnp.zeros_like(top)
                for m, l, tt in found[2 * h + half]:
                    a = jnp.exp(m - top)
                    total += a * l
                    term += a * tt
                row = 2 * half + h
                SM[c, row : row + 1, :] = top + jnp.log(total)
                SM[c, 4 + row : 5 + row, :] = term / total
        for d in REL[1:]:
            remote(SM.at[c], SR.at[NZ - d, c], ds_.at[d], dr.at[NZ - d], zpeer(d)).start()

        @pl.when(c < NC - 2)
        def _():
            for part in range(2):
                for one in (3, 4):
                    arrived(part, 2 * c + one)

                    @pl.when(c < NC - 3)
                    def _():
                        hop(part, 2 * c + one, 2 * c + one + 2).start()

                @pl.when(c == NC - 3)
                def _():
                    last_hop(part).start()

        @pl.when(c == NC - 2)
        def _():
            for part in range(2):
                arrived(part, NZ - 1)

        return 0

    lax.fori_loop(0, NC, pass1, 0)

    DK[...] = jnp.zeros_like(DK)
    DV[...] = jnp.zeros_like(DV)
    DQT[...] = jnp.zeros_like(DQT)

    for d in range(1, NZ):
        remote(SM, SR.at[d], ds_.at[d], dr.at[d], zpeer(d)).wait_recv()

    def combine(p):
        parts, terms = [], []
        for d in range(NZ):
            theirs = POS[(REL[p] - d) % NZ]
            ref = SM if d == 0 else SR.at[d]
            row = 2 * (theirs % 2)
            parts.append(ref[theirs // 2, row : row + 2, :])
            terms.append(ref[theirs // 2, 4 + row : 6 + row, :])
        top = parts[0]
        for part in parts[1:]:
            top = jnp.maximum(top, part)
        total = jnp.zeros_like(top)
        term = jnp.zeros_like(top)
        for part, other in zip(parts, terms):
            weight = jnp.exp(part - top)
            total += weight
            term += weight * other
        piece = slice((p % 2) * TOK, (p % 2 + 1) * TOK)
        CF[p // 2, :, piece] = top + jnp.log(total)
        RT[p // 2, :, piece] = term / total

    for p in range(NZ):
        combine(p)

    def make(c, r, PS, GS):
        for h in range(2):
            cf = jnp.exp(MR[c, r, h : h + 1, :] - CF[c, h : h + 1, :])
            term = RT[c, h : h + 1, :]
            for lo in range(0, F, 64):
                rows = slice(lo, lo + 64)
                p = W[c, r, h, rows, :] * cf
                PS[rows, h * CH : (h + 1) * CH] = p.astype(BF16)
                GS[rows, h * CH : (h + 1) * CH] = (p * (G[c, r, h, rows, :] - term)).astype(BF16)

    def use(c, r, PS, GS):
        DV[r] += jnp.dot(PS[...], G2[c], preferred_element_type=F32)
        DK[r] += jnp.dot(GS[...], Q2[c], preferred_element_type=F32)
        dq = jnp.dot(KT[r, :, 0:F], GS[:, 0:CH], preferred_element_type=F32)
        dq += jnp.dot(KT[r, :, F : 2 * F], GS[:, CH : 2 * CH], preferred_element_type=F32)
        DQT[c] += dq

    def send_dq(p, d, i, ssem, rsem):
        there = lax.rem(t + i, NT)
        back = lax.rem(NZ - d, NZ)
        dev = (there, x * NZ + lax.rem(z + d, NZ))
        remote(DQS.at[p, there], DQR.at[back, t], ssem, rsem, dev).start()

    def done_dq(c, own):
        DQS[pl.ds(2 * c, 2)] = DQT[c].T.astype(BF16).reshape(2, NT, R, COLS)

        def far(i, _):
            send_dq(2 * c + 1, c + 1, i, es.at[c + 1], er.at[NZ - 1 - c])
            if not own:
                send_dq(2 * c, NZ - c, i, es.at[NZ - c], er.at[c])
            return 0

        lax.fori_loop(0, NT, far, 0)
        if own:
            for i in range(1, NT):
                send_dq(0, 0, i, gs.at[i], gr.at[i])

    def frames(k):
        return jnp.where(k == 0, NX // 2, jnp.where(k == NX - 1, 0, jnp.where(k >= NX // 2, k + 1, k)))

    far_pairs = (NC - 2) * (NX // 2)

    def pair(j):
        far = j < far_pairs
        cf, kf = NC - 1 - j // (NX // 2), 2 * (j % (NX // 2))
        near = frames(j - far_pairs)
        one = (jnp.where(far, cf, 1), jnp.where(far, frames(kf), near))
        two = (jnp.where(far, cf, 0), jnp.where(far, frames(kf + 1), near))
        return one, two

    pairs = far_pairs + NX

    def pass2(j, _):
        one, two = pair(j)
        after, _ = pair(jnp.minimum(j + 1, pairs - 1))
        make(*two, PB, GB)
        use(*one, PA, GA)
        make(*after, PA, GA)
        use(*two, PB, GB)

        @pl.when((j < far_pairs) & (j % (NX // 2) == NX // 2 - 1))
        def _():
            done_dq(one[0], False)

        @pl.when((j >= far_pairs) & (j < pairs - 1))
        def _():
            r = one[1]
            DKVS[r, 0] = DK[r].astype(BF16)
            DKVS[r, 1] = DV[r].astype(BF16)
            remote(DKVS.at[r], DKVR.at[NX - r], fs.at[r], fr.at[NX - r], xpeer(r)).start()

        return 0

    make(*pair(0)[0], PA, GA)
    lax.fori_loop(0, pairs, pass2, 0)
    done_dq(1, False)
    done_dq(0, True)
    DQR[0, pl.ds(t, 1)] = DQS[0, pl.ds(t, 1)]

    for d in range(1, NX):
        remote(DKVS.at[d], DKVR.at[d], fs.at[d], fr.at[d], xpeer(d)).wait_recv()
    dk, dv = DK[0], DV[0]
    for d in range(1, NX):
        dk += DKVR[d, 0].astype(F32)
        dv += DKVR[d, 1].astype(F32)
    dk_out[...] = dk * SCALE
    dv_out[...] = dv

    for d in range(1, NT):
        source = lax.rem(t + NT - d, NT)
        remote(DQS.at[0, 0], DQR.at[0, source], gs.at[d], gr.at[d], tpeer(d)).wait_recv()
    for d in range(1, NZ):
        remote(DQS.at[POS[d]], DQR.at[d], es.at[d], er.at[d], zpeer(d)).wait_recv()
    for i in range(NT):
        dq = DQR[0, i].astype(F32)
        for d in range(1, NZ):
            dq += DQR[d, i].astype(F32)
        dq_out[:, i * COLS : (i + 1) * COLS] = dq
    for copy in sent:
        copy.wait_send()
    for part in range(2):
        for dest in range(3, NZ - 1):
            hop(part, dest - 2, dest).wait_send()
        last_hop(part).wait_send()
    for r in range(1, NX):
        remote(DKVS.at[r], DKVR.at[NX - r], fs.at[r], fr.at[NX - r], xpeer(r)).wait_send()
    for d in range(1, NT):
        remote(DQS.at[0, 0], DQR.at[0, 0], gs.at[d], gr.at[d], tpeer(d)).wait_send()
    for d in range(1, NZ):
        remote(DQS.at[POS[d]], DQR.at[d], es.at[d], er.at[d], zpeer(d)).wait_send()
    for d in range(1, NZ):
        remote(SM, SR.at[NZ - d], ds_.at[d], dr.at[NZ - d], zpeer(d)).wait_send()


def body(queries, keys, values, grad_out, read_len, *, NT):
    R, D = queries.shape
    F = keys.shape[0]
    TOK, CH, NC = NT * R, 2 * NT * R, NZ // 2
    lens = read_len.reshape(NX, NZ * R)
    hbm = pl.BlockSpec(memory_space=pltpu.HBM)
    vmem = pl.BlockSpec(memory_space=pltpu.VMEM)
    dma = pltpu.SemaphoreType.DMA
    V = pltpu.VMEM
    return pl.pallas_call(
        lambda *refs: kernel(NT, *refs),
        out_shape=(V((R, D), F32), V((F, COLS), F32), V((F, COLS), F32)),
        in_specs=[hbm] * 5,
        out_specs=(vmem, vmem, vmem),
        scratch_shapes=[
            V((NX, NZ * R), jnp.int32),
            V((R, D), BF16),
            V((R, D), BF16),
            V((NT, 2, R, COLS), BF16),
            V((NZ, 2, NT, R, COLS), BF16),
            V((NX, 2, F, COLS), BF16),
            V((NT, 8, COLS), F32),
            V((8, COLS), F32),
            V((NZ, COLS, TOK), BF16),
            V((NX, 2 * F, 2 * COLS), BF16),
            V((NX, 2 * F, COLS), BF16),
            V((NX, COLS, 2 * F), BF16),
            V((NC, NX, 2, F, CH), F32),
            V((NC, NX, 2, F, CH), F32),
            V((NC, NX, 2, CH), F32),
            V((NC, 8, TOK), F32),
            V((NZ, NC, 8, TOK), F32),
            V((NC, 2, CH), F32),
            V((NC, 2, CH), F32),
            V((F, 2 * CH), BF16),
            V((F, 2 * CH), BF16),
            V((F, 2 * CH), BF16),
            V((F, 2 * CH), BF16),
            V((NC, 2 * CH, COLS), BF16),
            V((NC, 2 * CH, COLS), BF16),
            V((NC, COLS, CH), F32),
            V((NZ, NT, R, COLS), BF16),
            V((NZ, NT, R, COLS), BF16),
            V((NX, F, COLS), F32),
            V((NX, F, COLS), F32),
            V((NX, 2, F, COLS), BF16),
            V((NX, 2, F, COLS), BF16),
            dma((5,)),
            dma((2, NT)), dma((2, NT)),
            dma((2, NZ)), dma((2, NZ)),
            dma((2, NX)), dma((2, NX)),
            dma((NZ,)), dma((NZ,)),
            dma((NZ,)), dma((NZ,)),
            dma((NX,)), dma((NX,)),
            dma((NT,)), dma((NT,)),
        ],
        compiler_params=pltpu.CompilerParams(
            collective_id=0, has_side_effects=True, vmem_limit_bytes=62 * 1024 * 1024
        ),
    )(queries, keys, values, grad_out, lens)


def solution(mesh):
    NT = mesh.shape["tgt"]
    return jax.shard_map(
        lambda *args: body(*args, NT=NT),
        mesh=mesh,
        in_specs=(
            P(("tgt", "src"), None),
            P("src", None),
            P("src", None),
            P(("tgt", "src"), None),
            P("tgt"),
        ),
        out_specs=(P(("tgt", "src"), None), P("src", "tgt"), P("src", "tgt")),
        check_vma=False,
    )
```

```python
import jax
import jax.numpy as jnp
from jax import lax
from jax.experimental import pallas as pl
from jax.experimental.pallas import tpu as pltpu
from jax.sharding import PartitionSpec as P

MESH = pl.DeviceIdType.MESH
NX, NZ = 4, 8
COLS = 128
HALF = COLS // 2
MASK_BLOCK = 128
F32, BF16 = jnp.float32, jnp.bfloat16
HIDDEN = -1e30
SCALE = 0.125

REL = [0]
for _d in range(1, NZ // 2 + 1):
    REL += [_d] if 2 * _d == NZ else [_d, NZ - _d]
POS = {d: p for p, d in enumerate(REL)}


def kernel(
    NT, q_hbm, k_hbm, v_hbm, g_hbm, len_hbm, dq_out, dk_out, dv_out,
    len_ref, QI, GI, QGI, QG, KV, L, lrow, M, K2, KT, W, G, MR, SM, SR, CF, RT, PS, GS, Q2, G2, DQT, DQS, DQR, DK, DV, DKVS, DKVR,
    lsem, as_, ar, bs, br, cs, cr, ds_, dr, es, er, fs, fr, gs, gr,
):
    t = lax.axis_index("tgt")
    s = lax.axis_index("src")
    x = s // NZ
    z = s % NZ
    R, F = q_hbm.shape[0], k_hbm.shape[0]
    TOK = NT * R
    CH = 2 * TOK
    NC = NZ // 2

    def tpeer(d):
        return (lax.rem(t + d, NT), s)

    def zpeer(d):
        return (t, x * NZ + lax.rem(z + NZ + d, NZ))

    def xpeer(d):
        return (t, lax.rem(x + d, NX) * NZ + z)

    def cols(i):
        return pl.ds(pl.multiple_of(i * COLS, COLS), COLS)

    def remote(src, dst, ssem, rsem, dev):
        return pltpu.make_async_remote_copy(
            src_ref=src, dst_ref=dst, send_sem=ssem, recv_sem=rsem, device_id=dev, device_id_type=MESH
        )

    local = [
        pltpu.make_async_copy(q_hbm, QI, lsem.at[0]),
        pltpu.make_async_copy(g_hbm, GI, lsem.at[1]),
        pltpu.make_async_copy(k_hbm.at[:, cols(t)], KV.at[0, 0], lsem.at[2]),
        pltpu.make_async_copy(v_hbm.at[:, cols(t)], KV.at[0, 1], lsem.at[3]),
        pltpu.make_async_copy(len_hbm, len_ref, lsem.at[4]),
    ]
    for copy in local:
        copy.start()
    barrier = pltpu.get_barrier_semaphore()
    peers = [tpeer(d) for d in range(1, NT)] + [zpeer(d) for d in range(1, NZ)] + [xpeer(d) for d in range(1, NX)]
    for dev in peers:
        pl.semaphore_signal(barrier, inc=1, device_id=dev, device_id_type=MESH)
    pl.semaphore_wait(barrier, len(peers))

    for copy in local:
        copy.wait()
    row = len_ref[pl.ds(x, 1), :].astype(F32)
    lrow[...] = jnp.broadcast_to(row, lrow.shape)
    L[pl.ds(t, 1)] = jnp.broadcast_to(row[None], (1,) + lrow.shape)
    sent = []
    for i in range(NT):
        QGI[i, 0] = QI[:, i * COLS : (i + 1) * COLS]
        QGI[i, 1] = GI[:, i * COLS : (i + 1) * COLS]
    for d in range(1, NT):
        sent.append(remote(QGI.at[lax.rem(t + d, NT)], QG.at[0, :, t], as_.at[0, d], ar.at[0, d], tpeer(d)))
    for d in range(1, NT):
        sent.append(remote(lrow, L.at[t], as_.at[1, d], ar.at[1, d], tpeer(d)))
    for d in range(1, NX):
        sent += [
            remote(KV.at[0, 0], KV.at[NX - d, 0], cs.at[0, d], cr.at[0, NX - d], xpeer(d)),
            remote(KV.at[0, 1], KV.at[NX - d, 1], cs.at[1, d], cr.at[1, NX - d], xpeer(d)),
        ]
    for copy in sent:
        copy.start()
    for part in range(2):
        QG[0, part, pl.ds(t, 1)] = QGI[pl.ds(t, 1), part]
    for d in range(1, NT):
        source = lax.rem(t + NT - d, NT)
        remote(QGI.at[0], QG.at[0, :, source], as_.at[0, d], ar.at[0, d], tpeer(d)).wait_recv()

    def hop(part, slot, dest):
        dev = zpeer(1 - 2 * (dest % 2)) if isinstance(dest, int) else zpeer(1 - 2 * lax.rem(dest, 2))
        return remote(QG.at[slot, part], QG.at[dest, part], bs.at[part, dest], br.at[part, dest], dev)

    for part in range(2):
        for dest in (1, 2):
            sent.append(hop(part, 0, dest))
            sent[-1].start()

    for d in range(1, NT):
        source = lax.rem(t + NT - d, NT)
        remote(lrow, L.at[source], as_.at[1, d], ar.at[1, d], tpeer(d)).wait_recv()
    lane3 = lax.broadcasted_iota(jnp.int32, (NT, R, COLS), 2)
    row3 = lax.broadcasted_iota(jnp.int32, (NT, R, COLS), 1)
    lens = jnp.broadcast_to(L[:, 0:1, :], (NT, R, COLS))
    per = F // MASK_BLOCK
    lanes = lax.broadcasted_iota(jnp.int32, (1, 1, COLS), 2)
    first = ((lax.rem(x + lanes // per, NX) * NZ + z) * per + lax.rem(lanes, per)) * MASK_BLOCK
    first = jnp.where(lanes < per * NX, first, -1).astype(F32)

    def mask_slot(p, rel):
        pick = lax.rem(z + rel, NZ) * R + row3
        column = jnp.sum(jnp.where(lane3 == pick, lens, 0.0), axis=2, keepdims=True)
        M[p] = jnp.where(first >= column, HIDDEN, 0.0).reshape(TOK, COLS).T[0:HALF].astype(BF16)

    for p in range(NZ):
        mask_slot(p, REL[p])

    def arrived(part, slot):
        remote(QG.at[0, part], QG.at[slot, part], bs.at[part, 1], br.at[part, slot], zpeer(1)).wait_recv()

    def last_hop(part):
        dev = zpeer(1) if part == 0 else zpeer(-1)
        slot = NZ - 2 - part
        return remote(QG.at[slot, part], QG.at[NZ - 1, part], bs.at[part, NZ - 1], br.at[part, NZ - 1], dev)

    for part in range(2):
        for slot in (1, 2):
            arrived(part, slot)
            hop(part, slot, slot + 2).start()

    lane2 = lax.broadcasted_iota(jnp.int32, (1, COLS), 1)
    head = [(lane2 < COLS // 2).astype(F32), (lane2 >= COLS // 2).astype(F32)]
    rows2 = lax.broadcasted_iota(jnp.int32, (F, COLS), 0)
    lanes2 = lax.broadcasted_iota(jnp.int32, (F, COLS), 1)
    for r in range(NX):
        if r > 0:
            remote(KV.at[0, 0], KV.at[r, 0], cs.at[0, r], cr.at[0, r], xpeer(r)).wait_recv()
            remote(KV.at[0, 0], KV.at[r, 1], cs.at[1, r], cr.at[1, r], xpeer(r)).wait_recv()
        kb = KV[r, 0].astype(F32) * SCALE
        block_of = rows2 // MASK_BLOCK + per * r
        for h in range(2):
            mine = (lanes2 < HALF) if h == 0 else (lanes2 >= HALF)
            hot = (lanes2 == block_of + HALF * (1 - h)).astype(F32)
            K2[h, r * F : (r + 1) * F, :] = jnp.where(mine, kb, hot).astype(BF16)
        KT[:, r * F : (r + 1) * F] = kb.T.astype(BF16)

    masks = [m.astype(BF16) for m in head]

    def block(ref, c, which):
        return ref[pl.ds(2 * c, 2), which].reshape(CH, COLS)

    def pass1(c, _):
        qt, gt = block(QG, c, 0).T, block(QG, c, 1).T
        mt = jnp.concatenate([M[2 * c], M[2 * c + 1]], axis=1)
        none = jnp.zeros((HALF, CH), BF16)
        qts = [jnp.concatenate([qt[0:HALF], mt], axis=0), jnp.concatenate([mt, qt[HALF:COLS]], axis=0)]
        gts = [jnp.concatenate([gt[0:HALF], none], axis=0), jnp.concatenate([none, gt[HALF:COLS]], axis=0)]
        for h in range(2):
            rows = slice(h * CH, (h + 1) * CH)
            Q2[c, rows] = block(QG, c, 0) * masks[h]
            G2[c, rows] = block(QG, c, 1) * masks[h]
        found = [[] for _ in range(4)]

        def products(two, h):
            rows = slice(two * 2 * F, (two + 1) * 2 * F)
            vb = KV[2 * two : 2 * two + 2, 1].reshape(2 * F, COLS)
            W[c, h, rows] = jnp.dot(K2[h, rows], qts[h], preferred_element_type=F32)
            G[c, h, rows] = jnp.dot(vb, gts[h], preferred_element_type=F32)

        def reduce(r, h):
            rows = slice(r * F, (r + 1) * F)
            for half in range(2):
                piece = slice(half * TOK, (half + 1) * TOK)
                sc = W[c, h, rows, piece]
                m = jnp.max(sc, axis=0, keepdims=True)
                w = jnp.exp(sc - m)
                W[c, h, rows, piece] = w
                MR[c, 2 * r + h : 2 * r + h + 1, piece] = m
                l = jnp.sum(w, axis=0, keepdims=True)
                found[2 * h + half].append((m, l, jnp.sum(w * G[c, h, rows, piece], axis=0, keepdims=True)))

        order = [(two, h) for two in range(NX // 2) for h in range(2)]
        products(*order[0])
        for (two, h), later in zip(order, order[1:] + [None]):
            if later is not None:
                products(*later)
            reduce(2 * two, h)
            reduce(2 * two + 1, h)
        for h in range(2):
            for half in range(2):
                top = found[2 * h + half][0][0]
                for m, _, _ in found[2 * h + half][1:]:
                    top = jnp.maximum(top, m)
                total = jnp.zeros_like(top)
                term = jnp.zeros_like(top)
                for m, l, tt in found[2 * h + half]:
                    a = jnp.exp(m - top)
                    total += a * l
                    term += a * tt
                row = 2 * half + h
                SM[c, row : row + 1, :] = top + jnp.log(total)
                SM[c, 4 + row : 5 + row, :] = term / total
        for d in REL[1:]:
            remote(SM.at[c], SR.at[NZ - d, c], ds_.at[d], dr.at[NZ - d], zpeer(d)).start()

        @pl.when(c < NC - 2)
        def _():
            for part in range(2):
                for one in (3, 4):
                    arrived(part, 2 * c + one)

                    @pl.when(c < NC - 3)
                    def _():
                        hop(part, 2 * c + one, 2 * c + one + 2).start()

                @pl.when(c == NC - 3)
                def _():
                    last_hop(part).start()

        @pl.when(c == NC - 2)
        def _():
            for part in range(2):
                arrived(part, NZ - 1)

        return 0

    lax.fori_loop(0, NC, pass1, 0)

    for d in range(1, NZ):
        remote(SM, SR.at[d], ds_.at[d], dr.at[d], zpeer(d)).wait_recv()

    def combine(p):
        parts, terms = [], []
        for d in range(NZ):
            theirs = POS[(REL[p] - d) % NZ]
            ref = SM if d == 0 else SR.at[d]
            row = 2 * (theirs % 2)
            parts.append(ref[theirs // 2, row : row + 2, :])
            terms.append(ref[theirs // 2, 4 + row : 6 + row, :])
        top = parts[0]
        for part in parts[1:]:
            top = jnp.maximum(top, part)
        total = jnp.zeros_like(top)
        term = jnp.zeros_like(top)
        for part, other in zip(parts, terms):
            weight = jnp.exp(part - top)
            total += weight
            term += weight * other
        CF[:, p * TOK : (p + 1) * TOK] = top + jnp.log(total)
        RT[:, p * TOK : (p + 1) * TOK] = term / total

    for p in range(NZ):
        combine(p)

    def make(c, r):
        piece = slice(c * CH, (c + 1) * CH)
        for h in range(2):
            cf = jnp.exp(MR[c, 2 * r + h : 2 * r + h + 1, :] - CF[h : h + 1, piece])
            term = RT[h : h + 1, piece]
            for lo in range(r * F, (r + 1) * F, 64):
                rows = slice(lo, lo + 64)
                p = W[c, h, rows, :] * cf
                PS[c, h, rows, :] = p.astype(BF16)
                GS[c, h, rows, :] = (p * (G[c, h, rows, :] - term)).astype(BF16)

    def use_dq(c, rows, start):
        for h in range(2):
            out = slice(h * HALF, (h + 1) * HALF)
            dq = jnp.dot(KT[out, rows], GS[c, h, rows], preferred_element_type=F32)
            DQT[c, out] = dq if start else DQT[c, out] + dq

    def use_far(c, two):
        rows = slice(two * 2 * F, (two + 1) * 2 * F)
        both = lambda ref: jnp.concatenate([ref[c, 0, rows], ref[c, 1, rows]], axis=1)
        dv = jnp.dot(both(PS), G2[c], preferred_element_type=F32)
        dk = jnp.dot(both(GS), Q2[c], preferred_element_type=F32)
        DV[rows] = dv if c == NC - 1 else DV[rows] + dv
        DK[rows] = dk if c == NC - 1 else DK[rows] + dk
        use_dq(c, rows, two == 0)

    def use_near(r):
        rows = slice(r * F, (r + 1) * F)
        all4 = lambda ref: jnp.concatenate([ref[c, h, rows] for c in (0, 1) for h in range(2)], axis=1)
        g4, q4 = G2[0:2].reshape(4 * CH, COLS), Q2[0:2].reshape(4 * CH, COLS)
        DV[rows] += jnp.dot(all4(PS), g4, preferred_element_type=F32)
        DK[rows] += jnp.dot(all4(GS), q4, preferred_element_type=F32)
        for c in (1, 0):
            use_dq(c, rows, r == ORDER[0])

    def send_dq(p):
        d = REL[p]
        for i in range(NT):
            if p > 0 or i > 0:
                there = lax.rem(t + i, NT)
                remote(
                    DQS.at[p, there], DQR.at[(NZ - d) % NZ, t],
                    es.at[d] if d else gs.at[i], er.at[(NZ - d) % NZ] if d else gr.at[i],
                    (there, x * NZ + lax.rem(z + d, NZ)),
                ).start()

    def done_dq(c):
        DQS[2 * c : 2 * c + 2] = DQT[c].T.astype(BF16).reshape(2, NT, R, COLS)
        send_dq(2 * c + 1)
        send_dq(2 * c)

    def done_kv(r):
        rows = slice(r * F, (r + 1) * F)
        DKVS[r, 0] = DK[rows].astype(BF16)
        DKVS[r, 1] = DV[rows].astype(BF16)
        sent.append(remote(DKVS.at[r], DKVR.at[NX - r], fs.at[r], fr.at[NX - r], xpeer(r)))
        sent[-1].start()

    ORDER = [NX // 2] + [i for i in range(1, NX) if i != NX // 2] + [0]
    steps = [(c, two) for c in range(NC - 1, 1, -1) for two in range(NX // 2)] + [(0, r) for r in ORDER]

    def make_step(c, i):
        for tile in [(c, 2 * i), (c, 2 * i + 1)] if c > 1 else [(1, i), (0, i)]:
            make(*tile)

    make_step(*steps[0])
    for (c, i), later in zip(steps, steps[1:] + [None]):
        if later is not None:
            make_step(*later)
        if c > 1:
            use_far(c, i)
            if i == NX // 2 - 1:
                done_dq(c)
        else:
            use_near(i)
            if i > 0:
                done_kv(i)
    done_dq(1)
    done_dq(0)
    DQR[0, pl.ds(t, 1)] = DQS[0, pl.ds(t, 1)]

    for d in range(1, NX):
        remote(DKVS.at[d], DKVR.at[d], fs.at[d], fr.at[d], xpeer(d)).wait_recv()
    dk, dv = DK[0:F], DV[0:F]
    for d in range(1, NX):
        dk += DKVR[d, 0].astype(F32)
        dv += DKVR[d, 1].astype(F32)
    dk_out[...] = dk * SCALE
    dv_out[...] = dv

    for d in range(1, NT):
        source = lax.rem(t + NT - d, NT)
        remote(DQS.at[0, 0], DQR.at[0, source], gs.at[d], gr.at[d], tpeer(d)).wait_recv()
    for d in range(1, NZ):
        remote(DQS.at[POS[d]], DQR.at[d], es.at[d], er.at[d], zpeer(d)).wait_recv()
    for i in range(NT):
        dq = DQR[0, i].astype(F32)
        for d in range(1, NZ):
            dq += DQR[d, i].astype(F32)
        dq_out[:, i * COLS : (i + 1) * COLS] = dq
    for copy in sent:
        copy.wait_send()
    for part in range(2):
        for dest in range(3, NZ - 1):
            hop(part, dest - 2, dest).wait_send()
        last_hop(part).wait_send()
    for d in range(1, NT):
        remote(DQS.at[0, 0], DQR.at[0, 0], gs.at[d], gr.at[d], tpeer(d)).wait_send()
    for d in range(1, NZ):
        remote(DQS.at[POS[d]], DQR.at[d], es.at[d], er.at[d], zpeer(d)).wait_send()
    for d in range(1, NZ):
        remote(SM, SR.at[NZ - d], ds_.at[d], dr.at[NZ - d], zpeer(d)).wait_send()


def body(queries, keys, values, grad_out, read_len, *, NT):
    R, D = queries.shape
    F = keys.shape[0]
    TOK, CH, NC = NT * R, 2 * NT * R, NZ // 2
    lens = read_len.reshape(NX, NZ * R)
    hbm = pl.BlockSpec(memory_space=pltpu.HBM)
    vmem = pl.BlockSpec(memory_space=pltpu.VMEM)
    dma = pltpu.SemaphoreType.DMA
    V = pltpu.VMEM
    return pl.pallas_call(
        lambda *refs: kernel(NT, *refs),
        out_shape=(V((R, D), F32), V((F, COLS), F32), V((F, COLS), F32)),
        in_specs=[hbm] * 5,
        out_specs=(vmem, vmem, vmem),
        scratch_shapes=[
            V((NX, NZ * R), jnp.int32),
            V((R, D), BF16),
            V((R, D), BF16),
            V((NT, 2, R, COLS), BF16),
            V((NZ, 2, NT, R, COLS), BF16),
            V((NX, 2, F, COLS), BF16),
            V((NT, 8, COLS), F32),
            V((8, COLS), F32),
            V((NZ, HALF, TOK), BF16),
            V((2, NX * F, COLS), BF16),
            V((COLS, NX * F), BF16),
            V((NC, 2, NX * F, CH), F32),
            V((NC, 2, NX * F, CH), F32),
            V((NC, 2 * NX, CH), F32),
            V((NC, 8, TOK), F32),
            V((NZ, NC, 8, TOK), F32),
            V((2, NZ * TOK), F32),
            V((2, NZ * TOK), F32),
            V((NC, 2, NX * F, CH), BF16),
            V((NC, 2, NX * F, CH), BF16),
            V((NC, 2 * CH, COLS), BF16),
            V((NC, 2 * CH, COLS), BF16),
            V((NC, COLS, CH), F32),
            V((NZ, NT, R, COLS), BF16),
            V((NZ, NT, R, COLS), BF16),
            V((NX * F, COLS), F32),
            V((NX * F, COLS), F32),
            V((NX, 2, F, COLS), BF16),
            V((NX, 2, F, COLS), BF16),
            dma((5,)),
            dma((2, NT)), dma((2, NT)),
            dma((2, NZ)), dma((2, NZ)),
            dma((2, NX)), dma((2, NX)),
            dma((NZ,)), dma((NZ,)),
            dma((NZ,)), dma((NZ,)),
            dma((NX,)), dma((NX,)),
            dma((NT,)), dma((NT,)),
        ],
        compiler_params=pltpu.CompilerParams(
            collective_id=0, has_side_effects=True, vmem_limit_bytes=62 * 1024 * 1024
        ),
    )(queries, keys, values, grad_out, lens)


def solution(mesh):
    NT = mesh.shape["tgt"]
    return jax.shard_map(
        lambda *args: body(*args, NT=NT),
        mesh=mesh,
        in_specs=(
            P(("tgt", "src"), None),
            P("src", None),
            P("src", None),
            P(("tgt", "src"), None),
            P("tgt"),
        ),
        out_specs=(P(("tgt", "src"), None), P("src", "tgt"), P("src", "tgt")),
        check_vma=False,
    )
```

```python
import jax
import jax.numpy as jnp
from jax import lax
from jax.experimental import pallas as pl
from jax.experimental.pallas import tpu as pltpu
from jax.sharding import PartitionSpec as P

MESH = pl.DeviceIdType.MESH
NX, NZ = 4, 8
COLS = 128
MASK_BLOCK = 128
F32, BF16 = jnp.float32, jnp.bfloat16
HIDDEN = -1e30
SCALE = 0.125

REL = [0]
for _d in range(1, NZ // 2 + 1):
    REL += [_d] if 2 * _d == NZ else [_d, NZ - _d]
POS = {d: p for p, d in enumerate(REL)}


def kernel(
    NT, q_hbm, k_hbm, v_hbm, g_hbm, len_hbm, dq_out, dk_out, dv_out,
    len_ref, QI, GI, QGI, QG, KV, L, lrow, M, K2, V2, KT, W, G, MR, SM, SR, CF, RT, PS, GS, Q2, G2, DQT, DQS, DQR, DK, DV, DKVS, DKVR,
    lsem, as_, ar, bs, br, cs, cr, ds_, dr, es, er, fs, fr, gs, gr,
):
    t = lax.axis_index("tgt")
    s = lax.axis_index("src")
    x = s // NZ
    z = s % NZ
    R, F = q_hbm.shape[0], k_hbm.shape[0]
    TOK = NT * R
    CH = 2 * TOK
    NC = NZ // 2

    def tpeer(d):
        return (lax.rem(t + d, NT), s)

    def zpeer(d):
        return (t, x * NZ + lax.rem(z + NZ + d, NZ))

    def xpeer(d):
        return (t, lax.rem(x + d, NX) * NZ + z)

    def cols(i):
        return pl.ds(pl.multiple_of(i * COLS, COLS), COLS)

    def remote(src, dst, ssem, rsem, dev):
        return pltpu.make_async_remote_copy(
            src_ref=src, dst_ref=dst, send_sem=ssem, recv_sem=rsem, device_id=dev, device_id_type=MESH
        )

    local = [
        pltpu.make_async_copy(q_hbm, QI, lsem.at[0]),
        pltpu.make_async_copy(g_hbm, GI, lsem.at[1]),
        pltpu.make_async_copy(k_hbm.at[:, cols(t)], KV.at[0, 0], lsem.at[2]),
        pltpu.make_async_copy(v_hbm.at[:, cols(t)], KV.at[0, 1], lsem.at[3]),
        pltpu.make_async_copy(len_hbm, len_ref, lsem.at[4]),
    ]
    for copy in local:
        copy.start()
    barrier = pltpu.get_barrier_semaphore()
    peers = [tpeer(d) for d in range(1, NT)] + [zpeer(d) for d in range(1, NZ)] + [xpeer(d) for d in range(1, NX)]
    for dev in peers:
        pl.semaphore_signal(barrier, inc=1, device_id=dev, device_id_type=MESH)
    pl.semaphore_wait(barrier, len(peers))

    for copy in local:
        copy.wait()
    row = len_ref[pl.ds(x, 1), :].astype(F32)
    lrow[...] = jnp.broadcast_to(row, lrow.shape)
    L[pl.ds(t, 1)] = jnp.broadcast_to(row[None], (1,) + lrow.shape)
    sent = []
    for i in range(NT):
        QGI[i, 0] = QI[:, i * COLS : (i + 1) * COLS]
        QGI[i, 1] = GI[:, i * COLS : (i + 1) * COLS]
    for d in range(1, NT):
        sent.append(remote(QGI.at[lax.rem(t + d, NT)], QG.at[0, :, t], as_.at[0, d], ar.at[0, d], tpeer(d)))
    for d in range(1, NT):
        sent.append(remote(lrow, L.at[t], as_.at[1, d], ar.at[1, d], tpeer(d)))
    for d in range(1, NX):
        sent += [
            remote(KV.at[0, 0], KV.at[NX - d, 0], cs.at[0, d], cr.at[0, NX - d], xpeer(d)),
            remote(KV.at[0, 1], KV.at[NX - d, 1], cs.at[1, d], cr.at[1, NX - d], xpeer(d)),
        ]
    for copy in sent:
        copy.start()
    for part in range(2):
        QG[0, part, pl.ds(t, 1)] = QGI[pl.ds(t, 1), part]
    for d in range(1, NT):
        source = lax.rem(t + NT - d, NT)
        remote(QGI.at[0], QG.at[0, :, source], as_.at[0, d], ar.at[0, d], tpeer(d)).wait_recv()

    def hop(part, slot, dest):
        dev = zpeer(1 - 2 * (dest % 2)) if isinstance(dest, int) else zpeer(1 - 2 * lax.rem(dest, 2))
        return remote(QG.at[slot, part], QG.at[dest, part], bs.at[part, dest], br.at[part, dest], dev)

    for part in range(2):
        for dest in (1, 2):
            sent.append(hop(part, 0, dest))
            sent[-1].start()

    for d in range(1, NT):
        source = lax.rem(t + NT - d, NT)
        remote(lrow, L.at[source], as_.at[1, d], ar.at[1, d], tpeer(d)).wait_recv()
    lane3 = lax.broadcasted_iota(jnp.int32, (NT, R, COLS), 2)
    row3 = lax.broadcasted_iota(jnp.int32, (NT, R, COLS), 1)
    lens = jnp.broadcast_to(L[:, 0:1, :], (NT, R, COLS))
    per = F // MASK_BLOCK
    lanes = lax.broadcasted_iota(jnp.int32, (1, 1, COLS), 2)
    first = ((lax.rem(x + lanes // per, NX) * NZ + z) * per + lax.rem(lanes, per)) * MASK_BLOCK
    first = jnp.where(lanes < per * NX, first, -1).astype(F32)

    def mask_slot(p, rel):
        pick = lax.rem(z + rel, NZ) * R + row3
        column = jnp.sum(jnp.where(lane3 == pick, lens, 0.0), axis=2, keepdims=True)
        M[p] = jnp.where(first >= column, HIDDEN, 0.0).reshape(TOK, COLS).T.astype(BF16)

    for p in range(NZ):
        mask_slot(p, REL[p])

    def arrived(part, slot):
        remote(QG.at[0, part], QG.at[slot, part], bs.at[part, 1], br.at[part, slot], zpeer(1)).wait_recv()

    def last_hop(part):
        dev = zpeer(1) if part == 0 else zpeer(-1)
        slot = NZ - 2 - part
        return remote(QG.at[slot, part], QG.at[NZ - 1, part], bs.at[part, NZ - 1], br.at[part, NZ - 1], dev)

    for part in range(2):
        for slot in (1, 2):
            arrived(part, slot)
            hop(part, slot, slot + 2).start()

    lane2 = lax.broadcasted_iota(jnp.int32, (1, COLS), 1)
    head = [(lane2 < COLS // 2).astype(F32), (lane2 >= COLS // 2).astype(F32)]
    rows2 = lax.broadcasted_iota(jnp.int32, (F, COLS), 0)
    lanes2 = lax.broadcasted_iota(jnp.int32, (F, COLS), 1)
    for r in range(NX):
        if r > 0:
            remote(KV.at[0, 0], KV.at[r, 0], cs.at[0, r], cr.at[0, r], xpeer(r)).wait_recv()
            remote(KV.at[0, 0], KV.at[r, 1], cs.at[1, r], cr.at[1, r], xpeer(r)).wait_recv()
        kb = KV[r, 0].astype(F32)
        vb = KV[r, 1].astype(F32)
        hot = (lanes2 == rows2 // MASK_BLOCK + per * r).astype(F32).astype(BF16)
        for h in range(2):
            kh = (kb * (head[h] * SCALE)).astype(F32)
            K2[r, h * F : (h + 1) * F, 0:COLS] = kh.astype(BF16)
            K2[r, h * F : (h + 1) * F, COLS : 2 * COLS] = hot
            V2[r, h * F : (h + 1) * F, :] = (vb * head[h]).astype(BF16)
            KT[r, :, h * F : (h + 1) * F] = kh.T.astype(BF16)

    masks = [m.astype(BF16) for m in head]

    def block(ref, c, which):
        return ref[pl.ds(2 * c, 2), which].reshape(CH, COLS)

    def send_stats(which):
        some = pl.ds(which.start, which.stop - which.start)
        for d in REL[1:]:
            remote(SM.at[some], SR.at[NZ - d, some], ds_.at[d], dr.at[NZ - d], zpeer(d)).start()

    def pass1(c, _):
        qt = jnp.concatenate([block(QG, c, 0).T, jnp.concatenate([M[2 * c], M[2 * c + 1]], axis=1)], axis=0)
        gt = block(QG, c, 1).T
        for h in range(2):
            rows = slice(h * CH, (h + 1) * CH)
            Q2[c, rows] = block(QG, c, 0) * masks[h]
            G2[c, rows] = block(QG, c, 1) * masks[h]
        found = [[] for _ in range(4)]

        def products(r, h):
            rows = slice(h * F, (h + 1) * F)
            W[c, r, h] = jnp.dot(K2[r, rows], qt, preferred_element_type=F32)
            G[c, r, h] = jnp.dot(V2[r, rows], gt, preferred_element_type=F32)

        def reduce(r, h):
            for half in range(2):
                piece = slice(half * TOK, (half + 1) * TOK)
                sc = W[c, r, h, :, piece]
                m = jnp.max(sc, axis=0, keepdims=True)
                w = jnp.exp(sc - m)
                W[c, r, h, :, piece] = w
                MR[c, 2 * r + h : 2 * r + h + 1, piece] = m
                l = jnp.sum(w, axis=0, keepdims=True)
                found[2 * h + half].append((m, l, jnp.sum(w * G[c, r, h, :, piece], axis=0, keepdims=True)))

        order = [(r, h) for r in range(NX) for h in range(2)]
        products(*order[0])
        for now, later in zip(order, order[1:] + [None]):
            if later is not None:
                products(*later)
            reduce(*now)
        for h in range(2):
            for half in range(2):
                top = found[2 * h + half][0][0]
                for m, _, _ in found[2 * h + half][1:]:
                    top = jnp.maximum(top, m)
                total = jnp.zeros_like(top)
                term = jnp.zeros_like(top)
                for m, l, tt in found[2 * h + half]:
                    a = jnp.exp(m - top)
                    total += a * l
                    term += a * tt
                row = 2 * half + h
                SM[c, row : row + 1, :] = top + jnp.log(total)
                SM[c, 4 + row : 5 + row, :] = term / total
        @pl.when(c == NC - 2)
        def _():
            send_stats(slice(0, NC - 1))

        @pl.when(c == NC - 1)
        def _():
            send_stats(slice(NC - 1, NC))

        @pl.when(c < NC - 2)
        def _():
            for part in range(2):
                for one in (3, 4):
                    arrived(part, 2 * c + one)

                    @pl.when(c < NC - 3)
                    def _():
                        hop(part, 2 * c + one, 2 * c + one + 2).start()

                @pl.when(c == NC - 3)
                def _():
                    last_hop(part).start()

        @pl.when(c == NC - 2)
        def _():
            for part in range(2):
                arrived(part, NZ - 1)

        return 0

    lax.fori_loop(0, NC, pass1, 0)

    for d in range(1, NZ):
        remote(SM, SR.at[d], ds_.at[d], dr.at[d], zpeer(d)).wait_recv()

    def combine(p):
        parts, terms = [], []
        for d in range(NZ):
            theirs = POS[(REL[p] - d) % NZ]
            ref = SM if d == 0 else SR.at[d]
            row = 2 * (theirs % 2)
            parts.append(ref[theirs // 2, row : row + 2, :])
            terms.append(ref[theirs // 2, 4 + row : 6 + row, :])
        top = parts[0]
        for part in parts[1:]:
            top = jnp.maximum(top, part)
        total = jnp.zeros_like(top)
        term = jnp.zeros_like(top)
        for part, other in zip(parts, terms):
            weight = jnp.exp(part - top)
            total += weight
            term += weight * other
        CF[:, p * TOK : (p + 1) * TOK] = top + jnp.log(total)
        RT[:, p * TOK : (p + 1) * TOK] = term / total

    for p in range(NZ):
        combine(p)

    def make(c, r):
        piece = slice(c * CH, (c + 1) * CH)
        for h in range(2):
            cf = jnp.exp(MR[c, 2 * r + h : 2 * r + h + 1, :] - CF[h : h + 1, piece])
            term = RT[h : h + 1, piece]
            for lo in range(0, F, 64):
                rows = slice(lo, lo + 64)
                p = W[c, r, h, rows, :] * cf
                PS[c, r, rows, h * CH : (h + 1) * CH] = p.astype(BF16)
                GS[c, r, rows, h * CH : (h + 1) * CH] = (p * (G[c, r, h, rows, :] - term)).astype(BF16)

    def use(c, r):
        first = c == NC - 1
        dv = jnp.dot(PS[c, r], G2[c], preferred_element_type=F32)
        dk = jnp.dot(GS[c, r], Q2[c], preferred_element_type=F32)
        DV[r] = dv if first else DV[r] + dv
        DK[r] = dk if first else DK[r] + dk
        dq = jnp.dot(KT[r, :, 0:F], GS[c, r, :, 0:CH], preferred_element_type=F32)
        dq += jnp.dot(KT[r, :, F : 2 * F], GS[c, r, :, CH : 2 * CH], preferred_element_type=F32)
        DQT[c] = dq if r == ORDER[0] else DQT[c] + dq

    def send_dq(p):
        d = REL[p]
        for i in range(NT):
            if p > 0 or i > 0:
                there = lax.rem(t + i, NT)
                remote(
                    DQS.at[p, there], DQR.at[(NZ - d) % NZ, t],
                    es.at[d] if d else gs.at[i], er.at[(NZ - d) % NZ] if d else gr.at[i],
                    (there, x * NZ + lax.rem(z + d, NZ)),
                ).start()

    def done_dq(c):
        DQS[2 * c : 2 * c + 2] = DQT[c].T.astype(BF16).reshape(2, NT, R, COLS)
        send_dq(2 * c + 1)
        send_dq(2 * c)

    def kv_send(part, src, dst, step):
        return remote(DKVS.at[src, part], DKVR.at[dst, part], fs.at[part, src], fr.at[part, dst], xpeer(step))

    def done_kv(r):
        for part, ref in enumerate((DK, DV)):
            total = ref[r]
            step = r
            if r == NX // 2:
                step = (1, NX - 1)[part]
                dst = NX // 2
            else:
                dst = NX - r
                if (r == 1) == (part == 0):
                    kv_send(part, r, NX // 2, 1).wait_recv()
                    total += DKVR[NX // 2, part].astype(F32)
            DKVS[r, part] = total.astype(BF16)
            sent.append(kv_send(part, r, dst, step))
            sent[-1].start()

    ORDER = [NX // 2] + [i for i in range(1, NX) if i != NX // 2] + [0]
    steps = [(c, r) for c in range(NC - 1, 1, -1) for r in ORDER] + [(c, r) for r in ORDER for c in (1, 0)]
    make(*steps[0])
    for (c, r), later in zip(steps, steps[1:] + [None]):
        if later is not None:
            make(*later)
        use(c, r)
        if r == ORDER[-1]:
            done_dq(c)
        if c == 0 and r > 0:
            done_kv(r)
    DQR[0, pl.ds(t, 1)] = DQS[0, pl.ds(t, 1)]

    dk, dv = DK[0], DV[0]
    for d in (1, NX - 1):
        for part in range(2):
            kv_send(part, d, d, 1).wait_recv()
        dk += DKVR[d, 0].astype(F32)
        dv += DKVR[d, 1].astype(F32)
    dk_out[...] = dk * SCALE
    dv_out[...] = dv

    for d in range(1, NT):
        source = lax.rem(t + NT - d, NT)
        remote(DQS.at[0, 0], DQR.at[0, source], gs.at[d], gr.at[d], tpeer(d)).wait_recv()
    for d in range(1, NZ):
        remote(DQS.at[POS[d]], DQR.at[d], es.at[d], er.at[d], zpeer(d)).wait_recv()
    for i in range(NT):
        dq = DQR[0, i].astype(F32)
        for d in range(1, NZ):
            dq += DQR[d, i].astype(F32)
        dq_out[:, i * COLS : (i + 1) * COLS] = dq
    for copy in sent:
        copy.wait_send()
    for part in range(2):
        for dest in range(3, NZ - 1):
            hop(part, dest - 2, dest).wait_send()
        last_hop(part).wait_send()
    for d in range(1, NT):
        remote(DQS.at[0, 0], DQR.at[0, 0], gs.at[d], gr.at[d], tpeer(d)).wait_send()
    for d in range(1, NZ):
        remote(DQS.at[POS[d]], DQR.at[d], es.at[d], er.at[d], zpeer(d)).wait_send()
    for d in range(1, NZ):
        remote(SM, SR.at[NZ - d], ds_.at[d], dr.at[NZ - d], zpeer(d)).wait_send()


def body(queries, keys, values, grad_out, read_len, *, NT):
    R, D = queries.shape
    F = keys.shape[0]
    TOK, CH, NC = NT * R, 2 * NT * R, NZ // 2
    lens = read_len.reshape(NX, NZ * R)
    hbm = pl.BlockSpec(memory_space=pltpu.HBM)
    vmem = pl.BlockSpec(memory_space=pltpu.VMEM)
    dma = pltpu.SemaphoreType.DMA
    V = pltpu.VMEM
    return pl.pallas_call(
        lambda *refs: kernel(NT, *refs),
        out_shape=(V((R, D), F32), V((F, COLS), F32), V((F, COLS), F32)),
        in_specs=[hbm] * 5,
        out_specs=(vmem, vmem, vmem),
        scratch_shapes=[
            V((NX, NZ * R), jnp.int32),
            V((R, D), BF16),
            V((R, D), BF16),
            V((NT, 2, R, COLS), BF16),
            V((NZ, 2, NT, R, COLS), BF16),
            V((NX, 2, F, COLS), BF16),
            V((NT, 8, COLS), F32),
            V((8, COLS), F32),
            V((NZ, COLS, TOK), BF16),
            V((NX, 2 * F, 2 * COLS), BF16),
            V((NX, 2 * F, COLS), BF16),
            V((NX, COLS, 2 * F), BF16),
            V((NC, NX, 2, F, CH), F32),
            V((NC, NX, 2, F, CH), F32),
            V((NC, 2 * NX, CH), F32),
            V((NC, 8, TOK), F32),
            V((NZ, NC, 8, TOK), F32),
            V((2, NZ * TOK), F32),
            V((2, NZ * TOK), F32),
            V((NC, NX, F, 2 * CH), BF16),
            V((NC, NX, F, 2 * CH), BF16),
            V((NC, 2 * CH, COLS), BF16),
            V((NC, 2 * CH, COLS), BF16),
            V((NC, COLS, CH), F32),
            V((NZ, NT, R, COLS), BF16),
            V((NZ, NT, R, COLS), BF16),
            V((NX, F, COLS), F32),
            V((NX, F, COLS), F32),
            V((NX, 2, F, COLS), BF16),
            V((NX, 2, F, COLS), BF16),
            dma((5,)),
            dma((2, NT)), dma((2, NT)),
            dma((2, NZ)), dma((2, NZ)),
            dma((2, NX)), dma((2, NX)),
            dma((NZ,)), dma((NZ,)),
            dma((NZ,)), dma((NZ,)),
            dma((2, NX)), dma((2, NX)),
            dma((NT,)), dma((NT,)),
        ],
        compiler_params=pltpu.CompilerParams(
            collective_id=0, has_side_effects=True, vmem_limit_bytes=62 * 1024 * 1024
        ),
    )(queries, keys, values, grad_out, lens)


def solution(mesh):
    NT = mesh.shape["tgt"]
    return jax.shard_map(
        lambda *args: body(*args, NT=NT),
        mesh=mesh,
        in_specs=(
            P(("tgt", "src"), None),
            P("src", None),
            P("src", None),
            P(("tgt", "src"), None),
            P("tgt"),
        ),
        out_specs=(P(("tgt", "src"), None), P("src", "tgt"), P("src", "tgt")),
        check_vma=False,
    )
```

```python
import jax
import jax.numpy as jnp
from jax import lax
from jax.experimental import pallas as pl
from jax.experimental.pallas import tpu as pltpu
from jax.sharding import PartitionSpec as P

MESH = pl.DeviceIdType.MESH
NX, NZ = 4, 8
COLS = 128
MASK_BLOCK = 128
F32, BF16 = jnp.float32, jnp.bfloat16
HIDDEN = -1e30
SCALE = 0.125

REL = [0]
for _d in range(1, NZ // 2 + 1):
    REL += [_d] if 2 * _d == NZ else [_d, NZ - _d]
POS = {d: p for p, d in enumerate(REL)}


def kernel(
    NT, q_hbm, k_hbm, v_hbm, g_hbm, len_hbm, dq_out, dk_out, dv_out,
    len_ref, QI, GI, QGI, QG, KV, L, lrow, M, K2, V2, KT, W, G, MR, SM, SR, CF, RT, PS, GS, Q2, G2, DQT, DQS, DQR, DK, DV, DKVS, DKVR,
    lsem, as_, ar, bs, br, cs, cr, ds_, dr, es, er, fs, fr, gs, gr,
):
    t = lax.axis_index("tgt")
    s = lax.axis_index("src")
    x = s // NZ
    z = s % NZ
    R, F = q_hbm.shape[0], k_hbm.shape[0]
    TOK = NT * R
    CH = 2 * TOK
    NC = NZ // 2

    def tpeer(d):
        return (lax.rem(t + d, NT), s)

    def zpeer(d):
        return (t, x * NZ + lax.rem(z + NZ + d, NZ))

    def diagonal(i, d):
        return (lax.rem(t + i, NT), x * NZ + lax.rem(z + NZ + d, NZ))

    def xpeer(d):
        return (t, lax.rem(x + d, NX) * NZ + z)

    def cols(i):
        return pl.ds(pl.multiple_of(i * COLS, COLS), COLS)

    def remote(src, dst, ssem, rsem, dev):
        return pltpu.make_async_remote_copy(
            src_ref=src, dst_ref=dst, send_sem=ssem, recv_sem=rsem, device_id=dev, device_id_type=MESH
        )

    local = [
        pltpu.make_async_copy(q_hbm, QI, lsem.at[0]),
        pltpu.make_async_copy(g_hbm, GI, lsem.at[1]),
        pltpu.make_async_copy(k_hbm.at[:, cols(t)], KV.at[0, 0], lsem.at[2]),
        pltpu.make_async_copy(v_hbm.at[:, cols(t)], KV.at[0, 1], lsem.at[3]),
        pltpu.make_async_copy(len_hbm, len_ref, lsem.at[4]),
    ]
    for copy in local:
        copy.start()
    barrier = pltpu.get_barrier_semaphore()
    peers = [tpeer(d) for d in range(1, NT)] + [diagonal(i, d) for i in range(1, NT) for d in (1, -1)]
    peers += [zpeer(d) for d in range(1, NZ)] + [xpeer(d) for d in range(1, NX)]
    for dev in peers:
        pl.semaphore_signal(barrier, inc=1, device_id=dev, device_id_type=MESH)
    pl.semaphore_wait(barrier, len(peers))

    for copy in local:
        copy.wait()
    row = len_ref[pl.ds(x, 1), :].astype(F32)
    lrow[...] = jnp.broadcast_to(row, lrow.shape)
    L[pl.ds(t, 1)] = jnp.broadcast_to(row[None], (1,) + lrow.shape)
    sent = []
    for i in range(NT):
        QGI[i, 0] = QI[:, i * COLS : (i + 1) * COLS]
        QGI[i, 1] = GI[:, i * COLS : (i + 1) * COLS]
    for i in range(NT):
        for slot, d in ((2, 1), (1, -1)):
            remote(QGI.at[lax.rem(t + i, NT)], QG.at[slot, :, t], bs.at[0, slot], br.at[0, slot], diagonal(i, d)).start()
    for d in range(1, NX):
        for part in range(2):
            sent.append(remote(KV.at[0, part], KV.at[NX - d, part], cs.at[part, d], cr.at[part, NX - d], xpeer(d)))
    for d in range(1, NT):
        sent.append(remote(lrow, L.at[t], as_.at[1, d], ar.at[1, d], tpeer(d)))
    for d in range(1, NT):
        sent.append(remote(QGI.at[lax.rem(t + d, NT)], QG.at[0, :, t], as_.at[0, d], ar.at[0, d], tpeer(d)))
    for copy in sent:
        copy.start()
    for part in range(2):
        QG[0, part, pl.ds(t, 1)] = QGI[pl.ds(t, 1), part]

    def hop(part, slot, dest):
        dev = zpeer(1 - 2 * (dest % 2)) if isinstance(dest, int) else zpeer(1 - 2 * lax.rem(dest, 2))
        return remote(QG.at[slot, part], QG.at[dest, part], bs.at[part, dest], br.at[part, dest], dev)

    def arrived(part, slot):
        remote(QG.at[0, part], QG.at[slot, part], bs.at[part, 3], br.at[part, slot], zpeer(1)).wait_recv()

    def last_hop(part):
        dev = zpeer(1) if part == 0 else zpeer(-1)
        slot = NZ - 2 - part
        return remote(QG.at[slot, part], QG.at[NZ - 1, part], bs.at[part, NZ - 1], br.at[part, NZ - 1], dev)

    lane2 = lax.broadcasted_iota(jnp.int32, (1, COLS), 1)
    head = [(lane2 < COLS // 2).astype(F32), (lane2 >= COLS // 2).astype(F32)]
    rows2 = lax.broadcasted_iota(jnp.int32, (F, COLS), 0)
    lanes2 = lax.broadcasted_iota(jnp.int32, (F, COLS), 1)
    per = F // MASK_BLOCK

    def build(r):
        kb = KV[r, 0].astype(F32)
        vb = KV[r, 1].astype(F32)
        hot = (lanes2 == rows2 // MASK_BLOCK + per * r).astype(F32).astype(BF16)
        for h in range(2):
            kh = kb * (head[h] * SCALE)
            K2[r, h * F : (h + 1) * F, 0:COLS] = kh.astype(BF16)
            K2[r, h * F : (h + 1) * F, COLS : 2 * COLS] = hot
            V2[r, h * F : (h + 1) * F, :] = (vb * head[h]).astype(BF16)
            KT[r, :, h * F : (h + 1) * F] = kh.T.astype(BF16)

    build(0)
    for slot in (1, 2):
        remote(QG.at[0], QG.at[slot], bs.at[0, slot], br.at[0, slot], zpeer(1)).wait_recv()
        for part in range(2):
            hop(part, slot, slot + 2).start()

    for d in range(1, NT):
        source = lax.rem(t + NT - d, NT)
        remote(lrow, L.at[source], as_.at[1, d], ar.at[1, d], tpeer(d)).wait_recv()
    lane3 = lax.broadcasted_iota(jnp.int32, (NT, R, COLS), 2)
    row3 = lax.broadcasted_iota(jnp.int32, (NT, R, COLS), 1)
    lens = jnp.broadcast_to(L[:, 0:1, :], (NT, R, COLS))
    lanes = lax.broadcasted_iota(jnp.int32, (1, 1, COLS), 2)
    first = ((lax.rem(x + lanes // per, NX) * NZ + z) * per + lax.rem(lanes, per)) * MASK_BLOCK
    first = jnp.where(lanes < per * NX, first, -1).astype(F32)

    def mask_slot(p, rel):
        pick = lax.rem(z + rel, NZ) * R + row3
        column = jnp.sum(jnp.where(lane3 == pick, lens, 0.0), axis=2, keepdims=True)
        M[p] = jnp.where(first >= column, HIDDEN, 0.0).reshape(TOK, COLS).T.astype(BF16)

    for p in range(NZ):
        mask_slot(p, REL[p])

    for r in range(1, NX):
        for part in range(2):
            remote(KV.at[0, part], KV.at[r, part], cs.at[part, r], cr.at[part, r], xpeer(r)).wait_recv()
        build(r)
    for d in range(1, NT):
        source = lax.rem(t + NT - d, NT)
        remote(QGI.at[0], QG.at[0, :, source], as_.at[0, d], ar.at[0, d], tpeer(d)).wait_recv()

    masks = [m.astype(BF16) for m in head]

    def block(ref, c, which):
        return ref[pl.ds(2 * c, 2), which].reshape(CH, COLS)

    def pass1(c, _):
        qt = jnp.concatenate([block(QG, c, 0).T, jnp.concatenate([M[2 * c], M[2 * c + 1]], axis=1)], axis=0)
        gt = block(QG, c, 1).T
        for h in range(2):
            rows = slice(h * CH, (h + 1) * CH)
            Q2[c, rows] = block(QG, c, 0) * masks[h]
            G2[c, rows] = block(QG, c, 1) * masks[h]
        found = [[] for _ in range(4)]

        def products(r, h):
            rows = slice(h * F, (h + 1) * F)
            W[c, r, h] = jnp.dot(K2[r, rows], qt, preferred_element_type=F32)
            G[c, r, h] = jnp.dot(V2[r, rows], gt, preferred_element_type=F32)

        def reduce(r, h):
            for half in range(2):
                piece = slice(half * TOK, (half + 1) * TOK)
                sc = W[c, r, h, :, piece]
                m = jnp.max(sc, axis=0, keepdims=True)
                w = jnp.exp(sc - m)
                W[c, r, h, :, piece] = w
                MR[c, 2 * r + h : 2 * r + h + 1, piece] = m
                l = jnp.sum(w, axis=0, keepdims=True)
                found[2 * h + half].append((m, l, jnp.sum(w * G[c, r, h, :, piece], axis=0, keepdims=True)))

        order = [(r, h) for r in range(NX) for h in range(2)]
        products(*order[0])
        for now, later in zip(order, order[1:] + [None]):
            if later is not None:
                products(*later)
            reduce(*now)
        for h in range(2):
            for half in range(2):
                top = found[2 * h + half][0][0]
                for m, _, _ in found[2 * h + half][1:]:
                    top = jnp.maximum(top, m)
                total = jnp.zeros_like(top)
                term = jnp.zeros_like(top)
                for m, l, tt in found[2 * h + half]:
                    a = jnp.exp(m - top)
                    total += a * l
                    term += a * tt
                row = 2 * half + h
                SM[c, row : row + 1, :] = top + jnp.log(total)
                SM[c, 4 + row : 5 + row, :] = term / total
        for d in REL[1:]:
            remote(SM.at[c], SR.at[NZ - d, c], ds_.at[d], dr.at[NZ - d], zpeer(d)).start()

        @pl.when(c < NC - 2)
        def _():
            for part in range(2):
                for one in (3, 4):
                    arrived(part, 2 * c + one)

                    @pl.when(c < NC - 3)
                    def _():
                        hop(part, 2 * c + one, 2 * c + one + 2).start()

                @pl.when(c == NC - 3)
                def _():
                    last_hop(part).start()

        @pl.when(c == NC - 2)
        def _():
            for part in range(2):
                arrived(part, NZ - 1)

        return 0

    lax.fori_loop(0, NC, pass1, 0)

    for d in range(1, NZ):
        remote(SM, SR.at[d], ds_.at[d], dr.at[d], zpeer(d)).wait_recv()

    def combine(p):
        parts, terms = [], []
        for d in range(NZ):
            theirs = POS[(REL[p] - d) % NZ]
            ref = SM if d == 0 else SR.at[d]
            row = 2 * (theirs % 2)
            parts.append(ref[theirs // 2, row : row + 2, :])
            terms.append(ref[theirs // 2, 4 + row : 6 + row, :])
        top = parts[0]
        for part in parts[1:]:
            top = jnp.maximum(top, part)
        total = jnp.zeros_like(top)
        term = jnp.zeros_like(top)
        for part, other in zip(parts, terms):
            weight = jnp.exp(part - top)
            total += weight
            term += weight * other
        CF[:, p * TOK : (p + 1) * TOK] = top + jnp.log(total)
        RT[:, p * TOK : (p + 1) * TOK] = term / total

    for p in range(NZ):
        combine(p)

    def make(c, r):
        piece = slice(c * CH, (c + 1) * CH)
        for h in range(2):
            cf = jnp.exp(MR[c, 2 * r + h : 2 * r + h + 1, :] - CF[h : h + 1, piece])
            term = RT[h : h + 1, piece]
            for lo in range(0, F, 64):
                rows = slice(lo, lo + 64)
                p = W[c, r, h, rows, :] * cf
                PS[c, r, rows, h * CH : (h + 1) * CH] = p.astype(BF16)
                GS[c, r, rows, h * CH : (h + 1) * CH] = (p * (G[c, r, h, rows, :] - term)).astype(BF16)

    def use(c, r):
        first = c == NC - 1
        dv = jnp.dot(PS[c, r], G2[c], preferred_element_type=F32)
        dk = jnp.dot(GS[c, r], Q2[c], preferred_element_type=F32)
        DV[r] = dv if first else DV[r] + dv
        DK[r] = dk if first else DK[r] + dk
        dq = jnp.dot(KT[r, :, 0:F], GS[c, r, :, 0:CH], preferred_element_type=F32)
        dq += jnp.dot(KT[r, :, F : 2 * F], GS[c, r, :, CH : 2 * CH], preferred_element_type=F32)
        DQT[c] = dq if r == ORDER[0] else DQT[c] + dq

    def send_dq(p):
        d = REL[p]
        for i in range(NT):
            if p > 0 or i > 0:
                there = lax.rem(t + i, NT)
                remote(
                    DQS.at[p, there], DQR.at[(NZ - d) % NZ, t],
                    es.at[d] if d else gs.at[i], er.at[(NZ - d) % NZ] if d else gr.at[i],
                    (there, x * NZ + lax.rem(z + d, NZ)),
                ).start()

    def done_dq(c):
        DQS[2 * c : 2 * c + 2] = DQT[c].T.astype(BF16).reshape(2, NT, R, COLS)
        send_dq(2 * c + 1)
        send_dq(2 * c)

    def done_kv(r):
        DKVS[r, 0] = DK[r].astype(BF16)
        DKVS[r, 1] = DV[r].astype(BF16)
        sent.append(remote(DKVS.at[r], DKVR.at[NX - r], fs.at[r], fr.at[NX - r], xpeer(r)))
        sent[-1].start()

    ORDER = [NX // 2] + [i for i in range(1, NX) if i != NX // 2] + [0]
    steps = [(c, r) for c in range(NC - 1, 1, -1) for r in ORDER] + [(c, r) for r in ORDER for c in (1, 0)]
    make(*steps[0])
    for (c, r), later in zip(steps, steps[1:] + [None]):
        if later is not None:
            make(*later)
        use(c, r)
        if r == ORDER[-1]:
            done_dq(c)
        if c == 0 and r > 0:
            done_kv(r)
    DQR[0, pl.ds(t, 1)] = DQS[0, pl.ds(t, 1)]

    for d in range(1, NX):
        remote(DKVS.at[d], DKVR.at[d], fs.at[d], fr.at[d], xpeer(d)).wait_recv()
    dk, dv = DK[0], DV[0]
    for d in range(1, NX):
        dk += DKVR[d, 0].astype(F32)
        dv += DKVR[d, 1].astype(F32)
    dk_out[...] = dk * SCALE
    dv_out[...] = dv

    for d in range(1, NT):
        source = lax.rem(t + NT - d, NT)
        remote(DQS.at[0, 0], DQR.at[0, source], gs.at[d], gr.at[d], tpeer(d)).wait_recv()
    for d in range(1, NZ):
        remote(DQS.at[POS[d]], DQR.at[d], es.at[d], er.at[d], zpeer(d)).wait_recv()
    for i in range(NT):
        dq = DQR[0, i].astype(F32)
        for d in range(1, NZ):
            dq += DQR[d, i].astype(F32)
        dq_out[:, i * COLS : (i + 1) * COLS] = dq
    for copy in sent:
        copy.wait_send()
    for slot in (1, 2):
        remote(QGI, QG.at[slot], bs.at[0, slot], br.at[0, slot], zpeer(1)).wait_send()
    for part in range(2):
        for dest in range(3, NZ - 1):
            hop(part, dest - 2, dest).wait_send()
        last_hop(part).wait_send()
    for d in range(1, NT):
        remote(DQS.at[0, 0], DQR.at[0, 0], gs.at[d], gr.at[d], tpeer(d)).wait_send()
    for d in range(1, NZ):
        remote(DQS.at[POS[d]], DQR.at[d], es.at[d], er.at[d], zpeer(d)).wait_send()
    for d in range(1, NZ):
        remote(SM, SR.at[NZ - d], ds_.at[d], dr.at[NZ - d], zpeer(d)).wait_send()


def body(queries, keys, values, grad_out, read_len, *, NT):
    R, D = queries.shape
    F = keys.shape[0]
    TOK, CH, NC = NT * R, 2 * NT * R, NZ // 2
    lens = read_len.reshape(NX, NZ * R)
    hbm = pl.BlockSpec(memory_space=pltpu.HBM)
    vmem = pl.BlockSpec(memory_space=pltpu.VMEM)
    dma = pltpu.SemaphoreType.DMA
    V = pltpu.VMEM
    return pl.pallas_call(
        lambda *refs: kernel(NT, *refs),
        out_shape=(V((R, D), F32), V((F, COLS), F32), V((F, COLS), F32)),
        in_specs=[hbm] * 5,
        out_specs=(vmem, vmem, vmem),
        scratch_shapes=[
            V((NX, NZ * R), jnp.int32),
            V((R, D), BF16),
            V((R, D), BF16),
            V((NT, 2, R, COLS), BF16),
            V((NZ, 2, NT, R, COLS), BF16),
            V((NX, 2, F, COLS), BF16),
            V((NT, 8, COLS), F32),
            V((8, COLS), F32),
            V((NZ, COLS, TOK), BF16),
            V((NX, 2 * F, 2 * COLS), BF16),
            V((NX, 2 * F, COLS), BF16),
            V((NX, COLS, 2 * F), BF16),
            V((NC, NX, 2, F, CH), F32),
            V((NC, NX, 2, F, CH), F32),
            V((NC, 2 * NX, CH), F32),
            V((NC, 8, TOK), F32),
            V((NZ, NC, 8, TOK), F32),
            V((2, NZ * TOK), F32),
            V((2, NZ * TOK), F32),
            V((NC, NX, F, 2 * CH), BF16),
            V((NC, NX, F, 2 * CH), BF16),
            V((NC, 2 * CH, COLS), BF16),
            V((NC, 2 * CH, COLS), BF16),
            V((NC, COLS, CH), F32),
            V((NZ, NT, R, COLS), BF16),
            V((NZ, NT, R, COLS), BF16),
            V((NX, F, COLS), F32),
            V((NX, F, COLS), F32),
            V((NX, 2, F, COLS), BF16),
            V((NX, 2, F, COLS), BF16),
            dma((5,)),
            dma((2, NT)), dma((2, NT)),
            dma((2, NZ)), dma((2, NZ)),
            dma((2, NX)), dma((2, NX)),
            dma((NZ,)), dma((NZ,)),
            dma((NZ,)), dma((NZ,)),
            dma((NX,)), dma((NX,)),
            dma((NT,)), dma((NT,)),
        ],
        compiler_params=pltpu.CompilerParams(
            collective_id=0, has_side_effects=True, vmem_limit_bytes=62 * 1024 * 1024
        ),
    )(queries, keys, values, grad_out, lens)


def solution(mesh):
    NT = mesh.shape["tgt"]
    return jax.shard_map(
        lambda *args: body(*args, NT=NT),
        mesh=mesh,
        in_specs=(
            P(("tgt", "src"), None),
            P("src", None),
            P("src", None),
            P(("tgt", "src"), None),
            P("tgt"),
        ),
        out_specs=(P(("tgt", "src"), None), P("src", "tgt"), P("src", "tgt")),
        check_vma=False,
    )
```

```python
import jax
import jax.numpy as jnp
from jax import lax
from jax.experimental import pallas as pl
from jax.experimental.pallas import tpu as pltpu
from jax.sharding import PartitionSpec as P

MESH = pl.DeviceIdType.MESH
NX, NZ = 4, 8
COLS = 128
MASK_BLOCK = 128
F32, BF16 = jnp.float32, jnp.bfloat16
HIDDEN = -1e30
SCALE = 0.125

REL = [0]
for _d in range(1, NZ // 2 + 1):
    REL += [_d] if 2 * _d == NZ else [_d, NZ - _d]
POS = {d: p for p, d in enumerate(REL)}


def kernel(
    NT, q_hbm, k_hbm, v_hbm, g_hbm, len_hbm, dq_out, dk_out, dv_out,
    len_ref, QI, GI, QGI, QG, KV, L, lrow, M, K2, V2, KT, W, G, MR, SM, SR, CF, RT, PS, GS, Q2, G2, DQT, DQS, DQR, DK, DV, DKVS, DKVR,
    lsem, as_, ar, bs, br, cs, cr, ds_, dr, es, er, fs, fr, gs, gr,
):
    t = lax.axis_index("tgt")
    s = lax.axis_index("src")
    x = s // NZ
    z = s % NZ
    R, F = q_hbm.shape[0], k_hbm.shape[0]
    TOK = NT * R
    CH = 2 * TOK
    NC = NZ // 2

    def tpeer(d):
        return (lax.rem(t + d, NT), s)

    def zpeer(d):
        return (t, x * NZ + lax.rem(z + NZ + d, NZ))

    def diagonal(i, d):
        return (lax.rem(t + i, NT), x * NZ + lax.rem(z + NZ + d, NZ))

    def xpeer(d):
        return (t, lax.rem(x + d, NX) * NZ + z)

    def cols(i):
        return pl.ds(pl.multiple_of(i * COLS, COLS), COLS)

    def remote(src, dst, ssem, rsem, dev):
        return pltpu.make_async_remote_copy(
            src_ref=src, dst_ref=dst, send_sem=ssem, recv_sem=rsem, device_id=dev, device_id_type=MESH
        )

    local = [
        pltpu.make_async_copy(q_hbm, QI, lsem.at[0]),
        pltpu.make_async_copy(g_hbm, GI, lsem.at[1]),
        pltpu.make_async_copy(k_hbm.at[:, cols(t)], KV.at[0, 0], lsem.at[2]),
        pltpu.make_async_copy(v_hbm.at[:, cols(t)], KV.at[0, 1], lsem.at[3]),
        pltpu.make_async_copy(len_hbm, len_ref, lsem.at[4]),
    ]
    for copy in local:
        copy.start()
    barrier = pltpu.get_barrier_semaphore()
    peers = [tpeer(d) for d in range(1, NT)] + [diagonal(i, d) for i in range(1, NT) for d in (1, -1, 2, -2)]
    peers += [zpeer(d) for d in range(1, NZ)] + [xpeer(d) for d in range(1, NX)]
    for dev in peers:
        pl.semaphore_signal(barrier, inc=1, device_id=dev, device_id_type=MESH)
    pl.semaphore_wait(barrier, len(peers))

    for copy in local:
        copy.wait()
    row = len_ref[pl.ds(x, 1), :].astype(F32)
    lrow[...] = jnp.broadcast_to(row, lrow.shape)
    L[pl.ds(t, 1)] = jnp.broadcast_to(row[None], (1,) + lrow.shape)
    sent = []
    for i in range(NT):
        QGI[i, 0] = QI[:, i * COLS : (i + 1) * COLS]
        QGI[i, 1] = GI[:, i * COLS : (i + 1) * COLS]
    def straight(slot, d):
        for i in range(NT):
            remote(QGI.at[lax.rem(t + i, NT)], QG.at[slot, :, t], bs.at[0, slot], br.at[0, slot], diagonal(i, d)).start()

    straight(2, 1)
    straight(1, -1)
    for d in range(1, NT):
        sent.append(remote(lrow, L.at[t], as_.at[1, d], ar.at[1, d], tpeer(d)))
    for d in range(1, NT):
        sent.append(remote(QGI.at[lax.rem(t + d, NT)], QG.at[0, :, t], as_.at[0, d], ar.at[0, d], tpeer(d)))
    for d in range(1, NX):
        for part in range(2):
            sent.append(remote(KV.at[0, part], KV.at[NX - d, part], cs.at[part, d], cr.at[part, NX - d], xpeer(d)))
    for copy in sent:
        copy.start()
    straight(4, 2)
    straight(3, -2)
    for part in range(2):
        QG[0, part, pl.ds(t, 1)] = QGI[pl.ds(t, 1), part]

    onward = [
        remote(QG.at[4], QG.at[6], bs.at[0, 6], br.at[0, 6], zpeer(1)),
        remote(QG.at[3], QG.at[5], bs.at[0, 5], br.at[0, 5], zpeer(-1)),
        remote(QG.at[4, 1], QG.at[7, 1], bs.at[1, 7], br.at[1, 7], zpeer(2)),
        remote(QG.at[3, 0], QG.at[7, 0], bs.at[0, 7], br.at[0, 7], zpeer(-2)),
    ]

    def arrived(slot):
        remote(QG.at[0], QG.at[slot], bs.at[0, 3], br.at[0, slot], zpeer(1)).wait_recv()

    lane2 = lax.broadcasted_iota(jnp.int32, (1, COLS), 1)
    head = [(lane2 < COLS // 2).astype(F32), (lane2 >= COLS // 2).astype(F32)]
    rows2 = lax.broadcasted_iota(jnp.int32, (F, COLS), 0)
    lanes2 = lax.broadcasted_iota(jnp.int32, (F, COLS), 1)
    per = F // MASK_BLOCK

    def build(r):
        kb = KV[r, 0].astype(F32)
        vb = KV[r, 1].astype(F32)
        hot = (lanes2 == rows2 // MASK_BLOCK + per * r).astype(F32).astype(BF16)
        for h in range(2):
            kh = kb * (head[h] * SCALE)
            K2[r, h * F : (h + 1) * F, 0:COLS] = kh.astype(BF16)
            K2[r, h * F : (h + 1) * F, COLS : 2 * COLS] = hot
            V2[r, h * F : (h + 1) * F, :] = (vb * head[h]).astype(BF16)
            KT[r, :, h * F : (h + 1) * F] = kh.T.astype(BF16)

    build(0)
    for d in range(1, NT):
        source = lax.rem(t + NT - d, NT)
        remote(lrow, L.at[source], as_.at[1, d], ar.at[1, d], tpeer(d)).wait_recv()
    lane3 = lax.broadcasted_iota(jnp.int32, (NT, R, COLS), 2)
    row3 = lax.broadcasted_iota(jnp.int32, (NT, R, COLS), 1)
    lens = jnp.broadcast_to(L[:, 0:1, :], (NT, R, COLS))
    lanes = lax.broadcasted_iota(jnp.int32, (1, 1, COLS), 2)
    first = ((lax.rem(x + lanes // per, NX) * NZ + z) * per + lax.rem(lanes, per)) * MASK_BLOCK
    first = jnp.where(lanes < per * NX, first, -1).astype(F32)

    def mask_slot(p, rel):
        pick = lax.rem(z + rel, NZ) * R + row3
        column = jnp.sum(jnp.where(lane3 == pick, lens, 0.0), axis=2, keepdims=True)
        M[p] = jnp.where(first >= column, HIDDEN, 0.0).reshape(TOK, COLS).T.astype(BF16)

    for p in range(NZ):
        mask_slot(p, REL[p])

    for r in range(1, NX):
        for part in range(2):
            remote(KV.at[0, part], KV.at[r, part], cs.at[part, r], cr.at[part, r], xpeer(r)).wait_recv()
        build(r)
    for d in range(1, NT):
        source = lax.rem(t + NT - d, NT)
        remote(QGI.at[0], QG.at[0, :, source], as_.at[0, d], ar.at[0, d], tpeer(d)).wait_recv()

    arrived(1)

    masks = [m.astype(BF16) for m in head]

    def block(ref, c, which):
        return ref[pl.ds(2 * c, 2), which].reshape(CH, COLS)

    def pass1(c, _):
        qt = jnp.concatenate([block(QG, c, 0).T, jnp.concatenate([M[2 * c], M[2 * c + 1]], axis=1)], axis=0)
        gt = block(QG, c, 1).T
        for h in range(2):
            rows = slice(h * CH, (h + 1) * CH)
            Q2[c, rows] = block(QG, c, 0) * masks[h]
            G2[c, rows] = block(QG, c, 1) * masks[h]
        found = [[] for _ in range(4)]

        def products(r, h):
            rows = slice(h * F, (h + 1) * F)
            W[c, r, h] = jnp.dot(K2[r, rows], qt, preferred_element_type=F32)
            G[c, r, h] = jnp.dot(V2[r, rows], gt, preferred_element_type=F32)

        def reduce(r, h):
            for half in range(2):
                piece = slice(half * TOK, (half + 1) * TOK)
                sc = W[c, r, h, :, piece]
                m = jnp.max(sc, axis=0, keepdims=True)
                w = jnp.exp(sc - m)
                W[c, r, h, :, piece] = w
                MR[c, 2 * r + h : 2 * r + h + 1, piece] = m
                l = jnp.sum(w, axis=0, keepdims=True)
                found[2 * h + half].append((m, l, jnp.sum(w * G[c, r, h, :, piece], axis=0, keepdims=True)))

        order = [(r, h) for r in range(NX) for h in range(2)]
        products(*order[0])
        for now, later in zip(order, order[1:] + [None]):
            if later is not None:
                products(*later)
            reduce(*now)
        for h in range(2):
            for half in range(2):
                top = found[2 * h + half][0][0]
                for m, _, _ in found[2 * h + half][1:]:
                    top = jnp.maximum(top, m)
                total = jnp.zeros_like(top)
                term = jnp.zeros_like(top)
                for m, l, tt in found[2 * h + half]:
                    a = jnp.exp(m - top)
                    total += a * l
                    term += a * tt
                row = 2 * half + h
                SM[c, row : row + 1, :] = top + jnp.log(total)
                SM[c, 4 + row : 5 + row, :] = term / total
        for d in REL[1:]:
            remote(SM.at[c], SR.at[NZ - d, c], ds_.at[d], dr.at[NZ - d], zpeer(d)).start()

        @pl.when(c == 0)
        def _():
            arrived(2)
            arrived(3)
            arrived(4)
            for copy in onward:
                copy.start()

        @pl.when(c == 1)
        def _():
            arrived(5)

        @pl.when(c == 2)
        def _():
            arrived(6)
            for part in range(2):
                onward[3 - part].wait_recv()

        return 0

    lax.fori_loop(0, NC, pass1, 0)

    for d in range(1, NZ):
        remote(SM, SR.at[d], ds_.at[d], dr.at[d], zpeer(d)).wait_recv()

    def combine(p):
        parts, terms = [], []
        for d in range(NZ):
            theirs = POS[(REL[p] - d) % NZ]
            ref = SM if d == 0 else SR.at[d]
            row = 2 * (theirs % 2)
            parts.append(ref[theirs // 2, row : row + 2, :])
            terms.append(ref[theirs // 2, 4 + row : 6 + row, :])
        top = parts[0]
        for part in parts[1:]:
            top = jnp.maximum(top, part)
        total = jnp.zeros_like(top)
        term = jnp.zeros_like(top)
        for part, other in zip(parts, terms):
            weight = jnp.exp(part - top)
            total += weight
            term += weight * other
        CF[:, p * TOK : (p + 1) * TOK] = top + jnp.log(total)
        RT[:, p * TOK : (p + 1) * TOK] = term / total

    for p in range(NZ):
        combine(p)

    def make(c, r):
        piece = slice(c * CH, (c + 1) * CH)
        for h in range(2):
            cf = jnp.exp(MR[c, 2 * r + h : 2 * r + h + 1, :] - CF[h : h + 1, piece])
            term = RT[h : h + 1, piece]
            for lo in range(0, F, 64):
                rows = slice(lo, lo + 64)
                p = W[c, r, h, rows, :] * cf
                PS[c, r, rows, h * CH : (h + 1) * CH] = p.astype(BF16)
                GS[c, r, rows, h * CH : (h + 1) * CH] = (p * (G[c, r, h, rows, :] - term)).astype(BF16)

    def use(c, r):
        first = c == NC - 1
        dv = jnp.dot(PS[c, r], G2[c], preferred_element_type=F32)
        dk = jnp.dot(GS[c, r], Q2[c], preferred_element_type=F32)
        DV[r] = dv if first else DV[r] + dv
        DK[r] = dk if first else DK[r] + dk
        dq = jnp.dot(KT[r, :, 0:F], GS[c, r, :, 0:CH], preferred_element_type=F32)
        dq += jnp.dot(KT[r, :, F : 2 * F], GS[c, r, :, CH : 2 * CH], preferred_element_type=F32)
        DQT[c] = dq if r == ORDER[0] else DQT[c] + dq

    def send_dq(p):
        d = REL[p]
        for i in range(NT):
            if p > 0 or i > 0:
                there = lax.rem(t + i, NT)
                remote(
                    DQS.at[p, there], DQR.at[(NZ - d) % NZ, t],
                    es.at[d] if d else gs.at[i], er.at[(NZ - d) % NZ] if d else gr.at[i],
                    (there, x * NZ + lax.rem(z + d, NZ)),
                ).start()

    def done_dq(c):
        DQS[2 * c : 2 * c + 2] = DQT[c].T.astype(BF16).reshape(2, NT, R, COLS)
        send_dq(2 * c + 1)
        send_dq(2 * c)

    def done_kv(r):
        DKVS[r, 0] = DK[r].astype(BF16)
        DKVS[r, 1] = DV[r].astype(BF16)
        sent.append(remote(DKVS.at[r], DKVR.at[NX - r], fs.at[r], fr.at[NX - r], xpeer(r)))
        sent[-1].start()

    ORDER = [NX // 2] + [i for i in range(1, NX) if i != NX // 2] + [0]
    steps = [(c, r) for c in range(NC - 1, 1, -1) for r in ORDER] + [(c, r) for r in ORDER for c in (1, 0)]
    make(*steps[0])
    for (c, r), later in zip(steps, steps[1:] + [None]):
        if later is not None:
            make(*later)
        use(c, r)
        if r == ORDER[-1]:
            done_dq(c)
        if c == 0 and r > 0:
            done_kv(r)
    DQR[0, pl.ds(t, 1)] = DQS[0, pl.ds(t, 1)]

    for d in range(1, NX):
        remote(DKVS.at[d], DKVR.at[d], fs.at[d], fr.at[d], xpeer(d)).wait_recv()
    dk, dv = DK[0], DV[0]
    for d in range(1, NX):
        dk += DKVR[d, 0].astype(F32)
        dv += DKVR[d, 1].astype(F32)
    dk_out[...] = dk * SCALE
    dv_out[...] = dv

    for d in range(1, NT):
        source = lax.rem(t + NT - d, NT)
        remote(DQS.at[0, 0], DQR.at[0, source], gs.at[d], gr.at[d], tpeer(d)).wait_recv()
    for d in range(1, NZ):
        remote(DQS.at[POS[d]], DQR.at[d], es.at[d], er.at[d], zpeer(d)).wait_recv()
    for i in range(NT):
        dq = DQR[0, i].astype(F32)
        for d in range(1, NZ):
            dq += DQR[d, i].astype(F32)
        dq_out[:, i * COLS : (i + 1) * COLS] = dq
    for copy in sent:
        copy.wait_send()
    for slot in range(1, 5):
        remote(QGI, QG.at[slot], bs.at[0, slot], br.at[0, slot], zpeer(1)).wait_send()
    for copy in onward:
        copy.wait_send()
    for d in range(1, NT):
        remote(DQS.at[0, 0], DQR.at[0, 0], gs.at[d], gr.at[d], tpeer(d)).wait_send()
    for d in range(1, NZ):
        remote(DQS.at[POS[d]], DQR.at[d], es.at[d], er.at[d], zpeer(d)).wait_send()
    for d in range(1, NZ):
        remote(SM, SR.at[NZ - d], ds_.at[d], dr.at[NZ - d], zpeer(d)).wait_send()


def body(queries, keys, values, grad_out, read_len, *, NT):
    R, D = queries.shape
    F = keys.shape[0]
    TOK, CH, NC = NT * R, 2 * NT * R, NZ // 2
    lens = read_len.reshape(NX, NZ * R)
    hbm = pl.BlockSpec(memory_space=pltpu.HBM)
    vmem = pl.BlockSpec(memory_space=pltpu.VMEM)
    dma = pltpu.SemaphoreType.DMA
    V = pltpu.VMEM
    return pl.pallas_call(
        lambda *refs: kernel(NT, *refs),
        out_shape=(V((R, D), F32), V((F, COLS), F32), V((F, COLS), F32)),
        in_specs=[hbm] * 5,
        out_specs=(vmem, vmem, vmem),
        scratch_shapes=[
            V((NX, NZ * R), jnp.int32),
            V((R, D), BF16),
            V((R, D), BF16),
            V((NT, 2, R, COLS), BF16),
            V((NZ, 2, NT, R, COLS), BF16),
            V((NX, 2, F, COLS), BF16),
            V((NT, 8, COLS), F32),
            V((8, COLS), F32),
            V((NZ, COLS, TOK), BF16),
            V((NX, 2 * F, 2 * COLS), BF16),
            V((NX, 2 * F, COLS), BF16),
            V((NX, COLS, 2 * F), BF16),
            V((NC, NX, 2, F, CH), F32),
            V((NC, NX, 2, F, CH), F32),
            V((NC, 2 * NX, CH), F32),
            V((NC, 8, TOK), F32),
            V((NZ, NC, 8, TOK), F32),
            V((2, NZ * TOK), F32),
            V((2, NZ * TOK), F32),
            V((NC, NX, F, 2 * CH), BF16),
            V((NC, NX, F, 2 * CH), BF16),
            V((NC, 2 * CH, COLS), BF16),
            V((NC, 2 * CH, COLS), BF16),
            V((NC, COLS, CH), F32),
            V((NZ, NT, R, COLS), BF16),
            V((NZ, NT, R, COLS), BF16),
            V((NX, F, COLS), F32),
            V((NX, F, COLS), F32),
            V((NX, 2, F, COLS), BF16),
            V((NX, 2, F, COLS), BF16),
            dma((5,)),
            dma((2, NT)), dma((2, NT)),
            dma((2, NZ)), dma((2, NZ)),
            dma((2, NX)), dma((2, NX)),
            dma((NZ,)), dma((NZ,)),
            dma((NZ,)), dma((NZ,)),
            dma((NX,)), dma((NX,)),
            dma((NT,)), dma((NT,)),
        ],
        compiler_params=pltpu.CompilerParams(
            collective_id=0, has_side_effects=True, vmem_limit_bytes=62 * 1024 * 1024
        ),
    )(queries, keys, values, grad_out, lens)


def solution(mesh):
    NT = mesh.shape["tgt"]
    return jax.shard_map(
        lambda *args: body(*args, NT=NT),
        mesh=mesh,
        in_specs=(
            P(("tgt", "src"), None),
            P("src", None),
            P("src", None),
            P(("tgt", "src"), None),
            P("tgt"),
        ),
        out_specs=(P(("tgt", "src"), None), P("src", "tgt"), P("src", "tgt")),
        check_vma=False,
    )
```

```python
import jax
import jax.numpy as jnp
from jax import lax
from jax.experimental import pallas as pl
from jax.experimental.pallas import tpu as pltpu
from jax.sharding import PartitionSpec as P

MESH = pl.DeviceIdType.MESH
NX, NZ = 4, 8
COLS = 128
MASK_BLOCK = 128
F32, BF16 = jnp.float32, jnp.bfloat16
HIDDEN = -1e30
SCALE = 0.125

REL = [0]
for _d in range(1, NZ // 2 + 1):
    REL += [_d] if 2 * _d == NZ else [_d, NZ - _d]
POS = {d: p for p, d in enumerate(REL)}


def kernel(
    NT, q_hbm, k_hbm, v_hbm, g_hbm, len_hbm, dq_out, dk_out, dv_out,
    len_ref, QI, GI, QGI, QG, KV, L, lrow, M, K2, V2, KT, W, G, MR, SM, SR, CF, RT, PS, GS, Q2, G2, DQT, DQS, DQR, DK, DV, DKVS, DKVR,
    lsem, as_, ar, bs, br, cs, cr, ds_, dr, es, er, fs, fr, gs, gr,
):
    t = lax.axis_index("tgt")
    s = lax.axis_index("src")
    x = s // NZ
    z = s % NZ
    R, F = q_hbm.shape[0], k_hbm.shape[0]
    TOK = NT * R
    CH = 2 * TOK
    NC = NZ // 2

    def tpeer(d):
        return (lax.rem(t + d, NT), s)

    def zpeer(d):
        return (t, x * NZ + lax.rem(z + NZ + d, NZ))

    def diagonal(i, d):
        return (lax.rem(t + i, NT), x * NZ + lax.rem(z + NZ + d, NZ))

    def xpeer(d):
        return (t, lax.rem(x + d, NX) * NZ + z)

    def cols(i):
        return pl.ds(pl.multiple_of(i * COLS, COLS), COLS)

    def remote(src, dst, ssem, rsem, dev):
        return pltpu.make_async_remote_copy(
            src_ref=src, dst_ref=dst, send_sem=ssem, recv_sem=rsem, device_id=dev, device_id_type=MESH
        )

    local = [
        pltpu.make_async_copy(q_hbm, QI, lsem.at[0]),
        pltpu.make_async_copy(g_hbm, GI, lsem.at[1]),
        pltpu.make_async_copy(k_hbm.at[:, cols(t)], KV.at[0, 0], lsem.at[2]),
        pltpu.make_async_copy(v_hbm.at[:, cols(t)], KV.at[0, 1], lsem.at[3]),
        pltpu.make_async_copy(len_hbm, len_ref, lsem.at[4]),
    ]
    for copy in local:
        copy.start()
    barrier = pltpu.get_barrier_semaphore()
    peers = [tpeer(d) for d in range(1, NT)] + [diagonal(i, d) for i in range(1, NT) for d in (1, -1, 2, -2)]
    peers += [zpeer(d) for d in range(1, NZ)] + [xpeer(d) for d in range(1, NX)]
    for dev in peers:
        pl.semaphore_signal(barrier, inc=1, device_id=dev, device_id_type=MESH)
    pl.semaphore_wait(barrier, len(peers))

    for copy in local:
        copy.wait()
    row = len_ref[pl.ds(x, 1), :].astype(F32)
    lrow[...] = jnp.broadcast_to(row, lrow.shape)
    L[pl.ds(t, 1)] = jnp.broadcast_to(row[None], (1,) + lrow.shape)
    sent = []
    for i in range(NT):
        QGI[i, 0] = QI[:, i * COLS : (i + 1) * COLS]
        QGI[i, 1] = GI[:, i * COLS : (i + 1) * COLS]
    def straight(slot, d):
        for i in range(NT):
            remote(QGI.at[lax.rem(t + i, NT)], QG.at[slot, :, t], bs.at[0, slot], br.at[0, slot], diagonal(i, d)).start()

    def share(d):
        for part in range(2):
            sent.append(remote(KV.at[0, part], KV.at[NX - d, part], cs.at[part, d], cr.at[part, NX - d], xpeer(d)))

    straight(2, 1)
    straight(1, -1)
    share(1)
    share(NX - 1)
    for d in range(1, NT):
        sent.append(remote(lrow, L.at[t], as_.at[1, d], ar.at[1, d], tpeer(d)))
    for d in range(1, NT):
        sent.append(remote(QGI.at[lax.rem(t + d, NT)], QG.at[0, :, t], as_.at[0, d], ar.at[0, d], tpeer(d)))
    for copy in sent:
        copy.start()
    straight(4, 2)
    straight(3, -2)
    share(NX // 2)
    for copy in sent[-2:]:
        copy.start()
    for part in range(2):
        QG[0, part, pl.ds(t, 1)] = QGI[pl.ds(t, 1), part]

    onward = [
        remote(QG.at[4], QG.at[6], bs.at[0, 6], br.at[0, 6], zpeer(1)),
        remote(QG.at[3], QG.at[5], bs.at[0, 5], br.at[0, 5], zpeer(-1)),
        remote(QG.at[4, 1], QG.at[7, 1], bs.at[1, 7], br.at[1, 7], zpeer(2)),
        remote(QG.at[3, 0], QG.at[7, 0], bs.at[0, 7], br.at[0, 7], zpeer(-2)),
    ]

    def arrived(slot):
        remote(QG.at[0], QG.at[slot], bs.at[0, 3], br.at[0, slot], zpeer(1)).wait_recv()

    lane2 = lax.broadcasted_iota(jnp.int32, (1, COLS), 1)
    head = [(lane2 < COLS // 2).astype(F32), (lane2 >= COLS // 2).astype(F32)]
    rows2 = lax.broadcasted_iota(jnp.int32, (F, COLS), 0)
    lanes2 = lax.broadcasted_iota(jnp.int32, (F, COLS), 1)
    per = F // MASK_BLOCK

    def build(r):
        kb = KV[r, 0].astype(F32)
        vb = KV[r, 1].astype(F32)
        hot = (lanes2 == rows2 // MASK_BLOCK + per * r).astype(F32).astype(BF16)
        for h in range(2):
            kh = kb * (head[h] * SCALE)
            K2[r, h * F : (h + 1) * F, 0:COLS] = kh.astype(BF16)
            K2[r, h * F : (h + 1) * F, COLS : 2 * COLS] = hot
            V2[r, h * F : (h + 1) * F, :] = (vb * head[h]).astype(BF16)
            KT[r, :, h * F : (h + 1) * F] = kh.T.astype(BF16)

    build(0)
    for d in range(1, NT):
        source = lax.rem(t + NT - d, NT)
        remote(lrow, L.at[source], as_.at[1, d], ar.at[1, d], tpeer(d)).wait_recv()
    lane3 = lax.broadcasted_iota(jnp.int32, (NT, R, COLS), 2)
    row3 = lax.broadcasted_iota(jnp.int32, (NT, R, COLS), 1)
    lens = jnp.broadcast_to(L[:, 0:1, :], (NT, R, COLS))
    lanes = lax.broadcasted_iota(jnp.int32, (1, 1, COLS), 2)
    first = ((lax.rem(x + lanes // per, NX) * NZ + z) * per + lax.rem(lanes, per)) * MASK_BLOCK
    first = jnp.where(lanes < per * NX, first, -1).astype(F32)

    def mask_slot(p, rel):
        pick = lax.rem(z + rel, NZ) * R + row3
        column = jnp.sum(jnp.where(lane3 == pick, lens, 0.0), axis=2, keepdims=True)
        M[p] = jnp.where(first >= column, HIDDEN, 0.0).reshape(TOK, COLS).T.astype(BF16)

    for p in range(NZ):
        mask_slot(p, REL[p])

    for d in range(1, NT):
        source = lax.rem(t + NT - d, NT)
        remote(QGI.at[0], QG.at[0, :, source], as_.at[0, d], ar.at[0, d], tpeer(d)).wait_recv()

    arrived(1)

    masks = [m.astype(BF16) for m in head]

    def block(ref, c, which):
        return ref[pl.ds(2 * c, 2), which].reshape(CH, COLS)

    def pass_on():
        for slot in (2, 3, 4):
            arrived(slot)
        for copy in onward:
            copy.start()

    def pass1(c, fresh):
        qt = jnp.concatenate([block(QG, c, 0).T, jnp.concatenate([M[2 * c], M[2 * c + 1]], axis=1)], axis=0)
        gt = block(QG, c, 1).T
        for h in range(2):
            rows = slice(h * CH, (h + 1) * CH)
            Q2[c, rows] = block(QG, c, 0) * masks[h]
            G2[c, rows] = block(QG, c, 1) * masks[h]
        found = [[] for _ in range(4)]

        def products(r, h):
            rows = slice(h * F, (h + 1) * F)
            W[c, r, h] = jnp.dot(K2[r, rows], qt, preferred_element_type=F32)
            G[c, r, h] = jnp.dot(V2[r, rows], gt, preferred_element_type=F32)

        def reduce(r, h):
            for half in range(2):
                piece = slice(half * TOK, (half + 1) * TOK)
                sc = W[c, r, h, :, piece]
                m = jnp.max(sc, axis=0, keepdims=True)
                w = jnp.exp(sc - m)
                W[c, r, h, :, piece] = w
                MR[c, 2 * r + h : 2 * r + h + 1, piece] = m
                l = jnp.sum(w, axis=0, keepdims=True)
                found[2 * h + half].append((m, l, jnp.sum(w * G[c, r, h, :, piece], axis=0, keepdims=True)))

        order = [(r, h) for r in (0, 1, NX - 1, NX // 2) for h in range(2)]
        products(*order[0])
        for now, later in zip(order, order[1:] + [None]):
            wait = fresh and later is not None and later[1] == 0
            if wait:
                reduce(*now)
                r = later[0]
                if r == NX // 2:
                    pass_on()
                for part in range(2):
                    remote(KV.at[0, part], KV.at[r, part], cs.at[part, r], cr.at[part, r], xpeer(r)).wait_recv()
                build(r)
            if later is not None:
                products(*later)
            if not wait:
                reduce(*now)
        for h in range(2):
            for half in range(2):
                top = found[2 * h + half][0][0]
                for m, _, _ in found[2 * h + half][1:]:
                    top = jnp.maximum(top, m)
                total = jnp.zeros_like(top)
                term = jnp.zeros_like(top)
                for m, l, tt in found[2 * h + half]:
                    a = jnp.exp(m - top)
                    total += a * l
                    term += a * tt
                row = 2 * half + h
                SM[c, row : row + 1, :] = top + jnp.log(total)
                SM[c, 4 + row : 5 + row, :] = term / total
        for d in REL[1:]:
            remote(SM.at[c], SR.at[NZ - d, c], ds_.at[d], dr.at[NZ - d], zpeer(d)).start()

        @pl.when(c == 1)
        def _():
            arrived(5)

        @pl.when(c == 2)
        def _():
            arrived(6)
            for part in range(2):
                onward[3 - part].wait_recv()

        return 0

    pass1(0, True)
    lax.fori_loop(1, NC, lambda c, _: pass1(c, False), 0)

    for d in range(1, NZ):
        remote(SM, SR.at[d], ds_.at[d], dr.at[d], zpeer(d)).wait_recv()

    def combine(p):
        parts, terms = [], []
        for d in range(NZ):
            theirs = POS[(REL[p] - d) % NZ]
            ref = SM if d == 0 else SR.at[d]
            row = 2 * (theirs % 2)
            parts.append(ref[theirs // 2, row : row + 2, :])
            terms.append(ref[theirs // 2, 4 + row : 6 + row, :])
        top = parts[0]
        for part in parts[1:]:
            top = jnp.maximum(top, part)
        total = jnp.zeros_like(top)
        term = jnp.zeros_like(top)
        for part, other in zip(parts, terms):
            weight = jnp.exp(part - top)
            total += weight
            term += weight * other
        CF[:, p * TOK : (p + 1) * TOK] = top + jnp.log(total)
        RT[:, p * TOK : (p + 1) * TOK] = term / total

    for p in range(NZ):
        combine(p)

    def make(c, r):
        piece = slice(c * CH, (c + 1) * CH)
        for h in range(2):
            cf = jnp.exp(MR[c, 2 * r + h : 2 * r + h + 1, :] - CF[h : h + 1, piece])
            term = RT[h : h + 1, piece]
            for lo in range(0, F, 64):
                rows = slice(lo, lo + 64)
                p = W[c, r, h, rows, :] * cf
                PS[c, r, rows, h * CH : (h + 1) * CH] = p.astype(BF16)
                GS[c, r, rows, h * CH : (h + 1) * CH] = (p * (G[c, r, h, rows, :] - term)).astype(BF16)

    def use(c, r):
        first = c == NC - 1
        dv = jnp.dot(PS[c, r], G2[c], preferred_element_type=F32)
        dk = jnp.dot(GS[c, r], Q2[c], preferred_element_type=F32)
        DV[r] = dv if first else DV[r] + dv
        DK[r] = dk if first else DK[r] + dk
        dq = jnp.dot(KT[r, :, 0:F], GS[c, r, :, 0:CH], preferred_element_type=F32)
        dq += jnp.dot(KT[r, :, F : 2 * F], GS[c, r, :, CH : 2 * CH], preferred_element_type=F32)
        DQT[c] = dq if r == ORDER[0] else DQT[c] + dq

    def send_dq(p):
        d = REL[p]
        for i in range(NT):
            if p > 0 or i > 0:
                there = lax.rem(t + i, NT)
                remote(
                    DQS.at[p, there], DQR.at[(NZ - d) % NZ, t],
                    es.at[d] if d else gs.at[i], er.at[(NZ - d) % NZ] if d else gr.at[i],
                    (there, x * NZ + lax.rem(z + d, NZ)),
                ).start()

    def done_dq(c):
        DQS[2 * c : 2 * c + 2] = DQT[c].T.astype(BF16).reshape(2, NT, R, COLS)
        send_dq(2 * c + 1)
        send_dq(2 * c)

    def done_kv(r):
        DKVS[r, 0] = DK[r].astype(BF16)
        DKVS[r, 1] = DV[r].astype(BF16)
        sent.append(remote(DKVS.at[r], DKVR.at[NX - r], fs.at[r], fr.at[NX - r], xpeer(r)))
        sent[-1].start()

    ORDER = [NX // 2] + [i for i in range(1, NX) if i != NX // 2] + [0]
    steps = [(c, r) for c in range(NC - 1, 1, -1) for r in ORDER] + [(c, r) for r in ORDER for c in (1, 0)]
    make(*steps[0])
    for (c, r), later in zip(steps, steps[1:] + [None]):
        if later is not None:
            make(*later)
        use(c, r)
        if r == ORDER[-1]:
            done_dq(c)
        if c == 0 and r > 0:
            done_kv(r)
    DQR[0, pl.ds(t, 1)] = DQS[0, pl.ds(t, 1)]

    for d in range(1, NX):
        remote(DKVS.at[d], DKVR.at[d], fs.at[d], fr.at[d], xpeer(d)).wait_recv()
    dk, dv = DK[0], DV[0]
    for d in range(1, NX):
        dk += DKVR[d, 0].astype(F32)
        dv += DKVR[d, 1].astype(F32)
    dk_out[...] = dk * SCALE
    dv_out[...] = dv

    for d in range(1, NT):
        source = lax.rem(t + NT - d, NT)
        remote(DQS.at[0, 0], DQR.at[0, source], gs.at[d], gr.at[d], tpeer(d)).wait_recv()
    for d in range(1, NZ):
        remote(DQS.at[POS[d]], DQR.at[d], es.at[d], er.at[d], zpeer(d)).wait_recv()
    for i in range(NT):
        dq = DQR[0, i].astype(F32)
        for d in range(1, NZ):
            dq += DQR[d, i].astype(F32)
        dq_out[:, i * COLS : (i + 1) * COLS] = dq
    for copy in sent:
        copy.wait_send()
    for slot in range(1, 5):
        remote(QGI, QG.at[slot], bs.at[0, slot], br.at[0, slot], zpeer(1)).wait_send()
    for copy in onward:
        copy.wait_send()
    for d in range(1, NT):
        remote(DQS.at[0, 0], DQR.at[0, 0], gs.at[d], gr.at[d], tpeer(d)).wait_send()
    for d in range(1, NZ):
        remote(DQS.at[POS[d]], DQR.at[d], es.at[d], er.at[d], zpeer(d)).wait_send()
    for d in range(1, NZ):
        remote(SM, SR.at[NZ - d], ds_.at[d], dr.at[NZ - d], zpeer(d)).wait_send()


def body(queries, keys, values, grad_out, read_len, *, NT):
    R, D = queries.shape
    F = keys.shape[0]
    TOK, CH, NC = NT * R, 2 * NT * R, NZ // 2
    lens = read_len.reshape(NX, NZ * R)
    hbm = pl.BlockSpec(memory_space=pltpu.HBM)
    vmem = pl.BlockSpec(memory_space=pltpu.VMEM)
    dma = pltpu.SemaphoreType.DMA
    V = pltpu.VMEM
    return pl.pallas_call(
        lambda *refs: kernel(NT, *refs),
        out_shape=(V((R, D), F32), V((F, COLS), F32), V((F, COLS), F32)),
        in_specs=[hbm] * 5,
        out_specs=(vmem, vmem, vmem),
        scratch_shapes=[
            V((NX, NZ * R), jnp.int32),
            V((R, D), BF16),
            V((R, D), BF16),
            V((NT, 2, R, COLS), BF16),
            V((NZ, 2, NT, R, COLS), BF16),
            V((NX, 2, F, COLS), BF16),
            V((NT, 8, COLS), F32),
            V((8, COLS), F32),
            V((NZ, COLS, TOK), BF16),
            V((NX, 2 * F, 2 * COLS), BF16),
            V((NX, 2 * F, COLS), BF16),
            V((NX, COLS, 2 * F), BF16),
            V((NC, NX, 2, F, CH), F32),
            V((NC, NX, 2, F, CH), F32),
            V((NC, 2 * NX, CH), F32),
            V((NC, 8, TOK), F32),
            V((NZ, NC, 8, TOK), F32),
            V((2, NZ * TOK), F32),
            V((2, NZ * TOK), F32),
            V((NC, NX, F, 2 * CH), BF16),
            V((NC, NX, F, 2 * CH), BF16),
            V((NC, 2 * CH, COLS), BF16),
            V((NC, 2 * CH, COLS), BF16),
            V((NC, COLS, CH), F32),
            V((NZ, NT, R, COLS), BF16),
            V((NZ, NT, R, COLS), BF16),
            V((NX, F, COLS), F32),
            V((NX, F, COLS), F32),
            V((NX, 2, F, COLS), BF16),
            V((NX, 2, F, COLS), BF16),
            dma((5,)),
            dma((2, NT)), dma((2, NT)),
            dma((2, NZ)), dma((2, NZ)),
            dma((2, NX)), dma((2, NX)),
            dma((NZ,)), dma((NZ,)),
            dma((NZ,)), dma((NZ,)),
            dma((NX,)), dma((NX,)),
            dma((NT,)), dma((NT,)),
        ],
        compiler_params=pltpu.CompilerParams(
            collective_id=0, has_side_effects=True, vmem_limit_bytes=62 * 1024 * 1024
        ),
    )(queries, keys, values, grad_out, lens)


def solution(mesh):
    NT = mesh.shape["tgt"]
    return jax.shard_map(
        lambda *args: body(*args, NT=NT),
        mesh=mesh,
        in_specs=(
            P(("tgt", "src"), None),
            P("src", None),
            P("src", None),
            P(("tgt", "src"), None),
            P("tgt"),
        ),
        out_specs=(P(("tgt", "src"), None), P("src", "tgt"), P("src", "tgt")),
        check_vma=False,
    )
```

```python
import jax
import jax.numpy as jnp
from jax import lax
from jax.experimental import pallas as pl
from jax.experimental.pallas import tpu as pltpu
from jax.sharding import PartitionSpec as P

MESH = pl.DeviceIdType.MESH
NX, NZ = 4, 8
COLS = 128
MASK_BLOCK = 128
F32, BF16 = jnp.float32, jnp.bfloat16
HIDDEN = -1e30
SCALE = 0.125

REL = [0]
for _d in range(1, NZ // 2 + 1):
    REL += [_d] if 2 * _d == NZ else [_d, NZ - _d]
POS = {d: p for p, d in enumerate(REL)}


def kernel(
    NT, q_hbm, k_hbm, v_hbm, g_hbm, len_hbm, dq_out, dk_out, dv_out,
    len_ref, QI, GI, QGI, QG, KV, L, lrow, M, K2, V2, KT, W, G, MR, SM, SR, CF, RT, PS, GS, Q2, G2, DQT, DQS, DQR, DK, DV, DKVS, DKVR, VIA,
    lsem, as_, ar, bs, br, cs, cr, ds_, dr, es, er, fs, fr, gs, gr,
):
    t = lax.axis_index("tgt")
    s = lax.axis_index("src")
    x = s // NZ
    z = s % NZ
    R, F = q_hbm.shape[0], k_hbm.shape[0]
    TOK = NT * R
    CH = 2 * TOK
    NC = NZ // 2

    def tpeer(d):
        return (lax.rem(t + d, NT), s)

    def zpeer(d):
        return (t, x * NZ + lax.rem(z + NZ + d, NZ))

    def diagonal(i, d):
        return (lax.rem(t + i, NT), x * NZ + lax.rem(z + NZ + d, NZ))

    def xpeer(d):
        return (t, lax.rem(x + d, NX) * NZ + z)

    def cols(i):
        return pl.ds(pl.multiple_of(i * COLS, COLS), COLS)

    def remote(src, dst, ssem, rsem, dev):
        return pltpu.make_async_remote_copy(
            src_ref=src, dst_ref=dst, send_sem=ssem, recv_sem=rsem, device_id=dev, device_id_type=MESH
        )

    local = [
        pltpu.make_async_copy(q_hbm, QI, lsem.at[0]),
        pltpu.make_async_copy(g_hbm, GI, lsem.at[1]),
        pltpu.make_async_copy(k_hbm.at[:, cols(t)], KV.at[0, 0], lsem.at[2]),
        pltpu.make_async_copy(v_hbm.at[:, cols(t)], KV.at[0, 1], lsem.at[3]),
        pltpu.make_async_copy(len_hbm, len_ref, lsem.at[4]),
    ]
    for copy in local:
        copy.start()
    barrier = pltpu.get_barrier_semaphore()
    peers = [tpeer(d) for d in range(1, NT)] + [diagonal(i, d) for i in range(1, NT) for d in (1, -1, 2, -2)]
    peers += [zpeer(d) for d in range(1, NZ)] + [xpeer(d) for d in range(1, NX)]
    for dev in peers:
        pl.semaphore_signal(barrier, inc=1, device_id=dev, device_id_type=MESH)
    pl.semaphore_wait(barrier, len(peers))

    for copy in local:
        copy.wait()
    row = len_ref[pl.ds(x, 1), :].astype(F32)
    lrow[...] = jnp.broadcast_to(row, lrow.shape)
    L[pl.ds(t, 1)] = jnp.broadcast_to(row[None], (1,) + lrow.shape)
    sent = []
    for i in range(NT):
        QGI[i, 0] = QI[:, i * COLS : (i + 1) * COLS]
        QGI[i, 1] = GI[:, i * COLS : (i + 1) * COLS]
    def straight(slot, d):
        for i in range(NT):
            remote(QGI.at[lax.rem(t + i, NT)], QG.at[slot, :, t], bs.at[0, slot], br.at[0, slot], diagonal(i, d)).start()

    def share(d):
        for part in range(2):
            sent.append(remote(KV.at[0, part], KV.at[NX - d, part], cs.at[part, d], cr.at[part, NX - d], xpeer(d)))

    straight(2, 1)
    straight(1, -1)
    share(1)
    share(NX - 1)
    for d in range(1, NT):
        sent.append(remote(lrow, L.at[t], as_.at[1, d], ar.at[1, d], tpeer(d)))
    for d in range(1, NT):
        sent.append(remote(QGI.at[lax.rem(t + d, NT)], QG.at[0, :, t], as_.at[0, d], ar.at[0, d], tpeer(d)))
    for copy in sent:
        copy.start()
    straight(4, 2)
    straight(3, -2)
    share(NX // 2)
    for copy in sent[-2:]:
        copy.start()
    for part in range(2):
        QG[0, part, pl.ds(t, 1)] = QGI[pl.ds(t, 1), part]

    onward = [
        remote(QG.at[4], QG.at[6], bs.at[0, 6], br.at[0, 6], zpeer(1)),
        remote(QG.at[3], QG.at[5], bs.at[0, 5], br.at[0, 5], zpeer(-1)),
        remote(QG.at[4, 1], QG.at[7, 1], bs.at[1, 7], br.at[1, 7], zpeer(2)),
        remote(QG.at[3, 0], QG.at[7, 0], bs.at[0, 7], br.at[0, 7], zpeer(-2)),
    ]

    def arrived(slot):
        remote(QG.at[0], QG.at[slot], bs.at[0, 3], br.at[0, slot], zpeer(1)).wait_recv()

    lane2 = lax.broadcasted_iota(jnp.int32, (1, COLS), 1)
    head = [(lane2 < COLS // 2).astype(F32), (lane2 >= COLS // 2).astype(F32)]
    rows2 = lax.broadcasted_iota(jnp.int32, (F, COLS), 0)
    lanes2 = lax.broadcasted_iota(jnp.int32, (F, COLS), 1)
    per = F // MASK_BLOCK

    def build(r):
        kb = KV[r, 0].astype(F32)
        vb = KV[r, 1].astype(F32)
        hot = (lanes2 == rows2 // MASK_BLOCK + per * r).astype(F32).astype(BF16)
        for h in range(2):
            kh = kb * (head[h] * SCALE)
            K2[r, h * F : (h + 1) * F, 0:COLS] = kh.astype(BF16)
            K2[r, h * F : (h + 1) * F, COLS : 2 * COLS] = hot
            V2[r, h * F : (h + 1) * F, :] = (vb * head[h]).astype(BF16)
            KT[r, :, h * F : (h + 1) * F] = kh.T.astype(BF16)

    build(0)
    for d in range(1, NT):
        source = lax.rem(t + NT - d, NT)
        remote(lrow, L.at[source], as_.at[1, d], ar.at[1, d], tpeer(d)).wait_recv()
    lane3 = lax.broadcasted_iota(jnp.int32, (NT, R, COLS), 2)
    row3 = lax.broadcasted_iota(jnp.int32, (NT, R, COLS), 1)
    lens = jnp.broadcast_to(L[:, 0:1, :], (NT, R, COLS))
    lanes = lax.broadcasted_iota(jnp.int32, (1, 1, COLS), 2)
    first = ((lax.rem(x + lanes // per, NX) * NZ + z) * per + lax.rem(lanes, per)) * MASK_BLOCK
    first = jnp.where(lanes < per * NX, first, -1).astype(F32)

    def mask_slot(p, rel):
        pick = lax.rem(z + rel, NZ) * R + row3
        column = jnp.sum(jnp.where(lane3 == pick, lens, 0.0), axis=2, keepdims=True)
        M[p] = jnp.where(first >= column, HIDDEN, 0.0).reshape(TOK, COLS).T.astype(BF16)

    for p in range(NZ):
        mask_slot(p, REL[p])

    for d in range(1, NT):
        source = lax.rem(t + NT - d, NT)
        remote(QGI.at[0], QG.at[0, :, source], as_.at[0, d], ar.at[0, d], tpeer(d)).wait_recv()

    arrived(1)

    masks = [m.astype(BF16) for m in head]

    def block(ref, c, which):
        return ref[pl.ds(2 * c, 2), which].reshape(CH, COLS)

    def pass_on():
        for slot in (2, 3, 4):
            arrived(slot)
        for copy in onward:
            copy.start()

    def pass1(c, fresh):
        qt = jnp.concatenate([block(QG, c, 0).T, jnp.concatenate([M[2 * c], M[2 * c + 1]], axis=1)], axis=0)
        gt = block(QG, c, 1).T
        for h in range(2):
            rows = slice(h * CH, (h + 1) * CH)
            Q2[c, rows] = block(QG, c, 0) * masks[h]
            G2[c, rows] = block(QG, c, 1) * masks[h]
        found = [[] for _ in range(4)]

        def products(r, h):
            rows = slice(h * F, (h + 1) * F)
            W[c, r, h] = jnp.dot(K2[r, rows], qt, preferred_element_type=F32)
            G[c, r, h] = jnp.dot(V2[r, rows], gt, preferred_element_type=F32)

        def reduce(r, h):
            for half in range(2):
                piece = slice(half * TOK, (half + 1) * TOK)
                sc = W[c, r, h, :, piece]
                m = jnp.max(sc, axis=0, keepdims=True)
                w = jnp.exp(sc - m)
                W[c, r, h, :, piece] = w
                MR[c, 2 * r + h : 2 * r + h + 1, piece] = m
                l = jnp.sum(w, axis=0, keepdims=True)
                found[2 * h + half].append((m, l, jnp.sum(w * G[c, r, h, :, piece], axis=0, keepdims=True)))

        order = [(r, h) for r in (0, 1, NX - 1, NX // 2) for h in range(2)]
        products(*order[0])
        for now, later in zip(order, order[1:] + [None]):
            wait = fresh and later is not None and later[1] == 0
            if wait:
                reduce(*now)
                r = later[0]
                if r == NX // 2:
                    pass_on()
                for part in range(2):
                    remote(KV.at[0, part], KV.at[r, part], cs.at[part, r], cr.at[part, r], xpeer(r)).wait_recv()
                build(r)
            if later is not None:
                products(*later)
            if not wait:
                reduce(*now)
        for h in range(2):
            for half in range(2):
                top = found[2 * h + half][0][0]
                for m, _, _ in found[2 * h + half][1:]:
                    top = jnp.maximum(top, m)
                total = jnp.zeros_like(top)
                term = jnp.zeros_like(top)
                for m, l, tt in found[2 * h + half]:
                    a = jnp.exp(m - top)
                    total += a * l
                    term += a * tt
                row = 2 * half + h
                SM[c, row : row + 1, :] = top + jnp.log(total)
                SM[c, 4 + row : 5 + row, :] = term / total
        for d in REL[1:]:
            remote(SM.at[c], SR.at[NZ - d, c], ds_.at[d], dr.at[NZ - d], zpeer(d)).start()

        @pl.when(c == 1)
        def _():
            arrived(5)

        @pl.when(c == 2)
        def _():
            arrived(6)
            for part in range(2):
                onward[3 - part].wait_recv()

        return 0

    pass1(0, True)
    lax.fori_loop(1, NC, lambda c, _: pass1(c, False), 0)

    for d in range(1, NZ):
        remote(SM, SR.at[d], ds_.at[d], dr.at[d], zpeer(d)).wait_recv()

    def combine(p):
        parts, terms = [], []
        for d in range(NZ):
            theirs = POS[(REL[p] - d) % NZ]
            ref = SM if d == 0 else SR.at[d]
            row = 2 * (theirs % 2)
            parts.append(ref[theirs // 2, row : row + 2, :])
            terms.append(ref[theirs // 2, 4 + row : 6 + row, :])
        top = parts[0]
        for part in parts[1:]:
            top = jnp.maximum(top, part)
        total = jnp.zeros_like(top)
        term = jnp.zeros_like(top)
        for part, other in zip(parts, terms):
            weight = jnp.exp(part - top)
            total += weight
            term += weight * other
        CF[:, p * TOK : (p + 1) * TOK] = top + jnp.log(total)
        RT[:, p * TOK : (p + 1) * TOK] = term / total


    def make(c, r):
        piece = slice(c * CH, (c + 1) * CH)
        for h in range(2):
            cf = jnp.exp(MR[c, 2 * r + h : 2 * r + h + 1, :] - CF[h : h + 1, piece])
            term = RT[h : h + 1, piece]
            for lo in range(0, F, 64):
                rows = slice(lo, lo + 64)
                p = W[c, r, h, rows, :] * cf
                PS[c, r, rows, h * CH : (h + 1) * CH] = p.astype(BF16)
                GS[c, r, rows, h * CH : (h + 1) * CH] = (p * (G[c, r, h, rows, :] - term)).astype(BF16)

    def use(c, r):
        first = c == NC - 1
        dv = jnp.dot(PS[c, r], G2[c], preferred_element_type=F32)
        dk = jnp.dot(GS[c, r], Q2[c], preferred_element_type=F32)
        DV[r] = dv if first else DV[r] + dv
        DK[r] = dk if first else DK[r] + dk
        dq = jnp.dot(KT[r, :, 0:F], GS[c, r, :, 0:CH], preferred_element_type=F32)
        dq += jnp.dot(KT[r, :, F : 2 * F], GS[c, r, :, CH : 2 * CH], preferred_element_type=F32)
        DQT[c] = dq if r == ORDER[0] else DQT[c] + dq

    def send_dq(p):
        d = REL[p]
        for i in range(NT):
            if p > 0 or i > 0:
                there = lax.rem(t + i, NT)
                remote(
                    DQS.at[p, there], DQR.at[(NZ - d) % NZ, t],
                    es.at[d] if d else gs.at[i], er.at[(NZ - d) % NZ] if d else gr.at[i],
                    (there, x * NZ + lax.rem(z + d, NZ)),
                ).start()

    def done_dq(c):
        DQS[2 * c : 2 * c + 2] = DQT[c].T.astype(BF16).reshape(2, NT, R, COLS)
        send_dq(2 * c + 1)
        send_dq(2 * c)

    def done_kv(r):
        DKVS[r, 0] = DK[r].astype(BF16)
        DKVS[r, 1] = DV[r].astype(BF16)
        if r == NX // 2:
            back = [
                remote(DKVS.at[r, 0], DKVR.at[r, 0], fs.at[0, r], fr.at[0, r], xpeer(r)),
                remote(DKVS.at[r, 1], VIA, fs.at[1, r], fr.at[1, 0], xpeer(NX - 1)),
            ]
        else:
            back = [remote(DKVS.at[r], DKVR.at[NX - r], fs.at[0, r], fr.at[0, NX - r], xpeer(r))]
        for copy in back:
            copy.start()
        sent.extend(back)

    via = remote(VIA, DKVR.at[NX // 2, 1], fs.at[1, 0], fr.at[1, NX // 2], xpeer(NX - 1))

    ORDER = [NX // 2] + [i for i in range(1, NX) if i != NX // 2] + [0]
    steps = [(c, r) for c in range(NC - 1, 1, -1) for r in ORDER] + [(c, r) for r in ORDER for c in (1, 0)]
    early = list(sent)
    sent.clear()
    combine(NZ - 2)
    combine(NZ - 1)
    make(*steps[0])
    for p in range(NZ - 2):
        combine(p)
    for (c, r), later in zip(steps, steps[1:] + [None]):
        if later is not None:
            make(*later)
        use(c, r)
        if later is None:
            remote(DKVS.at[1, 1], VIA, fs.at[1, 1], fr.at[1, 0], xpeer(1)).wait_recv()
            via.start()
            sent.append(via)
        if r == ORDER[-1]:
            done_dq(c)
        if c == 0 and r > 0:
            done_kv(r)
    DQR[0, pl.ds(t, 1)] = DQS[0, pl.ds(t, 1)]

    for copy in early:
        copy.wait_send()
    for slot in range(1, 5):
        remote(QGI, QG.at[slot], bs.at[0, slot], br.at[0, slot], zpeer(1)).wait_send()
    for copy in onward:
        copy.wait_send()
    for d in range(1, NZ):
        remote(SM, SR.at[NZ - d], ds_.at[d], dr.at[NZ - d], zpeer(d)).wait_send()
    for d in (1, NX - 1):
        remote(DKVS.at[d], DKVR.at[d], fs.at[0, d], fr.at[0, d], xpeer(d)).wait_recv()
    for part in range(2):
        remote(DKVS.at[1, part], DKVR.at[NX // 2, part], fs.at[part, 1], fr.at[part, NX // 2], xpeer(1)).wait_recv()
    dk, dv = DK[0], DV[0]
    for d in range(1, NX):
        dk += DKVR[d, 0].astype(F32)
        dv += DKVR[d, 1].astype(F32)
    dk_out[...] = dk * SCALE
    dv_out[...] = dv

    for d in range(1, NT):
        source = lax.rem(t + NT - d, NT)
        remote(DQS.at[0, 0], DQR.at[0, source], gs.at[d], gr.at[d], tpeer(d)).wait_recv()
    for d in range(1, NZ):
        remote(DQS.at[POS[d]], DQR.at[d], es.at[d], er.at[d], zpeer(d)).wait_recv()
    for i in range(NT):
        dq = DQR[0, i].astype(F32)
        for d in range(1, NZ):
            dq += DQR[d, i].astype(F32)
        dq_out[:, i * COLS : (i + 1) * COLS] = dq
    for copy in sent:
        copy.wait_send()
    for d in range(1, NT):
        remote(DQS.at[0, 0], DQR.at[0, 0], gs.at[d], gr.at[d], tpeer(d)).wait_send()
    for d in range(1, NZ):
        remote(DQS.at[POS[d]], DQR.at[d], es.at[d], er.at[d], zpeer(d)).wait_send()


def body(queries, keys, values, grad_out, read_len, *, NT):
    R, D = queries.shape
    F = keys.shape[0]
    TOK, CH, NC = NT * R, 2 * NT * R, NZ // 2
    lens = read_len.reshape(NX, NZ * R)
    hbm = pl.BlockSpec(memory_space=pltpu.HBM)
    vmem = pl.BlockSpec(memory_space=pltpu.VMEM)
    dma = pltpu.SemaphoreType.DMA
    V = pltpu.VMEM
    return pl.pallas_call(
        lambda *refs: kernel(NT, *refs),
        out_shape=(V((R, D), F32), V((F, COLS), F32), V((F, COLS), F32)),
        in_specs=[hbm] * 5,
        out_specs=(vmem, vmem, vmem),
        scratch_shapes=[
            V((NX, NZ * R), jnp.int32),
            V((R, D), BF16),
            V((R, D), BF16),
            V((NT, 2, R, COLS), BF16),
            V((NZ, 2, NT, R, COLS), BF16),
            V((NX, 2, F, COLS), BF16),
            V((NT, 8, COLS), F32),
            V((8, COLS), F32),
            V((NZ, COLS, TOK), BF16),
            V((NX, 2 * F, 2 * COLS), BF16),
            V((NX, 2 * F, COLS), BF16),
            V((NX, COLS, 2 * F), BF16),
            V((NC, NX, 2, F, CH), F32),
            V((NC, NX, 2, F, CH), F32),
            V((NC, 2 * NX, CH), F32),
            V((NC, 8, TOK), F32),
            V((NZ, NC, 8, TOK), F32),
            V((2, NZ * TOK), F32),
            V((2, NZ * TOK), F32),
            V((NC, NX, F, 2 * CH), BF16),
            V((NC, NX, F, 2 * CH), BF16),
            V((NC, 2 * CH, COLS), BF16),
            V((NC, 2 * CH, COLS), BF16),
            V((NC, COLS, CH), F32),
            V((NZ, NT, R, COLS), BF16),
            V((NZ, NT, R, COLS), BF16),
            V((NX, F, COLS), F32),
            V((NX, F, COLS), F32),
            V((NX, 2, F, COLS), BF16),
            V((NX, 2, F, COLS), BF16),
            V((F, COLS), BF16),
            dma((5,)),
            dma((2, NT)), dma((2, NT)),
            dma((2, NZ)), dma((2, NZ)),
            dma((2, NX)), dma((2, NX)),
            dma((NZ,)), dma((NZ,)),
            dma((NZ,)), dma((NZ,)),
            dma((2, NX)), dma((2, NX)),
            dma((NT,)), dma((NT,)),
        ],
        compiler_params=pltpu.CompilerParams(
            collective_id=0, has_side_effects=True, vmem_limit_bytes=62 * 1024 * 1024
        ),
    )(queries, keys, values, grad_out, lens)


def solution(mesh):
    NT = mesh.shape["tgt"]
    return jax.shard_map(
        lambda *args: body(*args, NT=NT),
        mesh=mesh,
        in_specs=(
            P(("tgt", "src"), None),
            P("src", None),
            P("src", None),
            P(("tgt", "src"), None),
            P("tgt"),
        ),
        out_specs=(P(("tgt", "src"), None), P("src", "tgt"), P("src", "tgt")),
        check_vma=False,
    )
```

```python
import jax
import jax.numpy as jnp
from jax import lax
from jax.experimental import pallas as pl
from jax.experimental.pallas import tpu as pltpu
from jax.sharding import PartitionSpec as P

MESH = pl.DeviceIdType.MESH
NX, NZ = 4, 8
COLS = 128
MASK_BLOCK = 128
F32, BF16 = jnp.float32, jnp.bfloat16
HIDDEN = -1e30
SCALE = 0.125

REL = [0]
for _d in range(1, NZ // 2 + 1):
    REL += [_d] if 2 * _d == NZ else [_d, NZ - _d]
POS = {d: p for p, d in enumerate(REL)}


def kernel(
    NT, q_hbm, k_hbm, v_hbm, g_hbm, len_hbm, dq_out, dk_out, dv_out,
    len_ref, QI, GI, QGI, QG, KV, L, lrow, M, K2, V2, KT, W, G, MR, SM, SR, CF, RT, PS, GS, Q2, G2, DQT, DQS, DQR, DK, DV, DKVS, DKVR,
    lsem, as_, ar, bs, br, cs, cr, ds_, dr, es, er, fs, fr, gs, gr,
):
    t = lax.axis_index("tgt")
    s = lax.axis_index("src")
    x = s // NZ
    z = s % NZ
    R, F = q_hbm.shape[0], k_hbm.shape[0]
    TOK = NT * R
    CH = 2 * TOK
    NC = NZ // 2

    def tpeer(d):
        return (lax.rem(t + d, NT), s)

    def zpeer(d):
        return (t, x * NZ + lax.rem(z + NZ + d, NZ))

    def diagonal(i, d):
        return (lax.rem(t + i, NT), x * NZ + lax.rem(z + NZ + d, NZ))

    def xpeer(d):
        return (t, lax.rem(x + d, NX) * NZ + z)

    def cols(i):
        return pl.ds(pl.multiple_of(i * COLS, COLS), COLS)

    def remote(src, dst, ssem, rsem, dev):
        return pltpu.make_async_remote_copy(
            src_ref=src, dst_ref=dst, send_sem=ssem, recv_sem=rsem, device_id=dev, device_id_type=MESH
        )

    local = [
        pltpu.make_async_copy(q_hbm, QI, lsem.at[0]),
        pltpu.make_async_copy(g_hbm, GI, lsem.at[1]),
        pltpu.make_async_copy(k_hbm.at[:, cols(t)], KV.at[0, 0], lsem.at[2]),
        pltpu.make_async_copy(v_hbm.at[:, cols(t)], KV.at[0, 1], lsem.at[3]),
        pltpu.make_async_copy(len_hbm, len_ref, lsem.at[4]),
    ]
    for copy in local:
        copy.start()
    barrier = pltpu.get_barrier_semaphore()
    peers = [tpeer(d) for d in range(1, NT)] + [diagonal(i, d) for i in range(1, NT) for d in (1, -1, 2, -2)]
    peers += [zpeer(d) for d in range(1, NZ)] + [xpeer(d) for d in range(1, NX)]
    for dev in peers:
        pl.semaphore_signal(barrier, inc=1, device_id=dev, device_id_type=MESH)
    pl.semaphore_wait(barrier, len(peers))

    for copy in local:
        copy.wait()
    row = len_ref[pl.ds(x, 1), :].astype(F32)
    lrow[...] = jnp.broadcast_to(row, lrow.shape)
    L[pl.ds(t, 1)] = jnp.broadcast_to(row[None], (1,) + lrow.shape)
    sent = []
    for i in range(NT):
        QGI[i, 0] = QI[:, i * COLS : (i + 1) * COLS]
        QGI[i, 1] = GI[:, i * COLS : (i + 1) * COLS]
    def straight(slot, d):
        for i in range(NT):
            remote(QGI.at[lax.rem(t + i, NT)], QG.at[slot, :, t], bs.at[0, slot], br.at[0, slot], diagonal(i, d)).start()

    def share(d):
        for part in range(2):
            sent.append(remote(KV.at[0, part], KV.at[NX - d, part], cs.at[part, d], cr.at[part, NX - d], xpeer(d)))

    straight(2, 1)
    straight(1, -1)
    share(1)
    share(NX - 1)
    for d in range(1, NT):
        sent.append(remote(lrow, L.at[t], as_.at[1, d], ar.at[1, d], tpeer(d)))
    for d in range(1, NT):
        sent.append(remote(QGI.at[lax.rem(t + d, NT)], QG.at[0, :, t], as_.at[0, d], ar.at[0, d], tpeer(d)))
    for copy in sent:
        copy.start()
    straight(4, 2)
    straight(3, -2)
    share(NX // 2)
    for copy in sent[-2:]:
        copy.start()
    for part in range(2):
        QG[0, part, pl.ds(t, 1)] = QGI[pl.ds(t, 1), part]

    onward = [
        remote(QG.at[4], QG.at[6], bs.at[0, 6], br.at[0, 6], zpeer(1)),
        remote(QG.at[3], QG.at[5], bs.at[0, 5], br.at[0, 5], zpeer(-1)),
        remote(QG.at[4, 1], QG.at[7, 1], bs.at[1, 7], br.at[1, 7], zpeer(2)),
        remote(QG.at[3, 0], QG.at[7, 0], bs.at[0, 7], br.at[0, 7], zpeer(-2)),
    ]

    def arrived(slot):
        remote(QG.at[0], QG.at[slot], bs.at[0, 3], br.at[0, slot], zpeer(1)).wait_recv()

    lane2 = lax.broadcasted_iota(jnp.int32, (1, COLS), 1)
    head = [(lane2 < COLS // 2).astype(F32), (lane2 >= COLS // 2).astype(F32)]
    rows2 = lax.broadcasted_iota(jnp.int32, (F, COLS), 0)
    lanes2 = lax.broadcasted_iota(jnp.int32, (F, COLS), 1)
    per = F // MASK_BLOCK

    def build(r):
        kb = KV[r, 0].astype(F32)
        vb = KV[r, 1].astype(F32)
        hot = (lanes2 == rows2 // MASK_BLOCK + per * r).astype(F32).astype(BF16)
        for h in range(2):
            kh = kb * (head[h] * SCALE)
            K2[r, h * F : (h + 1) * F, 0:COLS] = kh.astype(BF16)
            K2[r, h * F : (h + 1) * F, COLS : 2 * COLS] = hot
            V2[r, h * F : (h + 1) * F, :] = (vb * head[h]).astype(BF16)
            KT[r, :, h * F : (h + 1) * F] = kh.T.astype(BF16)

    build(0)
    for d in range(1, NT):
        source = lax.rem(t + NT - d, NT)
        remote(lrow, L.at[source], as_.at[1, d], ar.at[1, d], tpeer(d)).wait_recv()
    lane3 = lax.broadcasted_iota(jnp.int32, (NT, R, COLS), 2)
    row3 = lax.broadcasted_iota(jnp.int32, (NT, R, COLS), 1)
    lens = jnp.broadcast_to(L[:, 0:1, :], (NT, R, COLS))
    lanes = lax.broadcasted_iota(jnp.int32, (1, 1, COLS), 2)
    first = ((lax.rem(x + lanes // per, NX) * NZ + z) * per + lax.rem(lanes, per)) * MASK_BLOCK
    first = jnp.where(lanes < per * NX, first, -1).astype(F32)

    def mask_slot(p, rel):
        pick = lax.rem(z + rel, NZ) * R + row3
        column = jnp.sum(jnp.where(lane3 == pick, lens, 0.0), axis=2, keepdims=True)
        M[p] = jnp.where(first >= column, HIDDEN, 0.0).reshape(TOK, COLS).T.astype(BF16)

    for p in range(NZ):
        mask_slot(p, REL[p])

    for d in range(1, NT):
        source = lax.rem(t + NT - d, NT)
        remote(QGI.at[0], QG.at[0, :, source], as_.at[0, d], ar.at[0, d], tpeer(d)).wait_recv()

    arrived(1)

    masks = [m.astype(BF16) for m in head]

    def block(ref, c, which):
        return ref[pl.ds(2 * c, 2), which].reshape(CH, COLS)

    def pass_on():
        for slot in (2, 3, 4):
            arrived(slot)
        for copy in onward:
            copy.start()

    def pass1(c, fresh):
        qt = jnp.concatenate([block(QG, c, 0).T, jnp.concatenate([M[2 * c], M[2 * c + 1]], axis=1)], axis=0)
        gt = block(QG, c, 1).T
        for h in range(2):
            rows = slice(h * CH, (h + 1) * CH)
            Q2[c, rows] = block(QG, c, 0) * masks[h]
            G2[c, rows] = block(QG, c, 1) * masks[h]
        found = [[] for _ in range(4)]

        def products(r, h):
            rows = slice(h * F, (h + 1) * F)
            W[c, r, h] = jnp.dot(K2[r, rows], qt, preferred_element_type=F32)
            G[c, r, h] = jnp.dot(V2[r, rows], gt, preferred_element_type=F32)

        def reduce(r, h):
            for half in range(2):
                piece = slice(half * TOK, (half + 1) * TOK)
                sc = W[c, r, h, :, piece]
                m = jnp.max(sc, axis=0, keepdims=True)
                w = jnp.exp(sc - m)
                W[c, r, h, :, piece] = w
                MR[c, 2 * r + h : 2 * r + h + 1, piece] = m
                l = jnp.sum(w, axis=0, keepdims=True)
                found[2 * h + half].append((m, l, jnp.sum(w * G[c, r, h, :, piece], axis=0, keepdims=True)))

        order = [(r, h) for r in (0, 1, NX - 1, NX // 2) for h in range(2)]
        products(*order[0])
        for now, later in zip(order, order[1:] + [None]):
            wait = fresh and later is not None and later[1] == 0
            if wait:
                reduce(*now)
                r = later[0]
                if r == NX // 2:
                    pass_on()
                for part in range(2):
                    remote(KV.at[0, part], KV.at[r, part], cs.at[part, r], cr.at[part, r], xpeer(r)).wait_recv()
                build(r)
            if later is not None:
                products(*later)
            if not wait:
                reduce(*now)
        for h in range(2):
            for half in range(2):
                top = found[2 * h + half][0][0]
                for m, _, _ in found[2 * h + half][1:]:
                    top = jnp.maximum(top, m)
                total = jnp.zeros_like(top)
                term = jnp.zeros_like(top)
                for m, l, tt in found[2 * h + half]:
                    a = jnp.exp(m - top)
                    total += a * l
                    term += a * tt
                row = 2 * half + h
                SM[c, row : row + 1, :] = top + jnp.log(total)
                SM[c, 4 + row : 5 + row, :] = term / total
        for d in REL[1:]:
            remote(SM.at[c], SR.at[NZ - d, c], ds_.at[d], dr.at[NZ - d], zpeer(d)).start()

        @pl.when(c == 1)
        def _():
            arrived(5)

        @pl.when(c == 2)
        def _():
            arrived(6)
            for part in range(2):
                onward[3 - part].wait_recv()

        return 0

    pass1(0, True)
    lax.fori_loop(1, NC, lambda c, _: pass1(c, False), 0)

    for d in range(1, NZ):
        remote(SM, SR.at[d], ds_.at[d], dr.at[d], zpeer(d)).wait_recv()

    def combine(p):
        parts, terms = [], []
        for d in range(NZ):
            theirs = POS[(REL[p] - d) % NZ]
            ref = SM if d == 0 else SR.at[d]
            row = 2 * (theirs % 2)
            parts.append(ref[theirs // 2, row : row + 2, :])
            terms.append(ref[theirs // 2, 4 + row : 6 + row, :])
        top = parts[0]
        for part in parts[1:]:
            top = jnp.maximum(top, part)
        total = jnp.zeros_like(top)
        term = jnp.zeros_like(top)
        for part, other in zip(parts, terms):
            weight = jnp.exp(part - top)
            total += weight
            term += weight * other
        CF[:, p * TOK : (p + 1) * TOK] = top + jnp.log(total)
        RT[:, p * TOK : (p + 1) * TOK] = term / total


    def make(c, r):
        piece = slice(c * CH, (c + 1) * CH)
        for h in range(2):
            cf = jnp.exp(MR[c, 2 * r + h : 2 * r + h + 1, :] - CF[h : h + 1, piece])
            term = RT[h : h + 1, piece]
            for lo in range(0, F, 64):
                rows = slice(lo, lo + 64)
                p = W[c, r, h, rows, :] * cf
                PS[c, r, rows, h * CH : (h + 1) * CH] = p.astype(BF16)
                GS[c, r, rows, h * CH : (h + 1) * CH] = (p * (G[c, r, h, rows, :] - term)).astype(BF16)

    def use(c, r):
        first = c == NC - 1
        dv = jnp.dot(PS[c, r], G2[c], preferred_element_type=F32)
        dk = jnp.dot(GS[c, r], Q2[c], preferred_element_type=F32)
        DV[r] = dv if first else DV[r] + dv
        DK[r] = dk if first else DK[r] + dk
        dq = jnp.dot(KT[r, :, 0:F], GS[c, r, :, 0:CH], preferred_element_type=F32)
        dq += jnp.dot(KT[r, :, F : 2 * F], GS[c, r, :, CH : 2 * CH], preferred_element_type=F32)
        DQT[c] = dq if r == ORDER[0] else DQT[c] + dq

    def send_dq(p):
        d = REL[p]
        for i in range(NT):
            if p > 0 or i > 0:
                there = lax.rem(t + i, NT)
                remote(
                    DQS.at[p, there], DQR.at[(NZ - d) % NZ, t],
                    es.at[d] if d else gs.at[i], er.at[(NZ - d) % NZ] if d else gr.at[i],
                    (there, x * NZ + lax.rem(z + d, NZ)),
                ).start()

    def done_dq(c):
        DQS[2 * c : 2 * c + 2] = DQT[c].T.astype(BF16).reshape(2, NT, R, COLS)
        send_dq(2 * c + 1)
        send_dq(2 * c)

    def done_kv(r):
        DKVS[r, 0] = DK[r].astype(BF16)
        DKVS[r, 1] = DV[r].astype(BF16)
        sent.append(remote(DKVS.at[r], DKVR.at[NX - r], fs.at[r], fr.at[NX - r], xpeer(r)))
        sent[-1].start()

    ORDER = [NX // 2] + [i for i in range(1, NX) if i != NX // 2] + [0]
    steps = [(c, r) for c in range(NC - 1, 1, -1) for r in ORDER] + [(c, r) for r in ORDER for c in (1, 0)]
    early = list(sent)
    sent.clear()
    combine(NZ - 2)
    combine(NZ - 1)
    make(*steps[0])
    for p in range(NZ - 2):
        combine(p)
    for (c, r), later in zip(steps, steps[1:] + [None]):
        if later is not None:
            make(*later)
        use(c, r)
        if r == ORDER[-1]:
            done_dq(c)
        if c == 0 and r > 0:
            done_kv(r)
    DQR[0, pl.ds(t, 1)] = DQS[0, pl.ds(t, 1)]

    for copy in early:
        copy.wait_send()
    for slot in range(1, 5):
        remote(QGI, QG.at[slot], bs.at[0, slot], br.at[0, slot], zpeer(1)).wait_send()
    for copy in onward:
        copy.wait_send()
    for d in range(1, NZ):
        remote(SM, SR.at[NZ - d], ds_.at[d], dr.at[NZ - d], zpeer(d)).wait_send()
    for d in range(1, NX):
        remote(DKVS.at[d], DKVR.at[d], fs.at[d], fr.at[d], xpeer(d)).wait_recv()
    dk, dv = DK[0], DV[0]
    for d in range(1, NX):
        dk += DKVR[d, 0].astype(F32)
        dv += DKVR[d, 1].astype(F32)
    dk_out[...] = dk * SCALE
    dv_out[...] = dv

    for d in range(1, NT):
        source = lax.rem(t + NT - d, NT)
        remote(DQS.at[0, 0], DQR.at[0, source], gs.at[d], gr.at[d], tpeer(d)).wait_recv()
    for d in range(1, NZ):
        remote(DQS.at[POS[d]], DQR.at[d], es.at[d], er.at[d], zpeer(d)).wait_recv()
    for i in range(NT):
        dq = DQR[0, i].astype(F32)
        for d in range(1, NZ):
            dq += DQR[d, i].astype(F32)
        dq_out[:, i * COLS : (i + 1) * COLS] = dq
    for copy in sent:
        copy.wait_send()
    for d in range(1, NT):
        remote(DQS.at[0, 0], DQR.at[0, 0], gs.at[d], gr.at[d], tpeer(d)).wait_send()
    for d in range(1, NZ):
        remote(DQS.at[POS[d]], DQR.at[d], es.at[d], er.at[d], zpeer(d)).wait_send()


def body(queries, keys, values, grad_out, read_len, *, NT):
    R, D = queries.shape
    F = keys.shape[0]
    TOK, CH, NC = NT * R, 2 * NT * R, NZ // 2
    lens = read_len.reshape(NX, NZ * R)
    hbm = pl.BlockSpec(memory_space=pltpu.HBM)
    vmem = pl.BlockSpec(memory_space=pltpu.VMEM)
    dma = pltpu.SemaphoreType.DMA
    V = pltpu.VMEM
    return pl.pallas_call(
        lambda *refs: kernel(NT, *refs),
        out_shape=(V((R, D), F32), V((F, COLS), F32), V((F, COLS), F32)),
        in_specs=[hbm] * 5,
        out_specs=(vmem, vmem, vmem),
        scratch_shapes=[
            V((NX, NZ * R), jnp.int32),
            V((R, D), BF16),
            V((R, D), BF16),
            V((NT, 2, R, COLS), BF16),
            V((NZ, 2, NT, R, COLS), BF16),
            V((NX, 2, F, COLS), BF16),
            V((NT, 8, COLS), F32),
            V((8, COLS), F32),
            V((NZ, COLS, TOK), BF16),
            V((NX, 2 * F, 2 * COLS), BF16),
            V((NX, 2 * F, COLS), BF16),
            V((NX, COLS, 2 * F), BF16),
            V((NC, NX, 2, F, CH), F32),
            V((NC, NX, 2, F, CH), F32),
            V((NC, 2 * NX, CH), F32),
            V((NC, 8, TOK), F32),
            V((NZ, NC, 8, TOK), F32),
            V((2, NZ * TOK), F32),
            V((2, NZ * TOK), F32),
            V((NC, NX, F, 2 * CH), BF16),
            V((NC, NX, F, 2 * CH), BF16),
            V((NC, 2 * CH, COLS), BF16),
            V((NC, 2 * CH, COLS), BF16),
            V((NC, COLS, CH), F32),
            V((NZ, NT, R, COLS), BF16),
            V((NZ, NT, R, COLS), BF16),
            V((NX, F, COLS), F32),
            V((NX, F, COLS), F32),
            V((NX, 2, F, COLS), BF16),
            V((NX, 2, F, COLS), BF16),
            dma((5,)),
            dma((2, NT)), dma((2, NT)),
            dma((2, NZ)), dma((2, NZ)),
            dma((2, NX)), dma((2, NX)),
            dma((NZ,)), dma((NZ,)),
            dma((NZ,)), dma((NZ,)),
            dma((NX,)), dma((NX,)),
            dma((NT,)), dma((NT,)),
        ],
        compiler_params=pltpu.CompilerParams(
            collective_id=0, has_side_effects=True, vmem_limit_bytes=62 * 1024 * 1024
        ),
    )(queries, keys, values, grad_out, lens)


def solution(mesh):
    NT = mesh.shape["tgt"]
    return jax.shard_map(
        lambda *args: body(*args, NT=NT),
        mesh=mesh,
        in_specs=(
            P(("tgt", "src"), None),
            P("src", None),
            P("src", None),
            P(("tgt", "src"), None),
            P("tgt"),
        ),
        out_specs=(P(("tgt", "src"), None), P("src", "tgt"), P("src", "tgt")),
        check_vma=False,
    )
```

```python
import jax
import jax.numpy as jnp
from jax import lax
from jax.experimental import pallas as pl
from jax.experimental.pallas import tpu as pltpu
from jax.sharding import PartitionSpec as P

MESH = pl.DeviceIdType.MESH
NX, NZ = 4, 8
COLS = 128
HALF = COLS // 2
MASK_BLOCK = 128
F32, BF16 = jnp.float32, jnp.bfloat16
HIDDEN = -1e30
SCALE = 0.125

REL = [0]
for _d in range(1, NZ // 2 + 1):
    REL += [_d] if 2 * _d == NZ else [_d, NZ - _d]
POS = {d: p for p, d in enumerate(REL)}


def kernel(
    NT, q_hbm, k_hbm, v_hbm, g_hbm, len_hbm, dq_out, dk_out, dv_out,
    len_ref, QI, GI, QGI, QG, KV, L, lrow, M, K2, KT, W, G, MR, SM, SR, CF, RT, PS, GS, Q2, G2, DQT, DQS, DQR, DK, DV, DKVS, DKVR,
    lsem, as_, ar, bs, br, cs, cr, ds_, dr, es, er, fs, fr, gs, gr,
):
    t = lax.axis_index("tgt")
    s = lax.axis_index("src")
    x = s // NZ
    z = s % NZ
    R, F = q_hbm.shape[0], k_hbm.shape[0]
    TOK = NT * R
    CH = 2 * TOK
    NC = NZ // 2

    def tpeer(d):
        return (lax.rem(t + d, NT), s)

    def zpeer(d):
        return (t, x * NZ + lax.rem(z + NZ + d, NZ))

    def diagonal(i, d):
        return (lax.rem(t + i, NT), x * NZ + lax.rem(z + NZ + d, NZ))

    def xpeer(d):
        return (t, lax.rem(x + d, NX) * NZ + z)

    def cols(i):
        return pl.ds(pl.multiple_of(i * COLS, COLS), COLS)

    def remote(src, dst, ssem, rsem, dev):
        return pltpu.make_async_remote_copy(
            src_ref=src, dst_ref=dst, send_sem=ssem, recv_sem=rsem, device_id=dev, device_id_type=MESH
        )

    local = [
        pltpu.make_async_copy(q_hbm, QI, lsem.at[0]),
        pltpu.make_async_copy(g_hbm, GI, lsem.at[1]),
        pltpu.make_async_copy(k_hbm.at[:, cols(t)], KV.at[0, 0], lsem.at[2]),
        pltpu.make_async_copy(v_hbm.at[:, cols(t)], KV.at[0, 1], lsem.at[3]),
        pltpu.make_async_copy(len_hbm, len_ref, lsem.at[4]),
    ]
    for copy in local:
        copy.start()
    barrier = pltpu.get_barrier_semaphore()
    peers = [tpeer(d) for d in range(1, NT)] + [diagonal(i, d) for i in range(1, NT) for d in (1, -1, 2, -2)]
    peers += [zpeer(d) for d in range(1, NZ)] + [xpeer(d) for d in range(1, NX)]
    for dev in peers:
        pl.semaphore_signal(barrier, inc=1, device_id=dev, device_id_type=MESH)
    pl.semaphore_wait(barrier, len(peers))

    for copy in local:
        copy.wait()
    row = len_ref[pl.ds(x, 1), :].astype(F32)
    lrow[...] = jnp.broadcast_to(row, lrow.shape)
    L[pl.ds(t, 1)] = jnp.broadcast_to(row[None], (1,) + lrow.shape)
    sent = []
    for i in range(NT):
        QGI[i, 0] = QI[:, i * COLS : (i + 1) * COLS]
        QGI[i, 1] = GI[:, i * COLS : (i + 1) * COLS]
    def straight(slot, d):
        for i in range(NT):
            remote(QGI.at[lax.rem(t + i, NT)], QG.at[slot, :, t], bs.at[0, slot], br.at[0, slot], diagonal(i, d)).start()

    def share(d):
        for part in range(2):
            sent.append(remote(KV.at[0, part], KV.at[NX - d, part], cs.at[part, d], cr.at[part, NX - d], xpeer(d)))

    straight(2, 1)
    straight(1, -1)
    share(1)
    share(NX - 1)
    for d in range(1, NT):
        sent.append(remote(lrow, L.at[t], as_.at[1, d], ar.at[1, d], tpeer(d)))
    for d in range(1, NT):
        sent.append(remote(QGI.at[lax.rem(t + d, NT)], QG.at[0, :, t], as_.at[0, d], ar.at[0, d], tpeer(d)))
    for copy in sent:
        copy.start()
    straight(4, 2)
    straight(3, -2)
    share(NX // 2)
    for copy in sent[-2:]:
        copy.start()
    for part in range(2):
        QG[0, part, pl.ds(t, 1)] = QGI[pl.ds(t, 1), part]

    onward = [
        remote(QG.at[4], QG.at[6], bs.at[0, 6], br.at[0, 6], zpeer(1)),
        remote(QG.at[3], QG.at[5], bs.at[0, 5], br.at[0, 5], zpeer(-1)),
        remote(QG.at[4, 1], QG.at[7, 1], bs.at[1, 7], br.at[1, 7], zpeer(2)),
        remote(QG.at[3, 0], QG.at[7, 0], bs.at[0, 7], br.at[0, 7], zpeer(-2)),
    ]

    def arrived(slot):
        remote(QG.at[0], QG.at[slot], bs.at[0, 3], br.at[0, slot], zpeer(1)).wait_recv()

    lane2 = lax.broadcasted_iota(jnp.int32, (1, COLS), 1)
    head = [(lane2 < COLS // 2).astype(F32), (lane2 >= COLS // 2).astype(F32)]
    rows2 = lax.broadcasted_iota(jnp.int32, (F, COLS), 0)
    lanes2 = lax.broadcasted_iota(jnp.int32, (F, COLS), 1)
    per = F // MASK_BLOCK

    def build(r):
        kb = KV[r, 0].astype(F32) * SCALE
        block_of = rows2 // MASK_BLOCK + per * r
        for h in range(2):
            mine = (lanes2 < HALF) if h == 0 else (lanes2 >= HALF)
            hot = (lanes2 == block_of + HALF * (1 - h)).astype(F32)
            K2[r, h * F : (h + 1) * F] = jnp.where(mine, kb, hot).astype(BF16)
        KT[r] = kb.T.astype(BF16)

    build(0)
    for d in range(1, NT):
        source = lax.rem(t + NT - d, NT)
        remote(lrow, L.at[source], as_.at[1, d], ar.at[1, d], tpeer(d)).wait_recv()
    lane3 = lax.broadcasted_iota(jnp.int32, (NT, R, COLS), 2)
    row3 = lax.broadcasted_iota(jnp.int32, (NT, R, COLS), 1)
    lens = jnp.broadcast_to(L[:, 0:1, :], (NT, R, COLS))
    lanes = lax.broadcasted_iota(jnp.int32, (1, 1, COLS), 2)
    first = ((lax.rem(x + lanes // per, NX) * NZ + z) * per + lax.rem(lanes, per)) * MASK_BLOCK
    first = jnp.where(lanes < per * NX, first, -1).astype(F32)

    def mask_slot(p, rel):
        pick = lax.rem(z + rel, NZ) * R + row3
        column = jnp.sum(jnp.where(lane3 == pick, lens, 0.0), axis=2, keepdims=True)
        M[p] = jnp.where(first >= column, HIDDEN, 0.0).reshape(TOK, COLS).T[0:HALF].astype(BF16)

    for p in range(NZ):
        mask_slot(p, REL[p])

    for d in range(1, NT):
        source = lax.rem(t + NT - d, NT)
        remote(QGI.at[0], QG.at[0, :, source], as_.at[0, d], ar.at[0, d], tpeer(d)).wait_recv()

    arrived(1)

    masks = [m.astype(BF16) for m in head]

    def block(ref, c, which):
        return ref[pl.ds(2 * c, 2), which].reshape(CH, COLS)

    def pass_on():
        for slot in (2, 3, 4):
            arrived(slot)
        for copy in onward:
            copy.start()

    def pass1(c, fresh):
        qt, gt = block(QG, c, 0).T, block(QG, c, 1).T
        mt = jnp.concatenate([M[2 * c], M[2 * c + 1]], axis=1)
        none = jnp.zeros((HALF, CH), BF16)
        qts = [jnp.concatenate([qt[0:HALF], mt], axis=0), jnp.concatenate([mt, qt[HALF:COLS]], axis=0)]
        gts = [jnp.concatenate([gt[0:HALF], none], axis=0), jnp.concatenate([none, gt[HALF:COLS]], axis=0)]
        for h in range(2):
            rows = slice(h * CH, (h + 1) * CH)
            Q2[c, rows] = block(QG, c, 0) * masks[h]
            G2[c, rows] = block(QG, c, 1) * masks[h]
        found = [[] for _ in range(4)]

        def products(r, h):
            rows = slice(h * F, (h + 1) * F)
            W[c, r, h] = jnp.dot(K2[r, rows], qts[h], preferred_element_type=F32)
            G[c, r, h] = jnp.dot(KV[r, 1], gts[h], preferred_element_type=F32)

        def reduce(r, h):
            for half in range(2):
                piece = slice(half * TOK, (half + 1) * TOK)
                sc = W[c, r, h, :, piece]
                m = jnp.max(sc, axis=0, keepdims=True)
                w = jnp.exp(sc - m)
                W[c, r, h, :, piece] = w
                MR[c, 2 * r + h : 2 * r + h + 1, piece] = m
                l = jnp.sum(w, axis=0, keepdims=True)
                found[2 * h + half].append((m, l, jnp.sum(w * G[c, r, h, :, piece], axis=0, keepdims=True)))

        order = [(r, h) for r in (0, 1, NX - 1, NX // 2) for h in range(2)]
        products(*order[0])
        for now, later in zip(order, order[1:] + [None]):
            wait = fresh and later is not None and later[1] == 0
            if wait:
                reduce(*now)
                r = later[0]
                if r == NX // 2:
                    pass_on()
                for part in range(2):
                    remote(KV.at[0, part], KV.at[r, part], cs.at[part, r], cr.at[part, r], xpeer(r)).wait_recv()
                build(r)
            if later is not None:
                products(*later)
            if not wait:
                reduce(*now)
        for h in range(2):
            for half in range(2):
                top = found[2 * h + half][0][0]
                for m, _, _ in found[2 * h + half][1:]:
                    top = jnp.maximum(top, m)
                total = jnp.zeros_like(top)
                term = jnp.zeros_like(top)
                for m, l, tt in found[2 * h + half]:
                    a = jnp.exp(m - top)
                    total += a * l
                    term += a * tt
                row = 2 * half + h
                SM[c, row : row + 1, :] = top + jnp.log(total)
                SM[c, 4 + row : 5 + row, :] = term / total
        for d in REL[1:]:
            remote(SM.at[c], SR.at[NZ - d, c], ds_.at[d], dr.at[NZ - d], zpeer(d)).start()

        @pl.when(c == 1)
        def _():
            arrived(5)

        @pl.when(c == 2)
        def _():
            arrived(6)
            for part in range(2):
                onward[3 - part].wait_recv()

        return 0

    pass1(0, True)
    lax.fori_loop(1, NC, lambda c, _: pass1(c, False), 0)

    for d in range(1, NZ):
        remote(SM, SR.at[d], ds_.at[d], dr.at[d], zpeer(d)).wait_recv()

    def combine(p):
        parts, terms = [], []
        for d in range(NZ):
            theirs = POS[(REL[p] - d) % NZ]
            ref = SM if d == 0 else SR.at[d]
            row = 2 * (theirs % 2)
            parts.append(ref[theirs // 2, row : row + 2, :])
            terms.append(ref[theirs // 2, 4 + row : 6 + row, :])
        top = parts[0]
        for part in parts[1:]:
            top = jnp.maximum(top, part)
        total = jnp.zeros_like(top)
        term = jnp.zeros_like(top)
        for part, other in zip(parts, terms):
            weight = jnp.exp(part - top)
            total += weight
            term += weight * other
        CF[:, p * TOK : (p + 1) * TOK] = top + jnp.log(total)
        RT[:, p * TOK : (p + 1) * TOK] = term / total


    def make(c, r):
        piece = slice(c * CH, (c + 1) * CH)
        for h in range(2):
            cf = jnp.exp(MR[c, 2 * r + h : 2 * r + h + 1, :] - CF[h : h + 1, piece])
            term = RT[h : h + 1, piece]
            for lo in range(0, F, 64):
                rows = slice(lo, lo + 64)
                p = W[c, r, h, rows, :] * cf
                PS[c, r, rows, h * CH : (h + 1) * CH] = p.astype(BF16)
                GS[c, r, rows, h * CH : (h + 1) * CH] = (p * (G[c, r, h, rows, :] - term)).astype(BF16)

    def use(c, r):
        first = c == NC - 1
        dv = jnp.dot(PS[c, r], G2[c], preferred_element_type=F32)
        dk = jnp.dot(GS[c, r], Q2[c], preferred_element_type=F32)
        DV[r] = dv if first else DV[r] + dv
        DK[r] = dk if first else DK[r] + dk
        for h in range(2):
            out = slice(h * HALF, (h + 1) * HALF)
            dq = jnp.dot(KT[r, out], GS[c, r, :, h * CH : (h + 1) * CH], preferred_element_type=F32)
            DQT[c, out] = dq if r == ORDER[0] else DQT[c, out] + dq

    def send_dq(p):
        d = REL[p]
        for i in range(NT):
            if p > 0 or i > 0:
                there = lax.rem(t + i, NT)
                remote(
                    DQS.at[p, there], DQR.at[(NZ - d) % NZ, t],
                    es.at[d] if d else gs.at[i], er.at[(NZ - d) % NZ] if d else gr.at[i],
                    (there, x * NZ + lax.rem(z + d, NZ)),
                ).start()

    def done_dq(c):
        DQS[2 * c : 2 * c + 2] = DQT[c].T.astype(BF16).reshape(2, NT, R, COLS)
        send_dq(2 * c + 1)
        send_dq(2 * c)

    def done_kv(r):
        DKVS[r, 0] = DK[r].astype(BF16)
        DKVS[r, 1] = DV[r].astype(BF16)
        sent.append(remote(DKVS.at[r], DKVR.at[NX - r], fs.at[r], fr.at[NX - r], xpeer(r)))
        sent[-1].start()

    ORDER = [NX // 2] + [i for i in range(1, NX) if i != NX // 2] + [0]
    steps = [(c, r) for c in range(NC - 1, 1, -1) for r in ORDER] + [(c, r) for r in ORDER for c in (1, 0)]
    early = list(sent)
    sent.clear()
    combine(NZ - 2)
    combine(NZ - 1)
    make(*steps[0])
    for p in range(NZ - 2):
        combine(p)
    for (c, r), later in zip(steps, steps[1:] + [None]):
        if later is not None:
            make(*later)
        use(c, r)
        if r == ORDER[-1]:
            done_dq(c)
        if c == 0 and r > 0:
            done_kv(r)
    DQR[0, pl.ds(t, 1)] = DQS[0, pl.ds(t, 1)]

    for copy in early:
        copy.wait_send()
    for slot in range(1, 5):
        remote(QGI, QG.at[slot], bs.at[0, slot], br.at[0, slot], zpeer(1)).wait_send()
    for copy in onward:
        copy.wait_send()
    for d in range(1, NZ):
        remote(SM, SR.at[NZ - d], ds_.at[d], dr.at[NZ - d], zpeer(d)).wait_send()
    for d in range(1, NX):
        remote(DKVS.at[d], DKVR.at[d], fs.at[d], fr.at[d], xpeer(d)).wait_recv()
    dk, dv = DK[0], DV[0]
    for d in range(1, NX):
        dk += DKVR[d, 0].astype(F32)
        dv += DKVR[d, 1].astype(F32)
    dk_out[...] = dk * SCALE
    dv_out[...] = dv

    for d in range(1, NT):
        source = lax.rem(t + NT - d, NT)
        remote(DQS.at[0, 0], DQR.at[0, source], gs.at[d], gr.at[d], tpeer(d)).wait_recv()
    for d in range(1, NZ):
        remote(DQS.at[POS[d]], DQR.at[d], es.at[d], er.at[d], zpeer(d)).wait_recv()
    for i in range(NT):
        dq = DQR[0, i].astype(F32)
        for d in range(1, NZ):
            dq += DQR[d, i].astype(F32)
        dq_out[:, i * COLS : (i + 1) * COLS] = dq
    for copy in sent:
        copy.wait_send()
    for d in range(1, NT):
        remote(DQS.at[0, 0], DQR.at[0, 0], gs.at[d], gr.at[d], tpeer(d)).wait_send()
    for d in range(1, NZ):
        remote(DQS.at[POS[d]], DQR.at[d], es.at[d], er.at[d], zpeer(d)).wait_send()


def body(queries, keys, values, grad_out, read_len, *, NT):
    R, D = queries.shape
    F = keys.shape[0]
    TOK, CH, NC = NT * R, 2 * NT * R, NZ // 2
    lens = read_len.reshape(NX, NZ * R)
    hbm = pl.BlockSpec(memory_space=pltpu.HBM)
    vmem = pl.BlockSpec(memory_space=pltpu.VMEM)
    dma = pltpu.SemaphoreType.DMA
    V = pltpu.VMEM
    return pl.pallas_call(
        lambda *refs: kernel(NT, *refs),
        out_shape=(V((R, D), F32), V((F, COLS), F32), V((F, COLS), F32)),
        in_specs=[hbm] * 5,
        out_specs=(vmem, vmem, vmem),
        scratch_shapes=[
            V((NX, NZ * R), jnp.int32),
            V((R, D), BF16),
            V((R, D), BF16),
            V((NT, 2, R, COLS), BF16),
            V((NZ, 2, NT, R, COLS), BF16),
            V((NX, 2, F, COLS), BF16),
            V((NT, 8, COLS), F32),
            V((8, COLS), F32),
            V((NZ, HALF, TOK), BF16),
            V((NX, 2 * F, COLS), BF16),
            V((NX, COLS, F), BF16),
            V((NC, NX, 2, F, CH), F32),
            V((NC, NX, 2, F, CH), F32),
            V((NC, 2 * NX, CH), F32),
            V((NC, 8, TOK), F32),
            V((NZ, NC, 8, TOK), F32),
            V((2, NZ * TOK), F32),
            V((2, NZ * TOK), F32),
            V((NC, NX, F, 2 * CH), BF16),
            V((NC, NX, F, 2 * CH), BF16),
            V((NC, 2 * CH, COLS), BF16),
            V((NC, 2 * CH, COLS), BF16),
            V((NC, COLS, CH), F32),
            V((NZ, NT, R, COLS), BF16),
            V((NZ, NT, R, COLS), BF16),
            V((NX, F, COLS), F32),
            V((NX, F, COLS), F32),
            V((NX, 2, F, COLS), BF16),
            V((NX, 2, F, COLS), BF16),
            dma((5,)),
            dma((2, NT)), dma((2, NT)),
            dma((2, NZ)), dma((2, NZ)),
            dma((2, NX)), dma((2, NX)),
            dma((NZ,)), dma((NZ,)),
            dma((NZ,)), dma((NZ,)),
            dma((NX,)), dma((NX,)),
            dma((NT,)), dma((NT,)),
        ],
        compiler_params=pltpu.CompilerParams(
            collective_id=0, has_side_effects=True, vmem_limit_bytes=62 * 1024 * 1024
        ),
    )(queries, keys, values, grad_out, lens)


def solution(mesh):
    NT = mesh.shape["tgt"]
    return jax.shard_map(
        lambda *args: body(*args, NT=NT),
        mesh=mesh,
        in_specs=(
            P(("tgt", "src"), None),
            P("src", None),
            P("src", None),
            P(("tgt", "src"), None),
            P("tgt"),
        ),
        out_specs=(P(("tgt", "src"), None), P("src", "tgt"), P("src", "tgt")),
        check_vma=False,
    )
```

```python
import jax
import jax.numpy as jnp
from jax import lax
from jax.experimental import pallas as pl
from jax.experimental.pallas import tpu as pltpu
from jax.sharding import PartitionSpec as P

MESH = pl.DeviceIdType.MESH
NX, NZ = 4, 8
COLS = 128
HALF = COLS // 2
MASK_BLOCK = 128
F32, BF16 = jnp.float32, jnp.bfloat16
HIDDEN = -1e30
SCALE = 0.125

REL = [0]
for _d in range(1, NZ // 2 + 1):
    REL += [_d] if 2 * _d == NZ else [_d, NZ - _d]
POS = {d: p for p, d in enumerate(REL)}


def kernel(
    NT, q_hbm, k_hbm, v_hbm, g_hbm, len_hbm, dq_out, dk_out, dv_out,
    len_ref, QI, GI, QGI, QG, KV, L, lrow, M, K2, KT, W, G, MR, SM, SR, CF, RT, PS, GS, Q2, G2, DQT, DQS, DQR, DK, DV, DKVS, DKVR,
    lsem, as_, ar, bs, br, cs, cr, ds_, dr, es, er, fs, fr, gs, gr,
):
    t = lax.axis_index("tgt")
    s = lax.axis_index("src")
    x = s // NZ
    z = s % NZ
    R, F = q_hbm.shape[0], k_hbm.shape[0]
    TOK = NT * R
    CH = 2 * TOK
    NC = NZ // 2

    def tpeer(d):
        return (lax.rem(t + d, NT), s)

    def zpeer(d):
        return (t, x * NZ + lax.rem(z + NZ + d, NZ))

    def diagonal(i, d):
        return (lax.rem(t + i, NT), x * NZ + lax.rem(z + NZ + d, NZ))

    def xpeer(d):
        return (t, lax.rem(x + d, NX) * NZ + z)

    def cols(i):
        return pl.ds(pl.multiple_of(i * COLS, COLS), COLS)

    def remote(src, dst, ssem, rsem, dev):
        return pltpu.make_async_remote_copy(
            src_ref=src, dst_ref=dst, send_sem=ssem, recv_sem=rsem, device_id=dev, device_id_type=MESH
        )

    local = [
        pltpu.make_async_copy(q_hbm, QI, lsem.at[0]),
        pltpu.make_async_copy(g_hbm, GI, lsem.at[1]),
        pltpu.make_async_copy(k_hbm.at[:, cols(t)], KV.at[0, 0], lsem.at[2]),
        pltpu.make_async_copy(v_hbm.at[:, cols(t)], KV.at[0, 1], lsem.at[3]),
        pltpu.make_async_copy(len_hbm, len_ref, lsem.at[4]),
    ]
    for copy in local:
        copy.start()
    barrier = pltpu.get_barrier_semaphore()
    peers = [tpeer(d) for d in range(1, NT)] + [diagonal(i, d) for i in range(1, NT) for d in (1, -1, 2, -2)]
    peers += [zpeer(d) for d in range(1, NZ)] + [xpeer(d) for d in range(1, NX)]
    for dev in peers:
        pl.semaphore_signal(barrier, inc=1, device_id=dev, device_id_type=MESH)
    pl.semaphore_wait(barrier, len(peers))

    for copy in local:
        copy.wait()
    row = len_ref[pl.ds(x, 1), :].astype(F32)
    lrow[...] = jnp.broadcast_to(row, lrow.shape)
    L[pl.ds(t, 1)] = jnp.broadcast_to(row[None], (1,) + lrow.shape)
    sent = []
    for i in range(NT):
        QGI[i, 0] = QI[:, i * COLS : (i + 1) * COLS]
        QGI[i, 1] = GI[:, i * COLS : (i + 1) * COLS]
    def straight(slot, d):
        for i in range(NT):
            remote(QGI.at[lax.rem(t + i, NT)], QG.at[slot, :, t], bs.at[0, slot], br.at[0, slot], diagonal(i, d)).start()

    def share(d):
        for part in range(2):
            sent.append(remote(KV.at[0, part], KV.at[NX - d, part], cs.at[part, d], cr.at[part, NX - d], xpeer(d)))

    straight(2, 1)
    straight(1, -1)
    share(1)
    share(NX - 1)
    for d in range(1, NT):
        sent.append(remote(lrow, L.at[t], as_.at[1, d], ar.at[1, d], tpeer(d)))
    for d in range(1, NT):
        sent.append(remote(QGI.at[lax.rem(t + d, NT)], QG.at[0, :, t], as_.at[0, d], ar.at[0, d], tpeer(d)))
    for copy in sent:
        copy.start()
    straight(4, 2)
    straight(3, -2)
    share(NX // 2)
    for copy in sent[-2:]:
        copy.start()
    for part in range(2):
        QG[0, part, pl.ds(t, 1)] = QGI[pl.ds(t, 1), part]

    onward = [
        remote(QG.at[4], QG.at[6], bs.at[0, 6], br.at[0, 6], zpeer(1)),
        remote(QG.at[3], QG.at[5], bs.at[0, 5], br.at[0, 5], zpeer(-1)),
        remote(QG.at[4, 1], QG.at[7, 1], bs.at[1, 7], br.at[1, 7], zpeer(2)),
        remote(QG.at[3, 0], QG.at[7, 0], bs.at[0, 7], br.at[0, 7], zpeer(-2)),
    ]

    def arrived(slot):
        remote(QG.at[0], QG.at[slot], bs.at[0, 3], br.at[0, slot], zpeer(1)).wait_recv()

    lane2 = lax.broadcasted_iota(jnp.int32, (1, COLS), 1)
    head = [(lane2 < COLS // 2).astype(F32), (lane2 >= COLS // 2).astype(F32)]
    rows2 = lax.broadcasted_iota(jnp.int32, (F, COLS), 0)
    lanes2 = lax.broadcasted_iota(jnp.int32, (F, COLS), 1)
    per = F // MASK_BLOCK

    def build(r):
        kb = KV[r, 0].astype(F32) * SCALE
        block_of = rows2 // MASK_BLOCK + per * r
        for h in range(2):
            mine = (lanes2 < HALF) if h == 0 else (lanes2 >= HALF)
            hot = (lanes2 == block_of + HALF * (1 - h)).astype(F32)
            K2[r, h * F : (h + 1) * F] = jnp.where(mine, kb, hot).astype(BF16)
        KT[r] = kb.T.astype(BF16)

    build(0)
    for d in range(1, NT):
        source = lax.rem(t + NT - d, NT)
        remote(lrow, L.at[source], as_.at[1, d], ar.at[1, d], tpeer(d)).wait_recv()
    lane3 = lax.broadcasted_iota(jnp.int32, (NT, R, COLS), 2)
    row3 = lax.broadcasted_iota(jnp.int32, (NT, R, COLS), 1)
    lens = jnp.broadcast_to(L[:, 0:1, :], (NT, R, COLS))
    lanes = lax.broadcasted_iota(jnp.int32, (1, 1, COLS), 2)
    first = ((lax.rem(x + lanes // per, NX) * NZ + z) * per + lax.rem(lanes, per)) * MASK_BLOCK
    first = jnp.where(lanes < per * NX, first, -1).astype(F32)

    def mask_slot(p, rel):
        pick = lax.rem(z + rel, NZ) * R + row3
        column = jnp.sum(jnp.where(lane3 == pick, lens, 0.0), axis=2, keepdims=True)
        M[p] = jnp.where(first >= column, HIDDEN, 0.0).reshape(TOK, COLS).T[0:HALF].astype(BF16)

    for p in range(2):
        mask_slot(p, REL[p])

    for d in range(1, NT):
        source = lax.rem(t + NT - d, NT)
        remote(QGI.at[0], QG.at[0, :, source], as_.at[0, d], ar.at[0, d], tpeer(d)).wait_recv()

    arrived(1)

    masks = [m.astype(BF16) for m in head]

    def block(ref, c, which):
        return ref[pl.ds(2 * c, 2), which].reshape(CH, COLS)

    def pass_on():
        arrived(4)
        onward[0].start()
        onward[2].start()
        arrived(3)
        onward[1].start()
        onward[3].start()

    def pass1(c, fresh):
        qt, gt = block(QG, c, 0).T, block(QG, c, 1).T
        mt = jnp.concatenate([M[2 * c], M[2 * c + 1]], axis=1)
        none = jnp.zeros((HALF, CH), BF16)
        qts = [jnp.concatenate([qt[0:HALF], mt], axis=0), jnp.concatenate([mt, qt[HALF:COLS]], axis=0)]
        gts = [jnp.concatenate([gt[0:HALF], none], axis=0), jnp.concatenate([none, gt[HALF:COLS]], axis=0)]
        for h in range(2):
            rows = slice(h * CH, (h + 1) * CH)
            Q2[c, rows] = block(QG, c, 0) * masks[h]
            G2[c, rows] = block(QG, c, 1) * masks[h]
        found = [[] for _ in range(4)]

        def products(r, h):
            rows = slice(h * F, (h + 1) * F)
            W[c, r, h] = jnp.dot(K2[r, rows], qts[h], preferred_element_type=F32)
            G[c, r, h] = jnp.dot(KV[r, 1], gts[h], preferred_element_type=F32)

        def reduce(r, h):
            for half in range(2):
                piece = slice(half * TOK, (half + 1) * TOK)
                sc = W[c, r, h, :, piece]
                m = jnp.max(sc, axis=0, keepdims=True)
                w = jnp.exp(sc - m)
                W[c, r, h, :, piece] = w
                MR[c, 2 * r + h : 2 * r + h + 1, piece] = m
                l = jnp.sum(w, axis=0, keepdims=True)
                found[2 * h + half].append((m, l, jnp.sum(w * G[c, r, h, :, piece], axis=0, keepdims=True)))

        order = [(r, h) for r in (0, 1, NX - 1, NX // 2) for h in range(2)]
        products(*order[0])
        for now, later in zip(order, order[1:] + [None]):
            wait = fresh and later is not None and later[1] == 0
            if wait:
                reduce(*now)
                r = later[0]
                if r == NX // 2:
                    pass_on()
                    for p in range(2, NZ):
                        mask_slot(p, REL[p])
                    arrived(2)
                for part in range(2):
                    remote(KV.at[0, part], KV.at[r, part], cs.at[part, r], cr.at[part, r], xpeer(r)).wait_recv()
                build(r)
            if later is not None:
                products(*later)
            if not wait:
                reduce(*now)
        for h in range(2):
            for half in range(2):
                top = found[2 * h + half][0][0]
                for m, _, _ in found[2 * h + half][1:]:
                    top = jnp.maximum(top, m)
                total = jnp.zeros_like(top)
                term = jnp.zeros_like(top)
                for m, l, tt in found[2 * h + half]:
                    a = jnp.exp(m - top)
                    total += a * l
                    term += a * tt
                row = 2 * half + h
                SM[c, row : row + 1, :] = top + jnp.log(total)
                SM[c, 4 + row : 5 + row, :] = term / total
        for d in REL[1:]:
            remote(SM.at[c], SR.at[NZ - d, c], ds_.at[d], dr.at[NZ - d], zpeer(d)).start()

        @pl.when(c == 1)
        def _():
            arrived(5)

        @pl.when(c == 2)
        def _():
            arrived(6)
            for part in range(2):
                onward[3 - part].wait_recv()

        return 0

    pass1(0, True)
    lax.fori_loop(1, NC, lambda c, _: pass1(c, False), 0)

    for d in range(1, NZ):
        remote(SM, SR.at[d], ds_.at[d], dr.at[d], zpeer(d)).wait_recv()

    def combine(p):
        parts, terms = [], []
        for d in range(NZ):
            theirs = POS[(REL[p] - d) % NZ]
            ref = SM if d == 0 else SR.at[d]
            row = 2 * (theirs % 2)
            parts.append(ref[theirs // 2, row : row + 2, :])
            terms.append(ref[theirs // 2, 4 + row : 6 + row, :])
        top = parts[0]
        for part in parts[1:]:
            top = jnp.maximum(top, part)
        total = jnp.zeros_like(top)
        term = jnp.zeros_like(top)
        for part, other in zip(parts, terms):
            weight = jnp.exp(part - top)
            total += weight
            term += weight * other
        CF[:, p * TOK : (p + 1) * TOK] = top + jnp.log(total)
        RT[:, p * TOK : (p + 1) * TOK] = term / total


    def make(c, r):
        piece = slice(c * CH, (c + 1) * CH)
        for h in range(2):
            cf = jnp.exp(MR[c, 2 * r + h : 2 * r + h + 1, :] - CF[h : h + 1, piece])
            term = RT[h : h + 1, piece]
            for lo in range(0, F, 64):
                rows = slice(lo, lo + 64)
                p = W[c, r, h, rows, :] * cf
                PS[c, r, rows, h * CH : (h + 1) * CH] = p.astype(BF16)
                GS[c, r, rows, h * CH : (h + 1) * CH] = (p * (G[c, r, h, rows, :] - term)).astype(BF16)

    def use(c, r):
        first = c == NC - 1
        dv = jnp.dot(PS[c, r], G2[c], preferred_element_type=F32)
        dk = jnp.dot(GS[c, r], Q2[c], preferred_element_type=F32)
        DV[r] = dv if first else DV[r] + dv
        DK[r] = dk if first else DK[r] + dk
        for h in range(2):
            out = slice(h * HALF, (h + 1) * HALF)
            dq = jnp.dot(KT[r, out], GS[c, r, :, h * CH : (h + 1) * CH], preferred_element_type=F32)
            DQT[c, out] = dq if r == ORDER[0] else DQT[c, out] + dq

    def send_dq(p):
        d = REL[p]
        for i in range(NT):
            if p > 0 or i > 0:
                there = lax.rem(t + i, NT)
                remote(
                    DQS.at[p, there], DQR.at[(NZ - d) % NZ, t],
                    es.at[d] if d else gs.at[i], er.at[(NZ - d) % NZ] if d else gr.at[i],
                    (there, x * NZ + lax.rem(z + d, NZ)),
                ).start()

    def done_dq(c):
        DQS[2 * c : 2 * c + 2] = DQT[c].T.astype(BF16).reshape(2, NT, R, COLS)
        send_dq(2 * c + 1)
        send_dq(2 * c)

    def done_kv(r):
        DKVS[r, 0] = DK[r].astype(BF16)
        DKVS[r, 1] = DV[r].astype(BF16)
        sent.append(remote(DKVS.at[r], DKVR.at[NX - r], fs.at[r], fr.at[NX - r], xpeer(r)))
        sent[-1].start()

    ORDER = [NX // 2] + [i for i in range(1, NX) if i != NX // 2] + [0]
    steps = [(c, r) for c in range(NC - 1, 1, -1) for r in ORDER] + [(c, r) for r in ORDER for c in (1, 0)]
    early = list(sent)
    sent.clear()
    combine(NZ - 2)
    combine(NZ - 1)
    make(*steps[0])
    for p in range(NZ - 2):
        combine(p)
    for (c, r), later in zip(steps, steps[1:] + [None]):
        if later is not None:
            make(*later)
        use(c, r)
        if r == ORDER[-1]:
            done_dq(c)
        if c == 0 and r > 0:
            done_kv(r)
    DQR[0, pl.ds(t, 1)] = DQS[0, pl.ds(t, 1)]

    for copy in early:
        copy.wait_send()
    for slot in range(1, 5):
        remote(QGI, QG.at[slot], bs.at[0, slot], br.at[0, slot], zpeer(1)).wait_send()
    for copy in onward:
        copy.wait_send()
    for d in range(1, NZ):
        remote(SM, SR.at[NZ - d], ds_.at[d], dr.at[NZ - d], zpeer(d)).wait_send()
    for d in range(1, NX):
        remote(DKVS.at[d], DKVR.at[d], fs.at[d], fr.at[d], xpeer(d)).wait_recv()
    dk, dv = DK[0], DV[0]
    for d in range(1, NX):
        dk += DKVR[d, 0].astype(F32)
        dv += DKVR[d, 1].astype(F32)
    dk_out[...] = dk * SCALE
    dv_out[...] = dv

    for d in range(1, NT):
        source = lax.rem(t + NT - d, NT)
        remote(DQS.at[0, 0], DQR.at[0, source], gs.at[d], gr.at[d], tpeer(d)).wait_recv()
    for d in range(1, NZ):
        remote(DQS.at[POS[d]], DQR.at[d], es.at[d], er.at[d], zpeer(d)).wait_recv()
    for i in range(NT):
        dq = DQR[0, i].astype(F32)
        for d in range(1, NZ):
            dq += DQR[d, i].astype(F32)
        dq_out[:, i * COLS : (i + 1) * COLS] = dq
    for copy in sent:
        copy.wait_send()
    for d in range(1, NT):
        remote(DQS.at[0, 0], DQR.at[0, 0], gs.at[d], gr.at[d], tpeer(d)).wait_send()
    for d in range(1, NZ):
        remote(DQS.at[POS[d]], DQR.at[d], es.at[d], er.at[d], zpeer(d)).wait_send()


def body(queries, keys, values, grad_out, read_len, *, NT):
    R, D = queries.shape
    F = keys.shape[0]
    TOK, CH, NC = NT * R, 2 * NT * R, NZ // 2
    lens = read_len.reshape(NX, NZ * R)
    hbm = pl.BlockSpec(memory_space=pltpu.HBM)
    vmem = pl.BlockSpec(memory_space=pltpu.VMEM)
    dma = pltpu.SemaphoreType.DMA
    V = pltpu.VMEM
    return pl.pallas_call(
        lambda *refs: kernel(NT, *refs),
        out_shape=(V((R, D), F32), V((F, COLS), F32), V((F, COLS), F32)),
        in_specs=[hbm] * 5,
        out_specs=(vmem, vmem, vmem),
        scratch_shapes=[
            V((NX, NZ * R), jnp.int32),
            V((R, D), BF16),
            V((R, D), BF16),
            V((NT, 2, R, COLS), BF16),
            V((NZ, 2, NT, R, COLS), BF16),
            V((NX, 2, F, COLS), BF16),
            V((NT, 8, COLS), F32),
            V((8, COLS), F32),
            V((NZ, HALF, TOK), BF16),
            V((NX, 2 * F, COLS), BF16),
            V((NX, COLS, F), BF16),
            V((NC, NX, 2, F, CH), F32),
            V((NC, NX, 2, F, CH), F32),
            V((NC, 2 * NX, CH), F32),
            V((NC, 8, TOK), F32),
            V((NZ, NC, 8, TOK), F32),
            V((2, NZ * TOK), F32),
            V((2, NZ * TOK), F32),
            V((NC, NX, F, 2 * CH), BF16),
            V((NC, NX, F, 2 * CH), BF16),
            V((NC, 2 * CH, COLS), BF16),
            V((NC, 2 * CH, COLS), BF16),
            V((NC, COLS, CH), F32),
            V((NZ, NT, R, COLS), BF16),
            V((NZ, NT, R, COLS), BF16),
            V((NX, F, COLS), F32),
            V((NX, F, COLS), F32),
            V((NX, 2, F, COLS), BF16),
            V((NX, 2, F, COLS), BF16),
            dma((5,)),
            dma((2, NT)), dma((2, NT)),
            dma((2, NZ)), dma((2, NZ)),
            dma((2, NX)), dma((2, NX)),
            dma((NZ,)), dma((NZ,)),
            dma((NZ,)), dma((NZ,)),
            dma((NX,)), dma((NX,)),
            dma((NT,)), dma((NT,)),
        ],
        compiler_params=pltpu.CompilerParams(
            collective_id=0, has_side_effects=True, vmem_limit_bytes=62 * 1024 * 1024
        ),
    )(queries, keys, values, grad_out, lens)


def solution(mesh):
    NT = mesh.shape["tgt"]
    return jax.shard_map(
        lambda *args: body(*args, NT=NT),
        mesh=mesh,
        in_specs=(
            P(("tgt", "src"), None),
            P("src", None),
            P("src", None),
            P(("tgt", "src"), None),
            P("tgt"),
        ),
        out_specs=(P(("tgt", "src"), None), P("src", "tgt"), P("src", "tgt")),
        check_vma=False,
    )
```

```python
import jax
import jax.numpy as jnp
from jax import lax
from jax.experimental import pallas as pl
from jax.experimental.pallas import tpu as pltpu
from jax.sharding import PartitionSpec as P

MESH = pl.DeviceIdType.MESH
NX, NZ = 4, 8
COLS = 128
HALF = COLS // 2
MASK_BLOCK = 128
F32, BF16 = jnp.float32, jnp.bfloat16
HIDDEN = -1e30
SCALE = 0.125

REL = [0]
for _d in range(1, NZ // 2 + 1):
    REL += [_d] if 2 * _d == NZ else [_d, NZ - _d]
POS = {d: p for p, d in enumerate(REL)}


def kernel(
    NT, q_hbm, k_hbm, v_hbm, g_hbm, len_hbm, dq_out, dk_out, dv_out,
    len_ref, QI, GI, QGI, QG, KV, L, lrow, M, K2, KT, W, G, MR, SM, SR, CF, RT, PS, GS, Q2, G2, DQT, DQS, DQR, DK, DV, DKVS, DKVR,
    lsem, as_, ar, bs, br, cs, cr, ds_, dr, es, er, fs, fr, gs, gr,
):
    t = lax.axis_index("tgt")
    s = lax.axis_index("src")
    x = s // NZ
    z = s % NZ
    R, F = q_hbm.shape[0], k_hbm.shape[0]
    TOK = NT * R
    CH = 2 * TOK
    NC = NZ // 2

    def tpeer(d):
        return (lax.rem(t + d, NT), s)

    def zpeer(d):
        return (t, x * NZ + lax.rem(z + NZ + d, NZ))

    def diagonal(i, d):
        return (lax.rem(t + i, NT), x * NZ + lax.rem(z + NZ + d, NZ))

    def xpeer(d):
        return (t, lax.rem(x + d, NX) * NZ + z)

    def cols(i):
        return pl.ds(pl.multiple_of(i * COLS, COLS), COLS)

    def remote(src, dst, ssem, rsem, dev):
        return pltpu.make_async_remote_copy(
            src_ref=src, dst_ref=dst, send_sem=ssem, recv_sem=rsem, device_id=dev, device_id_type=MESH
        )

    local = [
        pltpu.make_async_copy(q_hbm, QI, lsem.at[0]),
        pltpu.make_async_copy(g_hbm, GI, lsem.at[1]),
        pltpu.make_async_copy(k_hbm.at[:, cols(t)], KV.at[0, 0], lsem.at[2]),
        pltpu.make_async_copy(v_hbm.at[:, cols(t)], KV.at[0, 1], lsem.at[3]),
        pltpu.make_async_copy(len_hbm, len_ref, lsem.at[4]),
    ]
    for copy in local:
        copy.start()
    barrier = pltpu.get_barrier_semaphore()
    peers = [tpeer(d) for d in range(1, NT)] + [diagonal(i, d) for i in range(1, NT) for d in (1, -1, 2, -2)]
    peers += [zpeer(d) for d in range(1, NZ)] + [xpeer(d) for d in range(1, NX)]
    for dev in peers:
        pl.semaphore_signal(barrier, inc=1, device_id=dev, device_id_type=MESH)
    pl.semaphore_wait(barrier, len(peers))

    for copy in local:
        copy.wait()
    row = len_ref[pl.ds(x, 1), :].astype(F32)
    lrow[...] = jnp.broadcast_to(row, lrow.shape)
    L[pl.ds(t, 1)] = jnp.broadcast_to(row[None], (1,) + lrow.shape)
    sent = []
    for i in range(NT):
        QGI[i, 0] = QI[:, i * COLS : (i + 1) * COLS]
        QGI[i, 1] = GI[:, i * COLS : (i + 1) * COLS]
    def straight(slot, d):
        for i in range(NT):
            remote(QGI.at[lax.rem(t + i, NT)], QG.at[slot, :, t], bs.at[0, slot], br.at[0, slot], diagonal(i, d)).start()

    def share(d):
        for part in range(2):
            sent.append(remote(KV.at[0, part], KV.at[NX - d, part], cs.at[part, d], cr.at[part, NX - d], xpeer(d)))

    straight(2, 1)
    straight(1, -1)
    share(1)
    share(NX - 1)
    for d in range(1, NT):
        sent.append(remote(lrow, L.at[t], as_.at[1, d], ar.at[1, d], tpeer(d)))
    for d in range(1, NT):
        sent.append(remote(QGI.at[lax.rem(t + d, NT)], QG.at[0, :, t], as_.at[0, d], ar.at[0, d], tpeer(d)))
    for copy in sent:
        copy.start()
    straight(4, 2)
    straight(3, -2)
    share(NX // 2)
    for copy in sent[-2:]:
        copy.start()
    for part in range(2):
        QG[0, part, pl.ds(t, 1)] = QGI[pl.ds(t, 1), part]

    onward = [
        remote(QG.at[4], QG.at[6], bs.at[0, 6], br.at[0, 6], zpeer(1)),
        remote(QG.at[3], QG.at[5], bs.at[0, 5], br.at[0, 5], zpeer(-1)),
        remote(QG.at[4, 1], QG.at[7, 1], bs.at[1, 7], br.at[1, 7], zpeer(2)),
        remote(QG.at[3, 0], QG.at[7, 0], bs.at[0, 7], br.at[0, 7], zpeer(-2)),
    ]

    def arrived(slot):
        remote(QG.at[0], QG.at[slot], bs.at[0, 3], br.at[0, slot], zpeer(1)).wait_recv()

    lane2 = lax.broadcasted_iota(jnp.int32, (1, COLS), 1)
    head = [(lane2 < COLS // 2).astype(F32), (lane2 >= COLS // 2).astype(F32)]
    rows2 = lax.broadcasted_iota(jnp.int32, (F, COLS), 0)
    lanes2 = lax.broadcasted_iota(jnp.int32, (F, COLS), 1)
    per = F // MASK_BLOCK

    def build(r):
        kb = KV[r, 0].astype(F32) * SCALE
        block_of = rows2 // MASK_BLOCK + per * r
        for h in range(2):
            mine = (lanes2 < HALF) if h == 0 else (lanes2 >= HALF)
            hot = (lanes2 == block_of + HALF * (1 - h)).astype(F32)
            K2[r, h * F : (h + 1) * F] = jnp.where(mine, kb, hot).astype(BF16)
        KT[r] = kb.T.astype(BF16)

    build(0)
    for d in range(1, NT):
        source = lax.rem(t + NT - d, NT)
        remote(lrow, L.at[source], as_.at[1, d], ar.at[1, d], tpeer(d)).wait_recv()
    lane3 = lax.broadcasted_iota(jnp.int32, (NT, R, COLS), 2)
    row3 = lax.broadcasted_iota(jnp.int32, (NT, R, COLS), 1)
    lens = jnp.broadcast_to(L[:, 0:1, :], (NT, R, COLS))
    lanes = lax.broadcasted_iota(jnp.int32, (1, 1, COLS), 2)
    first = ((lax.rem(x + lanes // per, NX) * NZ + z) * per + lax.rem(lanes, per)) * MASK_BLOCK
    first = jnp.where(lanes < per * NX, first, -1).astype(F32)

    def mask_slot(p, rel):
        pick = lax.rem(z + rel, NZ) * R + row3
        column = jnp.sum(jnp.where(lane3 == pick, lens, 0.0), axis=2, keepdims=True)
        M[p] = jnp.where(first >= column, HIDDEN, 0.0).reshape(TOK, COLS).T[0:HALF].astype(BF16)

    for p in range(NZ):
        mask_slot(p, REL[p])

    for d in range(1, NT):
        source = lax.rem(t + NT - d, NT)
        remote(QGI.at[0], QG.at[0, :, source], as_.at[0, d], ar.at[0, d], tpeer(d)).wait_recv()

    arrived(1)

    masks = [m.astype(BF16) for m in head]

    def block(ref, c, which):
        return ref[pl.ds(2 * c, 2), which].reshape(CH, COLS)

    def pass_on():
        for slot in (2, 3, 4):
            arrived(slot)
        for copy in onward:
            copy.start()

    def pass1(c, fresh):
        qt, gt = block(QG, c, 0).T, block(QG, c, 1).T
        mt = jnp.concatenate([M[2 * c], M[2 * c + 1]], axis=1)
        none = jnp.zeros((HALF, CH), BF16)
        qts = [jnp.concatenate([qt[0:HALF], mt], axis=0), jnp.concatenate([mt, qt[HALF:COLS]], axis=0)]
        gts = [jnp.concatenate([gt[0:HALF], none], axis=0), jnp.concatenate([none, gt[HALF:COLS]], axis=0)]
        for h in range(2):
            rows = slice(h * CH, (h + 1) * CH)
            Q2[c, rows] = block(QG, c, 0) * masks[h]
            G2[c, rows] = block(QG, c, 1) * masks[h]
        found = [[] for _ in range(4)]

        def products(r, h):
            rows = slice(h * F, (h + 1) * F)
            W[c, r, h] = jnp.dot(K2[r, rows], qts[h], preferred_element_type=F32)
            G[c, r, h] = jnp.dot(KV[r, 1], gts[h], preferred_element_type=F32)

        def reduce(r, h):
            for half in range(2):
                piece = slice(half * TOK, (half + 1) * TOK)
                sc = W[c, r, h, :, piece]
                m = jnp.max(sc, axis=0, keepdims=True)
                w = jnp.exp(sc - m)
                W[c, r, h, :, piece] = w
                MR[c, 2 * r + h : 2 * r + h + 1, piece] = m
                l = jnp.sum(w, axis=0, keepdims=True)
                found[2 * h + half].append((m, l, jnp.sum(w * G[c, r, h, :, piece], axis=0, keepdims=True)))

        order = [(r, h) for r in (0, 1, NX - 1, NX // 2) for h in range(2)]
        products(*order[0])
        for now, later in zip(order, order[1:] + [None]):
            wait = fresh and later is not None and later[1] == 0
            if wait:
                reduce(*now)
                r = later[0]
                if r == NX // 2:
                    pass_on()
                for part in range(2):
                    remote(KV.at[0, part], KV.at[r, part], cs.at[part, r], cr.at[part, r], xpeer(r)).wait_recv()
                build(r)
            if later is not None:
                products(*later)
            if not wait:
                reduce(*now)
        for h in range(2):
            for half in range(2):
                top = found[2 * h + half][0][0]
                for m, _, _ in found[2 * h + half][1:]:
                    top = jnp.maximum(top, m)
                total = jnp.zeros_like(top)
                term = jnp.zeros_like(top)
                for m, l, tt in found[2 * h + half]:
                    a = jnp.exp(m - top)
                    total += a * l
                    term += a * tt
                row = 2 * half + h
                SM[c, row : row + 1, :] = top + jnp.log(total)
                SM[c, 4 + row : 5 + row, :] = term / total
        for d in REL[1:]:
            remote(SM.at[c], SR.at[NZ - d, c], ds_.at[d], dr.at[NZ - d], zpeer(d)).start()

        @pl.when(c == 1)
        def _():
            arrived(5)

        @pl.when(c == 2)
        def _():
            arrived(6)
            for part in range(2):
                onward[3 - part].wait_recv()

        return 0

    pass1(0, True)
    for c in range(1, NC):
        pass1(c, False)

    for d in range(1, NZ):
        remote(SM, SR.at[d], ds_.at[d], dr.at[d], zpeer(d)).wait_recv()

    def combine(p):
        parts, terms = [], []
        for d in range(NZ):
            theirs = POS[(REL[p] - d) % NZ]
            ref = SM if d == 0 else SR.at[d]
            row = 2 * (theirs % 2)
            parts.append(ref[theirs // 2, row : row + 2, :])
            terms.append(ref[theirs // 2, 4 + row : 6 + row, :])
        top = parts[0]
        for part in parts[1:]:
            top = jnp.maximum(top, part)
        total = jnp.zeros_like(top)
        term = jnp.zeros_like(top)
        for part, other in zip(parts, terms):
            weight = jnp.exp(part - top)
            total += weight
            term += weight * other
        CF[:, p * TOK : (p + 1) * TOK] = top + jnp.log(total)
        RT[:, p * TOK : (p + 1) * TOK] = term / total


    def make(c, r):
        piece = slice(c * CH, (c + 1) * CH)
        for h in range(2):
            cf = jnp.exp(MR[c, 2 * r + h : 2 * r + h + 1, :] - CF[h : h + 1, piece])
            term = RT[h : h + 1, piece]
            for lo in range(0, F, 64):
                rows = slice(lo, lo + 64)
                p = W[c, r, h, rows, :] * cf
                PS[c, r, rows, h * CH : (h + 1) * CH] = p.astype(BF16)
                GS[c, r, rows, h * CH : (h + 1) * CH] = (p * (G[c, r, h, rows, :] - term)).astype(BF16)

    def use(c, r):
        first = c == NC - 1
        dv = jnp.dot(PS[c, r], G2[c], preferred_element_type=F32)
        dk = jnp.dot(GS[c, r], Q2[c], preferred_element_type=F32)
        DV[r] = dv if first else DV[r] + dv
        DK[r] = dk if first else DK[r] + dk
        for h in range(2):
            out = slice(h * HALF, (h + 1) * HALF)
            dq = jnp.dot(KT[r, out], GS[c, r, :, h * CH : (h + 1) * CH], preferred_element_type=F32)
            DQT[c, out] = dq if r == ORDER[0] else DQT[c, out] + dq

    def send_dq(p):
        d = REL[p]
        for i in range(NT):
            if p > 0 or i > 0:
                there = lax.rem(t + i, NT)
                remote(
                    DQS.at[p, there], DQR.at[(NZ - d) % NZ, t],
                    es.at[d] if d else gs.at[i], er.at[(NZ - d) % NZ] if d else gr.at[i],
                    (there, x * NZ + lax.rem(z + d, NZ)),
                ).start()

    def done_dq(c):
        DQS[2 * c : 2 * c + 2] = DQT[c].T.astype(BF16).reshape(2, NT, R, COLS)
        send_dq(2 * c + 1)
        send_dq(2 * c)

    def done_kv(r):
        DKVS[r, 0] = DK[r].astype(BF16)
        DKVS[r, 1] = DV[r].astype(BF16)
        sent.append(remote(DKVS.at[r], DKVR.at[NX - r], fs.at[r], fr.at[NX - r], xpeer(r)))
        sent[-1].start()

    ORDER = [NX // 2] + [i for i in range(1, NX) if i != NX // 2] + [0]
    steps = [(c, r) for c in range(NC - 1, 1, -1) for r in ORDER] + [(c, r) for r in ORDER for c in (1, 0)]
    early = list(sent)
    sent.clear()
    combine(NZ - 2)
    combine(NZ - 1)
    make(*steps[0])
    for p in range(NZ - 2):
        combine(p)
    for (c, r), later in zip(steps, steps[1:] + [None]):
        if later is not None:
            make(*later)
        use(c, r)
        if r == ORDER[-1]:
            done_dq(c)
        if c == 0 and r > 0:
            done_kv(r)
    DQR[0, pl.ds(t, 1)] = DQS[0, pl.ds(t, 1)]

    for copy in early:
        copy.wait_send()
    for slot in range(1, 5):
        remote(QGI, QG.at[slot], bs.at[0, slot], br.at[0, slot], zpeer(1)).wait_send()
    for copy in onward:
        copy.wait_send()
    for d in range(1, NZ):
        remote(SM, SR.at[NZ - d], ds_.at[d], dr.at[NZ - d], zpeer(d)).wait_send()
    for d in range(1, NX):
        remote(DKVS.at[d], DKVR.at[d], fs.at[d], fr.at[d], xpeer(d)).wait_recv()
    dk, dv = DK[0], DV[0]
    for d in range(1, NX):
        dk += DKVR[d, 0].astype(F32)
        dv += DKVR[d, 1].astype(F32)
    dk_out[...] = dk * SCALE
    dv_out[...] = dv

    for d in range(1, NT):
        source = lax.rem(t + NT - d, NT)
        remote(DQS.at[0, 0], DQR.at[0, source], gs.at[d], gr.at[d], tpeer(d)).wait_recv()
    for d in range(1, NZ):
        remote(DQS.at[POS[d]], DQR.at[d], es.at[d], er.at[d], zpeer(d)).wait_recv()
    for i in range(NT):
        dq = DQR[0, i].astype(F32)
        for d in range(1, NZ):
            dq += DQR[d, i].astype(F32)
        dq_out[:, i * COLS : (i + 1) * COLS] = dq
    for copy in sent:
        copy.wait_send()
    for d in range(1, NT):
        remote(DQS.at[0, 0], DQR.at[0, 0], gs.at[d], gr.at[d], tpeer(d)).wait_send()
    for d in range(1, NZ):
        remote(DQS.at[POS[d]], DQR.at[d], es.at[d], er.at[d], zpeer(d)).wait_send()


def body(queries, keys, values, grad_out, read_len, *, NT):
    R, D = queries.shape
    F = keys.shape[0]
    TOK, CH, NC = NT * R, 2 * NT * R, NZ // 2
    lens = read_len.reshape(NX, NZ * R)
    hbm = pl.BlockSpec(memory_space=pltpu.HBM)
    vmem = pl.BlockSpec(memory_space=pltpu.VMEM)
    dma = pltpu.SemaphoreType.DMA
    V = pltpu.VMEM
    return pl.pallas_call(
        lambda *refs: kernel(NT, *refs),
        out_shape=(V((R, D), F32), V((F, COLS), F32), V((F, COLS), F32)),
        in_specs=[hbm] * 5,
        out_specs=(vmem, vmem, vmem),
        scratch_shapes=[
            V((NX, NZ * R), jnp.int32),
            V((R, D), BF16),
            V((R, D), BF16),
            V((NT, 2, R, COLS), BF16),
            V((NZ, 2, NT, R, COLS), BF16),
            V((NX, 2, F, COLS), BF16),
            V((NT, 8, COLS), F32),
            V((8, COLS), F32),
            V((NZ, HALF, TOK), BF16),
            V((NX, 2 * F, COLS), BF16),
            V((NX, COLS, F), BF16),
            V((NC, NX, 2, F, CH), F32),
            V((NC, NX, 2, F, CH), F32),
            V((NC, 2 * NX, CH), F32),
            V((NC, 8, TOK), F32),
            V((NZ, NC, 8, TOK), F32),
            V((2, NZ * TOK), F32),
            V((2, NZ * TOK), F32),
            V((NC, NX, F, 2 * CH), BF16),
            V((NC, NX, F, 2 * CH), BF16),
            V((NC, 2 * CH, COLS), BF16),
            V((NC, 2 * CH, COLS), BF16),
            V((NC, COLS, CH), F32),
            V((NZ, NT, R, COLS), BF16),
            V((NZ, NT, R, COLS), BF16),
            V((NX, F, COLS), F32),
            V((NX, F, COLS), F32),
            V((NX, 2, F, COLS), BF16),
            V((NX, 2, F, COLS), BF16),
            dma((5,)),
            dma((2, NT)), dma((2, NT)),
            dma((2, NZ)), dma((2, NZ)),
            dma((2, NX)), dma((2, NX)),
            dma((NZ,)), dma((NZ,)),
            dma((NZ,)), dma((NZ,)),
            dma((NX,)), dma((NX,)),
            dma((NT,)), dma((NT,)),
        ],
        compiler_params=pltpu.CompilerParams(
            collective_id=0, has_side_effects=True, vmem_limit_bytes=62 * 1024 * 1024
        ),
    )(queries, keys, values, grad_out, lens)


def solution(mesh):
    NT = mesh.shape["tgt"]
    return jax.shard_map(
        lambda *args: body(*args, NT=NT),
        mesh=mesh,
        in_specs=(
            P(("tgt", "src"), None),
            P("src", None),
            P("src", None),
            P(("tgt", "src"), None),
            P("tgt"),
        ),
        out_specs=(P(("tgt", "src"), None), P("src", "tgt"), P("src", "tgt")),
        check_vma=False,
    )
```
